32 devices in a mesh: dp: 4 (over z), ctx: 4 (over x, core), fsdp: 2 (over y).
Axes of the slice: x: 2, y: 2, z: 4, core: 2. Of those that a mesh axis runs over, the one named last changes fastest.
Arguments:
- hidden: bfloat16 [8, 1024, 2048], P(('dp', 'fsdp'), 'ctx'), may hold values from -6 to 6
- segment_ids: int32 [8, 1024], P(('dp', 'fsdp')), may hold values from 0 to 4, as said below
- positions: int32 [8, 1024], P(('dp', 'fsdp')), may hold values from 0 to 799, as said below
- attn_gain: bfloat16 [2048], P(('dp', 'ctx', 'fsdp')), may hold values from 0.099609375 to 1.8984375
- w_query: bfloat16 [2048, 2048], P(('dp', 'fsdp'), 'ctx'), may hold values from -0.015625 to 0.015625
- w_key: bfloat16 [2048, 2048], P(('dp', 'fsdp'), 'ctx'), may hold values from -0.125 to 0.125
- w_value: bfloat16 [2048, 2048], P(('dp', 'fsdp'), 'ctx'), may hold values from -0.125 to 0.125
- w_attn_out: bfloat16 [2048, 2048], P('ctx', ('dp', 'fsdp')), may hold values from -1.5 to 1.5
- rel_table: bfloat16 [1024], P(('dp', 'ctx', 'fsdp')), may hold values from -4 to 4
- ffn_gain: bfloat16 [2048], P(('dp', 'ctx', 'fsdp')), may hold values from 0.099609375 to 1.8984375
- w_gate: bfloat16 [2048, 5120], P(('dp', 'fsdp'), 'ctx'), may hold values from -0.125 to 0.125
- w_up: bfloat16 [2048, 5120], P(('dp', 'fsdp'), 'ctx'), may hold values from -0.125 to 0.125
- w_down: bfloat16 [5120, 2048], P('ctx', ('dp', 'fsdp')), may hold values from -0.078125 to 0.078125
- cotangent: bfloat16 [8, 1024, 2048], P(('dp', 'fsdp'), 'ctx'), may hold values from -6 to 6
Outputs:
- output: bfloat16 [8, 1024, 2048], P(('dp', 'fsdp'), 'ctx')
- grad_hidden: float32 [8, 1024, 2048], P(('dp', 'fsdp'), 'ctx')
- grad_attn_gain: float32 [2048], P(('dp', 'ctx', 'fsdp'))
- grad_query: float32 [2048, 2048], P(('dp', 'fsdp'), 'ctx')
- grad_key: float32 [2048, 2048], P(('dp', 'fsdp'), 'ctx')
- grad_value: float32 [2048, 2048], P(('dp', 'fsdp'), 'ctx')
- grad_attn_out: float32 [2048, 2048], P('ctx', ('dp', 'fsdp'))
- bias_table_gradient: float32 [1024], P(('dp', 'ctx', 'fsdp'))
- grad_ffn_gain: float32 [2048], P(('dp', 'ctx', 'fsdp'))
- grad_gate: float32 [2048, 5120], P(('dp', 'fsdp'), 'ctx')
- grad_up: float32 [2048, 5120], P(('dp', 'fsdp'), 'ctx')
- grad_down: float32 [5120, 2048], P('ctx', ('dp', 'fsdp'))
The draws below stay inside these ranges and needn't reach their ends.
Inputs may be any that keep to these rules, and one draw needn't show every extreme that they name: `segment_ids`: within each sequence the ids number its documents from 0 and never fall. One document of each sequence, its first or its second, holds exactly 800 tokens; every other document holds 60 to 800 tokens, except the last one, which the end of the sequence may cut short. `positions`: 0 at a document's first token and rising by one along it, consistent with segment_ids.
All inputs are finite; a program needn't handle non-finite values.
Results may differ from the reference program's by a relative error of at most 0.018.
Values may be sent and summed in bfloat16 or wider, within the bound.
A program may use at most 256 MiB of HBM per device.

```python
from functools import partial
import jax
import jax.numpy as jnp
from jax import lax

D = 2048
H = 32
DH = 64
FF = 5120
NB = 32
LEN = 1024
DOC_MOST = 800
DOC_LEAST = 60
SEQS = 8


def document_layout(key):
    doc_count = LEN // DOC_LEAST + 2
    sequence_keys = jax.random.split(jax.random.fold_in(key, 5), SEQS)
    sequence_numbers = jnp.arange(SEQS, dtype=jnp.int32)

    def one_sequence(sequence_key, sequence_number):
        forced = sequence_number == 0
        lengths = jax.random.randint(jax.random.fold_in(sequence_key, 1), (doc_count,), DOC_LEAST, DOC_MOST + 1)
        lengths = jnp.where(forced, DOC_LEAST, lengths).astype(jnp.int32)
        long_slot = jax.random.randint(jax.random.fold_in(sequence_key, 2), (), 0, 2)
        long_slot = jnp.where(forced, 0, long_slot)
        first_length = jax.random.randint(jax.random.fold_in(sequence_key, 3), (), DOC_LEAST, LEN - DOC_MOST + 1)
        lengths = lengths.at[0].set(jnp.where(long_slot == 0, DOC_MOST, first_length))
        lengths = lengths.at[1].set(jnp.where(long_slot == 1, DOC_MOST, lengths[1]))
        doc_ends = jnp.cumsum(lengths)
        token_index = jnp.arange(LEN, dtype=jnp.int32)
        finished = doc_ends[None, :] <= token_index[:, None]
        segment_number = jnp.sum(finished.astype(jnp.int32), axis=1)
        doc_begin = jnp.sum(jnp.where(finished, lengths[None, :], 0), axis=1)
        return (segment_number.astype(jnp.int32), (token_index - doc_begin).astype(jnp.int32))
    return jax.vmap(one_sequence)(sequence_keys, sequence_numbers)


def draw_segment_ids(key, part):
    return document_layout(key)[0]


def draw_positions(key, part):
    return document_layout(key)[1]


def levels(rng, shape, cuts, least, top_value):
    def one(dim, parts):
        steps = jax.random.uniform(jax.random.fold_in(jax.random.fold_in(rng, 6), dim), (parts,), jnp.float32, least / len(cuts), top_value / len(cuts))
        return jnp.repeat(jnp.exp(steps), shape[dim] // parts).reshape((-1,) + (1,) * (len(shape) - dim - 1))

    loudness = one(*cuts[0])
    for cut in cuts[1:]:
        loudness = loudness * one(*cut)
    return loudness


def noise(stream_key, dims, deviation, limit, shards=(), kind=jnp.bfloat16):
    loudness = levels(stream_key, dims, shards, -0.22, 0.18) if shards else 1.0
    values = jax.random.normal(stream_key, dims, jnp.float32) * deviation * loudness
    return jnp.minimum(jnp.maximum(values, -limit), limit).astype(kind)


def setup_inputs(seed: int = 0) -> dict:
    splits = jax.random.split(jax.random.key(seed), 15)
    return {
        "hidden": noise(splits[0], (SEQS, LEN, D), 1.0, 6.0, ((0, 8), (1, 4))),
        "segment_ids": draw_segment_ids(jax.random.fold_in(splits[14], 71), 0),
        "positions": draw_positions(jax.random.fold_in(splits[14], 71), 0),
        "attn_gain": jnp.clip(1.0 + 0.18 * jax.random.normal(splits[3], (D,), jnp.float32), 0.099609375, 1.8984375).astype(jnp.bfloat16),
        "w_query": noise(splits[4], (D, H * DH), (D * DH) ** -0.5, 0.015625, ((0, 8), (1, 4))),
        "w_key": noise(splits[5], (D, H * DH), D ** -0.5, 0.125, ((0, 8), (1, 4))),
        "w_value": noise(splits[6], (D, H * DH), D ** -0.5, 0.125, ((0, 8), (1, 4))),
        "w_attn_out": noise(splits[7], (H * DH, D), (H * DH // 128) ** -0.5, 1.5, ((0, 4), (1, 8))),
        "rel_table": noise(splits[8], (NB * H,), 1.0, 4.0, ((0, 32),)),
        "ffn_gain": jnp.clip(1.0 + 0.18 * jax.random.normal(splits[9], (D,), jnp.float32), 0.099609375, 1.8984375).astype(jnp.bfloat16),
        "w_gate": noise(splits[10], (D, FF), D ** -0.5, 0.125, ((0, 8), (1, 4))),
        "w_up": noise(splits[11], (D, FF), D ** -0.5, 0.125, ((0, 8), (1, 4))),
        "w_down": noise(splits[12], (FF, D), FF ** -0.5, 0.078125, ((0, 4), (1, 8))),
        "cotangent": noise(splits[13], (SEQS, LEN, D), 1.0, 6.0, ((0, 8), (1, 4))),
    }


EPSILON = 1e-06
THRESHOLDS = (12, 16, 23, 32, 46, 64, 91)
MASKED = -1e+30
PRECISION_TOP = lax.Precision.HIGHEST

@jax.custom_vjp
def low(v):
    return lax.optimization_barrier(v.astype(jnp.bfloat16)).astype(jnp.float32)

@jax.custom_vjp
def low_back(v):
    return v

def low_keep(v):
    return (low(v), None)

def low_pass(kept, grad):
    return (grad,)

def back_keep(v):
    return (v, None)

def back_low(kept, grad):
    return (low(grad),)
low.defvjp(low_keep, low_pass)
low_back.defvjp(back_keep, back_low)

def rms_norm(values, gain):
    return values * lax.rsqrt(lax.optimization_barrier(jnp.mean(values * values, axis=-1, keepdims=True)) + EPSILON) * gain

def gelu_tanh(values):
    return 0.5 * values * (1.0 + jnp.tanh(0.7978845608028654 * (values + 0.044715 * values * values * values)))

def bucket_table(query_pos, key_pos):
    relative = key_pos[None, :] - query_pos[:, None]
    distance = jnp.abs(relative)
    log_bucket = 8 + sum(((distance >= threshold).astype(jnp.int32) for threshold in THRESHOLDS))
    bucket = jnp.where(distance < 8, distance, log_bucket)
    return (bucket + 16 * (relative > 0).astype(jnp.int32)).astype(jnp.int32)

def project(normalized_rows, weight_matrix):
    return jnp.einsum('nwh,hj->nwj', normalized_rows, weight_matrix, precision=PRECISION_TOP)

def attend_sequence(operands, table):
    query_rows, key_rows, value_rows, segment_row, position_row = operands
    buckets = bucket_table(position_row, position_row)
    bias = jnp.transpose(table[buckets], (2, 0, 1))
    attention_scores = jnp.einsum('ihd,jhd->hij', query_rows, key_rows, precision=PRECISION_TOP) + bias
    attention_scores = low_back(attention_scores)
    same_doc = segment_row[:, None] == segment_row[None, :]
    attention_scores = jnp.where(same_doc[None], attention_scores, MASKED)
    row_peak = lax.optimization_barrier(jnp.max(attention_scores, axis=-1, keepdims=True))
    lifted = jnp.exp(attention_scores - row_peak)
    weights = low(lifted / lax.optimization_barrier(jnp.sum(lifted, axis=-1, keepdims=True)))
    return jnp.einsum('hij,jhd->ihd', weights, value_rows, precision=PRECISION_TOP)

def layer(hidden, attn_gain, w_query, w_key, w_value, w_attn_out, rel_table, ffn_gain, w_gate, w_up, w_down, segment_ids, positions):
    seq_count = hidden.shape[0]
    sequence_length = hidden.shape[1]
    normalized_rows = low(rms_norm(hidden, attn_gain))
    queries = low(low_back(project(normalized_rows, w_query))).reshape(seq_count, sequence_length, H, DH)
    key_rows = low(low_back(project(normalized_rows, w_key))).reshape(seq_count, sequence_length, H, DH)
    value_rows = low(low_back(project(normalized_rows, w_value))).reshape(seq_count, sequence_length, H, DH)
    table = rel_table.reshape(NB, H)
    attended = lax.map(jax.checkpoint(partial(attend_sequence, table=table)), (queries, key_rows, value_rows, segment_ids, positions))
    attended = low(low_back(attended.reshape(seq_count, sequence_length, H * DH)))
    residual = hidden + low_back(project(attended, w_attn_out))
    normed_ffn = low(rms_norm(residual, ffn_gain))
    gate_value = low_back(project(normed_ffn, w_gate))
    up_value = low_back(project(normed_ffn, w_up))
    ffn_hidden = low(gelu_tanh(gate_value) * up_value)
    return residual + low_back(project(ffn_hidden, w_down))

def reference(hidden, segment_ids, positions, attn_gain, w_query, w_key, w_value, w_attn_out, rel_table, ffn_gain, w_gate, w_up, w_down, cotangent):
    params = (hidden, attn_gain, w_query, w_key, w_value, w_attn_out, rel_table, ffn_gain, w_gate, w_up, w_down)
    floats = [item.astype(jnp.float32) for item in params]

    def wrapped(*operands):
        return layer(*operands, segment_ids, positions)
    result, pullback = jax.vjp(wrapped, *floats)
    grads = pullback(cotangent.astype(jnp.float32))
    return (result.astype(jnp.bfloat16), grads[0], grads[1], grads[2], grads[3], grads[4], grads[5], grads[6], grads[7], grads[8], grads[9], grads[10])
```

```python
import functools

import jax
import jax.numpy as jnp
from jax import lax
from jax.experimental import pallas as pl
from jax.experimental.pallas import tpu as pltpu
from jax.sharding import PartitionSpec as P

H = 32
DH = 64
NB = 32
EPSILON = 1e-06
THRESHOLDS = (12, 16, 23, 32, 46, 64, 91)
MASKED = -1e30
BF = jnp.bfloat16
F32 = jnp.float32
ANY = pl.BlockSpec(memory_space=pl.ANY)
VM = pl.BlockSpec(memory_space=pltpu.VMEM)
MESH = pl.DeviceIdType.MESH
DMA = pltpu.SemaphoreType.DMA


class Place:
    def __init__(self):
        self.z = lax.axis_index("dp")
        self.c = lax.axis_index("ctx")
        self.y = lax.axis_index("fsdp")
        self.x = self.c // 2
        self.k = self.c % 2

    def device(self, z=None, x=None, k=None, y=None):
        z = self.z if z is None else z
        x = self.x if x is None else x
        k = self.k if k is None else k
        y = self.y if y is None else y
        return {"dp": z, "ctx": x * 2 + k, "fsdp": y}

    def x_peer(self):
        return self.device(x=1 - self.x)

    def y_peer(self):
        return self.device(y=1 - self.y)

    def core_peer(self):
        return self.device(k=1 - self.k)


def block_of(x, k, y):
    return y * 4 + x * 2 + k


def remote(src, dst, send_sem, recv_sem, device):
    return pltpu.make_async_remote_copy(
        src_ref=src,
        dst_ref=dst,
        send_sem=send_sem,
        recv_sem=recv_sem,
        device_id=device,
        device_id_type=MESH,
    )


def greet(devices):
    barrier = pltpu.get_barrier_semaphore()
    for device in devices:
        pl.semaphore_signal(barrier, inc=1, device_id=device, device_id_type=MESH)
    pl.semaphore_wait(barrier, len(devices))


class ActGather:
    def __init__(self, me, own, out, send, recv, local):
        self.me, self.own, self.out = me, own, out
        self.send, self.recv, self.local = send, recv, local
        self.rows = own.shape[0]
        self.half = self.rows // 2

    def part(self, ref, block, h):
        return ref.at[block, pl.ds(h * self.half, self.half)]

    def copy(self, i):
        me = self.me
        x, k, y = me.x, me.k, me.y
        own = block_of(x, k, y)
        if i == 0:
            src, dst, dev = self.own.at[pl.ds(0, self.half)], self.part(self.out, own, 0), me.x_peer()
        elif i == 1:
            src, dst, dev = self.own.at[pl.ds(self.half, self.half)], self.part(self.out, own, 1), me.y_peer()
        elif i == 2:
            src, dst, dev = self.own.at[pl.ds(0, self.half)], self.part(self.out, own, 0), me.y_peer()
        elif i == 3:
            b = block_of(1 - x, k, y)
            src, dst, dev = self.part(self.out, b, 0), self.part(self.out, b, 0), me.y_peer()
        elif i == 4:
            src, dst, dev = self.own.at[pl.ds(self.half, self.half)], self.part(self.out, own, 1), me.x_peer()
        elif i == 5:
            b = block_of(x, k, 1 - y)
            src, dst, dev = self.part(self.out, b, 1), self.part(self.out, b, 1), me.x_peer()
        elif i == 6:
            src, dst, dev = self.own, self.out.at[own], me.core_peer()
        else:
            px, py, h = ((1, 0, 0), (0, 1, 1), (0, 1, 0), (1, 1, 0), (1, 0, 1), (1, 1, 1))[i - 7]
            b = block_of(1 - x if px else x, k, 1 - y if py else y)
            src, dst, dev = self.part(self.out, b, h), self.part(self.out, b, h), me.core_peer()
        return remote(src, dst, self.send.at[i], self.recv.at[i], dev)

    def start(self):
        for i in (0, 1, 2, 4, 6):
            self.copy(i).start()
        own = block_of(self.me.x, self.me.k, self.me.y)
        pltpu.make_async_copy(self.own, self.out.at[own], self.local).start()

    def forward(self):
        self.copy(0).wait_recv()
        self.copy(3).start()
        self.copy(7).start()
        self.copy(1).wait_recv()
        self.copy(5).start()
        self.copy(8).start()

    def forward_core(self):
        for i in (2, 4, 3, 5):
            self.copy(i).wait_recv()
            self.copy(i + 7).start()

    def finish(self):
        for i in range(6, 13):
            self.copy(i).wait_recv()
        for i in range(13):
            self.copy(i).wait_send()
        own = block_of(self.me.x, self.me.k, self.me.y)
        pltpu.make_async_copy(self.own, self.out.at[own], self.local).wait()


def gather_sems():
    return [DMA((13,)), DMA((13,)), DMA]


class ActReduce:
    def __init__(self, me, part, core_in, mine, a_y, b_x, a_x, b_y, send, recv, local):
        self.me, self.part, self.core_in, self.mine = me, part, core_in, mine
        self.a_y, self.b_x, self.a_x, self.b_y = a_y, b_x, a_x, b_y
        self.send, self.recv, self.local = send, recv, local
        self.half = part.shape[1] // 2

    def order(self):
        x, y = self.me.x, self.me.y
        return ((1 - x, 1 - y), (x, 1 - y), (1 - x, y), (x, y))

    def core_copy(self, i):
        me = self.me
        ox, oy = self.order()[i]
        return remote(
            self.part.at[block_of(ox, 1 - me.k, oy)],
            self.core_in.at[oy * 2 + ox],
            self.send.at[i],
            self.recv.at[i],
            me.core_peer(),
        )

    def local_copy(self, i):
        ox, oy = self.order()[i]
        return pltpu.make_async_copy(
            self.part.at[block_of(ox, self.me.k, oy)], self.mine.at[oy * 2 + ox], self.local.at[i]
        )

    def start(self):
        for i in range(4):
            self.core_copy(i).start()
            self.local_copy(i).start()

    def rows(self, h):
        return pl.ds(h * self.half, self.half)

    def add(self, slot, h, extra=None):
        steps = self.half // 16

        def body(i, carry):
            r = pl.ds(pl.multiple_of(h * self.half + i * 16, 16), 16)
            total = self.mine[slot, r, :].astype(F32) + self.core_in[slot, r, :].astype(F32)
            if extra is not None:
                total = total + extra[pl.ds(pl.multiple_of(i * 16, 16), 16), :].astype(F32)
            self.mine[slot, r, :] = total.astype(BF)
            return carry

        lax.fori_loop(0, steps, body, 0)

    def copies(self):
        me = self.me
        x, y = me.x, me.y
        out = {}
        out["ay0"] = remote(self.mine.at[(1 - y) * 2 + (1 - x), self.rows(0)], self.a_y.at[0], self.send.at[4], self.recv.at[4], me.y_peer())
        out["ay1"] = remote(self.mine.at[(1 - y) * 2 + x, self.rows(0)], self.a_y.at[1], self.send.at[5], self.recv.at[5], me.y_peer())
        out["bx0"] = remote(self.mine.at[(1 - y) * 2 + (1 - x), self.rows(1)], self.b_x.at[0], self.send.at[6], self.recv.at[6], me.x_peer())
        out["bx1"] = remote(self.mine.at[y * 2 + (1 - x), self.rows(1)], self.b_x.at[1], self.send.at[7], self.recv.at[7], me.x_peer())
        out["ax"] = remote(self.mine.at[y * 2 + (1 - x), self.rows(0)], self.a_x, self.send.at[8], self.recv.at[8], me.x_peer())
        out["by"] = remote(self.mine.at[(1 - y) * 2 + x, self.rows(1)], self.b_y, self.send.at[9], self.recv.at[9], me.y_peer())
        return out

    def run(self):
        x, y = self.me.x, self.me.y
        c = self.copies()
        self.core_copy(0).wait_recv()
        self.local_copy(0).wait()
        self.add((1 - y) * 2 + (1 - x), 0)
        c["ay0"].start()
        self.add((1 - y) * 2 + (1 - x), 1)
        c["bx0"].start()
        self.core_copy(1).wait_recv()
        self.local_copy(1).wait()
        self.add((1 - y) * 2 + x, 0)
        c["ay1"].start()
        self.core_copy(2).wait_recv()
        self.local_copy(2).wait()
        self.add(y * 2 + (1 - x), 1)
        c["bx1"].start()
        c["ay0"].wait_recv()
        self.add(y * 2 + (1 - x), 0, self.a_y.at[0])
        c["ax"].start()
        c["bx0"].wait_recv()
        self.add((1 - y) * 2 + x, 1, self.b_x.at[0])
        c["by"].start()
        self.core_copy(3).wait_recv()
        self.local_copy(3).wait()
        for name in ("ay1", "bx1", "ax", "by"):
            c[name].wait_recv()

    def total(self, h, i):
        slot = self.me.y * 2 + self.me.x
        r = pl.ds(pl.multiple_of(h * self.half + i * 16, 16), 16)
        q = pl.ds(pl.multiple_of(i * 16, 16), 16)
        total = self.mine[slot, r, :].astype(F32) + self.core_in[slot, r, :].astype(F32)
        if h == 0:
            return total + self.a_y[1, q, :].astype(F32) + self.a_x[q, :].astype(F32)
        return total + self.b_x[1, q, :].astype(F32) + self.b_y[q, :].astype(F32)

    def finish(self):
        for i in range(4):
            self.core_copy(i).wait_send()
        for copy in self.copies().values():
            copy.wait_send()


def reduce_scratch(rows, width):
    half = rows // 2
    return [
        pltpu.VMEM((4, rows, width), BF),
        pltpu.VMEM((4, rows, width), BF),
        pltpu.VMEM((2, half, width), BF),
        pltpu.VMEM((2, half, width), BF),
        pltpu.VMEM((half, width), BF),
        pltpu.VMEM((half, width), BF),
        DMA((10,)),
        DMA((10,)),
        DMA((4,)),
    ]


def first_kernel(
    n, wq, wk, wv, wo, wg, wu, wd, xin, small, seg,
    wqkv, wof, wgu_y, wd_y, xall, smalls, segs,
    y_send, y_recv, y_local, r_send, l_send, z_recv,
    ag_send, ag_recv, ag_local, s_send, s_recv, s2_send, s2_recv, s_local,
):
    me = Place()
    z, y = me.z, me.y
    rows = wq.shape[0]
    heads = wq.shape[1] // 2
    hid = wg.shape[1] // 2
    group = [me.device(x=ox, k=ok, y=oy) for ox in (me.x, 1 - me.x) for ok in (me.k, 1 - me.k) for oy in (me.y, 1 - me.y)][1:]
    others = [me.device(z=lax.rem(z + s, n)) for s in range(1, n)]
    greet(group + others)

    piece = z * 2 + y
    row = pl.ds(pl.multiple_of(piece * rows, rows), rows)

    def y_copies(yh):
        col = pl.ds(pl.multiple_of(yh * heads, heads), heads)
        fcol = pl.ds(pl.multiple_of(yh * hid, hid), hid)
        sub = pl.ds(pl.multiple_of(y * rows, rows), rows)
        return [
            (wq.at[:, col], wqkv.at[row, pl.ds(0, heads)]),
            (wk.at[:, col], wqkv.at[row, pl.ds(heads, heads)]),
            (wv.at[:, col], wqkv.at[row, pl.ds(2 * heads, heads)]),
            (wo.at[col, :], wof.at[:, row]),
            (wg.at[:, fcol], wgu_y.at[sub, pl.ds(0, hid)]),
            (wu.at[:, fcol], wgu_y.at[sub, pl.ds(hid, hid)]),
            (wd.at[fcol, :], wd_y.at[:, sub]),
        ]

    sends = [
        remote(src, dst, y_send.at[i], y_recv.at[i], me.y_peer())
        for i, (src, dst) in enumerate(y_copies(1 - y))
    ]
    keeps = [
        pltpu.make_async_copy(src, dst, y_local.at[i]) for i, (src, dst) in enumerate(y_copies(y))
    ]
    me_small = z * 8 + me.c * 2 + y
    small_local = pltpu.make_async_copy(small, smalls.at[me_small], s_local.at[0])
    seg_local = pltpu.make_async_copy(seg, segs.at[y], s_local.at[1])
    small_sends = [
        remote(small, smalls.at[me_small], s_send.at[i], s_recv.at[i], dev) for i, dev in enumerate(group)
    ]
    seg_send = remote(seg, segs.at[y], s_send.at[7], s_recv.at[7], me.y_peer())
    for i in range(4):
        sends[i].start()
        keeps[i].start()
    small_local.start()
    seg_local.start()
    for copy in small_sends:
        copy.start()
    seg_send.start()
    act = ActGather(me, xin, xall, ag_send, ag_recv, ag_local)
    act.start()
    for i in range(4, 7):
        sends[i].start()
        keeps[i].start()

    def slot_copies(t, yy, sem, right):
        r = pl.ds(pl.multiple_of((t * 2 + yy) * rows, rows), rows)
        dev = me.device(z=z + 1 if right else z - 1)
        recv = z_recv.at[t, yy, 0], z_recv.at[t, yy, 1]
        return (
            remote(wqkv.at[r, :], wqkv.at[r, :], sem.at[t, yy, 0], recv[0], dev),
            remote(wof.at[:, r], wof.at[:, r], sem.at[t, yy, 1], recv[1], dev),
        )

    def send_both(t, yy, do):
        @pl.when(z + 1 <= n - 1)
        def _():
            for copy in slot_copies(t, yy, r_send, True):
                do(copy)

        @pl.when(z >= 1)
        def _():
            for copy in slot_copies(t, yy, l_send, False):
                do(copy)

    for i in range(4):
        keeps[i].wait()
    send_both(z, y, lambda copy: copy.start())
    for i in range(4):
        sends[i].wait_recv()
    send_both(z, 1 - y, lambda copy: copy.start())

    small_local.wait()
    for copy in small_sends:
        copy.wait_recv()
    block8 = smalls.at[pl.ds(pl.multiple_of(z * 8, 8), 8)]
    small_z = [remote(block8, block8, s2_send.at[i], s2_recv.at[i], dev) for i, dev in enumerate(others)]
    for copy in small_z:
        copy.start()
    act.forward()
    act.forward_core()

    for s in range(1, n):
        for first in range(2):
            yy = y if first == 0 else 1 - y

            @pl.when(z - s >= 0)
            def _():
                for copy in slot_copies(z - s, yy, r_send, True):
                    copy.wait_recv()

                @pl.when(z + 1 <= n - 1)
                def _():
                    for copy in slot_copies(z - s, yy, r_send, True):
                        copy.start()

            @pl.when(z + s <= n - 1)
            def _():
                for copy in slot_copies(z + s, yy, l_send, False):
                    copy.wait_recv()

                @pl.when(z >= 1)
                def _():
                    for copy in slot_copies(z + s, yy, l_send, False):
                        copy.start()

    act.finish()
    for copy in small_z:
        copy.wait()
    for copy in small_sends:
        copy.wait_send()
    seg_send.wait()
    seg_local.wait()
    for i in range(7):
        sends[i].wait_send()
    for i in range(4, 7):
        sends[i].wait_recv()
        keeps[i].wait()
    for yy in range(2):
        send_both(z, yy, lambda copy: copy.wait_send())
        for s in range(1, n):

            @pl.when((z - s >= 0) & (z + 1 <= n - 1))
            def _():
                for copy in slot_copies(z - s, yy, r_send, True):
                    copy.wait_send()

            @pl.when((z + s <= n - 1) & (z >= 1))
            def _():
                for copy in slot_copies(z + s, yy, l_send, False):
                    copy.wait_send()


def first_gather(n, wq, wk, wv, wo, wg, wu, wd, xin, small, seg):
    rows, width = wq.shape[0], xin.shape[1]
    heads = wq.shape[1] // 2
    hid = wg.shape[1] // 2
    shapes = [
        ((2 * n * rows, 3 * heads), BF),
        ((heads, 2 * n * rows), BF),
        ((2 * rows, 2 * hid), BF),
        ((hid, 2 * rows), BF),
        ((8,) + xin.shape, BF),
        ((8 * n,) + small.shape, F32),
        ((2,) + seg.shape, jnp.int32),
    ]
    return pl.pallas_call(
        functools.partial(first_kernel, n),
        out_shape=[jax.ShapeDtypeStruct(s, d) for s, d in shapes],
        in_specs=[ANY] * 10,
        out_specs=[ANY] * 7,
        scratch_shapes=[DMA((7,)), DMA((7,)), DMA((7,)), DMA((n, 2, 2)), DMA((n, 2, 2)), DMA((n, 2, 2))]
        + gather_sems()
        + [DMA((8,)), DMA((8,)), DMA((n - 1,)), DMA((n - 1,)), DMA((2,))],
        compiler_params=pltpu.CompilerParams(collective_id=0, has_side_effects=True),
        name="first_gather",
    )(wq, wk, wv, wo, wg, wu, wd, xin, small, seg)


def neighbours(me):
    return [me.x_peer(), me.y_peer(), me.core_peer()]


def mid_kernel(part, xin, gain, mid, a2all, *scratch):
    red = scratch[:9]
    a2, = scratch[9:10]
    gs = scratch[10:]
    me = Place()
    greet(neighbours(me))
    r = ActReduce(me, part, *red)
    r.start()
    r.run()
    half = xin.shape[0] // 2
    for h in range(2):

        def body(i, carry):
            rr = pl.ds(pl.multiple_of(h * half + i * 16, 16), 16)
            m = xin[rr, :].astype(F32) + r.total(h, i)
            mid[rr, :] = m
            inv = lax.rsqrt(jnp.mean(m * m, axis=-1, keepdims=True) + EPSILON)
            a2[rr, :] = (m * inv * gain[...]).astype(BF)
            return carry

        lax.fori_loop(0, half // 16, body, 0)
    g = ActGather(me, a2, a2all, *gs)
    g.start()
    g.forward()
    g.forward_core()
    g.finish()
    r.finish()


def mid_step(part, xin, gain):
    rows, width = xin.shape
    return pl.pallas_call(
        mid_kernel,
        out_shape=[jax.ShapeDtypeStruct((rows, width), F32), jax.ShapeDtypeStruct((8, rows, width), BF)],
        in_specs=[ANY, VM, VM],
        out_specs=[VM, ANY],
        scratch_shapes=reduce_scratch(rows, width) + [pltpu.VMEM((rows, width), BF)] + gather_sems(),
        compiler_params=pltpu.CompilerParams(collective_id=1, has_side_effects=True, vmem_limit_bytes=40 << 20),
        name="mid_step",
    )(part, xin, gain)


def dz_kernel(part, mid, cot, gain, gmid, dzall, ggain, *scratch):
    red = scratch[:9]
    dz, = scratch[9:10]
    gs = scratch[10:]
    me = Place()
    greet(neighbours(me))
    r = ActReduce(me, part, *red)
    r.start()
    r.run()
    half = mid.shape[0] // 2
    ggain[...] = jnp.zeros_like(ggain)
    for h in range(2):

        def body(i, carry):
            rr = pl.ds(pl.multiple_of(h * half + i * 16, 16), 16)
            ga = r.total(h, i)
            m = mid[rr, :]
            inv = lax.rsqrt(jnp.mean(m * m, axis=-1, keepdims=True) + EPSILON)
            prod = ga * (m * inv)
            ggain[...] += prod[:8] + prod[8:]
            u = ga * gain[...]
            corr = jnp.mean(u * m, axis=-1, keepdims=True) * inv * inv * inv
            gm = cot[rr, :].astype(F32) + inv * u - m * corr
            gmid[rr, :] = gm
            dz[rr, :] = gm.astype(BF)
            return carry

        lax.fori_loop(0, half // 16, body, 0)
    g = ActGather(me, dz, dzall, *gs)
    g.start()
    g.forward()
    g.forward_core()
    g.finish()
    r.finish()


def dz_step(part, mid, cot, gain):
    rows, width = mid.shape
    return pl.pallas_call(
        dz_kernel,
        out_shape=[
            jax.ShapeDtypeStruct((rows, width), F32),
            jax.ShapeDtypeStruct((8, rows, width), BF),
            jax.ShapeDtypeStruct((8, width), F32),
        ],
        in_specs=[ANY, VM, VM, VM],
        out_specs=[VM, ANY, VM],
        scratch_shapes=reduce_scratch(rows, width) + [pltpu.VMEM((rows, width), BF)] + gather_sems(),
        compiler_params=pltpu.CompilerParams(collective_id=2, has_side_effects=True, vmem_limit_bytes=40 << 20),
        name="dz_step",
    )(part, mid, cot, gain)


def last_kernel(ga_part, out_part, xin, gmid, mid, gain, gx, out, ggain, *scratch):
    me = Place()
    greet(neighbours(me))
    r = ActReduce(me, ga_part, *scratch[:9])
    q = ActReduce(me, out_part, *scratch[9:18])
    r.start()
    q.start()
    r.run()
    q.run()
    half = xin.shape[0] // 2
    ggain[...] = jnp.zeros_like(ggain)
    for h in range(2):

        def body(i, carry):
            rr = pl.ds(pl.multiple_of(h * half + i * 16, 16), 16)
            ga = r.total(h, i)
            m = xin[rr, :].astype(F32)
            inv = lax.rsqrt(jnp.mean(m * m, axis=-1, keepdims=True) + EPSILON)
            prod = ga * (m * inv)
            ggain[...] += prod[:8] + prod[8:]
            u = ga * gain[...]
            corr = jnp.mean(u * m, axis=-1, keepdims=True) * inv * inv * inv
            gx[rr, :] = gmid[rr, :] + inv * u - m * corr
            out[rr, :] = (mid[rr, :] + q.total(h, i)).astype(BF)
            return carry

        lax.fori_loop(0, half // 16, body, 0)
    r.finish()
    q.finish()


def last_step(ga_part, out_part, xin, gmid, mid, gain):
    rows, width = xin.shape
    return pl.pallas_call(
        last_kernel,
        out_shape=[
            jax.ShapeDtypeStruct((rows, width), F32),
            jax.ShapeDtypeStruct((rows, width), BF),
            jax.ShapeDtypeStruct((8, width), F32),
        ],
        in_specs=[ANY, ANY, VM, VM, VM, VM],
        out_specs=[VM, VM, VM],
        scratch_shapes=reduce_scratch(rows, width) * 2,
        compiler_params=pltpu.CompilerParams(collective_id=3, has_side_effects=True, vmem_limit_bytes=50 << 20),
        name="last_step",
    )(ga_part, out_part, xin, gmid, mid, gain)


TQ = 256


def attention_forward(fvec, q, k, v, segr, segc, o, p, toep):
    length = q.shape[0]
    for h in range(2):
        cols = slice(h * DH, (h + 1) * DH)
        toep[...] = pltpu.roll(
            jnp.broadcast_to(fvec[h], toep.shape), 0, 1, stride=1, stride_axis=0
        )
        kh = k[:, cols]
        vh = v[:, cols]
        for t in range(length // TQ):
            rows = slice(t * TQ, (t + 1) * TQ)
            s = lax.dot_general(q[rows, cols], kh, (((1,), (1,)), ((), ())), preferred_element_type=F32)
            s = s + toep[:, length - t * TQ : 2 * length - t * TQ]
            s = jnp.where(segc[0, rows, :] == segr[0], s, MASKED)
            e = jnp.exp(s - jnp.max(s, axis=-1, keepdims=True))
            pb = (e * (1.0 / jnp.sum(e, axis=-1, keepdims=True))).astype(BF)
            p[h, rows, :] = pb
            o[rows, cols] = jnp.dot(pb, vh, preferred_element_type=F32).astype(BF)


def run_attention_forward(fvec, qkv, segr, segc):
    total, width = qkv.shape
    heads = width // 3 // DH
    length = segr.shape[-1]
    seqs = total // length
    pairs = heads // 2
    qspec = lambda off: pl.BlockSpec((length, 2 * DH), lambda s, h: (s, off * pairs + h))
    return pl.pallas_call(
        attention_forward,
        grid=(seqs, pairs),
        out_shape=[
            jax.ShapeDtypeStruct((total, heads * DH), BF),
            jax.ShapeDtypeStruct((seqs * heads, length, length), BF),
        ],
        in_specs=[
            pl.BlockSpec((2, 1, 2 * length), lambda s, h: (h, 0, 0)),
            qspec(0),
            qspec(1),
            qspec(2),
            pl.BlockSpec((1, 1, length), lambda s, h: (s, 0, 0)),
            pl.BlockSpec((1, length, 1), lambda s, h: (s, 0, 0)),
        ],
        out_specs=[
            pl.BlockSpec((length, 2 * DH), lambda s, h: (s, h)),
            pl.BlockSpec((2, length, length), lambda s, h: (s * pairs + h, 0, 0)),
        ],
        scratch_shapes=[pltpu.VMEM((TQ, 2 * length), F32)],
        compiler_params=pltpu.CompilerParams(vmem_limit_bytes=48 << 20),
        name="attention_forward",
    )(fvec, qkv, qkv, qkv, segr, segc)


def attention_backward(q, k, v, do, p, dq, dk, dv, diag, acc, dkt, dvt):
    length = q.shape[0]
    for h in range(2):
        cols = slice(h * DH, (h + 1) * DH)
        kh = k[:, cols]
        vh = v[:, cols]
        acc[...] = jnp.zeros_like(acc)
        for t in range(length // TQ):
            rows = slice(t * TQ, (t + 1) * TQ)
            pb = p[h, rows, :]
            doh = do[rows, cols]
            qh = q[rows, cols]
            dp = lax.dot_general(doh, vh, (((1,), (1,)), ((), ())), preferred_element_type=F32)
            pf = pb.astype(F32)
            ds = (pf * (dp - jnp.sum(pf * dp, axis=-1, keepdims=True))).astype(BF)
            dq[rows, cols] = jnp.dot(ds, kh, preferred_element_type=F32).astype(BF)
            ck = lax.dot_general(qh, ds, (((0,), (0,)), ((), ())), preferred_element_type=F32)
            cv = lax.dot_general(doh, pb, (((0,), (0,)), ((), ())), preferred_element_type=F32)
            if t == 0:
                dkt[...] = ck
                dvt[...] = cv
            else:
                dkt[...] += ck
                dvt[...] += cv
            acc[:, length - t * TQ : 2 * length - t * TQ] += ds.astype(F32)
        dk[:, cols] = dkt[...].T.astype(BF)
        dv[:, cols] = dvt[...].T.astype(BF)
        n = TQ // 2
        while n >= 8:
            acc[0:n, :] += pltpu.roll(acc[n : 2 * n, :], 2 * length - n, 1)
            n //= 2
        diag[h] = acc[0:8, :]


def run_attention_backward(qkv, do, p):
    total, width = qkv.shape
    heads = width // 3 // DH
    length = p.shape[1]
    seqs = total // length
    pairs = heads // 2
    qspec = lambda off: pl.BlockSpec((length, 2 * DH), lambda s, h: (s, off * pairs + h))
    flat = pl.BlockSpec((length, 2 * DH), lambda s, h: (s, h))
    return pl.pallas_call(
        attention_backward,
        grid=(seqs, pairs),
        out_shape=[jax.ShapeDtypeStruct((total, heads * DH), BF)] * 3
        + [jax.ShapeDtypeStruct((seqs * heads, 8, 2 * length), F32)],
        in_specs=[
            qspec(0),
            qspec(1),
            qspec(2),
            flat,
            pl.BlockSpec((2, length, length), lambda s, h: (s * pairs + h, 0, 0)),
        ],
        out_specs=[flat, flat, flat, pl.BlockSpec((2, 8, 2 * length), lambda s, h: (s * pairs + h, 0, 0))],
        scratch_shapes=[
            pltpu.VMEM((TQ, 2 * length), F32),
            pltpu.VMEM((DH, length), F32),
            pltpu.VMEM((DH, length), F32),
        ],
        compiler_params=pltpu.CompilerParams(vmem_limit_bytes=48 << 20),
        name="attention_backward",
    )(qkv, qkv, qkv, do, p)


def offset_buckets(length):
    relative = jnp.arange(2 * length, dtype=jnp.int32) - length
    distance = jnp.abs(relative)
    log_bucket = 8 + sum((distance >= t).astype(jnp.int32) for t in THRESHOLDS)
    bucket = jnp.where(distance < 8, distance, log_bucket) + 16 * (relative > 0).astype(jnp.int32)
    return (bucket[:, None] == jnp.arange(NB, dtype=jnp.int32)[None, :]).astype(F32)


def swap_rows(part, y, swap):
    rows = part.shape[0] // 2
    mine = lax.dynamic_slice_in_dim(part, y * rows, rows, 0)
    theirs = lax.ppermute(lax.dynamic_slice_in_dim(part, (1 - y) * rows, rows, 0), "fsdp", swap)
    return jnp.where(y == 0, mine, theirs), jnp.where(y == 0, theirs, mine)


def on_device(
    n, hidden, segment_ids, positions, attn_gain, w_query, w_key, w_value, w_attn_out,
    rel_table, ffn_gain, w_gate, w_up, w_down, cotangent,
):
    xin = hidden[0]
    cot = cotangent[0]
    rows, width = xin.shape
    length = segment_ids.shape[1]
    heads = w_query.shape[1] // 2
    hid = w_gate.shape[1] // 2
    y = lax.axis_index("fsdp")
    c = lax.axis_index("ctx")
    swap = [(0, 1), (1, 0)]
    share = attn_gain.shape[0]
    packed = jnp.concatenate([attn_gain.astype(F32), ffn_gain.astype(F32), rel_table.astype(F32)])
    packed = jnp.pad(packed, (0, 256 - packed.shape[0]))
    small = jnp.broadcast_to(packed[None, :], (8, 256))
    seg = jnp.broadcast_to(segment_ids, (8, length))
    wqkv, wo, wgu_y, wd_y, xall, smalls, segs = first_gather(
        n, w_query, w_key, w_value, w_attn_out, w_gate, w_up, w_down, xin, small, seg
    )
    wgu = lax.all_gather(wgu_y, "dp", axis=0, tiled=True)
    wd = lax.all_gather(wd_y, "dp", axis=1, tiled=True)
    gain1 = smalls[:, 0, 0:share].reshape(1, width)
    gain2 = smalls[:, 0, share : 2 * share].reshape(1, width)
    table = smalls[:, 0, 2 * share : 2 * share + NB * H // (8 * n)].reshape(NB, H)
    local_heads = heads // DH
    table_local = lax.dynamic_slice_in_dim(table, (c * 2 + y) * local_heads, local_heads, 1)
    one_hot = offset_buckets(length)
    fvec = lax.dot_general(
        table_local, one_hot, (((0,), (1,)), ((), ())), precision=lax.Precision.HIGHEST
    ).reshape(local_heads, 1, 2 * length)
    segr = segs[:, 0:1, :]
    segc = segs[:, 0, :, None]
    xf = xall.reshape(8 * rows, width).astype(F32)
    a1 = (xf * lax.rsqrt(jnp.mean(xf * xf, axis=-1, keepdims=True) + EPSILON) * gain1).astype(BF)
    qkv = jnp.dot(a1, wqkv, preferred_element_type=F32).astype(BF)
    o, p = run_attention_forward(fvec, qkv, segr, segc)
    attn_part = jnp.dot(o, wo, preferred_element_type=F32).astype(BF)
    mid, a2all = mid_step(attn_part.reshape(8, rows, width), xin, gain2)
    a2 = a2all.reshape(8 * rows, width)
    gall = gather_cot(cot, mid).reshape(8 * rows, width)
    gate_up = jnp.dot(a2, wgu, preferred_element_type=F32)
    gate, up = gate_up[:, :hid], gate_up[:, hid:]
    inner = 0.7978845608028654 * (gate + 0.044715 * gate * gate * gate)
    th = jnp.tanh(inner)
    gelu = 0.5 * gate * (1.0 + th)
    slope = 0.5 * (1.0 + th) + 0.5 * gate * (1.0 - th * th) * 0.7978845608028654 * (
        1.0 + 3 * 0.044715 * gate * gate
    )
    m = (gelu * up).astype(BF)
    gm = lax.dot_general(gall, wd, (((1,), (1,)), ((), ())), preferred_element_type=F32)
    dgu = jnp.concatenate([(gm * up * slope).astype(BF), (gm * gelu).astype(BF)], axis=1)
    gw_gu = lax.dot_general(a2, dgu, (((0,), (0,)), ((), ())), preferred_element_type=F32).astype(BF)
    gw_d = lax.dot_general(m, gall, (((0,), (0,)), ((), ())), preferred_element_type=F32).astype(BF)
    ga2 = lax.dot_general(dgu, wgu, (((1,), (1,)), ((), ())), preferred_element_type=F32).astype(BF)
    out_part = jnp.dot(m, wd, preferred_element_type=F32).astype(BF)
    rs_gu = lax.psum_scatter(gw_gu, "dp", scatter_dimension=0, tiled=True)
    rs_d = lax.psum_scatter(gw_d, "dp", scatter_dimension=1, tiled=True)
    gmid, dzall, ggain2 = dz_step(ga2.reshape(8, rows, width), mid, cot, gain2)
    dz = dzall.reshape(8 * rows, width)
    do = lax.dot_general(dz, wo, (((1,), (1,)), ((), ())), preferred_element_type=F32).astype(BF)
    gw_o = lax.dot_general(o, dz, (((0,), (0,)), ((), ())), preferred_element_type=F32).astype(BF)
    rs_o = lax.psum_scatter(gw_o, "dp", scatter_dimension=1, tiled=True)
    dq, dk, dv, diag = run_attention_backward(qkv, do, p)
    dqkv = jnp.concatenate([dq, dk, dv], axis=1)
    gw_qkv = lax.dot_general(a1, dqkv, (((0,), (0,)), ((), ())), preferred_element_type=F32).astype(BF)
    rs_qkv = lax.psum_scatter(gw_qkv, "dp", scatter_dimension=0, tiled=True)
    ga1 = lax.dot_general(dqkv, wqkv, (((1,), (1,)), ((), ())), preferred_element_type=F32).astype(BF)
    gx, out, ggain1 = last_step(
        ga1.reshape(8, rows, width), out_part.reshape(8, rows, width), xin, gmid, mid, gain1
    )

    d8 = jnp.sum(diag.reshape(-1, local_heads, 8, 2 * length), axis=0)
    lanes = sum(jnp.roll(d8[:, r, :], -r, axis=-1) for r in range(8))
    bias = lax.dot_general(
        one_hot, lanes, (((0,), (1,)), ((), ())), precision=lax.Precision.HIGHEST
    )
    table_term = lax.dynamic_update_slice(
        jnp.zeros((NB, H), F32), bias, (jnp.int32(0), (c * 2 + y) * local_heads)
    )
    axes = ("dp", "ctx", "fsdp")
    g_attn_gain = lax.psum_scatter(jnp.sum(ggain1, axis=0), axes, scatter_dimension=0, tiled=True)
    g_ffn_gain = lax.psum_scatter(jnp.sum(ggain2, axis=0), axes, scatter_dimension=0, tiled=True)
    g_table = lax.psum_scatter(table_term.reshape(NB * H), axes, scatter_dimension=0, tiled=True)

    lo, hi = swap_rows(rs_gu, y, swap)
    g_gate = jnp.concatenate([lo[:, :hid], hi[:, :hid]], axis=1).astype(F32)
    g_up = jnp.concatenate([lo[:, hid:], hi[:, hid:]], axis=1).astype(F32)
    lo, hi = swap_rows(rs_qkv, y, swap)
    g_q, g_k, g_v = (
        jnp.concatenate([lo[:, i * heads : (i + 1) * heads], hi[:, i * heads : (i + 1) * heads]], axis=1).astype(F32)
        for i in range(3)
    )

    def swap_cols(part):
        mine = lax.dynamic_slice_in_dim(part, y * rows, rows, 1)
        theirs = lax.ppermute(lax.dynamic_slice_in_dim(part, (1 - y) * rows, rows, 1), "fsdp", swap)
        return jnp.concatenate(
            [jnp.where(y == 0, mine, theirs), jnp.where(y == 0, theirs, mine)], axis=0
        ).astype(F32)

    return (
        out[None], gx[None], g_attn_gain, g_q, g_k, g_v, swap_cols(rs_o), g_table, g_ffn_gain,
        g_gate, g_up, swap_cols(rs_d),
    )


def gather_cot_kernel(cot, after, gall, send, recv, local):
    me = Place()
    greet(neighbours(me))
    g = ActGather(me, cot, gall, send, recv, local)
    g.start()
    g.forward()
    g.forward_core()
    g.finish()


def gather_cot(cot, after):
    return pl.pallas_call(
        gather_cot_kernel,
        out_shape=jax.ShapeDtypeStruct((8,) + cot.shape, BF),
        in_specs=[ANY, ANY],
        out_specs=ANY,
        scratch_shapes=gather_sems(),
        compiler_params=pltpu.CompilerParams(collective_id=4, has_side_effects=True),
        name="gather_cot",
    )(cot, after)


QB = 512


def rms_norm(values, gain):
    return values * lax.rsqrt(jnp.mean(values * values, axis=-1, keepdims=True) + EPSILON) * gain


def gelu_tanh(values):
    return (
        0.5
        * values
        * (1.0 + jnp.tanh(0.7978845608028654 * (values + 0.044715 * values * values * values)))
    )


def bucket_table(query_pos, key_pos):
    relative = key_pos[None, :] - query_pos[:, None]
    distance = jnp.abs(relative)
    log_bucket = 8 + sum(((distance >= threshold).astype(jnp.int32) for threshold in THRESHOLDS))
    bucket = jnp.where(distance < 8, distance, log_bucket)
    return bucket + 16 * (relative > 0).astype(jnp.int32)


def gather_attention(w_query, w_key, w_value, w_attn_out):
    return (
        lax.all_gather(w_query, ("dp", "fsdp"), axis=0, tiled=True),
        lax.all_gather(w_key, ("dp", "fsdp"), axis=0, tiled=True),
        lax.all_gather(w_value, ("dp", "fsdp"), axis=0, tiled=True),
        lax.all_gather(w_attn_out, ("dp", "fsdp"), axis=1, tiled=True),
    )


def gather_feedforward(w_gate, w_up, w_down):
    return (
        lax.all_gather(w_gate, ("dp", "fsdp"), axis=0, tiled=True),
        lax.all_gather(w_up, ("dp", "fsdp"), axis=0, tiled=True),
        lax.all_gather(w_down, ("dp", "fsdp"), axis=1, tiled=True),
    )


def block_masks(segment_row, position_row, start):
    query_pos = lax.dynamic_slice_in_dim(position_row, start, QB)
    query_seg = lax.dynamic_slice_in_dim(segment_row, start, QB)
    buckets = bucket_table(query_pos, position_row)
    one_hot = (buckets[None] == jnp.arange(NB, dtype=jnp.int32)[:, None, None]).astype(jnp.bfloat16)
    same_doc = query_seg[:, None] == segment_row[None, :]
    return (one_hot, same_doc)


def block_scores(query_block, key_rows, table_local, one_hot, same_doc):
    attention_scores = jnp.einsum(
        "ihd,jhd->hij", query_block, key_rows, preferred_element_type=jnp.float32
    )
    attention_scores = attention_scores + jnp.einsum(
        "bij,bh->hij", one_hot, table_local, preferred_element_type=jnp.float32
    )
    return jnp.where(same_doc[None], attention_scores, MASKED)


def layer_forward(tokens, small_set, attn_set, ffn_set, segment_row, position_row):
    attn_gain, ffn_gain, table_flat = small_set
    w_query, w_key, w_value, w_attn_out = attn_set
    w_gate, w_up, w_down = ffn_set
    heads_here = w_query.shape[1] // DH
    head_start = lax.axis_index("ctx") * heads_here
    table_local = lax.dynamic_slice_in_dim(table_flat.reshape(NB, H), head_start, heads_here, 1)
    normalized_rows, attn_back = jax.vjp(rms_norm, tokens, attn_gain.astype(jnp.float32))
    normed_rows = lax.all_gather(normalized_rows.astype(jnp.bfloat16), "ctx", axis=0, tiled=True)
    seq_len = normed_rows.shape[0]
    queries = (
        jnp.dot(normed_rows, w_query, preferred_element_type=jnp.float32)
        .astype(jnp.bfloat16)
        .reshape(seq_len, heads_here, DH)
    )
    key_rows = (
        jnp.dot(normed_rows, w_key, preferred_element_type=jnp.float32)
        .astype(jnp.bfloat16)
        .reshape(seq_len, heads_here, DH)
    )
    value_rows = (
        jnp.dot(normed_rows, w_value, preferred_element_type=jnp.float32)
        .astype(jnp.bfloat16)
        .reshape(seq_len, heads_here, DH)
    )
    starts = jnp.arange(seq_len // QB, dtype=jnp.int32) * QB

    def forward_block(start):
        one_hot, same_doc = block_masks(segment_row, position_row, start)
        query_block = lax.dynamic_slice_in_dim(queries, start, QB, 0)
        attention_scores = block_scores(query_block, key_rows, table_local, one_hot, same_doc)
        row_peak = jnp.max(attention_scores, axis=-1, keepdims=True)
        lifted = jnp.exp(attention_scores - row_peak)
        row_total = jnp.sum(lifted, axis=-1, keepdims=True)
        prob_low = (lifted / row_total).astype(jnp.bfloat16)
        attended_part = jnp.einsum(
            "hij,jhd->ihd", prob_low, value_rows, preferred_element_type=jnp.float32
        )
        return (attended_part, row_peak + jnp.log(row_total))

    attended, log_total = lax.map(forward_block, starts)
    attended_low = attended.reshape(seq_len, heads_here * DH).astype(jnp.bfloat16)
    attn_term = jnp.dot(attended_low, w_attn_out, preferred_element_type=jnp.float32)
    residual = tokens + lax.psum_scatter(attn_term, "ctx", scatter_dimension=0, tiled=True)
    normed_ffn, ffn_back = jax.vjp(rms_norm, residual, ffn_gain.astype(jnp.float32))
    ffn_rows = lax.all_gather(normed_ffn.astype(jnp.bfloat16), "ctx", axis=0, tiled=True)
    gate_value = jnp.dot(ffn_rows, w_gate, preferred_element_type=jnp.float32)
    up_value = jnp.dot(ffn_rows, w_up, preferred_element_type=jnp.float32)
    gelu_gate, gelu_back = jax.vjp(gelu_tanh, gate_value)
    ffn_hidden = (gelu_gate * up_value).astype(jnp.bfloat16)
    down_term = jnp.dot(ffn_hidden, w_down, preferred_element_type=jnp.float32)
    result = residual + lax.psum_scatter(
        down_term.astype(jnp.bfloat16), "ctx", scatter_dimension=0, tiled=True
    ).astype(jnp.float32)
    stored = (
        attn_back,
        normed_rows,
        queries,
        key_rows,
        value_rows,
        table_local,
        head_start,
        starts,
        log_total,
        attended_low,
        ffn_back,
        ffn_rows,
        up_value,
        gelu_gate,
        gelu_back,
        ffn_hidden,
    )
    return (result, stored)


def plain_on_device(
    hidden,
    segment_ids,
    positions,
    attn_gain,
    w_query,
    w_key,
    w_value,
    w_attn_out,
    rel_table,
    ffn_gain,
    w_gate,
    w_up,
    w_down,
    cotangent,
):
    tokens = hidden[0].astype(jnp.float32)
    segment_row = segment_ids[0]
    position_row = positions[0]
    small_set = (
        lax.all_gather(attn_gain, ("dp", "ctx", "fsdp"), axis=0, tiled=True),
        lax.all_gather(ffn_gain, ("dp", "ctx", "fsdp"), axis=0, tiled=True),
        lax.all_gather(rel_table, ("dp", "ctx", "fsdp"), axis=0, tiled=True),
    )
    attn_set = gather_attention(w_query, w_key, w_value, w_attn_out)
    ffn_set = gather_feedforward(w_gate, w_up, w_down)
    result, unused_stored = layer_forward(
        tokens, small_set, attn_set, ffn_set, segment_row, position_row
    )
    back_attn = gather_attention(w_query, w_key, w_value, w_attn_out)
    back_ffn = gather_feedforward(w_gate, w_up, w_down)
    recomputed, stored = layer_forward(
        tokens, small_set, back_attn, back_ffn, segment_row, position_row
    )
    (
        attn_back,
        normed_rows,
        queries,
        key_rows,
        value_rows,
        table_local,
        head_start,
        starts,
        log_total,
        attended_low,
        ffn_back,
        ffn_rows,
        up_value,
        gelu_gate,
        gelu_back,
        ffn_hidden,
    ) = stored
    full_query, full_key, full_value, full_attn_out = back_attn
    full_gate, full_up, full_down = back_ffn
    seq_len = normed_rows.shape[0]
    heads_here = queries.shape[1]
    grad_rows = lax.all_gather(cotangent[0], "ctx", axis=0, tiled=True)
    grad_w_down = jnp.einsum("tf,td->fd", ffn_hidden, grad_rows, preferred_element_type=jnp.float32)
    grad_hidden_ffn = jnp.einsum(
        "td,fd->tf", grad_rows, full_down, preferred_element_type=jnp.float32
    )
    up_value_gradient = (grad_hidden_ffn * gelu_gate).astype(jnp.bfloat16)
    grad_gate_value = gelu_back(grad_hidden_ffn * up_value)[0].astype(jnp.bfloat16)
    grad_w_gate = jnp.einsum(
        "td,tf->df", ffn_rows, grad_gate_value, preferred_element_type=jnp.float32
    )
    grad_w_up = jnp.einsum(
        "td,tf->df", ffn_rows, up_value_gradient, preferred_element_type=jnp.float32
    )
    ffn_normed_term = jnp.einsum(
        "tf,df->td", grad_gate_value, full_gate, preferred_element_type=jnp.float32
    )
    ffn_normed_term = ffn_normed_term + jnp.einsum(
        "tf,df->td", up_value_gradient, full_up, preferred_element_type=jnp.float32
    )
    grad_normed_ffn = lax.psum_scatter(ffn_normed_term, "ctx", scatter_dimension=0, tiled=True)
    grad_residual_norm, grad_ffn_gain = ffn_back(grad_normed_ffn)
    grad_residual = cotangent[0].astype(jnp.float32) + grad_residual_norm
    ffn_sums = (
        lax.psum_scatter(
            grad_w_gate.astype(jnp.bfloat16), ("dp", "fsdp"), scatter_dimension=0, tiled=True
        ).astype(jnp.float32),
        lax.psum_scatter(
            grad_w_up.astype(jnp.bfloat16), ("dp", "fsdp"), scatter_dimension=0, tiled=True
        ).astype(jnp.float32),
        lax.psum_scatter(
            grad_w_down.astype(jnp.bfloat16), ("dp", "fsdp"), scatter_dimension=1, tiled=True
        ).astype(jnp.float32),
    )
    branch_rows = lax.all_gather(grad_residual.astype(jnp.bfloat16), "ctx", axis=0, tiled=True)
    grad_w_attn_out = jnp.einsum(
        "ti,td->id", attended_low, branch_rows, preferred_element_type=jnp.float32
    )
    grad_attended = jnp.einsum(
        "td,id->ti", branch_rows, full_attn_out, preferred_element_type=jnp.float32
    )
    grad_attended = grad_attended.astype(jnp.bfloat16).reshape(seq_len, heads_here, DH)

    def backward_block(operands):
        start, block_total = operands
        one_hot, same_doc = block_masks(segment_row, position_row, start)
        query_block = lax.dynamic_slice_in_dim(queries, start, QB, 0)
        grad_part = lax.dynamic_slice_in_dim(grad_attended, start, QB, 0)
        attention_scores = block_scores(query_block, key_rows, table_local, one_hot, same_doc)
        weights = jnp.exp(attention_scores - block_total)
        prob_low = weights.astype(jnp.bfloat16)
        grad_probs = jnp.einsum(
            "ihd,jhd->hij", grad_part, value_rows, preferred_element_type=jnp.float32
        )
        centred = grad_probs - jnp.sum(weights * grad_probs, axis=-1, keepdims=True)
        grad_scores = (weights * centred).astype(jnp.bfloat16)
        grad_query_part = jnp.einsum(
            "hij,jhd->ihd", grad_scores, key_rows, preferred_element_type=jnp.float32
        )
        grad_key_part = jnp.einsum(
            "hij,ihd->jhd", grad_scores, query_block, preferred_element_type=jnp.float32
        )
        grad_value_part = jnp.einsum(
            "hij,ihd->jhd", prob_low, grad_part, preferred_element_type=jnp.float32
        )
        grad_bias_part = jnp.einsum(
            "hij,bij->bh", grad_scores, one_hot, preferred_element_type=jnp.float32
        )
        return (grad_query_part, grad_key_part, grad_value_part, grad_bias_part)

    query_blocks, key_blocks, value_blocks, bias_blocks = lax.map(
        backward_block, (starts, log_total)
    )
    grad_queries_low = query_blocks.reshape(seq_len, heads_here * DH).astype(jnp.bfloat16)
    grad_keys_low = (
        jnp.sum(key_blocks, axis=0).reshape(seq_len, heads_here * DH).astype(jnp.bfloat16)
    )
    grad_values_low = (
        jnp.sum(value_blocks, axis=0).reshape(seq_len, heads_here * DH).astype(jnp.bfloat16)
    )
    grad_w_query = jnp.einsum(
        "td,te->de", normed_rows, grad_queries_low, preferred_element_type=jnp.float32
    )
    grad_w_key = jnp.einsum(
        "td,te->de", normed_rows, grad_keys_low, preferred_element_type=jnp.float32
    )
    grad_w_value = jnp.einsum(
        "td,te->de", normed_rows, grad_values_low, preferred_element_type=jnp.float32
    )
    normed_term = jnp.einsum(
        "te,de->td", grad_queries_low, full_query, preferred_element_type=jnp.float32
    )
    normed_term = normed_term + jnp.einsum(
        "te,de->td", grad_keys_low, full_key, preferred_element_type=jnp.float32
    )
    normed_term = normed_term + jnp.einsum(
        "te,de->td", grad_values_low, full_value, preferred_element_type=jnp.float32
    )
    grad_normed = lax.psum_scatter(
        normed_term.astype(jnp.bfloat16), "ctx", scatter_dimension=0, tiled=True
    ).astype(jnp.float32)
    token_norm_gradient, grad_attn_gain = attn_back(grad_normed)
    grad_tokens = grad_residual + token_norm_gradient
    attn_sums = (
        lax.psum_scatter(
            grad_w_query.astype(jnp.bfloat16), ("dp", "fsdp"), scatter_dimension=0, tiled=True
        ).astype(jnp.float32),
        lax.psum_scatter(
            grad_w_key.astype(jnp.bfloat16), ("dp", "fsdp"), scatter_dimension=0, tiled=True
        ).astype(jnp.float32),
        lax.psum_scatter(
            grad_w_value.astype(jnp.bfloat16), ("dp", "fsdp"), scatter_dimension=0, tiled=True
        ).astype(jnp.float32),
        lax.psum_scatter(
            grad_w_attn_out.astype(jnp.bfloat16), ("dp", "fsdp"), scatter_dimension=1, tiled=True
        ).astype(jnp.float32),
    )
    bias_sum = jnp.sum(bias_blocks, axis=0)
    table_term = lax.dynamic_update_slice(
        jnp.zeros((NB, H), jnp.float32), bias_sum, (jnp.int32(0), head_start)
    )
    small_sums = (
        lax.psum_scatter(grad_attn_gain, ("dp", "ctx", "fsdp"), scatter_dimension=0, tiled=True),
        lax.psum_scatter(grad_ffn_gain, ("dp", "ctx", "fsdp"), scatter_dimension=0, tiled=True),
        lax.psum_scatter(
            table_term.reshape(NB * H), ("dp", "ctx", "fsdp"), scatter_dimension=0, tiled=True
        ),
    )
    return (
        result[None].astype(jnp.bfloat16),
        grad_tokens[None],
        small_sums[0],
        attn_sums[0],
        attn_sums[1],
        attn_sums[2],
        attn_sums[3],
        small_sums[2],
        small_sums[1],
        ffn_sums[0],
        ffn_sums[1],
        ffn_sums[2],
    )


def plain_solution(mesh):
    in_specs = (
        P(("dp", "fsdp"), "ctx", None),
        P(("dp", "fsdp"), None),
        P(("dp", "fsdp"), None),
        P(("dp", "ctx", "fsdp")),
        P(("dp", "fsdp"), "ctx"),
        P(("dp", "fsdp"), "ctx"),
        P(("dp", "fsdp"), "ctx"),
        P("ctx", ("dp", "fsdp")),
        P(("dp", "ctx", "fsdp")),
        P(("dp", "ctx", "fsdp")),
        P(("dp", "fsdp"), "ctx"),
        P(("dp", "fsdp"), "ctx"),
        P("ctx", ("dp", "fsdp")),
        P(("dp", "fsdp"), "ctx", None),
    )
    out_specs = (
        P(("dp", "fsdp"), "ctx", None),
        P(("dp", "fsdp"), "ctx", None),
        P(("dp", "ctx", "fsdp")),
        P(("dp", "fsdp"), "ctx"),
        P(("dp", "fsdp"), "ctx"),
        P(("dp", "fsdp"), "ctx"),
        P("ctx", ("dp", "fsdp")),
        P(("dp", "ctx", "fsdp")),
        P(("dp", "ctx", "fsdp")),
        P(("dp", "fsdp"), "ctx"),
        P(("dp", "fsdp"), "ctx"),
        P("ctx", ("dp", "fsdp")),
    )
    return jax.shard_map(
        plain_on_device, mesh=mesh, in_specs=in_specs, out_specs=out_specs, check_vma=False
    )


def solution(mesh):
    if 2048 // (mesh.shape["dp"] * mesh.shape["fsdp"]) % 128 or mesh.shape["fsdp"] != 2 or mesh.shape["ctx"] != 4:
        return plain_solution(mesh)
    tokens = P(("dp", "fsdp"), "ctx", None)
    line = P(("dp", "fsdp"), None)
    every = P(("dp", "ctx", "fsdp"))
    into = P(("dp", "fsdp"), "ctx")
    back = P("ctx", ("dp", "fsdp"))
    return jax.shard_map(
        functools.partial(on_device, mesh.shape["dp"]),
        mesh=mesh,
        in_specs=(tokens, line, line, every, into, into, into, back, every, every, into, into, back, tokens),
        out_specs=(tokens, tokens, every, into, into, into, back, every, every, into, into, back),
        check_vma=False,
    )
```

```python
import functools

import jax
import jax.numpy as jnp
from jax import lax
from jax.experimental import pallas as pl
from jax.experimental.pallas import tpu as pltpu
from jax.sharding import PartitionSpec as P

H = 32
DH = 64
NB = 32
EPSILON = 1e-06
THRESHOLDS = (12, 16, 23, 32, 46, 64, 91)
MASKED = -1e30
BF = jnp.bfloat16
F32 = jnp.float32
ANY = pl.BlockSpec(memory_space=pl.ANY)
VM = pl.BlockSpec(memory_space=pltpu.VMEM)
MESH = pl.DeviceIdType.MESH
DMA = pltpu.SemaphoreType.DMA


class Place:
    def __init__(self):
        self.z = lax.axis_index("dp")
        self.c = lax.axis_index("ctx")
        self.y = lax.axis_index("fsdp")
        self.x = self.c // 2
        self.k = self.c % 2

    def device(self, z=None, x=None, k=None, y=None):
        z = self.z if z is None else z
        x = self.x if x is None else x
        k = self.k if k is None else k
        y = self.y if y is None else y
        return {"dp": z, "ctx": x * 2 + k, "fsdp": y}

    def x_peer(self):
        return self.device(x=1 - self.x)

    def y_peer(self):
        return self.device(y=1 - self.y)

    def core_peer(self):
        return self.device(k=1 - self.k)


def block_of(x, k, y):
    return y * 4 + x * 2 + k


def remote(src, dst, send_sem, recv_sem, device):
    return pltpu.make_async_remote_copy(
        src_ref=src,
        dst_ref=dst,
        send_sem=send_sem,
        recv_sem=recv_sem,
        device_id=device,
        device_id_type=MESH,
    )


def greet(devices):
    barrier = pltpu.get_barrier_semaphore()
    for device in devices:
        pl.semaphore_signal(barrier, inc=1, device_id=device, device_id_type=MESH)
    pl.semaphore_wait(barrier, len(devices))


class ActGather:
    def __init__(self, me, own, out, send, recv, local):
        self.me, self.own, self.out = me, own, out
        self.send, self.recv, self.local = send, recv, local
        self.rows = own.shape[0]
        self.half = self.rows // 2

    def part(self, ref, block, h):
        return ref.at[block, pl.ds(h * self.half, self.half)]

    def copy(self, i):
        me = self.me
        x, k, y = me.x, me.k, me.y
        own = block_of(x, k, y)
        if i == 0:
            src, dst, dev = self.own.at[pl.ds(0, self.half)], self.part(self.out, own, 0), me.x_peer()
        elif i == 1:
            src, dst, dev = self.own.at[pl.ds(self.half, self.half)], self.part(self.out, own, 1), me.y_peer()
        elif i == 2:
            src, dst, dev = self.own.at[pl.ds(0, self.half)], self.part(self.out, own, 0), me.y_peer()
        elif i == 3:
            b = block_of(1 - x, k, y)
            src, dst, dev = self.part(self.out, b, 0), self.part(self.out, b, 0), me.y_peer()
        elif i == 4:
            src, dst, dev = self.own.at[pl.ds(self.half, self.half)], self.part(self.out, own, 1), me.x_peer()
        elif i == 5:
            b = block_of(x, k, 1 - y)
            src, dst, dev = self.part(self.out, b, 1), self.part(self.out, b, 1), me.x_peer()
        elif i == 6:
            src, dst, dev = self.own, self.out.at[own], me.core_peer()
        else:
            px, py, h = ((1, 0, 0), (0, 1, 1), (0, 1, 0), (1, 1, 0), (1, 0, 1), (1, 1, 1))[i - 7]
            b = block_of(1 - x if px else x, k, 1 - y if py else y)
            src, dst, dev = self.part(self.out, b, h), self.part(self.out, b, h), me.core_peer()
        return remote(src, dst, self.send.at[i], self.recv.at[i], dev)

    def start_x(self):
        for i in (0, 4, 6):
            self.copy(i).start()
        own = block_of(self.me.x, self.me.k, self.me.y)
        pltpu.make_async_copy(self.own, self.out.at[own], self.local).start()

    def start_y(self):
        for i in (1, 2):
            self.copy(i).start()

    def start(self):
        self.start_x()
        self.start_y()

    def forward(self):
        self.copy(0).wait_recv()
        self.copy(3).start()
        self.copy(7).start()
        self.copy(1).wait_recv()
        self.copy(5).start()
        self.copy(8).start()

    def forward_core(self):
        for i in (2, 4, 3, 5):
            self.copy(i).wait_recv()
            self.copy(i + 7).start()

    def finish(self):
        for i in range(6, 13):
            self.copy(i).wait_recv()
        for i in range(13):
            self.copy(i).wait_send()
        own = block_of(self.me.x, self.me.k, self.me.y)
        pltpu.make_async_copy(self.own, self.out.at[own], self.local).wait()


def gather_sems():
    return [DMA((13,)), DMA((13,)), DMA]


class ActReduce:
    def __init__(self, me, peer_out, core_in, mine, a_y, b_x, a_x, b_y, send, recv):
        self.me, self.peer_out, self.core_in, self.mine = me, peer_out, core_in, mine
        self.a_y, self.b_x, self.a_x, self.b_y = a_y, b_x, a_x, b_y
        self.send, self.recv = send, recv
        self.half = mine.shape[1] // 2

    def order(self):
        x, y = self.me.x, self.me.y
        return ((1 - x, 1 - y), (x, 1 - y), (1 - x, y), (x, y))

    def core_copy(self, i):
        ox, oy = self.order()[i]
        return remote(
            self.peer_out.at[i], self.core_in.at[oy * 2 + ox], self.send.at[i], self.recv.at[i], self.me.core_peer()
        )

    def produce(self, i, make):
        ox, oy = self.order()[i]
        self.peer_out[i] = make(block_of(ox, 1 - self.me.k, oy))
        self.core_copy(i).start()
        self.mine[oy * 2 + ox] = make(block_of(ox, self.me.k, oy))

    def rows(self, h):
        return pl.ds(h * self.half, self.half)

    def add(self, slot, h, extra=None):
        def body(i, carry):
            r = pl.ds(pl.multiple_of(h * self.half + i * 16, 16), 16)
            total = self.mine[slot, r, :].astype(F32) + self.core_in[slot, r, :].astype(F32)
            if extra is not None:
                total = total + self.extra(extra, i)
            self.mine[slot, r, :] = total.astype(BF)
            return carry

        lax.fori_loop(0, self.half // 16, body, 0)

    def extra(self, name, i):
        q = pl.ds(pl.multiple_of(i * 16, 16), 16)
        return (self.a_y if name == "a" else self.b_x)[0, q, :].astype(F32)

    def copies(self):
        x, y = self.me.x, self.me.y
        xp, yp = self.me.x_peer(), self.me.y_peer()
        far, yfar, xfar = (1 - y) * 2 + (1 - x), (1 - y) * 2 + x, y * 2 + (1 - x)
        table = {
            "ay0": (far, 0, self.a_y.at[0], 4, yp),
            "ay1": (yfar, 0, self.a_y.at[1], 5, yp),
            "bx0": (far, 1, self.b_x.at[0], 6, xp),
            "bx1": (xfar, 1, self.b_x.at[1], 7, xp),
            "ax": (xfar, 0, self.a_x, 8, xp),
            "by": (yfar, 1, self.b_y, 9, yp),
        }
        return {
            name: remote(self.mine.at[slot, self.rows(h)], dst, self.send.at[i], self.recv.at[i], dev)
            for name, (slot, h, dst, i, dev) in table.items()
        }

    def run(self, make, between=None):
        x, y = self.me.x, self.me.y
        far, yfar, xfar = (1 - y) * 2 + (1 - x), (1 - y) * 2 + x, y * 2 + (1 - x)
        c = self.copies()
        self.produce(0, make)
        self.produce(1, make)
        self.core_copy(0).wait_recv()
        self.add(far, 0)
        c["ay0"].start()
        self.add(far, 1)
        c["bx0"].start()
        self.produce(2, make)
        self.core_copy(1).wait_recv()
        self.add(yfar, 0)
        c["ay1"].start()
        self.produce(3, make)
        self.core_copy(2).wait_recv()
        self.add(xfar, 1)
        c["bx1"].start()
        c["ay0"].wait_recv()
        self.add(xfar, 0, "a")
        c["ax"].start()
        c["bx0"].wait_recv()
        self.add(yfar, 1, "b")
        c["by"].start()
        self.core_copy(3).wait_recv()
        if between is not None:
            between()
        for name in ("ay1", "bx1", "ax", "by"):
            c[name].wait_recv()

    def total(self, h, i):
        slot = self.me.y * 2 + self.me.x
        r = pl.ds(pl.multiple_of(h * self.half + i * 16, 16), 16)
        q = pl.ds(pl.multiple_of(i * 16, 16), 16)
        total = self.mine[slot, r, :].astype(F32) + self.core_in[slot, r, :].astype(F32)
        if h == 0:
            return total + self.a_y[1, q, :].astype(F32) + self.a_x[q, :].astype(F32)
        return total + self.b_x[1, q, :].astype(F32) + self.b_y[q, :].astype(F32)

    def finish(self):
        for i in range(4):
            self.core_copy(i).wait_send()
        for copy in self.copies().values():
            copy.wait_send()


def reduce_scratch(rows, width):
    half = rows // 2
    return [
        pltpu.VMEM((4, rows, width), BF),
        pltpu.VMEM((4, rows, width), BF),
        pltpu.VMEM((4, rows, width), BF),
        pltpu.VMEM((2, half, width), BF),
        pltpu.VMEM((2, half, width), BF),
        pltpu.VMEM((half, width), BF),
        pltpu.VMEM((half, width), BF),
        DMA((10,)),
        DMA((10,)),
    ]


TQ = 256


def softmax_tile(q, k, v, bias, same):
    s = lax.dot_general(q, k, (((1,), (1,)), ((), ())), preferred_element_type=F32) + bias
    s = jnp.where(same, s, MASKED)
    e = jnp.exp(s - jnp.max(s, axis=-1, keepdims=True))
    pb = (e * (1.0 / jnp.sum(e, axis=-1, keepdims=True))).astype(BF)
    return pb, jnp.dot(pb, v, preferred_element_type=F32).astype(BF)


class Line:
    def __init__(self, me, n, views, send_r, send_l, recv):
        self.me, self.n, self.views = me, n, views
        self.send_r, self.send_l, self.recv = send_r, send_l, recv

    def copies(self, t, yy, right):
        me = self.me
        dev = me.device(z=me.z + 1 if right else me.z - 1)
        sem = self.send_r if right else self.send_l
        return [
            remote(view, view, sem.at[t, yy, i], self.recv.at[t, yy, i], dev)
            for i, view in enumerate(self.views(t, yy))
        ]

    def send(self, t, yy, keep, start):
        for right in (True, False):
            go = (self.me.z + 1 <= self.n - 1) if right else (self.me.z >= 1)
            if keep[right] is not None:
                go = go & keep[right]

            @pl.when(go)
            def _():
                for copy in self.copies(t, yy, right):
                    if start:
                        copy.start()
                    else:
                        copy.wait_send()

    def own(self, yy):
        self.send(self.me.z, yy, {True: None, False: None}, True)

    def pump(self, s, yy):
        z, n = self.me.z, self.n
        for right in (True, False):
            t = z - s if right else z + s
            here = (z - s >= 0) if right else (z + s <= n - 1)
            on = (z + 1 <= n - 1) if right else (z >= 1)

            @pl.when(here)
            def _():
                for copy in self.copies(t, yy, right):
                    copy.wait_recv()

            if s < n - 1:

                @pl.when(here & on)
                def _():
                    for copy in self.copies(t, yy, right):
                        copy.start()

    def finish(self):
        z, n = self.me.z, self.n
        for yy in range(2):
            self.send(z, yy, {True: None, False: None}, False)
            for s in range(1, n - 1):
                for right in (True, False):
                    t = z - s if right else z + s
                    here = (z - s >= 0) if right else (z + s <= n - 1)
                    on = (z + 1 <= n - 1) if right else (z >= 1)

                    @pl.when(here & on)
                    def _():
                        for copy in self.copies(t, yy, right):
                            copy.wait_send()


def line_sems(n, parts):
    return [DMA((n, 2, parts))] * 3


def forward_kernel(
    n, length, wq, wk, wv, wo, wg, wu, wd, cot, small, seg, xin,
    wqkv, wof, wgu, wdf, a1, qkv, o, p, mid, a2all, gall, gain1, gain2,
    smalls, segs, segt, xv, wqkv_v, wo_v, qkv_v, o_v, toep, pbuf, a2,
    peer_out, mine, core_in, ra_y, rb_x, ra_x, rb_y,
    y_send, y_recv, y_local, s_send, s_recv, s2_send, s2_recv, s_local, c_local, p_sem, red_send, red_recv,
    *rest,
):
    attn_sems, ffn_sems, x_sems, g_sems = rest[0:3], rest[3:6], rest[6:9], rest[9:12]
    me = Place()
    z, y = me.z, me.y
    rows, width = xin.shape
    piece_rows = wq.shape[0]
    heads = wq.shape[1] // 2
    hid = wg.shape[1] // 2
    group = [
        me.device(x=ox, k=ok, y=oy)
        for ox in (me.x, 1 - me.x)
        for ok in (me.k, 1 - me.k)
        for oy in (me.y, 1 - me.y)
    ][1:]
    others = [me.device(z=lax.rem(z + s, n)) for s in range(1, n)]
    greet(group + others)

    def piece(t, yy):
        return pl.ds(pl.multiple_of((t * 2 + yy) * piece_rows, piece_rows), piece_rows)

    row = piece(z, y)

    def y_copies(yh):
        col = pl.ds(pl.multiple_of(yh * heads, heads), heads)
        fcol = pl.ds(pl.multiple_of(yh * hid, hid), hid)
        return [
            (wq.at[:, col], wqkv.at[row, pl.ds(0, heads)]),
            (wk.at[:, col], wqkv.at[row, pl.ds(heads, heads)]),
            (wv.at[:, col], wqkv.at[row, pl.ds(2 * heads, heads)]),
            (wo.at[col, :], wof.at[:, row]),
            (wg.at[:, fcol], wgu.at[row, pl.ds(0, hid)]),
            (wu.at[:, fcol], wgu.at[row, pl.ds(hid, hid)]),
            (wd.at[fcol, :], wdf.at[:, row]),
        ]

    sends = [
        remote(src, dst, y_send.at[i], y_recv.at[i], me.y_peer())
        for i, (src, dst) in enumerate(y_copies(1 - y))
    ]
    keeps = [pltpu.make_async_copy(src, dst, y_local.at[i]) for i, (src, dst) in enumerate(y_copies(y))]
    me_small = z * 8 + me.c * 2 + y
    small_local = pltpu.make_async_copy(small, smalls.at[me_small], s_local.at[0])
    seg_local = pltpu.make_async_copy(seg, segs.at[y], s_local.at[1])
    small_sends = [
        remote(small, smalls.at[me_small], s_send.at[i], s_recv.at[i], dev) for i, dev in enumerate(group)
    ]
    seg_send = remote(seg, segs.at[y], s_send.at[7], s_recv.at[7], me.y_peer())
    attn = Line(me, n, lambda t, yy: (wqkv.at[piece(t, yy), :], wof.at[:, piece(t, yy)]), *attn_sems)
    ffn = Line(me, n, lambda t, yy: (wgu.at[piece(t, yy), :], wdf.at[:, piece(t, yy)]), *ffn_sems)
    xact = ActGather(me, xin, xv, *x_sems)
    gact = ActGather(me, cot, gall, *g_sems)

    for i in range(4):
        keeps[i].start()
        sends[i].start()
    small_local.start()
    seg_local.start()
    for copy in small_sends:
        copy.start()
    seg_send.start()
    xact.start_x()
    for i in range(4):
        keeps[i].wait()
    attn.own(y)
    for i in range(4):
        sends[i].wait_recv()
    attn.own(1 - y)
    xact.start_y()
    for i in range(4, 7):
        keeps[i].start()
        sends[i].start()
    small_local.wait()
    for copy in small_sends:
        copy.wait_recv()
    block8 = smalls.at[pl.ds(pl.multiple_of(z * 8, 8), 8)]
    small_z = [remote(block8, block8, s2_send.at[i], s2_recv.at[i], dev) for i, dev in enumerate(others)]
    for copy in small_z:
        copy.start()
    xact.forward()
    attn.pump(1, y)
    attn.pump(1, 1 - y)
    xact.forward_core()

    for copy in small_z:
        copy.wait_recv()
    for j in range(4 * n):
        gain1[:, 128 * j : 128 * j + 128] = (smalls[2 * j, :, 0:128] + smalls[2 * j + 1, :, 0:128])[0:1]
        gain2[:, 128 * j : 128 * j + 128] = (smalls[2 * j, :, 128:256] + smalls[2 * j + 1, :, 128:256])[0:1]
    seg_local.wait()
    seg_send.wait_recv()
    for s in range(2):
        wide = jnp.concatenate([segs[s]] * 16, axis=0).astype(F32)
        segt[s] = wide.T
    attn.pump(2, y)
    xact.finish()
    gact.start_x()
    gact.start_y()

    def norm_rows(i, carry):
        r = pl.ds(pl.multiple_of(lax.rem(i, rows // 16) * 16, 16), 16)
        b = i // (rows // 16)
        xf = xv[b, r, :].astype(F32)
        inv = lax.rsqrt(jnp.mean(xf * xf, axis=-1, keepdims=True) + EPSILON)
        xv[b, r, :] = (xf * inv * gain1[...]).astype(BF)
        return carry

    lax.fori_loop(0, 8 * rows // 16, norm_rows, 0)
    a1_out = pltpu.make_async_copy(xv, a1, c_local.at[0])
    a1_out.start()
    attn.pump(2, 1 - y)
    for i in range(4, 7):
        keeps[i].wait()
    ffn.own(y)
    for i in range(4, 7):
        sends[i].wait_recv()
    ffn.own(1 - y)
    gact.forward()
    for yy in (y, 1 - y):
        for s in range(3, n):
            attn.pump(s, yy)
    w_in = pltpu.make_async_copy(wqkv, wqkv_v, c_local.at[1])
    wo_in = pltpu.make_async_copy(wof, wo_v, c_local.at[2])
    w_in.start()
    wo_in.start()
    w_in.wait()

    def project(b, carry):
        r = pl.ds(pl.multiple_of(b * rows, rows), rows)
        qkv_v[r, :] = jnp.dot(xv[b], wqkv_v[...], preferred_element_type=F32).astype(BF)
        return carry

    lax.fori_loop(0, 8, project, 0)
    qkv_out = pltpu.make_async_copy(qkv_v, qkv, c_local.at[3])
    qkv_out.start()
    gact.forward_core()

    offset = lax.broadcasted_iota(jnp.int32, (NB, 2 * length), 1) - length
    far = jnp.abs(offset)
    bucket = jnp.where(far < 8, far, 8 + sum((far >= t).astype(jnp.int32) for t in THRESHOLDS))
    bucket = bucket + 16 * (offset > 0).astype(jnp.int32)
    own_bucket = bucket == lax.broadcasted_iota(jnp.int32, (NB, 2 * length), 0)
    table = smalls[:, 0, 256:384]
    lane = lax.broadcasted_iota(jnp.int32, (NB, 128), 1)
    local_heads = heads // DH
    tiles = length // TQ

    def p_copy(slot, head, t):
        return pltpu.make_async_copy(
            pbuf.at[slot], p.at[head, pl.ds(t * TQ, TQ)], p_sem.at[slot]
        )

    def head_pair(hp):
        for h in range(2):
            head = (me.c * 2 + y) * local_heads + hp * 2 + h
            value = jnp.sum(jnp.where(lane == head, table, 0.0), axis=1, keepdims=True)
            fvec = jnp.sum(jnp.where(own_bucket, value, 0.0), axis=0, keepdims=True)
            toep[h] = pltpu.roll(jnp.broadcast_to(fvec, (TQ, 2 * length)), 0, 1, stride=1, stride_axis=0)

        def sequence(s, carry):
            for h in range(2):
                first = hp * 128
                base = pl.multiple_of(s * length, length)
                kh = qkv_v[pl.ds(base, length), heads + first + h * DH : heads + first + (h + 1) * DH]
                vh = qkv_v[pl.ds(base, length), 2 * heads + first + h * DH : 2 * heads + first + (h + 1) * DH]
                head = s * local_heads + hp * 2 + h
                for t in range(tiles):
                    r = pl.ds(pl.multiple_of(base + t * TQ, TQ), TQ)
                    qt = qkv_v[r, first + h * DH : first + (h + 1) * DH]
                    same = segt[s, t * TQ : (t + 1) * TQ, 0:1] == segs[s, 0:1, :].astype(F32)
                    pb, ot = softmax_tile(
                        qt, kh, vh, toep[h, :, length - t * TQ : 2 * length - t * TQ], same
                    )
                    slot = t % 2
                    if hp or h or t >= 2:
                        p_copy(slot, head, t).wait()
                    else:

                        @pl.when(s > 0)
                        def _():
                            p_copy(slot, head, t).wait()

                    pbuf[slot] = pb
                    p_copy(slot, head, t).start()
                    o_v[r, first + h * DH : first + (h + 1) * DH] = ot
            return carry

        lax.fori_loop(0, 2, sequence, 0)

    head_pair(0)
    ffn.pump(1, y)
    head_pair(1)
    for slot in range(2):
        p_copy(slot, 0, slot).wait()
    o_out = pltpu.make_async_copy(o_v, o, c_local.at[4])
    o_out.start()
    ffn.pump(1, 1 - y)
    wo_in.wait()

    def attn_term(block):
        r = pl.ds(pl.multiple_of(block * rows, rows), rows)
        return jnp.dot(o_v[r, :], wo_v[...], preferred_element_type=F32).astype(BF)

    red = ActReduce(me, peer_out, core_in, mine, ra_y, rb_x, ra_x, rb_y, red_send, red_recv)
    red.run(attn_term, lambda: ffn.pump(2, y))

    half = rows // 2
    for h in range(2):

        def body(i, carry):
            rr = pl.ds(pl.multiple_of(h * half + i * 16, 16), 16)
            m = xin[rr, :].astype(F32) + red.total(h, i)
            mid[rr, :] = m
            inv = lax.rsqrt(jnp.mean(m * m, axis=-1, keepdims=True) + EPSILON)
            a2[rr, :] = (m * inv * gain2[...]).astype(BF)
            return carry

        lax.fori_loop(0, half // 16, body, 0)
    gact.finish()
    aact = ActGather(me, a2, a2all, *rest[12:15])
    aact.start_x()
    aact.start_y()
    aact.forward()
    ffn.pump(2, 1 - y)
    aact.forward_core()
    aact.finish()
    red.finish()
    for yy in (y, 1 - y):
        for s in range(3, n):
            ffn.pump(s, yy)
    attn.finish()
    ffn.finish()
    for copy in small_sends:
        copy.wait_send()
    for copy in small_z:
        copy.wait_send()
    seg_send.wait_send()
    for copy in sends:
        copy.wait_send()
    a1_out.wait()
    qkv_out.wait()
    o_out.wait()


def forward(n, wq, wk, wv, wo, wg, wu, wd, cot, small, seg, xin):
    rows, width = xin.shape
    heads = wq.shape[1] // 2
    hid = wg.shape[1] // 2
    length = seg.shape[1]
    local_heads = heads // DH
    shapes = [
        ((width, 3 * heads), BF),
        ((heads, width), BF),
        ((width, 2 * hid), BF),
        ((hid, width), BF),
        ((8, rows, width), BF),
        ((8 * rows, 3 * heads), BF),
        ((8 * rows, heads), BF),
        ((2 * local_heads, length, length), BF),
        ((rows, width), F32),
        ((8, rows, width), BF),
        ((8, rows, width), BF),
        ((1, width), F32),
        ((1, width), F32),
    ]
    half = rows // 2
    scratch = [
        pltpu.VMEM((8 * n,) + small.shape, F32),
        pltpu.VMEM((2,) + seg.shape, jnp.int32),
        pltpu.VMEM((2, length, 128), F32),
        pltpu.VMEM((8, rows, width), BF),
        pltpu.VMEM((width, 3 * heads), BF),
        pltpu.VMEM((heads, width), BF),
        pltpu.VMEM((8 * rows, 3 * heads), BF),
        pltpu.VMEM((8 * rows, heads), BF),
        pltpu.VMEM((2, TQ, 2 * length), F32),
        pltpu.VMEM((2, TQ, length), BF),
        pltpu.VMEM((rows, width), BF),
        pltpu.VMEM((4, rows, width), BF),
        pltpu.VMEM((4, rows, width), BF),
        pltpu.VMEM((4, rows, width), BF),
        pltpu.VMEM((2, half, width), BF),
        pltpu.VMEM((2, half, width), BF),
        pltpu.VMEM((half, width), BF),
        pltpu.VMEM((half, width), BF),
        DMA((7,)), DMA((7,)), DMA((7,)), DMA((8,)), DMA((8,)), DMA((n - 1,)), DMA((n - 1,)), DMA((2,)),
        DMA((5,)), DMA((2,)), DMA((10,)), DMA((10,)),
    ] + line_sems(n, 2) * 2 + gather_sems() * 3
    return pl.pallas_call(
        functools.partial(forward_kernel, n, length),
        out_shape=[jax.ShapeDtypeStruct(s, d) for s, d in shapes],
        in_specs=[ANY] * 10 + [VM],
        out_specs=[ANY] * 8 + [VM] + [ANY] * 2 + [VM] * 2,
        scratch_shapes=scratch,
        compiler_params=pltpu.CompilerParams(
            collective_id=0, has_side_effects=True, vmem_limit_bytes=60 << 20
        ),
        name="forward",
    )(wq, wk, wv, wo, wg, wu, wd, cot, small, seg, xin)


def neighbours(me):
    return [me.x_peer(), me.y_peer(), me.core_peer()]


def dz_kernel(part, mid, cot, gain, gmid, dzall, ggain, *scratch):
    red = scratch[:9]
    dz, = scratch[9:10]
    gs = scratch[10:]
    me = Place()
    greet(neighbours(me))
    r = ActReduce(me, *red)
    r.run(lambda b: part[b])
    half = mid.shape[0] // 2
    ggain[...] = jnp.zeros_like(ggain)
    for h in range(2):

        def body(i, carry):
            rr = pl.ds(pl.multiple_of(h * half + i * 16, 16), 16)
            ga = r.total(h, i)
            m = mid[rr, :]
            inv = lax.rsqrt(jnp.mean(m * m, axis=-1, keepdims=True) + EPSILON)
            prod = ga * (m * inv)
            ggain[...] += prod[:8] + prod[8:]
            u = ga * gain[...]
            corr = jnp.mean(u * m, axis=-1, keepdims=True) * inv * inv * inv
            gm = cot[rr, :].astype(F32) + inv * u - m * corr
            gmid[rr, :] = gm
            dz[rr, :] = gm.astype(BF)
            return carry

        lax.fori_loop(0, half // 16, body, 0)
    g = ActGather(me, dz, dzall, *gs)
    g.start()
    g.forward()
    g.forward_core()
    g.finish()
    r.finish()


def dz_step(part, mid, cot, gain):
    rows, width = mid.shape
    return pl.pallas_call(
        dz_kernel,
        out_shape=[
            jax.ShapeDtypeStruct((rows, width), F32),
            jax.ShapeDtypeStruct((8, rows, width), BF),
            jax.ShapeDtypeStruct((8, width), F32),
        ],
        in_specs=[VM, VM, VM, VM],
        out_specs=[VM, ANY, VM],
        scratch_shapes=reduce_scratch(rows, width) + [pltpu.VMEM((rows, width), BF)] + gather_sems(),
        compiler_params=pltpu.CompilerParams(collective_id=2, has_side_effects=True, vmem_limit_bytes=60 << 20),
        name="dz_step",
    )(part, mid, cot, gain)


def last_kernel(ga_part, out_part, xin, gmid, mid, gain, gx, out, ggain, *scratch):
    me = Place()
    greet(neighbours(me))
    r = ActReduce(me, *scratch[:9])
    q = ActReduce(me, *scratch[9:18])
    r.run(lambda b: ga_part[b])
    q.run(lambda b: out_part[b])
    half = xin.shape[0] // 2
    ggain[...] = jnp.zeros_like(ggain)
    for h in range(2):

        def body(i, carry):
            rr = pl.ds(pl.multiple_of(h * half + i * 16, 16), 16)
            ga = r.total(h, i)
            m = xin[rr, :].astype(F32)
            inv = lax.rsqrt(jnp.mean(m * m, axis=-1, keepdims=True) + EPSILON)
            prod = ga * (m * inv)
            ggain[...] += prod[:8] + prod[8:]
            u = ga * gain[...]
            corr = jnp.mean(u * m, axis=-1, keepdims=True) * inv * inv * inv
            gx[rr, :] = gmid[rr, :] + inv * u - m * corr
            out[rr, :] = (mid[rr, :] + q.total(h, i)).astype(BF)
            return carry

        lax.fori_loop(0, half // 16, body, 0)
    r.finish()
    q.finish()


def last_step(ga_part, out_part, xin, gmid, mid, gain):
    rows, width = xin.shape
    return pl.pallas_call(
        last_kernel,
        out_shape=[
            jax.ShapeDtypeStruct((rows, width), F32),
            jax.ShapeDtypeStruct((rows, width), BF),
            jax.ShapeDtypeStruct((8, width), F32),
        ],
        in_specs=[VM, VM, VM, VM, VM, VM],
        out_specs=[VM, VM, VM],
        scratch_shapes=reduce_scratch(rows, width) * 2,
        compiler_params=pltpu.CompilerParams(collective_id=3, has_side_effects=True, vmem_limit_bytes=62 << 20),
        name="last_step",
    )(ga_part, out_part, xin, gmid, mid, gain)


def attention_backward(q, k, v, do, p, dq, dk, dv, diag, acc, dkt, dvt):
    length = q.shape[0]
    for h in range(2):
        cols = slice(h * DH, (h + 1) * DH)
        kh = k[:, cols]
        vh = v[:, cols]
        acc[...] = jnp.zeros_like(acc)
        for t in range(length // TQ):
            rows = slice(t * TQ, (t + 1) * TQ)
            pb = p[h, rows, :]
            doh = do[rows, cols]
            qh = q[rows, cols]
            dp = lax.dot_general(doh, vh, (((1,), (1,)), ((), ())), preferred_element_type=F32)
            pf = pb.astype(F32)
            ds = (pf * (dp - jnp.sum(pf * dp, axis=-1, keepdims=True))).astype(BF)
            dq[rows, cols] = jnp.dot(ds, kh, preferred_element_type=F32).astype(BF)
            ck = lax.dot_general(qh, ds, (((0,), (0,)), ((), ())), preferred_element_type=F32)
            cv = lax.dot_general(doh, pb, (((0,), (0,)), ((), ())), preferred_element_type=F32)
            if t == 0:
                dkt[...] = ck
                dvt[...] = cv
            else:
                dkt[...] += ck
                dvt[...] += cv
            acc[:, length - t * TQ : 2 * length - t * TQ] += ds.astype(F32)
        dk[:, cols] = dkt[...].T.astype(BF)
        dv[:, cols] = dvt[...].T.astype(BF)
        n = TQ // 2
        while n >= 8:
            acc[0:n, :] += pltpu.roll(acc[n : 2 * n, :], 2 * length - n, 1)
            n //= 2
        diag[h] = acc[0:8, :]


def run_attention_backward(qkv, do, p):
    total, width = qkv.shape
    heads = width // 3 // DH
    length = p.shape[1]
    seqs = total // length
    pairs = heads // 2
    qspec = lambda off: pl.BlockSpec((length, 2 * DH), lambda s, h: (s, off * pairs + h))
    flat = pl.BlockSpec((length, 2 * DH), lambda s, h: (s, h))
    return pl.pallas_call(
        attention_backward,
        grid=(seqs, pairs),
        out_shape=[jax.ShapeDtypeStruct((total, heads * DH), BF)] * 3
        + [jax.ShapeDtypeStruct((seqs * heads, 8, 2 * length), F32)],
        in_specs=[
            qspec(0),
            qspec(1),
            qspec(2),
            flat,
            pl.BlockSpec((2, length, length), lambda s, h: (s * pairs + h, 0, 0)),
        ],
        out_specs=[flat, flat, flat, pl.BlockSpec((2, 8, 2 * length), lambda s, h: (s * pairs + h, 0, 0))],
        scratch_shapes=[
            pltpu.VMEM((TQ, 2 * length), F32),
            pltpu.VMEM((DH, length), F32),
            pltpu.VMEM((DH, length), F32),
        ],
        compiler_params=pltpu.CompilerParams(vmem_limit_bytes=48 << 20),
        name="attention_backward",
    )(qkv, qkv, qkv, do, p)


def offset_buckets(length):
    relative = jnp.arange(2 * length, dtype=jnp.int32) - length
    distance = jnp.abs(relative)
    log_bucket = 8 + sum((distance >= t).astype(jnp.int32) for t in THRESHOLDS)
    bucket = jnp.where(distance < 8, distance, log_bucket) + 16 * (relative > 0).astype(jnp.int32)
    return (bucket[:, None] == jnp.arange(NB, dtype=jnp.int32)[None, :]).astype(F32)


def swap_rows(part, y, swap):
    rows = part.shape[0] // 2
    mine = lax.dynamic_slice_in_dim(part, y * rows, rows, 0)
    theirs = lax.ppermute(lax.dynamic_slice_in_dim(part, (1 - y) * rows, rows, 0), "fsdp", swap)
    return jnp.where(y == 0, mine, theirs), jnp.where(y == 0, theirs, mine)


def on_device(
    n, hidden, segment_ids, positions, attn_gain, w_query, w_key, w_value, w_attn_out,
    rel_table, ffn_gain, w_gate, w_up, w_down, cotangent,
):
    xin = hidden[0]
    cot = cotangent[0]
    rows, width = xin.shape
    length = segment_ids.shape[1]
    heads = w_query.shape[1] // 2
    hid = w_gate.shape[1] // 2
    y = lax.axis_index("fsdp")
    c = lax.axis_index("ctx")
    swap = [(0, 1), (1, 0)]
    lanes = lambda v: jnp.where(y == 0, jnp.pad(v, (0, 64)), jnp.pad(v, (64, 0))).astype(F32)
    packed = jnp.concatenate([lanes(attn_gain), lanes(ffn_gain), jnp.pad(rel_table.astype(F32), (0, 96))])
    small = jnp.broadcast_to(packed[None, :], (8, packed.shape[0]))
    seg = jnp.broadcast_to(segment_ids, (8, length))
    wqkv, wo, wgu, wd, a1, qkv, o, p, mid, a2all, gall, gain1, gain2 = forward(
        n, w_query, w_key, w_value, w_attn_out, w_gate, w_up, w_down, cot, small, seg, xin
    )
    local_heads = heads // DH
    one_hot = offset_buckets(length)
    a1 = a1.reshape(8 * rows, width)
    a2 = a2all.reshape(8 * rows, width)
    gall = gall.reshape(8 * rows, width)
    gate_up = jnp.dot(a2, wgu, preferred_element_type=F32)
    gate, up = gate_up[:, :hid], gate_up[:, hid:]
    inner = 0.7978845608028654 * (gate + 0.044715 * gate * gate * gate)
    th = jnp.tanh(inner)
    gelu = 0.5 * gate * (1.0 + th)
    slope = 0.5 * (1.0 + th) + 0.5 * gate * (1.0 - th * th) * 0.7978845608028654 * (
        1.0 + 3 * 0.044715 * gate * gate
    )
    m = (gelu * up).astype(BF)
    gm = lax.dot_general(gall, wd, (((1,), (1,)), ((), ())), preferred_element_type=F32)
    dgu = jnp.concatenate([(gm * up * slope).astype(BF), (gm * gelu).astype(BF)], axis=1)
    gw_gu = lax.dot_general(a2, dgu, (((0,), (0,)), ((), ())), preferred_element_type=F32).astype(BF)
    gw_d = lax.dot_general(m, gall, (((0,), (0,)), ((), ())), preferred_element_type=F32).astype(BF)
    ga2 = lax.dot_general(dgu, wgu, (((1,), (1,)), ((), ())), preferred_element_type=F32).astype(BF)
    out_part = jnp.dot(m, wd, preferred_element_type=F32).astype(BF)
    rs_gu = lax.psum_scatter(gw_gu, "dp", scatter_dimension=0, tiled=True)
    rs_d = lax.psum_scatter(gw_d, "dp", scatter_dimension=1, tiled=True)
    gmid, dzall, ggain2 = dz_step(ga2.reshape(8, rows, width), mid, cot, gain2)
    dz = dzall.reshape(8 * rows, width)
    do = lax.dot_general(dz, wo, (((1,), (1,)), ((), ())), preferred_element_type=F32).astype(BF)
    gw_o = lax.dot_general(o, dz, (((0,), (0,)), ((), ())), preferred_element_type=F32).astype(BF)
    rs_o = lax.psum_scatter(gw_o, "dp", scatter_dimension=1, tiled=True)
    dq, dk, dv, diag = run_attention_backward(qkv, do, p)
    dqkv = jnp.concatenate([dq, dk, dv], axis=1)
    gw_qkv = lax.dot_general(a1, dqkv, (((0,), (0,)), ((), ())), preferred_element_type=F32).astype(BF)
    rs_qkv = lax.psum_scatter(gw_qkv, "dp", scatter_dimension=0, tiled=True)
    ga1 = lax.dot_general(dqkv, wqkv, (((1,), (1,)), ((), ())), preferred_element_type=F32).astype(BF)
    gx, out, ggain1 = last_step(
        ga1.reshape(8, rows, width), out_part.reshape(8, rows, width), xin, gmid, mid, gain1
    )

    d8 = jnp.sum(diag.reshape(-1, local_heads, 8, 2 * length), axis=0)
    shifted = sum(jnp.roll(d8[:, r, :], -r, axis=-1) for r in range(8))
    bias = lax.dot_general(
        one_hot, shifted, (((0,), (1,)), ((), ())), precision=lax.Precision.HIGHEST
    )
    table_term = lax.dynamic_update_slice(
        jnp.zeros((NB, H), F32), bias, (jnp.int32(0), (c * 2 + y) * local_heads)
    )
    axes = ("dp", "ctx", "fsdp")
    g_attn_gain = lax.psum_scatter(jnp.sum(ggain1, axis=0), axes, scatter_dimension=0, tiled=True)
    g_ffn_gain = lax.psum_scatter(jnp.sum(ggain2, axis=0), axes, scatter_dimension=0, tiled=True)
    g_table = lax.psum_scatter(table_term.reshape(NB * H), axes, scatter_dimension=0, tiled=True)

    lo, hi = swap_rows(rs_gu, y, swap)
    g_gate = jnp.concatenate([lo[:, :hid], hi[:, :hid]], axis=1).astype(F32)
    g_up = jnp.concatenate([lo[:, hid:], hi[:, hid:]], axis=1).astype(F32)
    lo, hi = swap_rows(rs_qkv, y, swap)
    g_q, g_k, g_v = (
        jnp.concatenate([lo[:, i * heads : (i + 1) * heads], hi[:, i * heads : (i + 1) * heads]], axis=1).astype(F32)
        for i in range(3)
    )

    def swap_cols(part):
        mine = lax.dynamic_slice_in_dim(part, y * rows, rows, 1)
        theirs = lax.ppermute(lax.dynamic_slice_in_dim(part, (1 - y) * rows, rows, 1), "fsdp", swap)
        return jnp.concatenate(
            [jnp.where(y == 0, mine, theirs), jnp.where(y == 0, theirs, mine)], axis=0
        ).astype(F32)

    return (
        out[None], gx[None], g_attn_gain, g_q, g_k, g_v, swap_cols(rs_o), g_table, g_ffn_gain,
        g_gate, g_up, swap_cols(rs_d),
    )


QB = 512


def rms_norm(values, gain):
    return values * lax.rsqrt(jnp.mean(values * values, axis=-1, keepdims=True) + EPSILON) * gain


def gelu_tanh(values):
    return (
        0.5
        * values
        * (1.0 + jnp.tanh(0.7978845608028654 * (values + 0.044715 * values * values * values)))
    )


def bucket_table(query_pos, key_pos):
    relative = key_pos[None, :] - query_pos[:, None]
    distance = jnp.abs(relative)
    log_bucket = 8 + sum(((distance >= threshold).astype(jnp.int32) for threshold in THRESHOLDS))
    bucket = jnp.where(distance < 8, distance, log_bucket)
    return bucket + 16 * (relative > 0).astype(jnp.int32)


def gather_attention(w_query, w_key, w_value, w_attn_out):
    return (
        lax.all_gather(w_query, ("dp", "fsdp"), axis=0, tiled=True),
        lax.all_gather(w_key, ("dp", "fsdp"), axis=0, tiled=True),
        lax.all_gather(w_value, ("dp", "fsdp"), axis=0, tiled=True),
        lax.all_gather(w_attn_out, ("dp", "fsdp"), axis=1, tiled=True),
    )


def gather_feedforward(w_gate, w_up, w_down):
    return (
        lax.all_gather(w_gate, ("dp", "fsdp"), axis=0, tiled=True),
        lax.all_gather(w_up, ("dp", "fsdp"), axis=0, tiled=True),
        lax.all_gather(w_down, ("dp", "fsdp"), axis=1, tiled=True),
    )


def block_masks(segment_row, position_row, start):
    query_pos = lax.dynamic_slice_in_dim(position_row, start, QB)
    query_seg = lax.dynamic_slice_in_dim(segment_row, start, QB)
    buckets = bucket_table(query_pos, position_row)
    one_hot = (buckets[None] == jnp.arange(NB, dtype=jnp.int32)[:, None, None]).astype(jnp.bfloat16)
    same_doc = query_seg[:, None] == segment_row[None, :]
    return (one_hot, same_doc)


def block_scores(query_block, key_rows, table_local, one_hot, same_doc):
    attention_scores = jnp.einsum(
        "ihd,jhd->hij", query_block, key_rows, preferred_element_type=jnp.float32
    )
    attention_scores = attention_scores + jnp.einsum(
        "bij,bh->hij", one_hot, table_local, preferred_element_type=jnp.float32
    )
    return jnp.where(same_doc[None], attention_scores, MASKED)


def layer_forward(tokens, small_set, attn_set, ffn_set, segment_row, position_row):
    attn_gain, ffn_gain, table_flat = small_set
    w_query, w_key, w_value, w_attn_out = attn_set
    w_gate, w_up, w_down = ffn_set
    heads_here = w_query.shape[1] // DH
    head_start = lax.axis_index("ctx") * heads_here
    table_local = lax.dynamic_slice_in_dim(table_flat.reshape(NB, H), head_start, heads_here, 1)
    normalized_rows, attn_back = jax.vjp(rms_norm, tokens, attn_gain.astype(jnp.float32))
    normed_rows = lax.all_gather(normalized_rows.astype(jnp.bfloat16), "ctx", axis=0, tiled=True)
    seq_len = normed_rows.shape[0]
    queries = (
        jnp.dot(normed_rows, w_query, preferred_element_type=jnp.float32)
        .astype(jnp.bfloat16)
        .reshape(seq_len, heads_here, DH)
    )
    key_rows = (
        jnp.dot(normed_rows, w_key, preferred_element_type=jnp.float32)
        .astype(jnp.bfloat16)
        .reshape(seq_len, heads_here, DH)
    )
    value_rows = (
        jnp.dot(normed_rows, w_value, preferred_element_type=jnp.float32)
        .astype(jnp.bfloat16)
        .reshape(seq_len, heads_here, DH)
    )
    starts = jnp.arange(seq_len // QB, dtype=jnp.int32) * QB

    def forward_block(start):
        one_hot, same_doc = block_masks(segment_row, position_row, start)
        query_block = lax.dynamic_slice_in_dim(queries, start, QB, 0)
        attention_scores = block_scores(query_block, key_rows, table_local, one_hot, same_doc)
        row_peak = jnp.max(attention_scores, axis=-1, keepdims=True)
        lifted = jnp.exp(attention_scores - row_peak)
        row_total = jnp.sum(lifted, axis=-1, keepdims=True)
        prob_low = (lifted / row_total).astype(jnp.bfloat16)
        attended_part = jnp.einsum(
            "hij,jhd->ihd", prob_low, value_rows, preferred_element_type=jnp.float32
        )
        return (attended_part, row_peak + jnp.log(row_total))

    attended, log_total = lax.map(forward_block, starts)
    attended_low = attended.reshape(seq_len, heads_here * DH).astype(jnp.bfloat16)
    attn_term = jnp.dot(attended_low, w_attn_out, preferred_element_type=jnp.float32)
    residual = tokens + lax.psum_scatter(attn_term, "ctx", scatter_dimension=0, tiled=True)
    normed_ffn, ffn_back = jax.vjp(rms_norm, residual, ffn_gain.astype(jnp.float32))
    ffn_rows = lax.all_gather(normed_ffn.astype(jnp.bfloat16), "ctx", axis=0, tiled=True)
    gate_value = jnp.dot(ffn_rows, w_gate, preferred_element_type=jnp.float32)
    up_value = jnp.dot(ffn_rows, w_up, preferred_element_type=jnp.float32)
    gelu_gate, gelu_back = jax.vjp(gelu_tanh, gate_value)
    ffn_hidden = (gelu_gate * up_value).astype(jnp.bfloat16)
    down_term = jnp.dot(ffn_hidden, w_down, preferred_element_type=jnp.float32)
    result = residual + lax.psum_scatter(
        down_term.astype(jnp.bfloat16), "ctx", scatter_dimension=0, tiled=True
    ).astype(jnp.float32)
    stored = (
        attn_back,
        normed_rows,
        queries,
        key_rows,
        value_rows,
        table_local,
        head_start,
        starts,
        log_total,
        attended_low,
        ffn_back,
        ffn_rows,
        up_value,
        gelu_gate,
        gelu_back,
        ffn_hidden,
    )
    return (result, stored)


def plain_on_device(
    hidden,
    segment_ids,
    positions,
    attn_gain,
    w_query,
    w_key,
    w_value,
    w_attn_out,
    rel_table,
    ffn_gain,
    w_gate,
    w_up,
    w_down,
    cotangent,
):
    tokens = hidden[0].astype(jnp.float32)
    segment_row = segment_ids[0]
    position_row = positions[0]
    small_set = (
        lax.all_gather(attn_gain, ("dp", "ctx", "fsdp"), axis=0, tiled=True),
        lax.all_gather(ffn_gain, ("dp", "ctx", "fsdp"), axis=0, tiled=True),
        lax.all_gather(rel_table, ("dp", "ctx", "fsdp"), axis=0, tiled=True),
    )
    attn_set = gather_attention(w_query, w_key, w_value, w_attn_out)
    ffn_set = gather_feedforward(w_gate, w_up, w_down)
    result, unused_stored = layer_forward(
        tokens, small_set, attn_set, ffn_set, segment_row, position_row
    )
    back_attn = gather_attention(w_query, w_key, w_value, w_attn_out)
    back_ffn = gather_feedforward(w_gate, w_up, w_down)
    recomputed, stored = layer_forward(
        tokens, small_set, back_attn, back_ffn, segment_row, position_row
    )
    (
        attn_back,
        normed_rows,
        queries,
        key_rows,
        value_rows,
        table_local,
        head_start,
        starts,
        log_total,
        attended_low,
        ffn_back,
        ffn_rows,
        up_value,
        gelu_gate,
        gelu_back,
        ffn_hidden,
    ) = stored
    full_query, full_key, full_value, full_attn_out = back_attn
    full_gate, full_up, full_down = back_ffn
    seq_len = normed_rows.shape[0]
    heads_here = queries.shape[1]
    grad_rows = lax.all_gather(cotangent[0], "ctx", axis=0, tiled=True)
    grad_w_down = jnp.einsum("tf,td->fd", ffn_hidden, grad_rows, preferred_element_type=jnp.float32)
    grad_hidden_ffn = jnp.einsum(
        "td,fd->tf", grad_rows, full_down, preferred_element_type=jnp.float32
    )
    up_value_gradient = (grad_hidden_ffn * gelu_gate).astype(jnp.bfloat16)
    grad_gate_value = gelu_back(grad_hidden_ffn * up_value)[0].astype(jnp.bfloat16)
    grad_w_gate = jnp.einsum(
        "td,tf->df", ffn_rows, grad_gate_value, preferred_element_type=jnp.float32
    )
    grad_w_up = jnp.einsum(
        "td,tf->df", ffn_rows, up_value_gradient, preferred_element_type=jnp.float32
    )
    ffn_normed_term = jnp.einsum(
        "tf,df->td", grad_gate_value, full_gate, preferred_element_type=jnp.float32
    )
    ffn_normed_term = ffn_normed_term + jnp.einsum(
        "tf,df->td", up_value_gradient, full_up, preferred_element_type=jnp.float32
    )
    grad_normed_ffn = lax.psum_scatter(ffn_normed_term, "ctx", scatter_dimension=0, tiled=True)
    grad_residual_norm, grad_ffn_gain = ffn_back(grad_normed_ffn)
    grad_residual = cotangent[0].astype(jnp.float32) + grad_residual_norm
    ffn_sums = (
        lax.psum_scatter(
            grad_w_gate.astype(jnp.bfloat16), ("dp", "fsdp"), scatter_dimension=0, tiled=True
        ).astype(jnp.float32),
        lax.psum_scatter(
            grad_w_up.astype(jnp.bfloat16), ("dp", "fsdp"), scatter_dimension=0, tiled=True
        ).astype(jnp.float32),
        lax.psum_scatter(
            grad_w_down.astype(jnp.bfloat16), ("dp", "fsdp"), scatter_dimension=1, tiled=True
        ).astype(jnp.float32),
    )
    branch_rows = lax.all_gather(grad_residual.astype(jnp.bfloat16), "ctx", axis=0, tiled=True)
    grad_w_attn_out = jnp.einsum(
        "ti,td->id", attended_low, branch_rows, preferred_element_type=jnp.float32
    )
    grad_attended = jnp.einsum(
        "td,id->ti", branch_rows, full_attn_out, preferred_element_type=jnp.float32
    )
    grad_attended = grad_attended.astype(jnp.bfloat16).reshape(seq_len, heads_here, DH)

    def backward_block(operands):
        start, block_total = operands
        one_hot, same_doc = block_masks(segment_row, position_row, start)
        query_block = lax.dynamic_slice_in_dim(queries, start, QB, 0)
        grad_part = lax.dynamic_slice_in_dim(grad_attended, start, QB, 0)
        attention_scores = block_scores(query_block, key_rows, table_local, one_hot, same_doc)
        weights = jnp.exp(attention_scores - block_total)
        prob_low = weights.astype(jnp.bfloat16)
        grad_probs = jnp.einsum(
            "ihd,jhd->hij", grad_part, value_rows, preferred_element_type=jnp.float32
        )
        centred = grad_probs - jnp.sum(weights * grad_probs, axis=-1, keepdims=True)
        grad_scores = (weights * centred).astype(jnp.bfloat16)
        grad_query_part = jnp.einsum(
            "hij,jhd->ihd", grad_scores, key_rows, preferred_element_type=jnp.float32
        )
        grad_key_part = jnp.einsum(
            "hij,ihd->jhd", grad_scores, query_block, preferred_element_type=jnp.float32
        )
        grad_value_part = jnp.einsum(
            "hij,ihd->jhd", prob_low, grad_part, preferred_element_type=jnp.float32
        )
        grad_bias_part = jnp.einsum(
            "hij,bij->bh", grad_scores, one_hot, preferred_element_type=jnp.float32
        )
        return (grad_query_part, grad_key_part, grad_value_part, grad_bias_part)

    query_blocks, key_blocks, value_blocks, bias_blocks = lax.map(
        backward_block, (starts, log_total)
    )
    grad_queries_low = query_blocks.reshape(seq_len, heads_here * DH).astype(jnp.bfloat16)
    grad_keys_low = (
        jnp.sum(key_blocks, axis=0).reshape(seq_len, heads_here * DH).astype(jnp.bfloat16)
    )
    grad_values_low = (
        jnp.sum(value_blocks, axis=0).reshape(seq_len, heads_here * DH).astype(jnp.bfloat16)
    )
    grad_w_query = jnp.einsum(
        "td,te->de", normed_rows, grad_queries_low, preferred_element_type=jnp.float32
    )
    grad_w_key = jnp.einsum(
        "td,te->de", normed_rows, grad_keys_low, preferred_element_type=jnp.float32
    )
    grad_w_value = jnp.einsum(
        "td,te->de", normed_rows, grad_values_low, preferred_element_type=jnp.float32
    )
    normed_term = jnp.einsum(
        "te,de->td", grad_queries_low, full_query, preferred_element_type=jnp.float32
    )
    normed_term = normed_term + jnp.einsum(
        "te,de->td", grad_keys_low, full_key, preferred_element_type=jnp.float32
    )
    normed_term = normed_term + jnp.einsum(
        "te,de->td", grad_values_low, full_value, preferred_element_type=jnp.float32
    )
    grad_normed = lax.psum_scatter(
        normed_term.astype(jnp.bfloat16), "ctx", scatter_dimension=0, tiled=True
    ).astype(jnp.float32)
    token_norm_gradient, grad_attn_gain = attn_back(grad_normed)
    grad_tokens = grad_residual + token_norm_gradient
    attn_sums = (
        lax.psum_scatter(
            grad_w_query.astype(jnp.bfloat16), ("dp", "fsdp"), scatter_dimension=0, tiled=True
        ).astype(jnp.float32),
        lax.psum_scatter(
            grad_w_key.astype(jnp.bfloat16), ("dp", "fsdp"), scatter_dimension=0, tiled=True
        ).astype(jnp.float32),
        lax.psum_scatter(
            grad_w_value.astype(jnp.bfloat16), ("dp", "fsdp"), scatter_dimension=0, tiled=True
        ).astype(jnp.float32),
        lax.psum_scatter(
            grad_w_attn_out.astype(jnp.bfloat16), ("dp", "fsdp"), scatter_dimension=1, tiled=True
        ).astype(jnp.float32),
    )
    bias_sum = jnp.sum(bias_blocks, axis=0)
    table_term = lax.dynamic_update_slice(
        jnp.zeros((NB, H), jnp.float32), bias_sum, (jnp.int32(0), head_start)
    )
    small_sums = (
        lax.psum_scatter(grad_attn_gain, ("dp", "ctx", "fsdp"), scatter_dimension=0, tiled=True),
        lax.psum_scatter(grad_ffn_gain, ("dp", "ctx", "fsdp"), scatter_dimension=0, tiled=True),
        lax.psum_scatter(
            table_term.reshape(NB * H), ("dp", "ctx", "fsdp"), scatter_dimension=0, tiled=True
        ),
    )
    return (
        result[None].astype(jnp.bfloat16),
        grad_tokens[None],
        small_sums[0],
        attn_sums[0],
        attn_sums[1],
        attn_sums[2],
        attn_sums[3],
        small_sums[2],
        small_sums[1],
        ffn_sums[0],
        ffn_sums[1],
        ffn_sums[2],
    )


def plain_solution(mesh):
    in_specs = (
        P(("dp", "fsdp"), "ctx", None),
        P(("dp", "fsdp"), None),
        P(("dp", "fsdp"), None),
        P(("dp", "ctx", "fsdp")),
        P(("dp", "fsdp"), "ctx"),
        P(("dp", "fsdp"), "ctx"),
        P(("dp", "fsdp"), "ctx"),
        P("ctx", ("dp", "fsdp")),
        P(("dp", "ctx", "fsdp")),
        P(("dp", "ctx", "fsdp")),
        P(("dp", "fsdp"), "ctx"),
        P(("dp", "fsdp"), "ctx"),
        P("ctx", ("dp", "fsdp")),
        P(("dp", "fsdp"), "ctx", None),
    )
    out_specs = (
        P(("dp", "fsdp"), "ctx", None),
        P(("dp", "fsdp"), "ctx", None),
        P(("dp", "ctx", "fsdp")),
        P(("dp", "fsdp"), "ctx"),
        P(("dp", "fsdp"), "ctx"),
        P(("dp", "fsdp"), "ctx"),
        P("ctx", ("dp", "fsdp")),
        P(("dp", "ctx", "fsdp")),
        P(("dp", "ctx", "fsdp")),
        P(("dp", "fsdp"), "ctx"),
        P(("dp", "fsdp"), "ctx"),
        P("ctx", ("dp", "fsdp")),
    )
    return jax.shard_map(
        plain_on_device, mesh=mesh, in_specs=in_specs, out_specs=out_specs, check_vma=False
    )


def solution(mesh):
    if 2048 // (mesh.shape["dp"] * mesh.shape["fsdp"]) % 128 or mesh.shape["fsdp"] != 2 or mesh.shape["ctx"] != 4:
        return plain_solution(mesh)
    tokens = P(("dp", "fsdp"), "ctx", None)
    line = P(("dp", "fsdp"), None)
    every = P(("dp", "ctx", "fsdp"))
    into = P(("dp", "fsdp"), "ctx")
    back = P("ctx", ("dp", "fsdp"))
    return jax.shard_map(
        functools.partial(on_device, mesh.shape["dp"]),
        mesh=mesh,
        in_specs=(tokens, line, line, every, into, into, into, back, every, every, into, into, back, tokens),
        out_specs=(tokens, tokens, every, into, into, into, back, every, every, into, into, back),
        check_vma=False,
    )
```

```python
import functools

import jax
import jax.numpy as jnp
from jax import lax
from jax.experimental import pallas as pl
from jax.experimental.pallas import tpu as pltpu
from jax.sharding import PartitionSpec as P

H = 32
DH = 64
NB = 32
EPSILON = 1e-06
THRESHOLDS = (12, 16, 23, 32, 46, 64, 91)
MASKED = -1e30
BF = jnp.bfloat16
F32 = jnp.float32
ANY = pl.BlockSpec(memory_space=pl.ANY)
VM = pl.BlockSpec(memory_space=pltpu.VMEM)
MESH = pl.DeviceIdType.MESH
DMA = pltpu.SemaphoreType.DMA


class Place:
    def __init__(self):
        self.z = lax.axis_index("dp")
        self.c = lax.axis_index("ctx")
        self.y = lax.axis_index("fsdp")
        self.x = self.c // 2
        self.k = self.c % 2

    def device(self, z=None, x=None, k=None, y=None):
        z = self.z if z is None else z
        x = self.x if x is None else x
        k = self.k if k is None else k
        y = self.y if y is None else y
        return {"dp": z, "ctx": x * 2 + k, "fsdp": y}

    def x_peer(self):
        return self.device(x=1 - self.x)

    def y_peer(self):
        return self.device(y=1 - self.y)

    def core_peer(self):
        return self.device(k=1 - self.k)


def block_of(x, k, y):
    return y * 4 + x * 2 + k


def remote(src, dst, send_sem, recv_sem, device):
    return pltpu.make_async_remote_copy(
        src_ref=src,
        dst_ref=dst,
        send_sem=send_sem,
        recv_sem=recv_sem,
        device_id=device,
        device_id_type=MESH,
    )


def greet(devices):
    barrier = pltpu.get_barrier_semaphore()
    for device in devices:
        pl.semaphore_signal(barrier, inc=1, device_id=device, device_id_type=MESH)
    pl.semaphore_wait(barrier, len(devices))


class ActGather:
    def __init__(self, me, own, out, send, recv, local):
        self.me, self.own, self.out = me, own, out
        self.send, self.recv, self.local = send, recv, local
        self.rows = own.shape[0]
        self.half = self.rows // 2

    def part(self, ref, block, h):
        return ref.at[block, pl.ds(h * self.half, self.half)]

    def copy(self, i):
        me = self.me
        x, k, y = me.x, me.k, me.y
        own = block_of(x, k, y)
        if i == 0:
            src, dst, dev = self.own.at[pl.ds(0, self.half)], self.part(self.out, own, 0), me.x_peer()
        elif i == 1:
            src, dst, dev = self.own.at[pl.ds(self.half, self.half)], self.part(self.out, own, 1), me.y_peer()
        elif i == 2:
            src, dst, dev = self.own.at[pl.ds(0, self.half)], self.part(self.out, own, 0), me.y_peer()
        elif i == 3:
            b = block_of(1 - x, k, y)
            src, dst, dev = self.part(self.out, b, 0), self.part(self.out, b, 0), me.y_peer()
        elif i == 4:
            src, dst, dev = self.own.at[pl.ds(self.half, self.half)], self.part(self.out, own, 1), me.x_peer()
        elif i == 5:
            b = block_of(x, k, 1 - y)
            src, dst, dev = self.part(self.out, b, 1), self.part(self.out, b, 1), me.x_peer()
        elif i == 6:
            src, dst, dev = self.own, self.out.at[own], me.core_peer()
        else:
            px, py, h = ((1, 0, 0), (0, 1, 1), (0, 1, 0), (1, 1, 0), (1, 0, 1), (1, 1, 1))[i - 7]
            b = block_of(1 - x if px else x, k, 1 - y if py else y)
            src, dst, dev = self.part(self.out, b, h), self.part(self.out, b, h), me.core_peer()
        return remote(src, dst, self.send.at[i], self.recv.at[i], dev)

    def start_x(self):
        for i in (0, 4, 6):
            self.copy(i).start()
        own = block_of(self.me.x, self.me.k, self.me.y)
        pltpu.make_async_copy(self.own, self.out.at[own], self.local).start()

    def start_y(self):
        for i in (1, 2):
            self.copy(i).start()

    def start(self):
        self.start_x()
        self.start_y()

    def forward(self):
        self.copy(0).wait_recv()
        self.copy(3).start()
        self.copy(7).start()
        self.copy(1).wait_recv()
        self.copy(5).start()
        self.copy(8).start()

    def forward_core(self):
        for i in (2, 4, 3, 5):
            self.copy(i).wait_recv()
            self.copy(i + 7).start()

    def finish(self):
        for i in range(6, 13):
            self.copy(i).wait_recv()
        for i in range(13):
            self.copy(i).wait_send()
        own = block_of(self.me.x, self.me.k, self.me.y)
        pltpu.make_async_copy(self.own, self.out.at[own], self.local).wait()


def gather_sems():
    return [DMA((13,)), DMA((13,)), DMA]


class ActReduce:
    def __init__(self, me, peer_out, core_in, mine, a_y, b_x, a_x, b_y, send, recv):
        self.me, self.peer_out, self.core_in, self.mine = me, peer_out, core_in, mine
        self.a_y, self.b_x, self.a_x, self.b_y = a_y, b_x, a_x, b_y
        self.send, self.recv = send, recv
        self.half = mine.shape[1] // 2

    def place(self, j):
        x, y = self.me.x, self.me.y
        return jnp.where(j % 2 == 0, 1 - x, x), jnp.where(j < 2, 1 - y, y)

    def core_copy(self, j):
        return remote(
            self.peer_out.at[j % 2], self.core_in.at[j], self.send.at[j], self.recv.at[j], self.me.core_peer()
        )

    def rows(self, h):
        return pl.ds(h * self.half, self.half)

    def add(self, slot, h, extra=None):
        def body(i, carry):
            r = pl.ds(pl.multiple_of(h * self.half + i * 16, 16), 16)
            total = self.mine[slot, r, :].astype(F32) + self.core_in[slot, r, :].astype(F32)
            if extra is not None:
                q = pl.ds(pl.multiple_of(i * 16, 16), 16)
                total = total + extra[0, q, :].astype(F32)
            self.mine[slot, r, :] = total.astype(BF)
            return carry

        lax.fori_loop(0, self.half // 16, body, 0)

    def copy(self, name):
        xp, yp = self.me.x_peer(), self.me.y_peer()
        slot, h, dst, i, dev = {
            "ay0": (0, 0, self.a_y.at[0], 4, yp),
            "ay1": (1, 0, self.a_y.at[1], 5, yp),
            "bx0": (0, 1, self.b_x.at[0], 6, xp),
            "bx1": (2, 1, self.b_x.at[1], 7, xp),
            "ax": (2, 0, self.a_x, 8, xp),
            "by": (1, 1, self.b_y, 9, yp),
        }[name]
        return remote(self.mine.at[slot, self.rows(h)], dst, self.send.at[i], self.recv.at[i], dev)

    def first_sends(self, j):
        for name in (("ay0", "bx0"), ("ay1",), ("bx1",))[j]:
            self.copy(name).start()

    def loop(self, make, send=True):
        def ready(j):
            self.core_copy(j).wait_recv()
            if j < 2:
                self.add(j, 0)
            if j != 1:
                self.add(j, 1)
            if send:
                self.first_sends(j)

        def body(j, carry):
            ox, oy = self.place(j)

            @pl.when(j >= 2)
            def _():
                self.core_copy(j - 2).wait_send()

            self.peer_out[j % 2] = make(block_of(ox, 1 - self.me.k, oy), 2 * j)
            self.core_copy(j).start()
            self.mine[j] = make(block_of(ox, self.me.k, oy), 2 * j + 1)
            for i in range(3):

                @pl.when(j == i + 1)
                def _():
                    ready(i)

            return carry

        lax.fori_loop(0, 4, body, 0)

    def second(self):
        self.copy("ay0").wait_recv()
        self.add(2, 0, self.a_y)
        self.copy("ax").start()
        self.copy("bx0").wait_recv()
        self.add(1, 1, self.b_x)
        self.copy("by").start()

    def arrive(self):
        self.core_copy(3).wait_recv()
        for name in ("ay1", "bx1", "ax", "by"):
            self.copy(name).wait_recv()

    def total(self, h, i):
        r = pl.ds(pl.multiple_of(h * self.half + i * 16, 16), 16)
        q = pl.ds(pl.multiple_of(i * 16, 16), 16)
        total = self.mine[3, r, :].astype(F32) + self.core_in[3, r, :].astype(F32)
        if h == 0:
            return total + self.a_y[1, q, :].astype(F32) + self.a_x[q, :].astype(F32)
        return total + self.b_x[1, q, :].astype(F32) + self.b_y[q, :].astype(F32)

    def finish(self):
        for j in (2, 3):
            self.core_copy(j).wait_send()
        for name in ("ay0", "ay1", "bx0", "bx1", "ax", "by"):
            self.copy(name).wait_send()


def reduce_scratch(rows, width):
    half = rows // 2
    return [
        pltpu.VMEM((2, rows, width), BF),
        pltpu.VMEM((4, rows, width), BF),
        pltpu.VMEM((4, rows, width), BF),
        pltpu.VMEM((2, half, width), BF),
        pltpu.VMEM((2, half, width), BF),
        pltpu.VMEM((half, width), BF),
        pltpu.VMEM((half, width), BF),
        DMA((10,)),
        DMA((10,)),
    ]


TQ = 256


def softmax_tile(q, k, v, bias, same):
    s = lax.dot_general(q, k, (((1,), (1,)), ((), ())), preferred_element_type=F32) + bias
    s = jnp.where(same, s, MASKED)
    e = jnp.exp(s - jnp.max(s, axis=-1, keepdims=True))
    pb = (e * (1.0 / jnp.sum(e, axis=-1, keepdims=True))).astype(BF)
    return pb, jnp.dot(pb, v, preferred_element_type=F32).astype(BF)


class Line:
    def __init__(self, me, n, views, send_r, send_l, recv):
        self.me, self.n, self.views = me, n, views
        self.send_r, self.send_l, self.recv = send_r, send_l, recv

    def copies(self, t, yy, right):
        me = self.me
        dev = me.device(z=me.z + 1 if right else me.z - 1)
        sem = self.send_r if right else self.send_l
        return [
            remote(view, view, sem.at[t, yy, i], self.recv.at[t, yy, i], dev)
            for i, view in enumerate(self.views(t, yy))
        ]

    def send(self, t, yy, keep, start):
        for right in (True, False):
            go = (self.me.z + 1 <= self.n - 1) if right else (self.me.z >= 1)
            if keep[right] is not None:
                go = go & keep[right]

            @pl.when(go)
            def _():
                for copy in self.copies(t, yy, right):
                    if start:
                        copy.start()
                    else:
                        copy.wait_send()

    def own(self, yy):
        self.send(self.me.z, yy, {True: None, False: None}, True)

    def pump(self, s, yy):
        z, n = self.me.z, self.n
        for right in (True, False):
            t = z - s if right else z + s
            here = (z - s >= 0) if right else (z + s <= n - 1)
            on = (z + 1 <= n - 1) if right else (z >= 1)

            @pl.when(here)
            def _():
                for copy in self.copies(t, yy, right):
                    copy.wait_recv()

            if s < n - 1:

                @pl.when(here & on)
                def _():
                    for copy in self.copies(t, yy, right):
                        copy.start()

    def finish(self):
        z, n = self.me.z, self.n
        for yy in range(2):
            self.send(z, yy, {True: None, False: None}, False)
            for s in range(1, n - 1):
                for right in (True, False):
                    t = z - s if right else z + s
                    here = (z - s >= 0) if right else (z + s <= n - 1)
                    on = (z + 1 <= n - 1) if right else (z >= 1)

                    @pl.when(here & on)
                    def _():
                        for copy in self.copies(t, yy, right):
                            copy.wait_send()


def line_sems(n, parts):
    return [DMA((n, 2, parts))] * 3


def forward_kernel(
    n, length, wq, wk, wv, wo, wg, wu, wd, cot, small, seg, xin,
    wqkv, wof, wgu, wdf, a1, qkv, o, p, mid, a2all, gall, gain1, gain2,
    smalls, segs, segt, xv, wqkv_v, wo_v, qkv_v, o_v, toep, pbuf, a2,
    peer_out, mine, core_in, ra_y, rb_x, ra_x, rb_y,
    y_send, y_recv, y_local, s_send, s_recv, s2_send, s2_recv, s_local, c_local, p_sem, red_send, red_recv,
    *rest,
):
    attn_sems, ffn_sems, x_sems, g_sems = rest[0:3], rest[3:6], rest[6:9], rest[9:12]
    me = Place()
    z, y = me.z, me.y
    rows, width = xin.shape
    piece_rows = wq.shape[0]
    heads = wq.shape[1] // 2
    hid = wg.shape[1] // 2
    group = [
        me.device(x=ox, k=ok, y=oy)
        for ox in (me.x, 1 - me.x)
        for ok in (me.k, 1 - me.k)
        for oy in (me.y, 1 - me.y)
    ][1:]
    others = [me.device(z=lax.rem(z + s, n)) for s in range(1, n)]
    greet(group + others)

    def piece(t, yy):
        return pl.ds(pl.multiple_of((t * 2 + yy) * piece_rows, piece_rows), piece_rows)

    row = piece(z, y)

    def y_copies(yh):
        col = pl.ds(pl.multiple_of(yh * heads, heads), heads)
        fcol = pl.ds(pl.multiple_of(yh * hid, hid), hid)
        return [
            (wq.at[:, col], wqkv.at[row, pl.ds(0, heads)]),
            (wk.at[:, col], wqkv.at[row, pl.ds(heads, heads)]),
            (wv.at[:, col], wqkv.at[row, pl.ds(2 * heads, heads)]),
            (wo.at[col, :], wof.at[:, row]),
            (wg.at[:, fcol], wgu.at[row, pl.ds(0, hid)]),
            (wu.at[:, fcol], wgu.at[row, pl.ds(hid, hid)]),
            (wd.at[fcol, :], wdf.at[:, row]),
        ]

    sends = [
        remote(src, dst, y_send.at[i], y_recv.at[i], me.y_peer())
        for i, (src, dst) in enumerate(y_copies(1 - y))
    ]
    keeps = [pltpu.make_async_copy(src, dst, y_local.at[i]) for i, (src, dst) in enumerate(y_copies(y))]
    me_small = z * 8 + me.c * 2 + y
    small_local = pltpu.make_async_copy(small, smalls.at[me_small], s_local.at[0])
    seg_local = pltpu.make_async_copy(seg, segs.at[y], s_local.at[1])
    small_sends = [
        remote(small, smalls.at[me_small], s_send.at[i], s_recv.at[i], dev) for i, dev in enumerate(group)
    ]
    seg_send = remote(seg, segs.at[y], s_send.at[7], s_recv.at[7], me.y_peer())
    attn = Line(me, n, lambda t, yy: (wqkv.at[piece(t, yy), :], wof.at[:, piece(t, yy)]), *attn_sems)
    ffn = Line(me, n, lambda t, yy: (wgu.at[piece(t, yy), :], wdf.at[:, piece(t, yy)]), *ffn_sems)
    xact = ActGather(me, xin, xv, *x_sems)
    gact = ActGather(me, cot, gall, *g_sems)

    for i in range(4):
        keeps[i].start()
        sends[i].start()
    small_local.start()
    seg_local.start()
    for copy in small_sends:
        copy.start()
    seg_send.start()
    xact.start_x()
    for i in range(4):
        keeps[i].wait()
    attn.own(y)
    for i in range(4):
        sends[i].wait_recv()
    attn.own(1 - y)
    xact.start_y()
    for i in range(4, 7):
        keeps[i].start()
        sends[i].start()
    small_local.wait()
    for copy in small_sends:
        copy.wait_recv()
    block8 = smalls.at[pl.ds(pl.multiple_of(z * 8, 8), 8)]
    small_z = [remote(block8, block8, s2_send.at[i], s2_recv.at[i], dev) for i, dev in enumerate(others)]
    for copy in small_z:
        copy.start()
    xact.forward()
    attn.pump(1, y)
    attn.pump(1, 1 - y)
    xact.forward_core()

    for copy in small_z:
        copy.wait_recv()
    for j in range(4 * n):
        gain1[:, 128 * j : 128 * j + 128] = (smalls[2 * j, :, 0:128] + smalls[2 * j + 1, :, 0:128])[0:1]
        gain2[:, 128 * j : 128 * j + 128] = (smalls[2 * j, :, 128:256] + smalls[2 * j + 1, :, 128:256])[0:1]
    seg_local.wait()
    seg_send.wait_recv()
    for s in range(2):
        wide = jnp.concatenate([segs[s]] * 16, axis=0).astype(F32)
        segt[s] = wide.T
    attn.pump(2, y)
    xact.finish()
    gact.start_x()
    gact.start_y()

    def norm_rows(i, carry):
        r = pl.ds(pl.multiple_of(lax.rem(i, rows // 16) * 16, 16), 16)
        b = i // (rows // 16)
        xf = xv[b, r, :].astype(F32)
        inv = lax.rsqrt(jnp.mean(xf * xf, axis=-1, keepdims=True) + EPSILON)
        xv[b, r, :] = (xf * inv * gain1[...]).astype(BF)
        return carry

    lax.fori_loop(0, 8 * rows // 16, norm_rows, 0)
    a1_out = pltpu.make_async_copy(xv, a1, c_local.at[0])
    a1_out.start()
    attn.pump(2, 1 - y)
    for i in range(4, 7):
        keeps[i].wait()
    ffn.own(y)
    for i in range(4, 7):
        sends[i].wait_recv()
    ffn.own(1 - y)
    gact.forward()
    for yy in (y, 1 - y):
        for s in range(3, n):
            attn.pump(s, yy)
    w_in = pltpu.make_async_copy(wqkv, wqkv_v, c_local.at[1])
    wo_in = pltpu.make_async_copy(wof, wo_v, c_local.at[2])
    w_in.start()
    wo_in.start()
    w_in.wait()

    def project(b, carry):
        r = pl.ds(pl.multiple_of(b * rows, rows), rows)
        qkv_v[r, :] = jnp.dot(xv[b], wqkv_v[...], preferred_element_type=F32).astype(BF)
        return carry

    lax.fori_loop(0, 8, project, 0)
    qkv_out = pltpu.make_async_copy(qkv_v, qkv, c_local.at[3])
    qkv_out.start()
    gact.forward_core()

    offset = lax.broadcasted_iota(jnp.int32, (NB, 2 * length), 1) - length
    far = jnp.abs(offset)
    bucket = jnp.where(far < 8, far, 8 + sum((far >= t).astype(jnp.int32) for t in THRESHOLDS))
    bucket = bucket + 16 * (offset > 0).astype(jnp.int32)
    own_bucket = bucket == lax.broadcasted_iota(jnp.int32, (NB, 2 * length), 0)
    table = smalls[:, 0, 256:384]
    lane = lax.broadcasted_iota(jnp.int32, (NB, 128), 1)
    local_heads = heads // DH
    tiles = length // TQ

    def p_copy(slot, head, t):
        return pltpu.make_async_copy(
            pbuf.at[slot], p.at[head, pl.ds(t * TQ, TQ)], p_sem.at[slot]
        )

    def head_pair(hp):
        for h in range(2):
            head = (me.c * 2 + y) * local_heads + hp * 2 + h
            value = jnp.sum(jnp.where(lane == head, table, 0.0), axis=1, keepdims=True)
            fvec = jnp.sum(jnp.where(own_bucket, value, 0.0), axis=0, keepdims=True)
            toep[h] = pltpu.roll(jnp.broadcast_to(fvec, (TQ, 2 * length)), 0, 1, stride=1, stride_axis=0)

        def sequence(s, carry):
            for h in range(2):
                first = hp * 128
                base = pl.multiple_of(s * length, length)
                kh = qkv_v[pl.ds(base, length), heads + first + h * DH : heads + first + (h + 1) * DH]
                vh = qkv_v[pl.ds(base, length), 2 * heads + first + h * DH : 2 * heads + first + (h + 1) * DH]
                head = s * local_heads + hp * 2 + h
                for t in range(tiles):
                    r = pl.ds(pl.multiple_of(base + t * TQ, TQ), TQ)
                    qt = qkv_v[r, first + h * DH : first + (h + 1) * DH]
                    same = segt[s, t * TQ : (t + 1) * TQ, 0:1] == segs[s, 0:1, :].astype(F32)
                    pb, ot = softmax_tile(
                        qt, kh, vh, toep[h, :, length - t * TQ : 2 * length - t * TQ], same
                    )
                    slot = t % 2
                    if hp or h or t >= 2:
                        p_copy(slot, head, t).wait()
                    else:

                        @pl.when(s > 0)
                        def _():
                            p_copy(slot, head, t).wait()

                    pbuf[slot] = pb
                    p_copy(slot, head, t).start()
                    o_v[r, first + h * DH : first + (h + 1) * DH] = ot
            return carry

        lax.fori_loop(0, 2, sequence, 0)

    head_pair(0)
    ffn.pump(1, y)
    head_pair(1)
    for slot in range(2):
        p_copy(slot, 0, slot).wait()
    o_out = pltpu.make_async_copy(o_v, o, c_local.at[4])
    o_out.start()
    ffn.pump(1, 1 - y)
    wo_in.wait()

    def attn_term(block, i):
        r = pl.ds(pl.multiple_of(block * rows, rows), rows)
        return jnp.dot(o_v[r, :], wo_v[...], preferred_element_type=F32).astype(BF)

    red = ActReduce(me, peer_out, core_in, mine, ra_y, rb_x, ra_x, rb_y, red_send, red_recv)
    red.loop(attn_term)
    red.second()
    ffn.pump(2, y)
    red.arrive()

    half = rows // 2
    for h in range(2):

        def body(i, carry):
            rr = pl.ds(pl.multiple_of(h * half + i * 16, 16), 16)
            m = xin[rr, :].astype(F32) + red.total(h, i)
            mid[rr, :] = m
            inv = lax.rsqrt(jnp.mean(m * m, axis=-1, keepdims=True) + EPSILON)
            a2[rr, :] = (m * inv * gain2[...]).astype(BF)
            return carry

        lax.fori_loop(0, half // 16, body, 0)
    gact.finish()
    aact = ActGather(me, a2, a2all, *rest[12:15])
    aact.start_x()
    aact.start_y()
    aact.forward()
    ffn.pump(2, 1 - y)
    aact.forward_core()
    aact.finish()
    red.finish()
    for yy in (y, 1 - y):
        for s in range(3, n):
            ffn.pump(s, yy)
    attn.finish()
    ffn.finish()
    for copy in small_sends:
        copy.wait_send()
    for copy in small_z:
        copy.wait_send()
    seg_send.wait_send()
    for copy in sends:
        copy.wait_send()
    a1_out.wait()
    qkv_out.wait()
    o_out.wait()


def forward(n, wq, wk, wv, wo, wg, wu, wd, cot, small, seg, xin):
    rows, width = xin.shape
    heads = wq.shape[1] // 2
    hid = wg.shape[1] // 2
    length = seg.shape[1]
    local_heads = heads // DH
    shapes = [
        ((width, 3 * heads), BF),
        ((heads, width), BF),
        ((width, 2 * hid), BF),
        ((hid, width), BF),
        ((8, rows, width), BF),
        ((8 * rows, 3 * heads), BF),
        ((8 * rows, heads), BF),
        ((2 * local_heads, length, length), BF),
        ((rows, width), F32),
        ((8, rows, width), BF),
        ((8, rows, width), BF),
        ((1, width), F32),
        ((1, width), F32),
    ]
    half = rows // 2
    scratch = [
        pltpu.VMEM((8 * n,) + small.shape, F32),
        pltpu.VMEM((2,) + seg.shape, jnp.int32),
        pltpu.VMEM((2, length, 128), F32),
        pltpu.VMEM((8, rows, width), BF),
        pltpu.VMEM((width, 3 * heads), BF),
        pltpu.VMEM((heads, width), BF),
        pltpu.VMEM((8 * rows, 3 * heads), BF),
        pltpu.VMEM((8 * rows, heads), BF),
        pltpu.VMEM((2, TQ, 2 * length), F32),
        pltpu.VMEM((2, TQ, length), BF),
        pltpu.VMEM((rows, width), BF),
        pltpu.VMEM((2, rows, width), BF),
        pltpu.VMEM((4, rows, width), BF),
        pltpu.VMEM((4, rows, width), BF),
        pltpu.VMEM((2, half, width), BF),
        pltpu.VMEM((2, half, width), BF),
        pltpu.VMEM((half, width), BF),
        pltpu.VMEM((half, width), BF),
        DMA((7,)), DMA((7,)), DMA((7,)), DMA((8,)), DMA((8,)), DMA((n - 1,)), DMA((n - 1,)), DMA((2,)),
        DMA((5,)), DMA((2,)), DMA((10,)), DMA((10,)),
    ] + line_sems(n, 2) * 2 + gather_sems() * 3
    return pl.pallas_call(
        functools.partial(forward_kernel, n, length),
        out_shape=[jax.ShapeDtypeStruct(s, d) for s, d in shapes],
        in_specs=[ANY] * 10 + [VM],
        out_specs=[ANY] * 8 + [VM] + [ANY] * 2 + [VM] * 2,
        scratch_shapes=scratch,
        compiler_params=pltpu.CompilerParams(
            collective_id=0, has_side_effects=True, vmem_limit_bytes=60 << 20
        ),
        name="forward",
    )(wq, wk, wv, wo, wg, wu, wd, cot, small, seg, xin)


class LineSum:
    def __init__(self, me, n, views, from_left, from_right, stage, sems, stage_sem):
        self.me, self.n, self.views = me, n, views
        self.inbox = {True: from_left, False: from_right}
        self.stage, self.stage_sem = stage, stage_sem
        self.sends = {True: sems[0], False: sems[1]}
        self.recvs = {True: sems[2], False: sems[3]}

    def copies(self, t, yy, right):
        me = self.me
        dev = me.device(z=me.z + 1 if right else me.z - 1)
        return [
            remote(
                view, self.inbox[right].at[t, yy, i], self.sends[right].at[t, yy, i],
                self.recvs[right].at[t, yy, i], dev,
            )
            for i, view in enumerate(self.views(t * 2 + yy))
        ]

    def start(self, t, yy, right):
        for copy in self.copies(t, yy, right):
            copy.start()

    def add(self, t, yy, right):
        for i, (copy, view) in enumerate(zip(self.copies(t, yy, right), self.views(t * 2 + yy))):
            copy.wait_recv()
            stage = self.stage[i]
            load = pltpu.make_async_copy(self.inbox[right].at[t, yy, i], stage, self.stage_sem)
            load.start()
            load.wait()

            def body(r, carry):
                rr = pl.ds(pl.multiple_of(r * 16, 16), 16)
                view[rr, :] = (view[rr, :].astype(F32) + stage[rr, :].astype(F32)).astype(BF)
                return carry

            lax.fori_loop(0, view.shape[0] // 16, body, 0)

    def first(self, t, yy):
        @pl.when((self.me.z == 0) & (t > 0))
        def _():
            self.start(t, yy, True)

        @pl.when((self.me.z == self.n - 1) & (t < self.n - 1))
        def _():
            self.start(t, yy, False)

    def pump(self, k, yy):
        z, n = self.me.z, self.n

        @pl.when((z + k <= n - 1) & (z > 0))
        def _():
            self.add(z + k, yy, True)
            self.start(z + k, yy, True)

        @pl.when((z - k >= 0) & (z < n - 1))
        def _():
            self.add(z - k, yy, False)
            self.start(z - k, yy, False)

    def own(self, yy):
        z, n = self.me.z, self.n

        @pl.when(z > 0)
        def _():
            self.add(z, yy, True)

        @pl.when(z < n - 1)
        def _():
            self.add(z, yy, False)

    def finish(self):
        z, n = self.me.z, self.n
        for yy in range(2):
            for k in range(1, n):

                @pl.when(z + k <= n - 1)
                def _():
                    for copy in self.copies(z + k, yy, True):
                        copy.wait_send()

                @pl.when(z - k >= 0)
                def _():
                    for copy in self.copies(z - k, yy, False):
                        copy.wait_send()


def far_first(n, z, i):
    slot = 0
    for a in range(n):
        order = sorted(range(n), key=lambda d: (-abs(d - a), d))
        for b in range(n):
            slot = slot + jnp.where((z == a) & (i == b), order[b], 0)
    return slot


def gelu_parts(gate):
    th = jnp.tanh(0.7978845608028654 * (gate + 0.044715 * gate * gate * gate))
    gelu = 0.5 * gate * (1.0 + th)
    slope = 0.5 * (1.0 + th) + 0.5 * gate * (1.0 - th * th) * 0.7978845608028654 * (
        1.0 + 3 * 0.044715 * gate * gate
    )
    return gelu, slope


def norm_back(ga, values, gain):
    inv = lax.rsqrt(jnp.mean(values * values, axis=-1, keepdims=True) + EPSILON)
    u = ga * gain
    corr = jnp.mean(u * values, axis=-1, keepdims=True) * inv * inv * inv
    return inv * u - values * corr, ga * (values * inv)


def backward_kernel(
    n, length, heads, hid,
    wgu, wdf, a2all, gall, p, a1, qkv, o, wqkv, wof, hidden, mid, cot, gain1, gain2,
    out, gx, fo, ao, sums, dzall, f_left, f_right, a_left, a_right,
    wgu_v, wd_v, row_a, row_g, col_a, col_g, m, dgu, gwf, stage, gmid, dz, wqkv_v,
    pbuf, acc, dkt, dvt, diag, gg1, gg2, sv, sv_in, sv_z, free,
    load, p_sem, stage_sem, y_send, y_recv, y_local, sv_send, sv_recv, sz_send, sz_recv,
    *rest,
):
    red_scratch, dz_sems, f_sems, a_sems = rest[:9], rest[9:12], rest[12:16], rest[16:20]
    me = Place()
    z, y = me.z, me.y
    rows, width = cot.shape
    group = [
        me.device(x=ox, k=ok, y=oy)
        for ox in (me.x, 1 - me.x)
        for ok in (me.k, 1 - me.k)
        for oy in (me.y, 1 - me.y)
    ][1:]
    others = [me.device(z=lax.rem(z + s, n)) for s in range(1, n)]
    greet(group + others)
    local_heads = heads // DH
    half = rows // 2

    def fetch(src, dst, i):
        return pltpu.make_async_copy(src, dst, load.at[i])

    red = ActReduce(me, *red_scratch)
    fsum = LineSum(me, n, lambda pc: [gwf.at[pc]], f_left, f_right, [stage], f_sems, stage_sem)

    def piece(pc):
        return pl.ds(pl.multiple_of(pc * rows, rows), rows)

    asum = LineSum(
        me, n,
        lambda pc: [dgu.at[piece(pc), pl.ds(3 * heads, 2 * heads)], m.at[piece(pc), pl.ds(0, 2 * heads)]],
        a_left, a_right, [stage.at[:, pl.ds(0, 2 * heads)], stage.at[:, pl.ds(2 * heads, 2 * heads)]],
        a_sems, stage_sem,
    )

    w_loads = [fetch(wgu, wgu_v, 0), fetch(wdf, wd_v, 1)]
    for copy in w_loads:
        copy.start()

    def block_at(i):
        j = i // 2
        ox, oy = red.place(j)
        return block_of(ox, jnp.where(i % 2 == 0, 1 - me.k, me.k), oy)

    fetch(a2all.at[block_at(0)], row_a, 2).start()
    fetch(gall.at[block_at(0)], row_g, 3).start()
    for copy in w_loads:
        copy.wait()

    def make_ffn(block, i):
        fetch(a2all.at[block], row_a, 2).wait()
        acc[:, 0 : 2 * hid] = jnp.dot(row_a[...], wgu_v[...], preferred_element_type=F32)

        @pl.when(i < 7)
        def _():
            fetch(a2all.at[block_at(i + 1)], row_a, 2).start()

        fetch(gall.at[block], row_g, 3).wait()
        acc[:, 2 * hid : 3 * hid] = lax.dot_general(
            row_g[...], wd_v[...], (((1,), (1,)), ((), ())), preferred_element_type=F32
        )

        @pl.when(i < 7)
        def _():
            fetch(gall.at[block_at(i + 1)], row_g, 3).start()

        def body(r, carry):
            rr = pl.ds(pl.multiple_of(r * 16, 16), 16)
            tr = pl.ds(pl.multiple_of(block * rows + r * 16, 16), 16)
            gate, up, gm = acc[rr, 0:hid], acc[rr, hid : 2 * hid], acc[rr, 2 * hid : 3 * hid]
            gelu, slope = gelu_parts(gate)
            m[tr, :] = (gelu * up).astype(BF)
            dgu[tr, 0:hid] = (gm * up * slope).astype(BF)
            dgu[tr, hid : 2 * hid] = (gm * gelu).astype(BF)
            return carry

        lax.fori_loop(0, rows // 16, body, 0)
        return lax.dot_general(
            dgu[piece(block), :], wgu_v[...], (((1,), (1,)), ((), ())), preferred_element_type=F32
        ).astype(BF)

    red.loop(make_ffn)

    fetch(wof, row_g, 3).start()

    def piece_at(i):
        return far_first(n, z, i // 2) * 2 + jnp.where(i % 2 == 0, 1 - y, y)

    def columns(ref, i):
        return ref.at[:, :, piece(piece_at(i))]

    fetch(columns(a2all, 0), col_a, 4).start()
    fetch(columns(gall, 0), col_g, 5).start()

    def ffn_grads(i, carry):
        pc = piece_at(i)
        fetch(columns(a2all, i), col_a, 4).wait()
        gwf[pc, :, 0 : 2 * hid] = lax.dot_general(
            col_a[...].reshape(8 * rows, rows), dgu[...], (((0,), (0,)), ((), ())), preferred_element_type=F32
        ).astype(BF)

        @pl.when(i < 2 * n - 1)
        def _():
            fetch(columns(a2all, i + 1), col_a, 4).start()

        fetch(columns(gall, i), col_g, 5).wait()
        gwf[pc, :, 2 * hid : 3 * hid] = lax.dot_general(
            col_g[...].reshape(8 * rows, rows), m[...], (((0,), (0,)), ((), ())), preferred_element_type=F32
        ).astype(BF)

        @pl.when(i < 2 * n - 1)
        def _():
            fetch(columns(gall, i + 1), col_g, 5).start()

        fsum.first(pc // 2, pc % 2)
        return carry

    lax.fori_loop(0, n, ffn_grads, 0)
    red.second()
    fetch(qkv, wgu_v.at[:, pl.ds(0, 3 * heads)], 0).start()
    fetch(o, wgu_v.at[:, pl.ds(3 * heads, heads)], 6).start()
    red.arrive()

    gg2[...] = jnp.zeros_like(gg2)
    for h in range(2):

        def body(i, carry):
            rr = pl.ds(pl.multiple_of(h * half + i * 16, 16), 16)
            back, gains = norm_back(red.total(h, i), mid[rr, :], gain2[...])
            gm = cot[rr, :].astype(F32) + back
            gmid[rr, :] = gm
            dz[rr, :] = gm.astype(BF)
            gg2[...] += gains[:8] + gains[8:]
            return carry

        lax.fori_loop(0, half // 16, body, 0)
    act = ActGather(me, dz, dzall, *dz_sems)
    act.start()
    red.finish()

    def release():
        for i, dev in enumerate((me.x_peer(), me.y_peer(), me.core_peer())):
            pl.semaphore_signal(free.at[i], inc=1, device_id=dev, device_id_type=MESH)

    def claim():
        for i in range(3):
            pl.semaphore_wait(free.at[i], 1)

    release()
    lax.fori_loop(n, 2 * n, ffn_grads, 0)
    act.forward()

    claim()

    def make_out(block, i):
        return jnp.dot(m[piece(block), :], wd_v[...], preferred_element_type=F32).astype(BF)

    red.loop(make_out, send=False)
    order = (1 - y, y)
    fsum.pump(2, order[0])
    act.forward_core()
    for j in range(3):
        red.first_sends(j)
    act.finish()
    fsum.pump(2, order[1])

    fetch(wof, row_g, 3).wait()
    fetch(dzall.at[0], row_a, 2).start()

    def project_back(b, carry):
        fetch(dzall.at[b], row_a, 2).wait()
        wgu_v[piece(b), 4 * heads : 5 * heads] = lax.dot_general(
            row_a[...], row_g[...], (((1,), (1,)), ((), ())), preferred_element_type=F32
        ).astype(BF)

        @pl.when(b < 7)
        def _():
            fetch(dzall.at[b + 1], row_a, 2).start()

        return carry

    lax.fori_loop(0, 8, project_back, 0)
    fetch(hidden, row_a, 2).start()
    fetch(wqkv, wqkv_v, 1).start()
    fetch(qkv, wgu_v.at[:, pl.ds(0, 3 * heads)], 0).wait()
    fetch(o, wgu_v.at[:, pl.ds(3 * heads, heads)], 6).wait()
    diag[...] = jnp.zeros_like(diag)
    tiles = length // TQ

    def p_load(head, t, slot):
        return pltpu.make_async_copy(p.at[head, pl.ds(t * TQ, TQ)], pbuf.at[slot], p_sem.at[slot])

    def head_pair(hp):
        def sequence(s, carry):
            head0 = s * local_heads + hp * 2
            base = pl.multiple_of(s * length, length)
            p_load(head0, 0, 0).start()
            p_load(head0, 1, 1).start()
            for h in range(2):
                lo = hp * 128 + h * DH
                seq = pl.ds(base, length)
                kh = wgu_v[seq, heads + lo : heads + lo + DH]
                vh = wgu_v[seq, 2 * heads + lo : 2 * heads + lo + DH]
                acc[...] = jnp.zeros_like(acc)
                for t in range(tiles):
                    slot = t % 2
                    r = pl.ds(pl.multiple_of(base + t * TQ, TQ), TQ)
                    qh = wgu_v[r, lo : lo + DH]
                    doh = wgu_v[r, 4 * heads + lo : 4 * heads + lo + DH]
                    p_load(head0 + h, t, slot).wait()
                    pb = pbuf[slot]
                    dp = lax.dot_general(doh, vh, (((1,), (1,)), ((), ())), preferred_element_type=F32)
                    pf = pb.astype(F32)
                    ds = (pf * (dp - jnp.sum(pf * dp, axis=-1, keepdims=True))).astype(BF)
                    dgu[r, lo : lo + DH] = jnp.dot(ds, kh, preferred_element_type=F32).astype(BF)
                    ck = lax.dot_general(qh, ds, (((0,), (0,)), ((), ())), preferred_element_type=F32)
                    cv = lax.dot_general(doh, pb, (((0,), (0,)), ((), ())), preferred_element_type=F32)
                    u = h * tiles + t + 2
                    if u < 2 * tiles:
                        p_load(head0 + u // tiles, u % tiles, slot).start()
                    if t == 0:
                        dkt[...] = ck
                        dvt[...] = cv
                    else:
                        dkt[...] += ck
                        dvt[...] += cv
                    acc[:, length - t * TQ : 2 * length - t * TQ] += ds.astype(F32)
                dgu[seq, heads + lo : heads + lo + DH] = dkt[...].T.astype(BF)
                dgu[seq, 2 * heads + lo : 2 * heads + lo + DH] = dvt[...].T.astype(BF)
                c = TQ // 2
                while c >= 8:
                    acc[0:c, :] += pltpu.roll(acc[c : 2 * c, :], 2 * length - c, 1)
                    c //= 2
                diag[hp * 2 + h] += acc[0:8, :]
            return carry

        lax.fori_loop(0, 2, sequence, 0)

    head_pair(0)
    fsum.pump(1, order[0])
    red.second()
    head_pair(1)
    fsum.pump(1, order[1])

    fetch(columns(a1, 0), col_a, 4).start()
    fetch(columns(dzall, 0), col_g, 5).start()

    def attn_grads(i, carry):
        pc = piece_at(i)
        fetch(columns(a1, i), col_a, 4).wait()
        part = lax.dot_general(
            col_a[...].reshape(8 * rows, rows), dgu[:, 0 : 3 * heads], (((0,), (0,)), ((), ())),
            preferred_element_type=F32,
        ).astype(BF)
        dgu[piece(pc), 3 * heads : 5 * heads] = part[:, 0 : 2 * heads]
        m[piece(pc), 0:heads] = part[:, 2 * heads : 3 * heads]

        @pl.when(i < 2 * n - 1)
        def _():
            fetch(columns(a1, i + 1), col_a, 4).start()

        fetch(columns(dzall, i), col_g, 5).wait()
        m[piece(pc), heads : 2 * heads] = lax.dot_general(
            col_g[...].reshape(8 * rows, rows), wgu_v[:, 3 * heads : 4 * heads], (((0,), (0,)), ((), ())),
            preferred_element_type=F32,
        ).astype(BF)

        @pl.when(i < 2 * n - 1)
        def _():
            fetch(columns(dzall, i + 1), col_g, 5).start()

        asum.first(pc // 2, pc % 2)
        return carry

    lax.fori_loop(0, 2 * n, attn_grads, 0)

    red.arrive()
    for h in range(2):

        def body(i, carry):
            rr = pl.ds(pl.multiple_of(h * half + i * 16, 16), 16)
            out[rr, :] = (mid[rr, :] + red.total(h, i)).astype(BF)
            return carry

        lax.fori_loop(0, half // 16, body, 0)
    red.finish()
    release()
    claim()
    fetch(wqkv, wqkv_v, 1).wait()

    def make_ga1(block, i):
        return lax.dot_general(
            dgu[piece(block), 0 : 3 * heads], wqkv_v[...], (((1,), (1,)), ((), ())), preferred_element_type=F32
        ).astype(BF)

    red.loop(make_ga1)

    offset = lax.broadcasted_iota(jnp.int32, (NB, 2 * length), 1) - length
    away = jnp.abs(offset)
    bucket = jnp.where(away < 8, away, 8 + sum((away >= t).astype(jnp.int32) for t in THRESHOLDS))
    bucket = bucket + 16 * (offset > 0).astype(jnp.int32)
    own_bucket = bucket == lax.broadcasted_iota(jnp.int32, (NB, 2 * length), 0)
    lane = lax.broadcasted_iota(jnp.int32, (NB, 128), 1)
    table = jnp.zeros((NB, 128), F32)
    for lh in range(local_heads):
        line = diag[lh, 0:1, :]
        for r in range(1, 8):
            line = line + pltpu.roll(diag[lh, r : r + 1, :], 2 * length - r, 1)
        value = jnp.sum(jnp.where(own_bucket, line, 0.0), axis=1, keepdims=True)
        table = jnp.where(lane == (me.c * 2 + y) * local_heads + lh, value, table)
    red.second()

    fsum.own(order[0])
    red.arrive()
    gg1[...] = jnp.zeros_like(gg1)
    fetch(hidden, row_a, 2).wait()
    for h in range(2):

        def body(i, carry):
            rr = pl.ds(pl.multiple_of(h * half + i * 16, 16), 16)
            back, gains = norm_back(red.total(h, i), row_a[rr, :].astype(F32), gain1[...])
            gx[rr, :] = gmid[rr, :] + back
            gg1[...] += gains[:8] + gains[8:]
            return carry

        lax.fori_loop(0, half // 16, body, 0)
    red.finish()

    first_row = lax.broadcasted_iota(jnp.int32, (8, 128), 0) == 0
    for d in range(8 * n):
        g, zz = d % 8, d // 8
        lanes = slice(d // 2 * 128, d // 2 * 128 + 128)
        sv[g, zz, :, 0:128] = gg1[:, lanes]
        sv[g, zz, :, 128:256] = gg2[:, lanes]
        sv[g, zz, :, 256:384] = jnp.where(first_row, jnp.broadcast_to(table[d : d + 1, :], (8, 128)), 0.0)
    peers = [
        (ox * 4 + ok * 2 + oy)
        for ox in (me.x, 1 - me.x)
        for ok in (me.k, 1 - me.k)
        for oy in (me.y, 1 - me.y)
    ]
    sv_copies = [
        remote(sv.at[peers[i + 1]], sv_in.at[i], sv_send.at[i], sv_recv.at[i], dev)
        for i, dev in enumerate(group)
    ]
    for copy in sv_copies:
        copy.start()

    def swap(line, slot, views, box, i, wait):
        copies = []
        for v, (dst, sem) in enumerate(zip(box, range(i, i + len(box)))):
            copies.append(
                remote(views(z * 2 + 1 - y)[v], dst.at[y], y_send.at[sem], y_recv.at[sem], me.y_peer())
            )
        keeps = [
            pltpu.make_async_copy(views(z * 2 + y)[v], dst.at[y], y_local.at[sem])
            for v, (dst, sem) in enumerate(zip(box, range(i, i + len(box))))
        ]
        return copies, keeps

    ao_boxes = [ao.at[0], ao.at[1]]
    f_out, f_keep = swap(fsum, None, fsum.views, [fo], 0, None)
    a_out, a_keep = swap(asum, None, asum.views, ao_boxes, 1, None)
    for copy in f_out:
        copy.start()
    fsum.own(order[1])
    for copy in f_keep:
        copy.start()
    for yy in order:
        asum.pump(2, yy)
    for copy in sv_copies:
        copy.wait_recv()
    me_g = me.c * 2 + y
    total = sv[me_g]
    for i in range(7):
        total = total + sv_in[i]
    sv_z[0] = total
    z_copies = [
        remote(sv_z.at[0, lax.rem(z + s, n)], sv_z.at[s, 0], sz_send.at[s - 1], sz_recv.at[s - 1], others[s - 1])
        for s in range(1, n)
    ]
    for copy in z_copies:
        copy.start()
    for yy in order:
        asum.pump(1, yy)
    asum.own(order[0])
    for copy in a_out:
        copy.start()
    asum.own(order[1])
    for copy in a_keep:
        copy.start()
    for copy in z_copies:
        copy.wait_recv()
    total = sv_z[0, z]
    for s in range(1, n):
        total = total + sv_z[s, 0]
    sums[...] = total
    for copy in f_out + a_out:
        copy.wait()
    for copy in f_keep + a_keep:
        copy.wait()
    for copy in sv_copies + z_copies:
        copy.wait_send()
    fsum.finish()
    asum.finish()


def backward(n, length, heads, hid, wgu, wdf, a2all, gall, p, a1, qkv, o, wqkv, wof, hidden, mid, cot, gain1, gain2):
    rows, width = cot.shape
    tokens = 8 * rows
    shapes = [
        ((rows, width), BF),
        ((rows, width), F32),
        ((2, rows, 3 * hid), BF),
        ((2, 2, rows, 2 * heads), BF),
        ((8, 384), F32),
        ((8, rows, width), BF),
        ((n, 2, 1, rows, 3 * hid), BF),
        ((n, 2, 1, rows, 3 * hid), BF),
        ((n, 2, 2, rows, 2 * heads), BF),
        ((n, 2, 2, rows, 2 * heads), BF),
    ]
    scratch = [
        pltpu.VMEM((width, 2 * hid), BF),
        pltpu.VMEM((hid, width), BF),
        pltpu.VMEM((rows, width), BF),
        pltpu.VMEM((rows, width), BF),
        pltpu.VMEM((8, rows, rows), BF),
        pltpu.VMEM((8, rows, rows), BF),
        pltpu.VMEM((tokens, hid), BF),
        pltpu.VMEM((tokens, 2 * hid), BF),
        pltpu.VMEM((2 * n, rows, 3 * hid), BF),
        pltpu.VMEM((rows, 3 * hid), BF),
        pltpu.VMEM((rows, width), F32),
        pltpu.VMEM((rows, width), BF),
        pltpu.VMEM((width, 3 * heads), BF),
        pltpu.VMEM((2, TQ, length), BF),
        pltpu.VMEM((TQ, 2 * length), F32),
        pltpu.VMEM((DH, length), F32),
        pltpu.VMEM((DH, length), F32),
        pltpu.VMEM((heads // DH, 8, 2 * length), F32),
        pltpu.VMEM((8, width), F32),
        pltpu.VMEM((8, width), F32),
        pltpu.VMEM((8, n, 8, 384), F32),
        pltpu.VMEM((7, n, 8, 384), F32),
        pltpu.VMEM((n, n, 8, 384), F32),
        pltpu.SemaphoreType.REGULAR((3,)),
        DMA((7,)), DMA((2,)), DMA, DMA((3,)), DMA((3,)), DMA((3,)), DMA((7,)), DMA((7,)), DMA((n - 1,)), DMA((n - 1,)),
    ] + reduce_scratch(rows, width) + gather_sems() + [DMA((n, 2, 1))] * 4 + [DMA((n, 2, 2))] * 4
    return pl.pallas_call(
        functools.partial(backward_kernel, n, length, heads, hid),
        out_shape=[jax.ShapeDtypeStruct(s, d) for s, d in shapes],
        in_specs=[ANY] * 11 + [VM] * 4,
        out_specs=[VM, VM, ANY, ANY, VM] + [ANY] * 5,
        scratch_shapes=scratch,
        compiler_params=pltpu.CompilerParams(
            collective_id=1, has_side_effects=True, vmem_limit_bytes=64 << 20
        ),
        name="backward",
    )(wgu, wdf, a2all, gall, p, a1, qkv, o, wqkv, wof, hidden, mid, cot, gain1, gain2)


def on_device(
    n, hidden, segment_ids, positions, attn_gain, w_query, w_key, w_value, w_attn_out,
    rel_table, ffn_gain, w_gate, w_up, w_down, cotangent,
):
    xin = hidden[0]
    cot = cotangent[0]
    length = segment_ids.shape[1]
    heads = w_query.shape[1] // 2
    hid = w_gate.shape[1] // 2
    share = attn_gain.shape[0]
    y = lax.axis_index("fsdp")
    lanes = lambda v: jnp.where(y == 0, jnp.pad(v, (0, 128 - share)), jnp.pad(v, (128 - share, 0))).astype(F32)
    packed = jnp.concatenate([lanes(attn_gain), lanes(ffn_gain), jnp.pad(rel_table.astype(F32), (0, 128 - H))])
    small = jnp.broadcast_to(packed[None, :], (8, packed.shape[0]))
    seg = jnp.broadcast_to(segment_ids, (8, length))
    wqkv, wo, wgu, wd, a1, qkv, o, p, mid, a2all, gall, gain1, gain2 = forward(
        n, w_query, w_key, w_value, w_attn_out, w_gate, w_up, w_down, cot, small, seg, xin
    )
    out, gx, fo, ao, sums = backward(
        n, length, heads, hid, wgu, wd, a2all, gall, p, a1, qkv, o, wqkv, wo, xin, mid, cot, gain1, gain2
    )[:5]
    sides = lambda part: jnp.concatenate([part[0], part[1]], axis=1).astype(F32)
    g_gate, g_up = sides(fo[:, :, :hid]), sides(fo[:, :, hid : 2 * hid])
    g_down = sides(fo[:, :, 2 * hid :]).T
    g_q, g_k = sides(ao[0, :, :, :heads]), sides(ao[0, :, :, heads:])
    g_v, g_o = sides(ao[1, :, :, :heads]), sides(ao[1, :, :, heads:]).T
    line = jnp.sum(sums, axis=0)
    half_of = lambda v: jnp.where(y == 0, v[:share], v[128 - share :])
    return (
        out[None], gx[None], half_of(line[:128]), g_q, g_k, g_v, g_o, line[256 : 256 + H],
        half_of(line[128:256]), g_gate, g_up, g_down,
    )


QB = 512


def rms_norm(values, gain):
    return values * lax.rsqrt(jnp.mean(values * values, axis=-1, keepdims=True) + EPSILON) * gain


def gelu_tanh(values):
    return (
        0.5
        * values
        * (1.0 + jnp.tanh(0.7978845608028654 * (values + 0.044715 * values * values * values)))
    )


def bucket_table(query_pos, key_pos):
    relative = key_pos[None, :] - query_pos[:, None]
    distance = jnp.abs(relative)
    log_bucket = 8 + sum(((distance >= threshold).astype(jnp.int32) for threshold in THRESHOLDS))
    bucket = jnp.where(distance < 8, distance, log_bucket)
    return bucket + 16 * (relative > 0).astype(jnp.int32)


def gather_attention(w_query, w_key, w_value, w_attn_out):
    return (
        lax.all_gather(w_query, ("dp", "fsdp"), axis=0, tiled=True),
        lax.all_gather(w_key, ("dp", "fsdp"), axis=0, tiled=True),
        lax.all_gather(w_value, ("dp", "fsdp"), axis=0, tiled=True),
        lax.all_gather(w_attn_out, ("dp", "fsdp"), axis=1, tiled=True),
    )


def gather_feedforward(w_gate, w_up, w_down):
    return (
        lax.all_gather(w_gate, ("dp", "fsdp"), axis=0, tiled=True),
        lax.all_gather(w_up, ("dp", "fsdp"), axis=0, tiled=True),
        lax.all_gather(w_down, ("dp", "fsdp"), axis=1, tiled=True),
    )


def block_masks(segment_row, position_row, start):
    query_pos = lax.dynamic_slice_in_dim(position_row, start, QB)
    query_seg = lax.dynamic_slice_in_dim(segment_row, start, QB)
    buckets = bucket_table(query_pos, position_row)
    one_hot = (buckets[None] == jnp.arange(NB, dtype=jnp.int32)[:, None, None]).astype(jnp.bfloat16)
    same_doc = query_seg[:, None] == segment_row[None, :]
    return (one_hot, same_doc)


def block_scores(query_block, key_rows, table_local, one_hot, same_doc):
    attention_scores = jnp.einsum(
        "ihd,jhd->hij", query_block, key_rows, preferred_element_type=jnp.float32
    )
    attention_scores = attention_scores + jnp.einsum(
        "bij,bh->hij", one_hot, table_local, preferred_element_type=jnp.float32
    )
    return jnp.where(same_doc[None], attention_scores, MASKED)


def layer_forward(tokens, small_set, attn_set, ffn_set, segment_row, position_row):
    attn_gain, ffn_gain, table_flat = small_set
    w_query, w_key, w_value, w_attn_out = attn_set
    w_gate, w_up, w_down = ffn_set
    heads_here = w_query.shape[1] // DH
    head_start = lax.axis_index("ctx") * heads_here
    table_local = lax.dynamic_slice_in_dim(table_flat.reshape(NB, H), head_start, heads_here, 1)
    normalized_rows, attn_back = jax.vjp(rms_norm, tokens, attn_gain.astype(jnp.float32))
    normed_rows = lax.all_gather(normalized_rows.astype(jnp.bfloat16), "ctx", axis=0, tiled=True)
    seq_len = normed_rows.shape[0]
    queries = (
        jnp.dot(normed_rows, w_query, preferred_element_type=jnp.float32)
        .astype(jnp.bfloat16)
        .reshape(seq_len, heads_here, DH)
    )
    key_rows = (
        jnp.dot(normed_rows, w_key, preferred_element_type=jnp.float32)
        .astype(jnp.bfloat16)
        .reshape(seq_len, heads_here, DH)
    )
    value_rows = (
        jnp.dot(normed_rows, w_value, preferred_element_type=jnp.float32)
        .astype(jnp.bfloat16)
        .reshape(seq_len, heads_here, DH)
    )
    starts = jnp.arange(seq_len // QB, dtype=jnp.int32) * QB

    def forward_block(start):
        one_hot, same_doc = block_masks(segment_row, position_row, start)
        query_block = lax.dynamic_slice_in_dim(queries, start, QB, 0)
        attention_scores = block_scores(query_block, key_rows, table_local, one_hot, same_doc)
        row_peak = jnp.max(attention_scores, axis=-1, keepdims=True)
        lifted = jnp.exp(attention_scores - row_peak)
        row_total = jnp.sum(lifted, axis=-1, keepdims=True)
        prob_low = (lifted / row_total).astype(jnp.bfloat16)
        attended_part = jnp.einsum(
            "hij,jhd->ihd", prob_low, value_rows, preferred_element_type=jnp.float32
        )
        return (attended_part, row_peak + jnp.log(row_total))

    attended, log_total = lax.map(forward_block, starts)
    attended_low = attended.reshape(seq_len, heads_here * DH).astype(jnp.bfloat16)
    attn_term = jnp.dot(attended_low, w_attn_out, preferred_element_type=jnp.float32)
    residual = tokens + lax.psum_scatter(attn_term, "ctx", scatter_dimension=0, tiled=True)
    normed_ffn, ffn_back = jax.vjp(rms_norm, residual, ffn_gain.astype(jnp.float32))
    ffn_rows = lax.all_gather(normed_ffn.astype(jnp.bfloat16), "ctx", axis=0, tiled=True)
    gate_value = jnp.dot(ffn_rows, w_gate, preferred_element_type=jnp.float32)
    up_value = jnp.dot(ffn_rows, w_up, preferred_element_type=jnp.float32)
    gelu_gate, gelu_back = jax.vjp(gelu_tanh, gate_value)
    ffn_hidden = (gelu_gate * up_value).astype(jnp.bfloat16)
    down_term = jnp.dot(ffn_hidden, w_down, preferred_element_type=jnp.float32)
    result = residual + lax.psum_scatter(
        down_term.astype(jnp.bfloat16), "ctx", scatter_dimension=0, tiled=True
    ).astype(jnp.float32)
    stored = (
        attn_back,
        normed_rows,
        queries,
        key_rows,
        value_rows,
        table_local,
        head_start,
        starts,
        log_total,
        attended_low,
        ffn_back,
        ffn_rows,
        up_value,
        gelu_gate,
        gelu_back,
        ffn_hidden,
    )
    return (result, stored)


def plain_on_device(
    hidden,
    segment_ids,
    positions,
    attn_gain,
    w_query,
    w_key,
    w_value,
    w_attn_out,
    rel_table,
    ffn_gain,
    w_gate,
    w_up,
    w_down,
    cotangent,
):
    tokens = hidden[0].astype(jnp.float32)
    segment_row = segment_ids[0]
    position_row = positions[0]
    small_set = (
        lax.all_gather(attn_gain, ("dp", "ctx", "fsdp"), axis=0, tiled=True),
        lax.all_gather(ffn_gain, ("dp", "ctx", "fsdp"), axis=0, tiled=True),
        lax.all_gather(rel_table, ("dp", "ctx", "fsdp"), axis=0, tiled=True),
    )
    attn_set = gather_attention(w_query, w_key, w_value, w_attn_out)
    ffn_set = gather_feedforward(w_gate, w_up, w_down)
    result, unused_stored = layer_forward(
        tokens, small_set, attn_set, ffn_set, segment_row, position_row
    )
    back_attn = gather_attention(w_query, w_key, w_value, w_attn_out)
    back_ffn = gather_feedforward(w_gate, w_up, w_down)
    recomputed, stored = layer_forward(
        tokens, small_set, back_attn, back_ffn, segment_row, position_row
    )
    (
        attn_back,
        normed_rows,
        queries,
        key_rows,
        value_rows,
        table_local,
        head_start,
        starts,
        log_total,
        attended_low,
        ffn_back,
        ffn_rows,
        up_value,
        gelu_gate,
        gelu_back,
        ffn_hidden,
    ) = stored
    full_query, full_key, full_value, full_attn_out = back_attn
    full_gate, full_up, full_down = back_ffn
    seq_len = normed_rows.shape[0]
    heads_here = queries.shape[1]
    grad_rows = lax.all_gather(cotangent[0], "ctx", axis=0, tiled=True)
    grad_w_down = jnp.einsum("tf,td->fd", ffn_hidden, grad_rows, preferred_element_type=jnp.float32)
    grad_hidden_ffn = jnp.einsum(
        "td,fd->tf", grad_rows, full_down, preferred_element_type=jnp.float32
    )
    up_value_gradient = (grad_hidden_ffn * gelu_gate).astype(jnp.bfloat16)
    grad_gate_value = gelu_back(grad_hidden_ffn * up_value)[0].astype(jnp.bfloat16)
    grad_w_gate = jnp.einsum(
        "td,tf->df", ffn_rows, grad_gate_value, preferred_element_type=jnp.float32
    )
    grad_w_up = jnp.einsum(
        "td,tf->df", ffn_rows, up_value_gradient, preferred_element_type=jnp.float32
    )
    ffn_normed_term = jnp.einsum(
        "tf,df->td", grad_gate_value, full_gate, preferred_element_type=jnp.float32
    )
    ffn_normed_term = ffn_normed_term + jnp.einsum(
        "tf,df->td", up_value_gradient, full_up, preferred_element_type=jnp.float32
    )
    grad_normed_ffn = lax.psum_scatter(ffn_normed_term, "ctx", scatter_dimension=0, tiled=True)
    grad_residual_norm, grad_ffn_gain = ffn_back(grad_normed_ffn)
    grad_residual = cotangent[0].astype(jnp.float32) + grad_residual_norm
    ffn_sums = (
        lax.psum_scatter(
            grad_w_gate.astype(jnp.bfloat16), ("dp", "fsdp"), scatter_dimension=0, tiled=True
        ).astype(jnp.float32),
        lax.psum_scatter(
            grad_w_up.astype(jnp.bfloat16), ("dp", "fsdp"), scatter_dimension=0, tiled=True
        ).astype(jnp.float32),
        lax.psum_scatter(
            grad_w_down.astype(jnp.bfloat16), ("dp", "fsdp"), scatter_dimension=1, tiled=True
        ).astype(jnp.float32),
    )
    branch_rows = lax.all_gather(grad_residual.astype(jnp.bfloat16), "ctx", axis=0, tiled=True)
    grad_w_attn_out = jnp.einsum(
        "ti,td->id", attended_low, branch_rows, preferred_element_type=jnp.float32
    )
    grad_attended = jnp.einsum(
        "td,id->ti", branch_rows, full_attn_out, preferred_element_type=jnp.float32
    )
    grad_attended = grad_attended.astype(jnp.bfloat16).reshape(seq_len, heads_here, DH)

    def backward_block(operands):
        start, block_total = operands
        one_hot, same_doc = block_masks(segment_row, position_row, start)
        query_block = lax.dynamic_slice_in_dim(queries, start, QB, 0)
        grad_part = lax.dynamic_slice_in_dim(grad_attended, start, QB, 0)
        attention_scores = block_scores(query_block, key_rows, table_local, one_hot, same_doc)
        weights = jnp.exp(attention_scores - block_total)
        prob_low = weights.astype(jnp.bfloat16)
        grad_probs = jnp.einsum(
            "ihd,jhd->hij", grad_part, value_rows, preferred_element_type=jnp.float32
        )
        centred = grad_probs - jnp.sum(weights * grad_probs, axis=-1, keepdims=True)
        grad_scores = (weights * centred).astype(jnp.bfloat16)
        grad_query_part = jnp.einsum(
            "hij,jhd->ihd", grad_scores, key_rows, preferred_element_type=jnp.float32
        )
        grad_key_part = jnp.einsum(
            "hij,ihd->jhd", grad_scores, query_block, preferred_element_type=jnp.float32
        )
        grad_value_part = jnp.einsum(
            "hij,ihd->jhd", prob_low, grad_part, preferred_element_type=jnp.float32
        )
        grad_bias_part = jnp.einsum(
            "hij,bij->bh", grad_scores, one_hot, preferred_element_type=jnp.float32
        )
        return (grad_query_part, grad_key_part, grad_value_part, grad_bias_part)

    query_blocks, key_blocks, value_blocks, bias_blocks = lax.map(
        backward_block, (starts, log_total)
    )
    grad_queries_low = query_blocks.reshape(seq_len, heads_here * DH).astype(jnp.bfloat16)
    grad_keys_low = (
        jnp.sum(key_blocks, axis=0).reshape(seq_len, heads_here * DH).astype(jnp.bfloat16)
    )
    grad_values_low = (
        jnp.sum(value_blocks, axis=0).reshape(seq_len, heads_here * DH).astype(jnp.bfloat16)
    )
    grad_w_query = jnp.einsum(
        "td,te->de", normed_rows, grad_queries_low, preferred_element_type=jnp.float32
    )
    grad_w_key = jnp.einsum(
        "td,te->de", normed_rows, grad_keys_low, preferred_element_type=jnp.float32
    )
    grad_w_value = jnp.einsum(
        "td,te->de", normed_rows, grad_values_low, preferred_element_type=jnp.float32
    )
    normed_term = jnp.einsum(
        "te,de->td", grad_queries_low, full_query, preferred_element_type=jnp.float32
    )
    normed_term = normed_term + jnp.einsum(
        "te,de->td", grad_keys_low, full_key, preferred_element_type=jnp.float32
    )
    normed_term = normed_term + jnp.einsum(
        "te,de->td", grad_values_low, full_value, preferred_element_type=jnp.float32
    )
    grad_normed = lax.psum_scatter(
        normed_term.astype(jnp.bfloat16), "ctx", scatter_dimension=0, tiled=True
    ).astype(jnp.float32)
    token_norm_gradient, grad_attn_gain = attn_back(grad_normed)
    grad_tokens = grad_residual + token_norm_gradient
    attn_sums = (
        lax.psum_scatter(
            grad_w_query.astype(jnp.bfloat16), ("dp", "fsdp"), scatter_dimension=0, tiled=True
        ).astype(jnp.float32),
        lax.psum_scatter(
            grad_w_key.astype(jnp.bfloat16), ("dp", "fsdp"), scatter_dimension=0, tiled=True
        ).astype(jnp.float32),
        lax.psum_scatter(
            grad_w_value.astype(jnp.bfloat16), ("dp", "fsdp"), scatter_dimension=0, tiled=True
        ).astype(jnp.float32),
        lax.psum_scatter(
            grad_w_attn_out.astype(jnp.bfloat16), ("dp", "fsdp"), scatter_dimension=1, tiled=True
        ).astype(jnp.float32),
    )
    bias_sum = jnp.sum(bias_blocks, axis=0)
    table_term = lax.dynamic_update_slice(
        jnp.zeros((NB, H), jnp.float32), bias_sum, (jnp.int32(0), head_start)
    )
    small_sums = (
        lax.psum_scatter(grad_attn_gain, ("dp", "ctx", "fsdp"), scatter_dimension=0, tiled=True),
        lax.psum_scatter(grad_ffn_gain, ("dp", "ctx", "fsdp"), scatter_dimension=0, tiled=True),
        lax.psum_scatter(
            table_term.reshape(NB * H), ("dp", "ctx", "fsdp"), scatter_dimension=0, tiled=True
        ),
    )
    return (
        result[None].astype(jnp.bfloat16),
        grad_tokens[None],
        small_sums[0],
        attn_sums[0],
        attn_sums[1],
        attn_sums[2],
        attn_sums[3],
        small_sums[2],
        small_sums[1],
        ffn_sums[0],
        ffn_sums[1],
        ffn_sums[2],
    )


def plain_solution(mesh):
    in_specs = (
        P(("dp", "fsdp"), "ctx", None),
        P(("dp", "fsdp"), None),
        P(("dp", "fsdp"), None),
        P(("dp", "ctx", "fsdp")),
        P(("dp", "fsdp"), "ctx"),
        P(("dp", "fsdp"), "ctx"),
        P(("dp", "fsdp"), "ctx"),
        P("ctx", ("dp", "fsdp")),
        P(("dp", "ctx", "fsdp")),
        P(("dp", "ctx", "fsdp")),
        P(("dp", "fsdp"), "ctx"),
        P(("dp", "fsdp"), "ctx"),
        P("ctx", ("dp", "fsdp")),
        P(("dp", "fsdp"), "ctx", None),
    )
    out_specs = (
        P(("dp", "fsdp"), "ctx", None),
        P(("dp", "fsdp"), "ctx", None),
        P(("dp", "ctx", "fsdp")),
        P(("dp", "fsdp"), "ctx"),
        P(("dp", "fsdp"), "ctx"),
        P(("dp", "fsdp"), "ctx"),
        P("ctx", ("dp", "fsdp")),
        P(("dp", "ctx", "fsdp")),
        P(("dp", "ctx", "fsdp")),
        P(("dp", "fsdp"), "ctx"),
        P(("dp", "fsdp"), "ctx"),
        P("ctx", ("dp", "fsdp")),
    )
    return jax.shard_map(
        plain_on_device, mesh=mesh, in_specs=in_specs, out_specs=out_specs, check_vma=False
    )


def solution(mesh):
    if 2048 // (mesh.shape["dp"] * mesh.shape["fsdp"]) % 128 or mesh.shape["fsdp"] != 2 or mesh.shape["ctx"] != 4:
        return plain_solution(mesh)
    tokens = P(("dp", "fsdp"), "ctx", None)
    line = P(("dp", "fsdp"), None)
    every = P(("dp", "ctx", "fsdp"))
    into = P(("dp", "fsdp"), "ctx")
    back = P("ctx", ("dp", "fsdp"))
    return jax.shard_map(
        functools.partial(on_device, mesh.shape["dp"]),
        mesh=mesh,
        in_specs=(tokens, line, line, every, into, into, into, back, every, every, into, into, back, tokens),
        out_specs=(tokens, tokens, every, into, into, into, back, every, every, into, into, back),
        check_vma=False,
    )
```

```python
import functools

import jax
import jax.numpy as jnp
from jax import lax
from jax.experimental import pallas as pl
from jax.experimental.pallas import tpu as pltpu
from jax.sharding import PartitionSpec as P

H = 32
DH = 64
NB = 32
EPSILON = 1e-06
THRESHOLDS = (12, 16, 23, 32, 46, 64, 91)
MASKED = -1e30
BF = jnp.bfloat16
F32 = jnp.float32
ANY = pl.BlockSpec(memory_space=pl.ANY)
VM = pl.BlockSpec(memory_space=pltpu.VMEM)
MESH = pl.DeviceIdType.MESH
DMA = pltpu.SemaphoreType.DMA


class Place:
    def __init__(self):
        self.z = lax.axis_index("dp")
        self.c = lax.axis_index("ctx")
        self.y = lax.axis_index("fsdp")
        self.x = self.c // 2
        self.k = self.c % 2

    def device(self, z=None, x=None, k=None, y=None):
        z = self.z if z is None else z
        x = self.x if x is None else x
        k = self.k if k is None else k
        y = self.y if y is None else y
        return {"dp": z, "ctx": x * 2 + k, "fsdp": y}

    def x_peer(self):
        return self.device(x=1 - self.x)

    def y_peer(self):
        return self.device(y=1 - self.y)

    def core_peer(self):
        return self.device(k=1 - self.k)


def block_of(x, k, y):
    return y * 4 + x * 2 + k


def remote(src, dst, send_sem, recv_sem, device):
    return pltpu.make_async_remote_copy(
        src_ref=src,
        dst_ref=dst,
        send_sem=send_sem,
        recv_sem=recv_sem,
        device_id=device,
        device_id_type=MESH,
    )


def greet(devices):
    barrier = pltpu.get_barrier_semaphore()
    for device in devices:
        pl.semaphore_signal(barrier, inc=1, device_id=device, device_id_type=MESH)
    pl.semaphore_wait(barrier, len(devices))


class ActGather:
    def __init__(self, me, own, out, send, recv, local):
        self.me, self.own, self.out = me, own, out
        self.send, self.recv, self.local = send, recv, local
        self.rows = own.shape[0]
        self.half = self.rows // 2

    def part(self, ref, block, h):
        return ref.at[block, pl.ds(h * self.half, self.half)]

    def copy(self, i):
        me = self.me
        x, k, y = me.x, me.k, me.y
        own = block_of(x, k, y)
        if i == 0:
            src, dst, dev = self.own.at[pl.ds(0, self.half)], self.part(self.out, own, 0), me.x_peer()
        elif i == 1:
            src, dst, dev = self.own.at[pl.ds(self.half, self.half)], self.part(self.out, own, 1), me.y_peer()
        elif i == 2:
            src, dst, dev = self.own.at[pl.ds(0, self.half)], self.part(self.out, own, 0), me.y_peer()
        elif i == 3:
            b = block_of(1 - x, k, y)
            src, dst, dev = self.part(self.out, b, 0), self.part(self.out, b, 0), me.y_peer()
        elif i == 4:
            src, dst, dev = self.own.at[pl.ds(self.half, self.half)], self.part(self.out, own, 1), me.x_peer()
        elif i == 5:
            b = block_of(x, k, 1 - y)
            src, dst, dev = self.part(self.out, b, 1), self.part(self.out, b, 1), me.x_peer()
        elif i == 6:
            src, dst, dev = self.own, self.out.at[own], me.core_peer()
        else:
            px, py, h = ((1, 0, 0), (0, 1, 1), (0, 1, 0), (1, 1, 0), (1, 0, 1), (1, 1, 1))[i - 7]
            b = block_of(1 - x if px else x, k, 1 - y if py else y)
            src, dst, dev = self.part(self.out, b, h), self.part(self.out, b, h), me.core_peer()
        return remote(src, dst, self.send.at[i], self.recv.at[i], dev)

    def start_x(self):
        for i in (0, 4, 6):
            self.copy(i).start()
        own = block_of(self.me.x, self.me.k, self.me.y)
        pltpu.make_async_copy(self.own, self.out.at[own], self.local).start()

    def start_y(self):
        for i in (1, 2):
            self.copy(i).start()

    def start(self):
        self.start_x()
        self.start_y()

    def onward(self, *steps):
        for i, after in steps:
            self.copy(i).wait_recv()
            if after:
                self.copy(after).start()
            self.copy(i + 7).start()

    def forward(self):
        self.onward((0, 3), (1, 5))

    def forward_core(self):
        self.onward((2, 0), (4, 0), (3, 0), (5, 0))

    def land(self, *pieces):
        for i in pieces:
            self.copy(i).wait_recv()

    def sent(self):
        for i in range(13):
            self.copy(i).wait_send()
        own = block_of(self.me.x, self.me.k, self.me.y)
        pltpu.make_async_copy(self.own, self.out.at[own], self.local).wait()

    def finish(self):
        self.land(*range(6, 13))
        self.sent()


def gather_sems():
    return [DMA((13,)), DMA((13,)), DMA]


class ActReduce:
    def __init__(self, me, peer_out, core_in, mine, a_y, b_x, a_x, b_y, send, recv):
        self.me, self.peer_out, self.core_in, self.mine = me, peer_out, core_in, mine
        self.a_y, self.b_x, self.a_x, self.b_y = a_y, b_x, a_x, b_y
        self.send, self.recv = send, recv
        self.half = mine.shape[1] // 2

    def place(self, j):
        x, y = self.me.x, self.me.y
        return jnp.where(j % 2 == 0, 1 - x, x), jnp.where(j < 2, 1 - y, y)

    def core_copy(self, j):
        return remote(
            self.peer_out.at[j % 2], self.core_in.at[j], self.send.at[j], self.recv.at[j], self.me.core_peer()
        )

    def rows(self, h):
        return pl.ds(h * self.half, self.half)

    def add(self, slot, h, extra=None):
        def body(i, carry):
            r = pl.ds(pl.multiple_of(h * self.half + i * 16, 16), 16)
            total = self.mine[slot, r, :].astype(F32) + self.core_in[slot, r, :].astype(F32)
            if extra is not None:
                q = pl.ds(pl.multiple_of(i * 16, 16), 16)
                total = total + extra[0, q, :].astype(F32)
            self.mine[slot, r, :] = total.astype(BF)
            return carry

        lax.fori_loop(0, self.half // 16, body, 0)

    def copy(self, name):
        xp, yp = self.me.x_peer(), self.me.y_peer()
        slot, h, dst, i, dev = {
            "ay0": (0, 0, self.a_y.at[0], 4, yp),
            "ay1": (1, 0, self.a_y.at[1], 5, yp),
            "bx0": (0, 1, self.b_x.at[0], 6, xp),
            "bx1": (2, 1, self.b_x.at[1], 7, xp),
            "ax": (2, 0, self.a_x, 8, xp),
            "by": (1, 1, self.b_y, 9, yp),
        }[name]
        return remote(self.mine.at[slot, self.rows(h)], dst, self.send.at[i], self.recv.at[i], dev)

    def first_sends(self, j):
        for name in (("ay0", "bx0"), ("ay1",), ("bx1",))[j]:
            self.copy(name).start()

    def loop(self, make, send=True, first=0, last=4, hooks=()):
        def ready(j):
            self.core_copy(j).wait_recv()
            if j < 2:
                self.add(j, 0)
            if j != 1:
                self.add(j, 1)
            if send:
                self.first_sends(j)

        def body(j, carry):
            ox, oy = self.place(j)

            @pl.when(j >= 2)
            def _():
                self.core_copy(j - 2).wait_send()

            self.peer_out[j % 2] = make(block_of(ox, 1 - self.me.k, oy), 2 * j)
            self.core_copy(j).start()
            self.mine[j] = make(block_of(ox, self.me.k, oy), 2 * j + 1)
            for i in range(3):

                @pl.when(j == i + 1)
                def _():
                    ready(i)

            for i, hook in hooks:

                @pl.when(j == i)
                def _():
                    hook()

            return carry

        lax.fori_loop(first, last, body, 0)

    def second(self):
        self.copy("ay0").wait_recv()
        self.add(2, 0, self.a_y)
        self.copy("ax").start()
        self.copy("bx0").wait_recv()
        self.add(1, 1, self.b_x)
        self.copy("by").start()

    def arrive(self):
        self.core_copy(3).wait_recv()
        for name in ("ay1", "bx1", "ax", "by"):
            self.copy(name).wait_recv()

    def total(self, h, i):
        r = pl.ds(pl.multiple_of(h * self.half + i * 16, 16), 16)
        q = pl.ds(pl.multiple_of(i * 16, 16), 16)
        total = self.mine[3, r, :].astype(F32) + self.core_in[3, r, :].astype(F32)
        if h == 0:
            return total + self.a_y[1, q, :].astype(F32) + self.a_x[q, :].astype(F32)
        return total + self.b_x[1, q, :].astype(F32) + self.b_y[q, :].astype(F32)

    def finish(self):
        for j in (2, 3):
            self.core_copy(j).wait_send()
        for name in ("ay0", "ay1", "bx0", "bx1", "ax", "by"):
            self.copy(name).wait_send()


def reduce_scratch(rows, width):
    half = rows // 2
    return [
        pltpu.VMEM((2, rows, width), BF),
        pltpu.VMEM((4, rows, width), BF),
        pltpu.VMEM((4, rows, width), BF),
        pltpu.VMEM((2, half, width), BF),
        pltpu.VMEM((2, half, width), BF),
        pltpu.VMEM((half, width), BF),
        pltpu.VMEM((half, width), BF),
        DMA((10,)),
        DMA((10,)),
    ]


TQ = 256


def softmax_tile(q, k, v, bias, same):
    s = lax.dot_general(q, k, (((1,), (1,)), ((), ())), preferred_element_type=F32) + bias
    s = jnp.where(same, s, MASKED)
    e = jnp.exp(s - jnp.max(s, axis=-1, keepdims=True))
    pb = (e * (1.0 / jnp.sum(e, axis=-1, keepdims=True))).astype(BF)
    return pb, jnp.dot(pb, v, preferred_element_type=F32).astype(BF)


class Line:
    def __init__(self, me, n, views, send_r, send_l, recv):
        self.me, self.n, self.views = me, n, views
        self.send_r, self.send_l, self.recv = send_r, send_l, recv

    def copies(self, t, yy, right):
        me = self.me
        dev = me.device(z=me.z + 1 if right else me.z - 1)
        sem = self.send_r if right else self.send_l
        return [
            remote(view, view, sem.at[t, yy, i], self.recv.at[t, yy, i], dev)
            for i, view in enumerate(self.views(t, yy))
        ]

    def send(self, t, yy, keep, start):
        for right in (True, False):
            go = (self.me.z + 1 <= self.n - 1) if right else (self.me.z >= 1)
            if keep[right] is not None:
                go = go & keep[right]

            @pl.when(go)
            def _():
                for copy in self.copies(t, yy, right):
                    if start:
                        copy.start()
                    else:
                        copy.wait_send()

    def own(self, yy):
        self.send(self.me.z, yy, {True: None, False: None}, True)

    def came(self, s):
        z, n = self.me.z, self.n
        return (
            (True, z - s, z - s >= 0, z + 1 <= n - 1),
            (False, z + s, z + s <= n - 1, z >= 1),
        )

    def pump(self, s, yy):
        for right, t, here, on in self.came(s):

            @pl.when(here & on)
            def _():
                for copy in self.copies(t, yy, right):
                    copy.wait_recv()
                    copy.start()

    def land(self, yys):
        for s in range(1, self.n):
            for yy in yys:
                for right, t, here, on in self.came(s):

                    @pl.when(here & jnp.logical_not(on))
                    def _():
                        for copy in self.copies(t, yy, right):
                            copy.wait_recv()

    def finish(self):
        for yy in range(2):
            self.send(self.me.z, yy, {True: None, False: None}, False)
            for s in range(1, self.n):
                for right, t, here, on in self.came(s):

                    @pl.when(here & on)
                    def _():
                        for copy in self.copies(t, yy, right):
                            copy.wait_send()


def line_sems(n, parts):
    return [DMA((n, 2, parts))] * 3


def forward_kernel(
    n, length, wq, wk, wv, wo, wg, wu, wd, cot, xin, seg_row, gain_a, gain_f, table_row,
    wqkv, wof, wg1, wd1, wg2, wd2, a1, qkv, o, p, mid, a2all, gall, m1, dgu1, gwf1, gain1, gain2,
    small, seg, smalls, segs, segt, xv, wqkv_v, wo_v, qkv_v, o_v, toep, pbuf, a2, wg1_v, wd1_v, gw_v, acc,
    y_send, y_recv, y_local, s_send, s_recv, s2_send, s2_recv, s_local, c_local, p_sem, f_sem,
    *rest,
):
    red_scratch, f1_sems, f2_sems, in_sems, wo_sems = rest[0:9], rest[9:12], rest[12:15], rest[15:18], rest[18:21]
    x_sems, g_sems, a_sems = rest[21:24], rest[24:27], rest[27:30]
    me = Place()
    z, y = me.z, me.y
    rows, width = xin.shape
    piece_rows = wq.shape[0]
    heads = wq.shape[1] // 2
    hid = wg.shape[1] // 2
    h1 = wd1.shape[0]
    h2 = hid - h1
    group = [
        me.device(x=ox, k=ok, y=oy)
        for ox in (me.x, 1 - me.x)
        for ok in (me.k, 1 - me.k)
        for oy in (me.y, 1 - me.y)
    ][1:]
    others = [me.device(z=lax.rem(z + s, n)) for s in range(1, n)]
    greet(group + others)
    small[...] = jnp.zeros_like(small)
    share = gain_a.shape[1]
    for yy in range(2):

        @pl.when(y == yy)
        def _():
            for i, ref in enumerate((gain_a, gain_f)):
                at = i * 128 + yy * share
                small[:, at : at + share] = jnp.broadcast_to(ref[...].astype(F32), (8, share))

    small[:, 256 : 256 + table_row.shape[1]] = jnp.broadcast_to(table_row[...].astype(F32), (8, table_row.shape[1]))
    seg[...] = jnp.broadcast_to(seg_row[...], seg.shape)

    def piece(t, yy):
        return pl.ds(pl.multiple_of((t * 2 + yy) * piece_rows, piece_rows), piece_rows)

    row = piece(z, y)

    def y_copies(yh):
        col = pl.ds(pl.multiple_of(yh * heads, heads), heads)
        at1 = pl.ds(pl.multiple_of(yh * hid, 128), h1)
        at2 = pl.ds(pl.multiple_of(yh * hid + h1, 128), h2)
        return [
            (wq.at[:, col], wqkv.at[row, pl.ds(0, heads)]),
            (wk.at[:, col], wqkv.at[row, pl.ds(heads, heads)]),
            (wv.at[:, col], wqkv.at[row, pl.ds(2 * heads, heads)]),
            (wo.at[col, :], wof.at[:, row]),
            (wg.at[:, at1], wg1.at[row, pl.ds(0, h1)]),
            (wu.at[:, at1], wg1.at[row, pl.ds(h1, h1)]),
            (wd.at[at1, :], wd1.at[:, row]),
            (wg.at[:, at2], wg2.at[row, pl.ds(0, h2)]),
            (wu.at[:, at2], wg2.at[row, pl.ds(h2, h2)]),
            (wd.at[at2, :], wd2.at[:, row]),
        ]

    sends = [
        remote(src, dst, y_send.at[i], y_recv.at[i], me.y_peer())
        for i, (src, dst) in enumerate(y_copies(1 - y))
    ]
    keeps = [pltpu.make_async_copy(src, dst, y_local.at[i]) for i, (src, dst) in enumerate(y_copies(y))]
    me_small = z * 8 + me.c * 2 + y
    small_local = pltpu.make_async_copy(small, smalls.at[me_small], s_local.at[0])
    seg_local = pltpu.make_async_copy(seg, segs.at[y], s_local.at[1])
    small_sends = [
        remote(small, smalls.at[me_small], s_send.at[i], s_recv.at[i], dev) for i, dev in enumerate(group)
    ]
    seg_send = remote(seg, segs.at[y], s_send.at[7], s_recv.at[7], me.y_peer())
    attn = Line(me, n, lambda t, yy: (wqkv.at[piece(t, yy), :],), *in_sems)
    attn_o = Line(me, n, lambda t, yy: (wof.at[:, piece(t, yy)],), *wo_sems)
    f1 = Line(me, n, lambda t, yy: (wg1.at[piece(t, yy), :], wd1.at[:, piece(t, yy)]), *f1_sems)
    f2 = Line(me, n, lambda t, yy: (wg2.at[piece(t, yy), :], wd2.at[:, piece(t, yy)]), *f2_sems)
    xact = ActGather(me, xin, xv, *x_sems)
    gact = ActGather(me, cot, gall, *g_sems)

    for i in range(4):
        keeps[i].start()
        sends[i].start()
    small_local.start()
    seg_local.start()
    for copy in small_sends:
        copy.start()
    seg_send.start()
    xact.start_x()
    for i in range(4, 10):
        keeps[i].start()
    for i in range(4):
        keeps[i].wait()
    attn.own(y)
    for i in range(4):
        sends[i].wait_recv()
    attn.own(1 - y)
    xact.start_y()
    small_local.wait()
    for copy in small_sends:
        copy.wait_recv()
    block8 = smalls.at[pl.ds(pl.multiple_of(z * 8, 8), 8)]
    small_z = [remote(block8, block8, s2_send.at[i], s2_recv.at[i], dev) for i, dev in enumerate(others)]
    for copy in small_z:
        copy.start()
    xact.onward((0, 3))
    attn.pump(1, y)
    attn.pump(1, 1 - y)
    xact.onward((1, 5))
    for i in range(4, 10):
        sends[i].start()
    gact.start()

    for copy in small_z:
        copy.wait_recv()
    for j in range(4 * n):
        gain1[:, 128 * j : 128 * j + 128] = (smalls[2 * j, :, 0:128] + smalls[2 * j + 1, :, 0:128])[0:1]
        gain2[:, 128 * j : 128 * j + 128] = (smalls[2 * j, :, 128:256] + smalls[2 * j + 1, :, 128:256])[0:1]
    seg_local.wait()
    seg_send.wait_recv()
    for s in range(2):
        wide = jnp.concatenate([segs[s]] * 16, axis=0).astype(F32)
        segt[s] = wide.T
    attn.pump(2, y)
    xact.onward((2, 0), (4, 0))
    attn.pump(2, 1 - y)
    attn_o.own(y)
    attn_o.own(1 - y)
    for i in range(4, 7):
        keeps[i].wait()
    f1.own(y)
    offset = lax.broadcasted_iota(jnp.int32, (NB, 2 * length), 1) - length
    far = jnp.abs(offset)
    bucket = jnp.where(far < 8, far, 8 + sum((far >= t).astype(jnp.int32) for t in THRESHOLDS))
    bucket = bucket + 16 * (offset > 0).astype(jnp.int32)
    own_bucket = bucket == lax.broadcasted_iota(jnp.int32, (NB, 2 * length), 0)
    table = smalls[:, 0, 256:384]
    lane = lax.broadcasted_iota(jnp.int32, (NB, 128), 1)
    local_heads = heads // DH
    for lh in range(local_heads):
        head = (me.c * 2 + y) * local_heads + lh
        value = jnp.sum(jnp.where(lane == head, table, 0.0), axis=1, keepdims=True)
        fvec = jnp.sum(jnp.where(own_bucket, value, 0.0), axis=0, keepdims=True)
        toep[lh] = pltpu.roll(jnp.broadcast_to(fvec, (TQ, 2 * length)), 0, 1, stride=1, stride_axis=0)
    xact.onward((3, 0), (5, 0))
    xact.finish()

    def norm_rows(i, carry):
        r = pl.ds(pl.multiple_of(lax.rem(i, rows // 16) * 16, 16), 16)
        b = i // (rows // 16)
        xf = xv[b, r, :].astype(F32)
        inv = lax.rsqrt(jnp.mean(xf * xf, axis=-1, keepdims=True) + EPSILON)
        xv[b, r, :] = (xf * inv * gain1[...]).astype(BF)
        return carry

    lax.fori_loop(0, 4 * rows // 16, norm_rows, 0)
    for i in range(4, 7):
        sends[i].wait_recv()
    f1.own(1 - y)
    attn_o.pump(1, y)
    attn_o.pump(1, 1 - y)
    lax.fori_loop(4 * rows // 16, 8 * rows // 16, norm_rows, 0)
    a1_out = pltpu.make_async_copy(xv, a1, c_local.at[0])
    a1_out.start()
    attn_o.pump(2, y)
    attn_o.pump(2, 1 - y)
    attn.land((y, 1 - y))
    w_in = pltpu.make_async_copy(wqkv, wqkv_v, c_local.at[1])
    w_in.start()
    w_in.wait()

    def project(b, carry):
        r = pl.ds(pl.multiple_of(b * rows, rows), rows)
        qkv_v[r, :] = jnp.dot(xv[b], wqkv_v[...], preferred_element_type=F32).astype(BF)
        return carry

    lax.fori_loop(0, 8, project, 0)
    qkv_out = pltpu.make_async_copy(qkv_v, qkv, c_local.at[3])
    qkv_out.start()
    f1.pump(1, y)
    tiles = length // TQ

    def p_copy(slot, head, t):
        return pltpu.make_async_copy(
            pbuf.at[slot], p.at[head, pl.ds(t * TQ, TQ)], p_sem.at[slot]
        )

    def sequence(s, fresh, between):
        base = pl.multiple_of(s * length, length)
        seq = pl.ds(base, length)

        def head_pair(hp, carry):
            def lanes(part):
                return pl.ds(pl.multiple_of(part * heads + hp * 2 * DH, 128), 2 * DH)

            k2 = qkv_v[seq, lanes(1)]
            v2 = qkv_v[seq, lanes(2)]
            for t in range(tiles):
                r = pl.ds(pl.multiple_of(base + t * TQ, TQ), TQ)
                q2 = qkv_v[r, lanes(0)]
                same = segt[s, t * TQ : (t + 1) * TQ, 0:1] == segs[s, 0:1, :].astype(F32)
                outs = []
                for h in range(2):
                    cut = slice(h * DH, (h + 1) * DH)
                    pb, ot = softmax_tile(
                        q2[:, cut], k2[:, cut], v2[:, cut],
                        toep[hp * 2 + h, :, length - t * TQ : 2 * length - t * TQ], same,
                    )
                    head = s * local_heads + hp * 2 + h
                    if fresh and t == 0:

                        @pl.when(hp > 0)
                        def _():
                            p_copy(h, head, t).wait()
                    else:
                        p_copy(h, head, t).wait()
                    pbuf[h] = pb
                    p_copy(h, head, t).start()
                    outs.append(ot)
                o_v[r, pl.ds(pl.multiple_of(hp * 2 * DH, 128), 2 * DH)] = jnp.concatenate(outs, axis=1)

            @pl.when(hp == 0)
            def _():
                between()

            return carry

        lax.fori_loop(0, local_heads // 2, head_pair, 0)

    def attn_term(block, i):
        r = pl.ds(pl.multiple_of(block * rows, rows), rows)
        return jnp.dot(o_v[r, :], wo_v[...], preferred_element_type=F32).astype(BF)

    red = ActReduce(me, *red_scratch)
    def beside_first():
        f1.pump(1, 1 - y)
        gact.forward()

    def beside_second():
        for i in range(7, 10):
            keeps[i].wait()
            sends[i].wait_recv()
        f2.own(y)
        f2.own(1 - y)
        gact.forward_core()

    sequence(1 - y, True, beside_first)
    attn_o.land((y, 1 - y))
    wo_in = pltpu.make_async_copy(wof, wo_v, c_local.at[2])
    wo_in.start()
    f1.pump(2, y)
    f1.pump(2, 1 - y)
    wo_in.wait()
    red.loop(attn_term, first=0, last=2)
    sequence(y, False, beside_second)
    for slot in range(2):
        p_copy(slot, 0, 0).wait()
    o_out = pltpu.make_async_copy(o_v, o, c_local.at[4])
    o_out.start()
    red.loop(attn_term, first=2, last=4)
    red.second()
    f2.pump(1, y)
    red.arrive()

    half = rows // 2
    for h in range(2):

        def body(i, carry):
            rr = pl.ds(pl.multiple_of(h * half + i * 16, 16), 16)
            m = xin[rr, :].astype(F32) + red.total(h, i)
            mid[rr, :] = m
            inv = lax.rsqrt(jnp.mean(m * m, axis=-1, keepdims=True) + EPSILON)
            a2[rr, :] = (m * inv * gain2[...]).astype(BF)
            return carry

        lax.fori_loop(0, half // 16, body, 0)
    aact = ActGather(me, a2, a2all, *a_sems)
    aact.start()
    f2.pump(1, 1 - y)
    f1.land((y, 1 - y))

    def fetch(src, dst, i):
        return pltpu.make_async_copy(src, dst, f_sem.at[i])

    a1_out.wait()
    fetch(wg1, wg1_v, 0).start()
    fetch(wd1, wd1_v, 1).start()
    gact.finish()

    def block_at(i):
        ox, oy = red.place(3 - i // 2)
        return block_of(ox, jnp.where(i % 2 == 0, me.k, 1 - me.k), oy)

    def load_rows(i):
        slot = lax.rem(i, 2)
        b = block_at(i)
        return fetch(a2all.at[b], xv.at[slot], 2 + slot), fetch(gall.at[b], xv.at[2 + slot], 4 + slot)

    def first_units(j, last, carry):
        b = block_at(j)

        @pl.when(j < last)
        def _():
            for copy in load_rows(j + 1):
                copy.start()

        for copy in load_rows(j):
            copy.wait()
        slot = lax.rem(j, 2)
        acc[:, 0 : 2 * h1] = jnp.dot(xv[slot], wg1_v[...], preferred_element_type=F32)
        acc[:, 2 * h1 : 3 * h1] = lax.dot_general(
            xv[2 + slot], wd1_v[...], (((1,), (1,)), ((), ())), preferred_element_type=F32
        )

        def body(i, inner):
            rr = pl.ds(pl.multiple_of(i * 16, 16), 16)
            tr = pl.ds(pl.multiple_of(b * rows + i * 16, 16), 16)
            gate, up, gm = acc[rr, 0:h1], acc[rr, h1 : 2 * h1], acc[rr, 2 * h1 : 3 * h1]
            gelu, slope = gelu_parts(gate)
            wqkv_v[tr, 0:h1] = (gm * up * slope).astype(BF)
            wqkv_v[tr, h1 : 2 * h1] = (gm * gelu).astype(BF)
            wqkv_v[tr, 2 * h1 : 3 * h1] = (gelu * up).astype(BF)
            return inner

        lax.fori_loop(0, rows // 16, body, 0)
        return carry

    def units(first, last):
        for copy in load_rows(first):
            copy.start()
        lax.fori_loop(first, last, lambda j, carry: first_units(j, last - 1, carry), 0)

    pltpu.make_async_copy(a2, a2all.at[block_at(0)], a_sems[2]).wait()
    fetch(wg1, wg1_v, 0).wait()
    fetch(wd1, wd1_v, 1).wait()
    aact.land(6)
    units(0, 2)
    aact.forward()
    f2.pump(2, y)
    aact.onward((2, 0), (4, 0))
    aact.land(7, 8, 9, 11)
    units(2, 6)
    aact.onward((3, 0), (5, 0))
    aact.land(10, 12)
    f2.pump(2, 1 - y)
    units(6, 8)
    red.finish()
    kept = [fetch(wqkv_v.at[:, pl.ds(0, 2 * h1)], dgu1, 0), fetch(wqkv_v.at[:, pl.ds(2 * h1, h1)], m1, 1)]
    for copy in kept:
        copy.start()

    def load_columns(i):
        slot = lax.rem(i, 2)
        at = pl.ds(pl.multiple_of(i * rows, rows), rows)
        here = pl.ds(pl.multiple_of(slot * rows, rows), rows)
        there = pl.ds(pl.multiple_of((2 + slot) * rows, rows), rows)
        return (
            fetch(a2all.at[:, :, at], xv.at[:, :, here], 2 + slot),
            fetch(gall.at[:, :, at], xv.at[:, :, there], 4 + slot),
        )

    for copy in load_columns(0):
        copy.start()

    def first_grads(i, carry):
        @pl.when(i < 2 * n - 1)
        def _():
            for copy in load_columns(i + 1):
                copy.start()

        for copy in load_columns(i):
            copy.wait()
        slot = lax.rem(i, 2)
        here = pl.ds(pl.multiple_of(slot * rows, rows), rows)
        there = pl.ds(pl.multiple_of((2 + slot) * rows, rows), rows)
        gw_v[i, :, 0 : 2 * h1] = lax.dot_general(
            xv[:, :, here].reshape(8 * rows, rows), wqkv_v[:, 0 : 2 * h1], (((0,), (0,)), ((), ())),
            preferred_element_type=F32,
        ).astype(BF)
        gw_v[i, :, 2 * h1 : 3 * h1] = lax.dot_general(
            xv[:, :, there].reshape(8 * rows, rows), wqkv_v[:, 2 * h1 : 3 * h1], (((0,), (0,)), ((), ())),
            preferred_element_type=F32,
        ).astype(BF)
        return carry

    lax.fori_loop(0, 2 * n, first_grads, 0)
    kept.append(fetch(gw_v, gwf1, 2))
    kept[2].start()
    for i in range(13):
        aact.copy(i).wait_send()
    f2.land((y, 1 - y))
    for line in (attn, attn_o, f1, f2):
        line.finish()
    for copy in small_sends:
        copy.wait_send()
    for copy in small_z:
        copy.wait_send()
    seg_send.wait_send()
    for copy in sends:
        copy.wait_send()
    qkv_out.wait()
    o_out.wait()
    for copy in kept:
        copy.wait()


def forward(n, h1, wq, wk, wv, wo, wg, wu, wd, cot, xin, seg_row, gain_a, gain_f, table_row):
    rows, width = xin.shape
    heads = wq.shape[1] // 2
    hid = wg.shape[1] // 2
    length = seg_row.shape[1]
    small, seg = (8, 384), (8, length)
    local_heads = heads // DH
    tokens = 8 * rows
    shapes = [
        ((width, 3 * heads), BF),
        ((heads, width), BF),
        ((width, 2 * h1), BF),
        ((h1, width), BF),
        ((width, 2 * (hid - h1)), BF),
        ((hid - h1, width), BF),
        ((8, rows, width), BF),
        ((tokens, 3 * heads), BF),
        ((tokens, heads), BF),
        ((2 * local_heads, length, length), BF),
        ((rows, width), F32),
        ((8, rows, width), BF),
        ((8, rows, width), BF),
        ((tokens, h1), BF),
        ((tokens, 2 * h1), BF),
        ((2 * n, rows, 3 * h1), BF),
        ((1, width), F32),
        ((1, width), F32),
    ]
    scratch = [
        pltpu.VMEM(small, F32),
        pltpu.VMEM(seg, jnp.int32),
        pltpu.VMEM((8 * n,) + small, F32),
        pltpu.VMEM((2,) + seg, jnp.int32),
        pltpu.VMEM((2, length, 128), F32),
        pltpu.VMEM((8, rows, width), BF),
        pltpu.VMEM((width, 3 * heads), BF),
        pltpu.VMEM((heads, width), BF),
        pltpu.VMEM((tokens, 3 * heads), BF),
        pltpu.VMEM((tokens, heads), BF),
        pltpu.VMEM((local_heads, TQ, 2 * length), F32),
        pltpu.VMEM((2, TQ, length), BF),
        pltpu.VMEM((rows, width), BF),
        pltpu.VMEM((width, 2 * h1), BF),
        pltpu.VMEM((h1, width), BF),
        pltpu.VMEM((2 * n, rows, 3 * h1), BF),
        pltpu.VMEM((rows, 3 * h1), F32),
        DMA((10,)), DMA((10,)), DMA((10,)), DMA((8,)), DMA((8,)), DMA((n - 1,)), DMA((n - 1,)), DMA((2,)),
        DMA((5,)), DMA((2,)), DMA((6,)),
    ] + reduce_scratch(rows, width) + line_sems(n, 2) * 2 + line_sems(n, 1) * 2 + gather_sems() * 3
    return pl.pallas_call(
        functools.partial(forward_kernel, n, length),
        out_shape=[jax.ShapeDtypeStruct(s, d) for s, d in shapes],
        in_specs=[ANY] * 8 + [VM] * 5,
        out_specs=[ANY] * 10 + [VM] + [ANY] * 5 + [VM] * 2,
        scratch_shapes=scratch,
        compiler_params=pltpu.CompilerParams(
            collective_id=0, has_side_effects=True, vmem_limit_bytes=64 << 20
        ),
        name="forward",
    )(wq, wk, wv, wo, wg, wu, wd, cot, xin, seg_row, gain_a, gain_f, table_row)


class LineSum:
    def __init__(self, me, n, views, from_left, from_right, stage, sems, stage_sem):
        self.me, self.n, self.views = me, n, views
        self.inbox = {True: from_left, False: from_right}
        self.stage, self.stage_sem = stage, stage_sem
        self.sends = {True: sems[0], False: sems[1]}
        self.recvs = {True: sems[2], False: sems[3]}

    def copies(self, t, yy, right):
        me = self.me
        dev = me.device(z=me.z + 1 if right else me.z - 1)
        return [
            remote(
                view, self.inbox[right].at[t, yy, i], self.sends[right].at[t, yy, i],
                self.recvs[right].at[t, yy, i], dev,
            )
            for i, view in enumerate(self.views(t * 2 + yy))
        ]

    def start(self, t, yy, right):
        for copy in self.copies(t, yy, right):
            copy.start()

    def add(self, t, yy, right):
        for i, (copy, view) in enumerate(zip(self.copies(t, yy, right), self.views(t * 2 + yy))):
            copy.wait_recv()
            stage = self.stage[i]
            load = pltpu.make_async_copy(self.inbox[right].at[t, yy, i], stage, self.stage_sem)
            load.start()
            load.wait()

            def body(r, carry):
                rr = pl.ds(pl.multiple_of(r * 16, 16), 16)
                view[rr, :] = (view[rr, :].astype(F32) + stage[rr, :].astype(F32)).astype(BF)
                return carry

            lax.fori_loop(0, view.shape[0] // 16, body, 0)

    def first(self, t, yy):
        @pl.when((self.me.z == 0) & (t > 0))
        def _():
            self.start(t, yy, True)

        @pl.when((self.me.z == self.n - 1) & (t < self.n - 1))
        def _():
            self.start(t, yy, False)

    def pump(self, k, yy):
        z, n = self.me.z, self.n

        @pl.when((z + k <= n - 1) & (z > 0))
        def _():
            self.add(z + k, yy, True)
            self.start(z + k, yy, True)

        @pl.when((z - k >= 0) & (z < n - 1))
        def _():
            self.add(z - k, yy, False)
            self.start(z - k, yy, False)

    def own(self, yy):
        z, n = self.me.z, self.n

        @pl.when(z > 0)
        def _():
            self.add(z, yy, True)

        @pl.when(z < n - 1)
        def _():
            self.add(z, yy, False)

    def finish(self):
        z, n = self.me.z, self.n
        for yy in range(2):
            for k in range(1, n):

                @pl.when(z + k <= n - 1)
                def _():
                    for copy in self.copies(z + k, yy, True):
                        copy.wait_send()

                @pl.when(z - k >= 0)
                def _():
                    for copy in self.copies(z - k, yy, False):
                        copy.wait_send()


def far_first(n, z, i):
    slot = 0
    for a in range(n):
        order = sorted(range(n), key=lambda d: (-abs(d - a), d))
        for b in range(n):
            slot = slot + jnp.where((z == a) & (i == b), order[b], 0)
    return slot


def gelu_parts(gate):
    th = jnp.tanh(0.7978845608028654 * (gate + 0.044715 * gate * gate * gate))
    gelu = 0.5 * gate * (1.0 + th)
    slope = 0.5 * (1.0 + th) + 0.5 * gate * (1.0 - th * th) * 0.7978845608028654 * (
        1.0 + 3 * 0.044715 * gate * gate
    )
    return gelu, slope


def norm_back(ga, values, gain):
    inv = lax.rsqrt(jnp.mean(values * values, axis=-1, keepdims=True) + EPSILON)
    u = ga * gain
    corr = jnp.mean(u * values, axis=-1, keepdims=True) * inv * inv * inv
    return inv * u - values * corr, ga * (values * inv)


def backward_kernel(
    n, length, heads, hid, h1,
    wg1, wd1, wg2, wd2, m1, dgu1, gwf1, a2all, gall, p, a1, qkv, o, wqkv, wof, hidden, mid, cot, gain1, gain2,
    out, gx, fo1, fo2, ao, bo, co, sums, dzall, e_left, e_right, f_left, f_right, a_left, a_right,
    b_left, b_right, c_left, c_right,
    wgu_v, wd_v, row_a, row_b, row_g, col_a, col_g, m, dgu, gw1, gw2, stage, gmid, dz, wqkv_v,
    pbuf, acc, dkt, dvt, diag, gg1, gg2, sv, sv_in, sv_z, free,
    load, p_sem, stage_sem, y_send, y_recv, y_local, sv_send, sv_recv, sz_send, sz_recv,
    *rest,
):
    red_scratch, dz_sems = rest[:9], rest[9:12]
    e_sems, f_sems, a_sems, b_sems, c_sems = (rest[i : i + 4] for i in range(12, 32, 4))
    h2 = hid - h1
    me = Place()
    z, y = me.z, me.y
    rows, width = cot.shape
    group = [
        me.device(x=ox, k=ok, y=oy)
        for ox in (me.x, 1 - me.x)
        for ok in (me.k, 1 - me.k)
        for oy in (me.y, 1 - me.y)
    ][1:]
    others = [me.device(z=lax.rem(z + s, n)) for s in range(1, n)]
    greet(group + others)
    local_heads = heads // DH
    half = rows // 2

    def fetch(src, dst, i):
        return pltpu.make_async_copy(src, dst, load.at[i])

    red = ActReduce(me, *red_scratch)
    stage1 = stage.at[:, pl.ds(0, 3 * h1)]
    esum = LineSum(me, n, lambda pc: [gw1.at[pc]], e_left, e_right, [stage1], e_sems, stage_sem)
    fsum = LineSum(me, n, lambda pc: [gw2.at[pc]], f_left, f_right, [stage], f_sems, stage_sem)
    order = (1 - y, y)

    def piece(pc):
        return pl.ds(pl.multiple_of(pc * rows, rows), rows)

    def line_sum(view, left, right, width, sems):
        return LineSum(me, n, lambda pc: [view(pc)], left, right, [stage.at[:, pl.ds(0, width)]], sems, stage_sem)

    pair = 3 * 2 * DH
    osum = line_sum(lambda pc: m.at[piece(pc), pl.ds(0, heads)], a_left, a_right, heads, a_sems)
    bsum = line_sum(lambda pc: dgu.at[piece(pc), pl.ds(3 * heads, pair)], b_left, b_right, pair, b_sems)
    csum = line_sum(lambda pc: m.at[piece(pc), pl.ds(heads, pair)], c_left, c_right, pair, c_sems)

    def piece_at(i):
        return far_first(n, z, i // 2) * 2 + jnp.where(i % 2 == 0, 1 - y, y)

    w_loads = [
        fetch(gwf1, gw1, 0),
        fetch(wg2, wgu_v.at[:, pl.ds(2 * h1, 2 * h2)], 1),
        fetch(wd2, wd_v.at[pl.ds(h1, h2), :], 6),
        fetch(wg1, wgu_v.at[:, pl.ds(0, 2 * h1)], 7),
        fetch(dgu1, dgu.at[:, pl.ds(0, 2 * h1)], 8),
        fetch(wd1, wd_v.at[pl.ds(0, h1), :], 9),
        fetch(m1, m.at[:, pl.ds(0, h1)], 10),
    ]
    for copy in w_loads:
        copy.start()

    def block_at(i):
        j = i // 2
        ox, oy = red.place(j)
        return block_of(ox, jnp.where(i % 2 == 0, 1 - me.k, me.k), oy)

    fetch(a2all.at[block_at(0)], row_a, 2).start()
    fetch(gall.at[block_at(0)], row_g, 3).start()
    w_loads[0].wait()

    def first_slots(i, carry):
        pc = piece_at(i)
        esum.first(pc // 2, pc % 2)
        return carry

    lax.fori_loop(0, 2 * n, first_slots, 0)
    for copy in w_loads[1:]:
        copy.wait()


    def make_ffn(block, i):
        fetch(a2all.at[block], row_a, 2).wait()
        acc[:, 0 : 2 * h2] = jnp.dot(row_a[...], wgu_v[:, 2 * h1 : 2 * hid], preferred_element_type=F32)

        @pl.when(i < 7)
        def _():
            fetch(a2all.at[block_at(i + 1)], row_a, 2).start()

        fetch(gall.at[block], row_g, 3).wait()
        acc[:, 2 * h2 : 3 * h2] = lax.dot_general(
            row_g[...], wd_v[h1:hid, :], (((1,), (1,)), ((), ())), preferred_element_type=F32
        )

        @pl.when(i < 7)
        def _():
            fetch(gall.at[block_at(i + 1)], row_g, 3).start()

        def body(r, carry):
            rr = pl.ds(pl.multiple_of(r * 16, 16), 16)
            tr = pl.ds(pl.multiple_of(block * rows + r * 16, 16), 16)
            gate, up, gm = acc[rr, 0:h2], acc[rr, h2 : 2 * h2], acc[rr, 2 * h2 : 3 * h2]
            gelu, slope = gelu_parts(gate)
            m[tr, h1:hid] = (gelu * up).astype(BF)
            dgu[tr, 2 * h1 : 2 * h1 + h2] = (gm * up * slope).astype(BF)
            dgu[tr, 2 * h1 + h2 : 2 * hid] = (gm * gelu).astype(BF)
            return carry

        lax.fori_loop(0, rows // 16, body, 0)
        return lax.dot_general(
            dgu[piece(block), :], wgu_v[...], (((1,), (1,)), ((), ())), preferred_element_type=F32
        ).astype(BF)

    red.loop(make_ffn, hooks=((1, lambda: esum.pump(2, order[0])), (2, lambda: esum.pump(2, order[1]))))
    esum.pump(1, order[0])

    fetch(wof, row_g, 3).start()

    def columns(ref, i):
        return ref.at[:, :, piece(piece_at(i))]

    def load_columns(left, right, i):
        slot = lax.rem(i, 2)
        return fetch(columns(left, i), col_a.at[slot], 11 + slot), fetch(columns(right, i), col_g.at[slot], 13 + slot)

    def next_columns(left, right, i):
        @pl.when(i < 2 * n - 1)
        def _():
            for copy in load_columns(left, right, i + 1):
                copy.start()

        for copy in load_columns(left, right, i):
            copy.wait()

    for copy in load_columns(a2all, gall, 0):
        copy.start()

    def ffn_grads(i, carry):
        pc = piece_at(i)
        slot = lax.rem(i, 2)
        next_columns(a2all, gall, i)
        gw2[pc, :, 0 : 2 * h2] = lax.dot_general(
            col_a[slot].reshape(8 * rows, rows), dgu[:, 2 * h1 : 2 * hid], (((0,), (0,)), ((), ())),
            preferred_element_type=F32,
        ).astype(BF)
        gw2[pc, :, 2 * h2 : 3 * h2] = lax.dot_general(
            col_g[slot].reshape(8 * rows, rows), m[:, h1:hid], (((0,), (0,)), ((), ())),
            preferred_element_type=F32,
        ).astype(BF)
        fsum.first(pc // 2, pc % 2)
        return carry

    lax.fori_loop(0, n, ffn_grads, 0)
    red.second()
    esum.pump(1, order[1])
    fetch(qkv, wgu_v.at[:, pl.ds(0, 3 * heads)], 0).start()
    fetch(o, wgu_v.at[:, pl.ds(3 * heads, heads)], 6).start()
    red.arrive()

    gg2[...] = jnp.zeros_like(gg2)
    for h in range(2):

        def body(i, carry):
            rr = pl.ds(pl.multiple_of(h * half + i * 16, 16), 16)
            back, gains = norm_back(red.total(h, i), mid[rr, :], gain2[...])
            gm = cot[rr, :].astype(F32) + back
            gmid[rr, :] = gm
            dz[rr, :] = gm.astype(BF)
            gg2[...] += gains[:8] + gains[8:]
            return carry

        lax.fori_loop(0, half // 16, body, 0)
    act = ActGather(me, dz, dzall, *dz_sems)
    act.start()
    red.finish()

    def release():
        for i, dev in enumerate((me.x_peer(), me.y_peer(), me.core_peer())):
            pl.semaphore_signal(free.at[i], inc=1, device_id=dev, device_id_type=MESH)

    def claim():
        for i in range(3):
            pl.semaphore_wait(free.at[i], 1)

    release()
    lax.fori_loop(n, 2 * n, ffn_grads, 0)
    act.forward()

    claim()

    def make_out(block, i):
        return jnp.dot(m[piece(block), :], wd_v[...], preferred_element_type=F32).astype(BF)

    red.loop(make_out, send=False)
    def swap(views, box, i):
        out = remote(views(z * 2 + 1 - y)[0], box.at[y], y_send.at[i], y_recv.at[i], me.y_peer())
        keep = pltpu.make_async_copy(views(z * 2 + y)[0], box.at[y], y_local.at[i])
        return out, keep

    lines = (esum, fsum, osum, bsum, csum)
    swaps = [swap(line.views, box, i) for i, (line, box) in enumerate(zip(lines, (fo1, fo2, ao, bo, co)))]

    def settle(i):
        lines[i].own(order[0])
        swaps[i][0].start()
        lines[i].own(order[1])
        swaps[i][1].start()

    fsum.pump(2, order[0])
    act.forward_core()
    for j in range(3):
        red.first_sends(j)
    settle(0)
    act.finish()

    fetch(wof, row_g, 3).wait()
    slots = ((row_a, 2), (row_b, 4))
    for b in range(2):
        fetch(dzall.at[b], *slots[b]).start()

    def project_back(i, carry):
        for b, (buffer, sem) in enumerate(slots):
            block = i * 2 + b
            fetch(dzall.at[block], buffer, sem).wait()
            wgu_v[piece(block), 4 * heads : 5 * heads] = lax.dot_general(
                buffer[...], row_g[...], (((1,), (1,)), ((), ())), preferred_element_type=F32
            ).astype(BF)

            @pl.when(i < 3)
            def _():
                fetch(dzall.at[block + 2], buffer, sem).start()

        return carry

    lax.fori_loop(0, 4, project_back, 0)
    fsum.pump(2, order[1])
    fetch(hidden, row_a, 2).start()
    w_parts = [
        fetch(
            wqkv.at[:, pl.ds(part * heads + hp * 2 * DH, 2 * DH)],
            wqkv_v.at[:, pl.ds(hp * pair + part * 2 * DH, 2 * DH)],
            15 + hp * 3 + part,
        )
        for hp in range(2)
        for part in range(3)
    ]
    for copy in w_parts:
        copy.start()
    fetch(qkv, wgu_v.at[:, pl.ds(0, 3 * heads)], 0).wait()
    fetch(o, wgu_v.at[:, pl.ds(3 * heads, heads)], 6).wait()
    diag[...] = jnp.zeros_like(diag)
    tiles = length // TQ

    def p_load(head, t, slot):
        return pltpu.make_async_copy(p.at[head, pl.ds(t * TQ, TQ)], pbuf.at[slot], p_sem.at[slot])

    def head_pair(hp):
        def sequence(s, carry):
            head0 = s * local_heads + hp * 2
            base = pl.multiple_of(s * length, length)
            p_load(head0, 0, 0).start()
            p_load(head0, 1, 1).start()
            for h in range(2):
                lo = hp * 128 + h * DH
                to = hp * pair + h * DH
                seq = pl.ds(base, length)
                kh = wgu_v[seq, heads + lo : heads + lo + DH]
                vh = wgu_v[seq, 2 * heads + lo : 2 * heads + lo + DH]
                acc[...] = jnp.zeros_like(acc)
                for t in range(tiles):
                    slot = t % 2
                    r = pl.ds(pl.multiple_of(base + t * TQ, TQ), TQ)
                    qh = wgu_v[r, lo : lo + DH]
                    doh = wgu_v[r, 4 * heads + lo : 4 * heads + lo + DH]
                    p_load(head0 + h, t, slot).wait()
                    pb = pbuf[slot]
                    dp = lax.dot_general(doh, vh, (((1,), (1,)), ((), ())), preferred_element_type=F32)
                    pf = pb.astype(F32)
                    ds = (pf * (dp - jnp.sum(pf * dp, axis=-1, keepdims=True))).astype(BF)
                    dgu[r, to : to + DH] = jnp.dot(ds, kh, preferred_element_type=F32).astype(BF)
                    ck = lax.dot_general(qh, ds, (((0,), (0,)), ((), ())), preferred_element_type=F32)
                    cv = lax.dot_general(doh, pb, (((0,), (0,)), ((), ())), preferred_element_type=F32)
                    u = h * tiles + t + 2
                    if u < 2 * tiles:
                        p_load(head0 + u // tiles, u % tiles, slot).start()
                    if t == 0:
                        dkt[...] = ck
                        dvt[...] = cv
                    else:
                        dkt[...] += ck
                        dvt[...] += cv
                    acc[:, length - t * TQ : 2 * length - t * TQ] += ds.astype(F32)
                dgu[seq, to + 2 * DH : to + 3 * DH] = dkt[...].T.astype(BF)
                dgu[seq, to + 4 * DH : to + 5 * DH] = dvt[...].T.astype(BF)
                c = TQ // 2
                while c >= 8:
                    acc[0:c, :] += pltpu.roll(acc[c : 2 * c, :], 2 * length - c, 1)
                    c //= 2
                diag[hp * 2 + h] += acc[0:8, :]
            return carry

        lax.fori_loop(0, 2, sequence, 0)

    def pair_grads(hp, line, with_o):
        for copy in load_columns(a1, dzall, 0):
            copy.start()

        def body(i, carry):
            pc = piece_at(i)
            slot = lax.rem(i, 2)
            next_columns(a1, dzall, i)
            if with_o:
                m[piece(pc), 0:heads] = lax.dot_general(
                    col_g[slot].reshape(8 * rows, rows), wgu_v[:, 3 * heads : 4 * heads], (((0,), (0,)), ((), ())),
                    preferred_element_type=F32,
                ).astype(BF)
                osum.first(pc // 2, pc % 2)
            part = lax.dot_general(
                col_a[slot].reshape(8 * rows, rows), dgu[:, hp * pair : (hp + 1) * pair], (((0,), (0,)), ((), ())),
                preferred_element_type=F32,
            ).astype(BF)
            line.views(pc)[0][...] = part
            line.first(pc // 2, pc % 2)
            return carry

        lax.fori_loop(0, 2 * n, body, 0)

    head_pair(0)
    fsum.pump(1, order[0])
    red.second()
    pair_grads(0, bsum, True)
    fsum.pump(1, order[1])
    head_pair(1)
    for yy in order:
        osum.pump(2, yy)
        bsum.pump(2, yy)

    red.arrive()
    for h in range(2):

        def body(i, carry):
            rr = pl.ds(pl.multiple_of(h * half + i * 16, 16), 16)
            out[rr, :] = (mid[rr, :] + red.total(h, i)).astype(BF)
            return carry

        lax.fori_loop(0, half // 16, body, 0)
    red.finish()
    release()
    claim()
    for copy in w_parts:
        copy.wait()

    def make_ga1(block, i):
        return lax.dot_general(
            dgu[piece(block), 0 : 3 * heads], wqkv_v[...], (((1,), (1,)), ((), ())), preferred_element_type=F32
        ).astype(BF)

    red.loop(make_ga1)
    pair_grads(1, csum, False)
    red.second()
    settle(1)
    for yy in order:
        osum.pump(1, yy)
        bsum.pump(1, yy)
        csum.pump(2, yy)

    offset = lax.broadcasted_iota(jnp.int32, (NB, 2 * length), 1) - length
    away = jnp.abs(offset)
    bucket = jnp.where(away < 8, away, 8 + sum((away >= t).astype(jnp.int32) for t in THRESHOLDS))
    bucket = bucket + 16 * (offset > 0).astype(jnp.int32)
    own_bucket = bucket == lax.broadcasted_iota(jnp.int32, (NB, 2 * length), 0)
    lane = lax.broadcasted_iota(jnp.int32, (NB, 128), 1)
    table = jnp.zeros((NB, 128), F32)
    for lh in range(local_heads):
        line = diag[lh, 0:1, :]
        for r in range(1, 8):
            line = line + pltpu.roll(diag[lh, r : r + 1, :], 2 * length - r, 1)
        value = jnp.sum(jnp.where(own_bucket, line, 0.0), axis=1, keepdims=True)
        table = jnp.where(lane == (me.c * 2 + y) * local_heads + lh, value, table)
    for yy in order:
        csum.pump(1, yy)
    red.arrive()
    gg1[...] = jnp.zeros_like(gg1)
    fetch(hidden, row_a, 2).wait()
    for h in range(2):

        def body(i, carry):
            rr = pl.ds(pl.multiple_of(h * half + i * 16, 16), 16)
            back, gains = norm_back(red.total(h, i), row_a[rr, :].astype(F32), gain1[...])
            gx[rr, :] = gmid[rr, :] + back
            gg1[...] += gains[:8] + gains[8:]
            return carry

        lax.fori_loop(0, half // 16, body, 0)
    red.finish()

    first_row = lax.broadcasted_iota(jnp.int32, (8, 128), 0) == 0
    for d in range(8 * n):
        g, zz = d % 8, d // 8
        lanes = slice(d // 2 * 128, d // 2 * 128 + 128)
        sv[g, zz, :, 0:128] = gg1[:, lanes]
        sv[g, zz, :, 128:256] = gg2[:, lanes]
        sv[g, zz, :, 256:384] = jnp.where(first_row, jnp.broadcast_to(table[d : d + 1, :], (8, 128)), 0.0)
    peers = [
        (ox * 4 + ok * 2 + oy)
        for ox in (me.x, 1 - me.x)
        for ok in (me.k, 1 - me.k)
        for oy in (me.y, 1 - me.y)
    ]
    sv_copies = [
        remote(sv.at[peers[i + 1]], sv_in.at[i], sv_send.at[i], sv_recv.at[i], dev)
        for i, dev in enumerate(group)
    ]
    for copy in sv_copies:
        copy.start()

    settle(2)
    settle(3)
    for copy in sv_copies:
        copy.wait_recv()
    me_g = me.c * 2 + y
    total = sv[me_g]
    for i in range(7):
        total = total + sv_in[i]
    sv_z[0] = total
    z_copies = [
        remote(sv_z.at[0, lax.rem(z + s, n)], sv_z.at[s, 0], sz_send.at[s - 1], sz_recv.at[s - 1], others[s - 1])
        for s in range(1, n)
    ]
    for copy in z_copies:
        copy.start()
    settle(4)
    for copy in z_copies:
        copy.wait_recv()
    total = sv_z[0, z]
    for s in range(1, n):
        total = total + sv_z[s, 0]
    sums[...] = total
    for pair_of in swaps:
        for copy in pair_of:
            copy.wait()
    for copy in sv_copies + z_copies:
        copy.wait_send()
    for line in lines:
        line.finish()


def backward(n, length, heads, hid, h1, *arrays):
    cot = arrays[-3]
    rows, width = cot.shape
    tokens = 8 * rows
    h2 = hid - h1
    pair = 3 * 2 * DH
    shapes = [
        ((rows, width), BF),
        ((rows, width), F32),
        ((2, rows, 3 * h1), BF),
        ((2, rows, 3 * h2), BF),
        ((2, rows, heads), BF),
        ((2, rows, pair), BF),
        ((2, rows, pair), BF),
        ((8, 384), F32),
        ((8, rows, width), BF),
        ((n, 2, 1, rows, 3 * h1), BF),
        ((n, 2, 1, rows, 3 * h1), BF),
        ((n, 2, 1, rows, 3 * h2), BF),
        ((n, 2, 1, rows, 3 * h2), BF),
        ((n, 2, 1, rows, heads), BF),
        ((n, 2, 1, rows, heads), BF),
    ] + [((n, 2, 1, rows, pair), BF)] * 4
    scratch = [
        pltpu.VMEM((width, 2 * hid), BF),
        pltpu.VMEM((hid, width), BF),
        pltpu.VMEM((rows, width), BF),
        pltpu.VMEM((rows, width), BF),
        pltpu.VMEM((rows, width), BF),
        pltpu.VMEM((2, 8, rows, rows), BF),
        pltpu.VMEM((2, 8, rows, rows), BF),
        pltpu.VMEM((tokens, hid), BF),
        pltpu.VMEM((tokens, 2 * hid), BF),
        pltpu.VMEM((2 * n, rows, 3 * h1), BF),
        pltpu.VMEM((2 * n, rows, 3 * h2), BF),
        pltpu.VMEM((rows, 3 * h2), BF),
        pltpu.VMEM((rows, width), F32),
        pltpu.VMEM((rows, width), BF),
        pltpu.VMEM((width, 3 * heads), BF),
        pltpu.VMEM((2, TQ, length), BF),
        pltpu.VMEM((TQ, 2 * length), F32),
        pltpu.VMEM((DH, length), F32),
        pltpu.VMEM((DH, length), F32),
        pltpu.VMEM((heads // DH, 8, 2 * length), F32),
        pltpu.VMEM((8, width), F32),
        pltpu.VMEM((8, width), F32),
        pltpu.VMEM((8, n, 8, 384), F32),
        pltpu.VMEM((7, n, 8, 384), F32),
        pltpu.VMEM((n, n, 8, 384), F32),
        pltpu.SemaphoreType.REGULAR((3,)),
        DMA((21,)), DMA((2,)), DMA, DMA((5,)), DMA((5,)), DMA((5,)), DMA((7,)), DMA((7,)), DMA((n - 1,)), DMA((n - 1,)),
    ] + reduce_scratch(rows, width) + gather_sems() + [DMA((n, 2, 1))] * 20
    return pl.pallas_call(
        functools.partial(backward_kernel, n, length, heads, hid, h1),
        out_shape=[jax.ShapeDtypeStruct(s, d) for s, d in shapes],
        in_specs=[ANY] * 16 + [VM] * 4,
        out_specs=[VM, VM] + [ANY] * 5 + [VM] + [ANY] * 11,
        scratch_shapes=scratch,
        compiler_params=pltpu.CompilerParams(
            collective_id=1, has_side_effects=True, vmem_limit_bytes=64 << 20
        ),
        name="backward",
    )(*arrays)


def on_device(
    n, hidden, segment_ids, positions, attn_gain, w_query, w_key, w_value, w_attn_out,
    rel_table, ffn_gain, w_gate, w_up, w_down, cotangent,
):
    xin = hidden[0]
    cot = cotangent[0]
    length = segment_ids.shape[1]
    heads = w_query.shape[1] // 2
    hid = w_gate.shape[1] // 2
    share = attn_gain.shape[0]
    y = lax.axis_index("fsdp")
    h1 = 256
    h2 = hid - h1
    wqkv, wo, wg1, wd1, wg2, wd2, a1, qkv, o, p, mid, a2all, gall, m1, dgu1, gwf1, gain1, gain2 = forward(
        n, h1, w_query, w_key, w_value, w_attn_out, w_gate, w_up, w_down, cot, xin, segment_ids,
        attn_gain[None], ffn_gain[None], rel_table[None],
    )
    out, gx, fo1, fo2, ao, bo, co, sums = backward(
        n, length, heads, hid, h1, wg1, wd1, wg2, wd2, m1, dgu1, gwf1, a2all, gall, p, a1, qkv, o, wqkv, wo,
        xin, mid, cot, gain1, gain2,
    )[:8]
    out, gx, g_q, g_k, g_v, g_o, g_gate, g_up, g_down = finish(h1, out, gx, fo1, fo2, ao, bo, co)
    line = jnp.sum(sums, axis=0)
    half_of = lambda v: jnp.where(y == 0, v[:share], v[128 - share :])
    return (
        out[None], gx[None], half_of(line[:128]), g_q, g_k, g_v, g_o, line[256 : 256 + H],
        half_of(line[128:256]), g_gate, g_up, g_down,
    )


def finish_kernel(h1, out_in, gx_in, *refs):
    sources, (out, gx, g_q, g_k, g_v, g_o, g_gate, g_up, g_down) = refs[:5], refs[5:14]
    fo1, fo2, ao, bo, co = held = refs[14:19]
    sem = refs[19]
    loads = [pltpu.make_async_copy(src, dst, sem.at[i + 2]) for i, (src, dst) in enumerate(zip(sources, held))]
    moves = [
        pltpu.make_async_copy(src, dst, sem.at[i]) for i, (src, dst) in enumerate(((out_in, out), (gx_in, gx)))
    ]
    for copy in loads + moves:
        copy.start()
    for copy in loads:
        copy.wait()
    heads = ao.shape[2]
    h2 = fo2.shape[2] // 3
    hid = h1 + h2
    for yy in range(2):
        for part, ref in enumerate((g_q, g_k, g_v)):
            ref[:, yy * heads : yy * heads + 128] = bo[yy, :, part * 128 : part * 128 + 128].astype(F32)
            ref[:, yy * heads + 128 : yy * heads + 256] = co[yy, :, part * 128 : part * 128 + 128].astype(F32)
        g_o[yy * heads : (yy + 1) * heads, :] = ao[yy].astype(F32).T
        for part, ref in enumerate((g_gate, g_up)):
            ref[:, yy * hid : yy * hid + h1] = fo1[yy, :, part * h1 : (part + 1) * h1].astype(F32)
            ref[:, yy * hid + h1 : (yy + 1) * hid] = fo2[yy, :, part * h2 : (part + 1) * h2].astype(F32)
        g_down[yy * hid : yy * hid + h1, :] = fo1[yy, :, 2 * h1 : 3 * h1].astype(F32).T
        g_down[yy * hid + h1 : (yy + 1) * hid, :] = fo2[yy, :, 2 * h2 : 3 * h2].astype(F32).T
    for copy in moves:
        copy.wait()


def finish(h1, out, gx, fo1, fo2, ao, bo, co):
    rows = out.shape[0]
    heads = ao.shape[2]
    hid = h1 + fo2.shape[2] // 3
    shapes = [(rows, 2 * heads)] * 3 + [(2 * heads, rows)] + [(rows, 2 * hid)] * 2 + [(2 * hid, rows)]
    return pl.pallas_call(
        functools.partial(finish_kernel, h1),
        out_shape=[jax.ShapeDtypeStruct(out.shape, BF), jax.ShapeDtypeStruct(gx.shape, F32)]
        + [jax.ShapeDtypeStruct(s, F32) for s in shapes],
        in_specs=[ANY] * 7,
        out_specs=[ANY] * 2 + [VM] * 7,
        scratch_shapes=[pltpu.VMEM(part.shape, BF) for part in (fo1, fo2, ao, bo, co)] + [DMA((7,))],
        compiler_params=pltpu.CompilerParams(vmem_limit_bytes=32 << 20),
        name="finish",
    )(out, gx, fo1, fo2, ao, bo, co)


QB = 512


def rms_norm(values, gain):
    return values * lax.rsqrt(jnp.mean(values * values, axis=-1, keepdims=True) + EPSILON) * gain


def gelu_tanh(values):
    return (
        0.5
        * values
        * (1.0 + jnp.tanh(0.7978845608028654 * (values + 0.044715 * values * values * values)))
    )


def bucket_table(query_pos, key_pos):
    relative = key_pos[None, :] - query_pos[:, None]
    distance = jnp.abs(relative)
    log_bucket = 8 + sum(((distance >= threshold).astype(jnp.int32) for threshold in THRESHOLDS))
    bucket = jnp.where(distance < 8, distance, log_bucket)
    return bucket + 16 * (relative > 0).astype(jnp.int32)


def gather_attention(w_query, w_key, w_value, w_attn_out):
    return (
        lax.all_gather(w_query, ("dp", "fsdp"), axis=0, tiled=True),
        lax.all_gather(w_key, ("dp", "fsdp"), axis=0, tiled=True),
        lax.all_gather(w_value, ("dp", "fsdp"), axis=0, tiled=True),
        lax.all_gather(w_attn_out, ("dp", "fsdp"), axis=1, tiled=True),
    )


def gather_feedforward(w_gate, w_up, w_down):
    return (
        lax.all_gather(w_gate, ("dp", "fsdp"), axis=0, tiled=True),
        lax.all_gather(w_up, ("dp", "fsdp"), axis=0, tiled=True),
        lax.all_gather(w_down, ("dp", "fsdp"), axis=1, tiled=True),
    )


def block_masks(segment_row, position_row, start):
    query_pos = lax.dynamic_slice_in_dim(position_row, start, QB)
    query_seg = lax.dynamic_slice_in_dim(segment_row, start, QB)
    buckets = bucket_table(query_pos, position_row)
    one_hot = (buckets[None] == jnp.arange(NB, dtype=jnp.int32)[:, None, None]).astype(jnp.bfloat16)
    same_doc = query_seg[:, None] == segment_row[None, :]
    return (one_hot, same_doc)


def block_scores(query_block, key_rows, table_local, one_hot, same_doc):
    attention_scores = jnp.einsum(
        "ihd,jhd->hij", query_block, key_rows, preferred_element_type=jnp.float32
    )
    attention_scores = attention_scores + jnp.einsum(
        "bij,bh->hij", one_hot, table_local, preferred_element_type=jnp.float32
    )
    return jnp.where(same_doc[None], attention_scores, MASKED)


def layer_forward(tokens, small_set, attn_set, ffn_set, segment_row, position_row):
    attn_gain, ffn_gain, table_flat = small_set
    w_query, w_key, w_value, w_attn_out = attn_set
    w_gate, w_up, w_down = ffn_set
    heads_here = w_query.shape[1] // DH
    head_start = lax.axis_index("ctx") * heads_here
    table_local = lax.dynamic_slice_in_dim(table_flat.reshape(NB, H), head_start, heads_here, 1)
    normalized_rows, attn_back = jax.vjp(rms_norm, tokens, attn_gain.astype(jnp.float32))
    normed_rows = lax.all_gather(normalized_rows.astype(jnp.bfloat16), "ctx", axis=0, tiled=True)
    seq_len = normed_rows.shape[0]
    queries = (
        jnp.dot(normed_rows, w_query, preferred_element_type=jnp.float32)
        .astype(jnp.bfloat16)
        .reshape(seq_len, heads_here, DH)
    )
    key_rows = (
        jnp.dot(normed_rows, w_key, preferred_element_type=jnp.float32)
        .astype(jnp.bfloat16)
        .reshape(seq_len, heads_here, DH)
    )
    value_rows = (
        jnp.dot(normed_rows, w_value, preferred_element_type=jnp.float32)
        .astype(jnp.bfloat16)
        .reshape(seq_len, heads_here, DH)
    )
    starts = jnp.arange(seq_len // QB, dtype=jnp.int32) * QB

    def forward_block(start):
        one_hot, same_doc = block_masks(segment_row, position_row, start)
        query_block = lax.dynamic_slice_in_dim(queries, start, QB, 0)
        attention_scores = block_scores(query_block, key_rows, table_local, one_hot, same_doc)
        row_peak = jnp.max(attention_scores, axis=-1, keepdims=True)
        lifted = jnp.exp(attention_scores - row_peak)
        row_total = jnp.sum(lifted, axis=-1, keepdims=True)
        prob_low = (lifted / row_total).astype(jnp.bfloat16)
        attended_part = jnp.einsum(
            "hij,jhd->ihd", prob_low, value_rows, preferred_element_type=jnp.float32
        )
        return (attended_part, row_peak + jnp.log(row_total))

    attended, log_total = lax.map(forward_block, starts)
    attended_low = attended.reshape(seq_len, heads_here * DH).astype(jnp.bfloat16)
    attn_term = jnp.dot(attended_low, w_attn_out, preferred_element_type=jnp.float32)
    residual = tokens + lax.psum_scatter(attn_term, "ctx", scatter_dimension=0, tiled=True)
    normed_ffn, ffn_back = jax.vjp(rms_norm, residual, ffn_gain.astype(jnp.float32))
    ffn_rows = lax.all_gather(normed_ffn.astype(jnp.bfloat16), "ctx", axis=0, tiled=True)
    gate_value = jnp.dot(ffn_rows, w_gate, preferred_element_type=jnp.float32)
    up_value = jnp.dot(ffn_rows, w_up, preferred_element_type=jnp.float32)
    gelu_gate, gelu_back = jax.vjp(gelu_tanh, gate_value)
    ffn_hidden = (gelu_gate * up_value).astype(jnp.bfloat16)
    down_term = jnp.dot(ffn_hidden, w_down, preferred_element_type=jnp.float32)
    result = residual + lax.psum_scatter(
        down_term.astype(jnp.bfloat16), "ctx", scatter_dimension=0, tiled=True
    ).astype(jnp.float32)
    stored = (
        attn_back,
        normed_rows,
        queries,
        key_rows,
        value_rows,
        table_local,
        head_start,
        starts,
        log_total,
        attended_low,
        ffn_back,
        ffn_rows,
        up_value,
        gelu_gate,
        gelu_back,
        ffn_hidden,
    )
    return (result, stored)


def plain_on_device(
    hidden,
    segment_ids,
    positions,
    attn_gain,
    w_query,
    w_key,
    w_value,
    w_attn_out,
    rel_table,
    ffn_gain,
    w_gate,
    w_up,
    w_down,
    cotangent,
):
    tokens = hidden[0].astype(jnp.float32)
    segment_row = segment_ids[0]
    position_row = positions[0]
    small_set = (
        lax.all_gather(attn_gain, ("dp", "ctx", "fsdp"), axis=0, tiled=True),
        lax.all_gather(ffn_gain, ("dp", "ctx", "fsdp"), axis=0, tiled=True),
        lax.all_gather(rel_table, ("dp", "ctx", "fsdp"), axis=0, tiled=True),
    )
    attn_set = gather_attention(w_query, w_key, w_value, w_attn_out)
    ffn_set = gather_feedforward(w_gate, w_up, w_down)
    result, unused_stored = layer_forward(
        tokens, small_set, attn_set, ffn_set, segment_row, position_row
    )
    back_attn = gather_attention(w_query, w_key, w_value, w_attn_out)
    back_ffn = gather_feedforward(w_gate, w_up, w_down)
    recomputed, stored = layer_forward(
        tokens, small_set, back_attn, back_ffn, segment_row, position_row
    )
    (
        attn_back,
        normed_rows,
        queries,
        key_rows,
        value_rows,
        table_local,
        head_start,
        starts,
        log_total,
        attended_low,
        ffn_back,
        ffn_rows,
        up_value,
        gelu_gate,
        gelu_back,
        ffn_hidden,
    ) = stored
    full_query, full_key, full_value, full_attn_out = back_attn
    full_gate, full_up, full_down = back_ffn
    seq_len = normed_rows.shape[0]
    heads_here = queries.shape[1]
    grad_rows = lax.all_gather(cotangent[0], "ctx", axis=0, tiled=True)
    grad_w_down = jnp.einsum("tf,td->fd", ffn_hidden, grad_rows, preferred_element_type=jnp.float32)
    grad_hidden_ffn = jnp.einsum(
        "td,fd->tf", grad_rows, full_down, preferred_element_type=jnp.float32
    )
    up_value_gradient = (grad_hidden_ffn * gelu_gate).astype(jnp.bfloat16)
    grad_gate_value = gelu_back(grad_hidden_ffn * up_value)[0].astype(jnp.bfloat16)
    grad_w_gate = jnp.einsum(
        "td,tf->df", ffn_rows, grad_gate_value, preferred_element_type=jnp.float32
    )
    grad_w_up = jnp.einsum(
        "td,tf->df", ffn_rows, up_value_gradient, preferred_element_type=jnp.float32
    )
    ffn_normed_term = jnp.einsum(
        "tf,df->td", grad_gate_value, full_gate, preferred_element_type=jnp.float32
    )
    ffn_normed_term = ffn_normed_term + jnp.einsum(
        "tf,df->td", up_value_gradient, full_up, preferred_element_type=jnp.float32
    )
    grad_normed_ffn = lax.psum_scatter(ffn_normed_term, "ctx", scatter_dimension=0, tiled=True)
    grad_residual_norm, grad_ffn_gain = ffn_back(grad_normed_ffn)
    grad_residual = cotangent[0].astype(jnp.float32) + grad_residual_norm
    ffn_sums = (
        lax.psum_scatter(
            grad_w_gate.astype(jnp.bfloat16), ("dp", "fsdp"), scatter_dimension=0, tiled=True
        ).astype(jnp.float32),
        lax.psum_scatter(
            grad_w_up.astype(jnp.bfloat16), ("dp", "fsdp"), scatter_dimension=0, tiled=True
        ).astype(jnp.float32),
        lax.psum_scatter(
            grad_w_down.astype(jnp.bfloat16), ("dp", "fsdp"), scatter_dimension=1, tiled=True
        ).astype(jnp.float32),
    )
    branch_rows = lax.all_gather(grad_residual.astype(jnp.bfloat16), "ctx", axis=0, tiled=True)
    grad_w_attn_out = jnp.einsum(
        "ti,td->id", attended_low, branch_rows, preferred_element_type=jnp.float32
    )
    grad_attended = jnp.einsum(
        "td,id->ti", branch_rows, full_attn_out, preferred_element_type=jnp.float32
    )
    grad_attended = grad_attended.astype(jnp.bfloat16).reshape(seq_len, heads_here, DH)

    def backward_block(operands):
        start, block_total = operands
        one_hot, same_doc = block_masks(segment_row, position_row, start)
        query_block = lax.dynamic_slice_in_dim(queries, start, QB, 0)
        grad_part = lax.dynamic_slice_in_dim(grad_attended, start, QB, 0)
        attention_scores = block_scores(query_block, key_rows, table_local, one_hot, same_doc)
        weights = jnp.exp(attention_scores - block_total)
        prob_low = weights.astype(jnp.bfloat16)
        grad_probs = jnp.einsum(
            "ihd,jhd->hij", grad_part, value_rows, preferred_element_type=jnp.float32
        )
        centred = grad_probs - jnp.sum(weights * grad_probs, axis=-1, keepdims=True)
        grad_scores = (weights * centred).astype(jnp.bfloat16)
        grad_query_part = jnp.einsum(
            "hij,jhd->ihd", grad_scores, key_rows, preferred_element_type=jnp.float32
        )
        grad_key_part = jnp.einsum(
            "hij,ihd->jhd", grad_scores, query_block, preferred_element_type=jnp.float32
        )
        grad_value_part = jnp.einsum(
            "hij,ihd->jhd", prob_low, grad_part, preferred_element_type=jnp.float32
        )
        grad_bias_part = jnp.einsum(
            "hij,bij->bh", grad_scores, one_hot, preferred_element_type=jnp.float32
        )
        return (grad_query_part, grad_key_part, grad_value_part, grad_bias_part)

    query_blocks, key_blocks, value_blocks, bias_blocks = lax.map(
        backward_block, (starts, log_total)
    )
    grad_queries_low = query_blocks.reshape(seq_len, heads_here * DH).astype(jnp.bfloat16)
    grad_keys_low = (
        jnp.sum(key_blocks, axis=0).reshape(seq_len, heads_here * DH).astype(jnp.bfloat16)
    )
    grad_values_low = (
        jnp.sum(value_blocks, axis=0).reshape(seq_len, heads_here * DH).astype(jnp.bfloat16)
    )
    grad_w_query = jnp.einsum(
        "td,te->de", normed_rows, grad_queries_low, preferred_element_type=jnp.float32
    )
    grad_w_key = jnp.einsum(
        "td,te->de", normed_rows, grad_keys_low, preferred_element_type=jnp.float32
    )
    grad_w_value = jnp.einsum(
        "td,te->de", normed_rows, grad_values_low, preferred_element_type=jnp.float32
    )
    normed_term = jnp.einsum(
        "te,de->td", grad_queries_low, full_query, preferred_element_type=jnp.float32
    )
    normed_term = normed_term + jnp.einsum(
        "te,de->td", grad_keys_low, full_key, preferred_element_type=jnp.float32
    )
    normed_term = normed_term + jnp.einsum(
        "te,de->td", grad_values_low, full_value, preferred_element_type=jnp.float32
    )
    grad_normed = lax.psum_scatter(
        normed_term.astype(jnp.bfloat16), "ctx", scatter_dimension=0, tiled=True
    ).astype(jnp.float32)
    token_norm_gradient, grad_attn_gain = attn_back(grad_normed)
    grad_tokens = grad_residual + token_norm_gradient
    attn_sums = (
        lax.psum_scatter(
            grad_w_query.astype(jnp.bfloat16), ("dp", "fsdp"), scatter_dimension=0, tiled=True
        ).astype(jnp.float32),
        lax.psum_scatter(
            grad_w_key.astype(jnp.bfloat16), ("dp", "fsdp"), scatter_dimension=0, tiled=True
        ).astype(jnp.float32),
        lax.psum_scatter(
            grad_w_value.astype(jnp.bfloat16), ("dp", "fsdp"), scatter_dimension=0, tiled=True
        ).astype(jnp.float32),
        lax.psum_scatter(
            grad_w_attn_out.astype(jnp.bfloat16), ("dp", "fsdp"), scatter_dimension=1, tiled=True
        ).astype(jnp.float32),
    )
    bias_sum = jnp.sum(bias_blocks, axis=0)
    table_term = lax.dynamic_update_slice(
        jnp.zeros((NB, H), jnp.float32), bias_sum, (jnp.int32(0), head_start)
    )
    small_sums = (
        lax.psum_scatter(grad_attn_gain, ("dp", "ctx", "fsdp"), scatter_dimension=0, tiled=True),
        lax.psum_scatter(grad_ffn_gain, ("dp", "ctx", "fsdp"), scatter_dimension=0, tiled=True),
        lax.psum_scatter(
            table_term.reshape(NB * H), ("dp", "ctx", "fsdp"), scatter_dimension=0, tiled=True
        ),
    )
    return (
        result[None].astype(jnp.bfloat16),
        grad_tokens[None],
        small_sums[0],
        attn_sums[0],
        attn_sums[1],
        attn_sums[2],
        attn_sums[3],
        small_sums[2],
        small_sums[1],
        ffn_sums[0],
        ffn_sums[1],
        ffn_sums[2],
    )


def plain_solution(mesh):
    in_specs = (
        P(("dp", "fsdp"), "ctx", None),
        P(("dp", "fsdp"), None),
        P(("dp", "fsdp"), None),
        P(("dp", "ctx", "fsdp")),
        P(("dp", "fsdp"), "ctx"),
        P(("dp", "fsdp"), "ctx"),
        P(("dp", "fsdp"), "ctx"),
        P("ctx", ("dp", "fsdp")),
        P(("dp", "ctx", "fsdp")),
        P(("dp", "ctx", "fsdp")),
        P(("dp", "fsdp"), "ctx"),
        P(("dp", "fsdp"), "ctx"),
        P("ctx", ("dp", "fsdp")),
        P(("dp", "fsdp"), "ctx", None),
    )
    out_specs = (
        P(("dp", "fsdp"), "ctx", None),
        P(("dp", "fsdp"), "ctx", None),
        P(("dp", "ctx", "fsdp")),
        P(("dp", "fsdp"), "ctx"),
        P(("dp", "fsdp"), "ctx"),
        P(("dp", "fsdp"), "ctx"),
        P("ctx", ("dp", "fsdp")),
        P(("dp", "ctx", "fsdp")),
        P(("dp", "ctx", "fsdp")),
        P(("dp", "fsdp"), "ctx"),
        P(("dp", "fsdp"), "ctx"),
        P("ctx", ("dp", "fsdp")),
    )
    return jax.shard_map(
        plain_on_device, mesh=mesh, in_specs=in_specs, out_specs=out_specs, check_vma=False
    )


def solution(mesh):
    if 2048 // (mesh.shape["dp"] * mesh.shape["fsdp"]) % 128 or mesh.shape["fsdp"] != 2 or mesh.shape["ctx"] != 4:
        return plain_solution(mesh)
    tokens = P(("dp", "fsdp"), "ctx", None)
    line = P(("dp", "fsdp"), None)
    every = P(("dp", "ctx", "fsdp"))
    into = P(("dp", "fsdp"), "ctx")
    back = P("ctx", ("dp", "fsdp"))
    return jax.shard_map(
        functools.partial(on_device, mesh.shape["dp"]),
        mesh=mesh,
        in_specs=(tokens, line, line, every, into, into, into, back, every, every, into, into, back, tokens),
        out_specs=(tokens, tokens, every, into, into, into, back, every, every, into, into, back),
        check_vma=False,
    )
```

```python
import functools

import jax
import jax.numpy as jnp
from jax import lax
from jax.experimental import pallas as pl
from jax.experimental.pallas import tpu as pltpu
from jax.sharding import PartitionSpec as P

H = 32
DH = 64
NB = 32
EPSILON = 1e-06
THRESHOLDS = (12, 16, 23, 32, 46, 64, 91)
MASKED = -1e30
BF = jnp.bfloat16
F32 = jnp.float32
ANY = pl.BlockSpec(memory_space=pl.ANY)
VM = pl.BlockSpec(memory_space=pltpu.VMEM)
MESH = pl.DeviceIdType.MESH
DMA = pltpu.SemaphoreType.DMA


class Place:
    def __init__(self):
        self.z = lax.axis_index("dp")
        self.c = lax.axis_index("ctx")
        self.y = lax.axis_index("fsdp")
        self.x = self.c // 2
        self.k = self.c % 2

    def device(self, z=None, x=None, k=None, y=None):
        z = self.z if z is None else z
        x = self.x if x is None else x
        k = self.k if k is None else k
        y = self.y if y is None else y
        return {"dp": z, "ctx": x * 2 + k, "fsdp": y}

    def x_peer(self):
        return self.device(x=1 - self.x)

    def y_peer(self):
        return self.device(y=1 - self.y)

    def core_peer(self):
        return self.device(k=1 - self.k)


def block_of(x, k, y):
    return y * 4 + x * 2 + k


def remote(src, dst, send_sem, recv_sem, device):
    return pltpu.make_async_remote_copy(
        src_ref=src,
        dst_ref=dst,
        send_sem=send_sem,
        recv_sem=recv_sem,
        device_id=device,
        device_id_type=MESH,
    )


def greet(devices):
    barrier = pltpu.get_barrier_semaphore()
    for device in devices:
        pl.semaphore_signal(barrier, inc=1, device_id=device, device_id_type=MESH)
    pl.semaphore_wait(barrier, len(devices))


class ActGather:
    def __init__(self, me, own, out, send, recv, local):
        self.me, self.own, self.out = me, own, out
        self.send, self.recv, self.local = send, recv, local
        self.rows = own.shape[0]
        self.half = self.rows // 2

    def part(self, ref, block, h):
        return ref.at[block, pl.ds(h * self.half, self.half)]

    def copy(self, i):
        me = self.me
        x, k, y = me.x, me.k, me.y
        own = block_of(x, k, y)
        if i == 0:
            src, dst, dev = self.own.at[pl.ds(0, self.half)], self.part(self.out, own, 0), me.x_peer()
        elif i == 1:
            src, dst, dev = self.own.at[pl.ds(self.half, self.half)], self.part(self.out, own, 1), me.y_peer()
        elif i == 2:
            src, dst, dev = self.own.at[pl.ds(0, self.half)], self.part(self.out, own, 0), me.y_peer()
        elif i == 3:
            b = block_of(1 - x, k, y)
            src, dst, dev = self.part(self.out, b, 0), self.part(self.out, b, 0), me.y_peer()
        elif i == 4:
            src, dst, dev = self.own.at[pl.ds(self.half, self.half)], self.part(self.out, own, 1), me.x_peer()
        elif i == 5:
            b = block_of(x, k, 1 - y)
            src, dst, dev = self.part(self.out, b, 1), self.part(self.out, b, 1), me.x_peer()
        elif i == 6:
            src, dst, dev = self.own, self.out.at[own], me.core_peer()
        else:
            px, py, h = ((1, 0, 0), (0, 1, 1), (0, 1, 0), (1, 1, 0), (1, 0, 1), (1, 1, 1))[i - 7]
            b = block_of(1 - x if px else x, k, 1 - y if py else y)
            src, dst, dev = self.part(self.out, b, h), self.part(self.out, b, h), me.core_peer()
        return remote(src, dst, self.send.at[i], self.recv.at[i], dev)

    def start_x(self):
        for i in (0, 4, 6):
            self.copy(i).start()
        own = block_of(self.me.x, self.me.k, self.me.y)
        pltpu.make_async_copy(self.own, self.out.at[own], self.local).start()

    def start_y(self):
        for i in (1, 2):
            self.copy(i).start()

    def start(self):
        self.start_x()
        self.start_y()

    def onward(self, *steps):
        for i, after in steps:
            self.copy(i).wait_recv()
            if after:
                self.copy(after).start()
            self.copy(i + 7).start()

    def forward(self):
        self.onward((0, 3), (1, 5))

    def forward_core(self):
        self.onward((2, 0), (4, 0), (3, 0), (5, 0))

    def land(self, *pieces):
        for i in pieces:
            self.copy(i).wait_recv()

    def sent(self):
        for i in range(13):
            self.copy(i).wait_send()
        own = block_of(self.me.x, self.me.k, self.me.y)
        pltpu.make_async_copy(self.own, self.out.at[own], self.local).wait()

    def finish(self):
        self.land(*range(6, 13))
        self.sent()


def gather_sems():
    return [DMA((13,)), DMA((13,)), DMA]


class ActReduce:
    def __init__(self, me, peer_out, core_in, mine, a_y, b_x, a_x, b_y, send, recv):
        self.me, self.peer_out, self.core_in, self.mine = me, peer_out, core_in, mine
        self.a_y, self.b_x, self.a_x, self.b_y = a_y, b_x, a_x, b_y
        self.send, self.recv = send, recv
        self.half = mine.shape[1] // 2

    def place(self, j):
        x, y = self.me.x, self.me.y
        return jnp.where(j % 2 == 0, 1 - x, x), jnp.where(j < 2, 1 - y, y)

    def core_copy(self, j):
        return remote(
            self.peer_out.at[j % 2], self.core_in.at[j], self.send.at[j], self.recv.at[j], self.me.core_peer()
        )

    def rows(self, h):
        return pl.ds(h * self.half, self.half)

    def add(self, slot, h, extra=None):
        def body(i, carry):
            r = pl.ds(pl.multiple_of(h * self.half + i * 16, 16), 16)
            total = self.mine[slot, r, :].astype(F32) + self.core_in[slot, r, :].astype(F32)
            if extra is not None:
                q = pl.ds(pl.multiple_of(i * 16, 16), 16)
                total = total + extra[0, q, :].astype(F32)
            self.mine[slot, r, :] = total.astype(BF)
            return carry

        lax.fori_loop(0, self.half // 16, body, 0)

    def copy(self, name):
        xp, yp = self.me.x_peer(), self.me.y_peer()
        slot, h, dst, i, dev = {
            "ay0": (0, 0, self.a_y.at[0], 4, yp),
            "ay1": (1, 0, self.a_y.at[1], 5, yp),
            "bx0": (0, 1, self.b_x.at[0], 6, xp),
            "bx1": (2, 1, self.b_x.at[1], 7, xp),
            "ax": (2, 0, self.a_x, 8, xp),
            "by": (1, 1, self.b_y, 9, yp),
        }[name]
        return remote(self.mine.at[slot, self.rows(h)], dst, self.send.at[i], self.recv.at[i], dev)

    def first_sends(self, j):
        for name in (("ay0", "bx0"), ("ay1",), ("bx1",))[j]:
            self.copy(name).start()

    def loop(self, make, send=True, first=0, last=4, hooks=()):
        def ready(j):
            self.core_copy(j).wait_recv()
            if j < 2:
                self.add(j, 0)
            if j != 1:
                self.add(j, 1)
            if send:
                self.first_sends(j)

        def body(j, carry):
            ox, oy = self.place(j)

            @pl.when(j >= 2)
            def _():
                self.core_copy(j - 2).wait_send()

            self.peer_out[j % 2] = make(block_of(ox, 1 - self.me.k, oy), 2 * j)
            self.core_copy(j).start()
            for i in range(3):

                @pl.when(j == i + 1)
                def _():
                    ready(i)

            self.mine[j] = make(block_of(ox, self.me.k, oy), 2 * j + 1)

            for i, hook in hooks:

                @pl.when(j == i)
                def _():
                    hook()

            return carry

        lax.fori_loop(first, last, body, 0)

    def second(self):
        self.copy("ay0").wait_recv()
        self.add(2, 0, self.a_y)
        self.copy("ax").start()
        self.copy("bx0").wait_recv()
        self.add(1, 1, self.b_x)
        self.copy("by").start()

    def arrive(self):
        self.core_copy(3).wait_recv()
        for name in ("ay1", "bx1", "ax", "by"):
            self.copy(name).wait_recv()

    def total(self, h, i):
        r = pl.ds(pl.multiple_of(h * self.half + i * 16, 16), 16)
        q = pl.ds(pl.multiple_of(i * 16, 16), 16)
        total = self.mine[3, r, :].astype(F32) + self.core_in[3, r, :].astype(F32)
        if h == 0:
            return total + self.a_y[1, q, :].astype(F32) + self.a_x[q, :].astype(F32)
        return total + self.b_x[1, q, :].astype(F32) + self.b_y[q, :].astype(F32)

    def finish(self):
        for j in (2, 3):
            self.core_copy(j).wait_send()
        for name in ("ay0", "ay1", "bx0", "bx1", "ax", "by"):
            self.copy(name).wait_send()


def reduce_scratch(rows, width):
    half = rows // 2
    return [
        pltpu.VMEM((2, rows, width), BF),
        pltpu.VMEM((4, rows, width), BF),
        pltpu.VMEM((4, rows, width), BF),
        pltpu.VMEM((2, half, width), BF),
        pltpu.VMEM((2, half, width), BF),
        pltpu.VMEM((half, width), BF),
        pltpu.VMEM((half, width), BF),
        DMA((10,)),
        DMA((10,)),
    ]


TQ = 256


def softmax_tile(q, k, v, bias, same):
    s = lax.dot_general(q, k, (((1,), (1,)), ((), ())), preferred_element_type=F32) + bias
    s = jnp.where(same, s, MASKED)
    e = jnp.exp(s - jnp.max(s, axis=-1, keepdims=True))
    pb = (e * (1.0 / jnp.sum(e, axis=-1, keepdims=True))).astype(BF)
    return pb, jnp.dot(pb, v, preferred_element_type=F32).astype(BF)


class Line:
    def __init__(self, me, n, views, send_r, send_l, recv):
        self.me, self.n, self.views = me, n, views
        self.send_r, self.send_l, self.recv = send_r, send_l, recv

    def copies(self, t, yy, right):
        me = self.me
        dev = me.device(z=me.z + 1 if right else me.z - 1)
        sem = self.send_r if right else self.send_l
        return [
            remote(view, view, sem.at[t, yy, i], self.recv.at[t, yy, i], dev)
            for i, view in enumerate(self.views(t, yy))
        ]

    def send(self, t, yy, keep, start):
        for right in (True, False):
            go = (self.me.z + 1 <= self.n - 1) if right else (self.me.z >= 1)
            if keep[right] is not None:
                go = go & keep[right]

            @pl.when(go)
            def _():
                for copy in self.copies(t, yy, right):
                    if start:
                        copy.start()
                    else:
                        copy.wait_send()

    def own(self, yy):
        self.send(self.me.z, yy, {True: None, False: None}, True)

    def came(self, s):
        z, n = self.me.z, self.n
        return (
            (True, z - s, z - s >= 0, z + 1 <= n - 1),
            (False, z + s, z + s <= n - 1, z >= 1),
        )

    def pump(self, s, yy):
        for right, t, here, on in self.came(s):

            @pl.when(here & on)
            def _():
                for copy in self.copies(t, yy, right):
                    copy.wait_recv()
                    copy.start()

    def land(self, yys):
        for s in range(1, self.n):
            for yy in yys:
                for right, t, here, on in self.came(s):

                    @pl.when(here & jnp.logical_not(on))
                    def _():
                        for copy in self.copies(t, yy, right):
                            copy.wait_recv()

    def finish(self):
        for yy in range(2):
            self.send(self.me.z, yy, {True: None, False: None}, False)
            for s in range(1, self.n):
                for right, t, here, on in self.came(s):

                    @pl.when(here & on)
                    def _():
                        for copy in self.copies(t, yy, right):
                            copy.wait_send()


def line_sems(n, parts):
    return [DMA((n, 2, parts))] * 3


def forward_kernel(
    n, length, wq, wk, wv, wo, wg, wu, wd, cot, xin, seg_row, gain_a, gain_f, table_row,
    wqkv, wof, wg1, wd1, wg2, wd2, a1, qkv, o, p, mid, a2all, gall, m1, dgu1, gwf1, gain1, gain2,
    st_in, st_o, st_1, st_d1, st_2, st_d2, small, seg, smalls, segs, segt, xv, wqkv_v, wo_v, qkv_v, o_v, toep, pbuf, a2, wg1_v, wd1_v, gw_v, acc,
    y_send, y_recv, y_local, s_send, s_recv, s2_send, s2_recv, s_local, c_local, p_sem, f_sem,
    *rest,
):
    red_scratch, f1_sems, f2_sems, in_sems, wo_sems = rest[0:9], rest[9:12], rest[12:15], rest[15:18], rest[18:21]
    x_sems, g_sems, a_sems = rest[21:24], rest[24:27], rest[27:30]
    me = Place()
    z, y = me.z, me.y
    rows, width = xin.shape
    piece_rows = wq.shape[0]
    heads = wq.shape[1] // 2
    hid = wg.shape[1] // 2
    h1 = wd1.shape[0]
    h2 = hid - h1
    group = [
        me.device(x=ox, k=ok, y=oy)
        for ox in (me.x, 1 - me.x)
        for ok in (me.k, 1 - me.k)
        for oy in (me.y, 1 - me.y)
    ][1:]
    others = [me.device(z=lax.rem(z + s, n)) for s in range(1, n)]
    greet(group + others)
    small[...] = jnp.zeros_like(small)
    share = gain_a.shape[1]
    for yy in range(2):

        @pl.when(y == yy)
        def _():
            for i, ref in enumerate((gain_a, gain_f)):
                at = i * 128 + yy * share
                small[:, at : at + share] = jnp.broadcast_to(ref[...].astype(F32), (8, share))

    small[:, 256 : 256 + table_row.shape[1]] = jnp.broadcast_to(table_row[...].astype(F32), (8, table_row.shape[1]))
    seg[...] = jnp.broadcast_to(seg_row[...], seg.shape)

    def piece(t, yy):
        return pl.ds(pl.multiple_of((t * 2 + yy) * piece_rows, piece_rows), piece_rows)

    row = piece(z, y)

    def y_copies(yh):
        col = pl.ds(pl.multiple_of(yh * heads, heads), heads)
        at1 = pl.ds(pl.multiple_of(yh * hid, 128), h1)
        at2 = pl.ds(pl.multiple_of(yh * hid + h1, 128), h2)
        return [
            (wq.at[:, col], wqkv.at[row, pl.ds(0, heads)]),
            (wk.at[:, col], wqkv.at[row, pl.ds(heads, heads)]),
            (wv.at[:, col], wqkv.at[row, pl.ds(2 * heads, heads)]),
            (wo.at[col, :], wof.at[:, row]),
            (wg.at[:, at1], wg1.at[row, pl.ds(0, h1)]),
            (wu.at[:, at1], wg1.at[row, pl.ds(h1, h1)]),
            (wd.at[at1, :], wd1.at[:, row]),
            (wg.at[:, at2], wg2.at[row, pl.ds(0, h2)]),
            (wu.at[:, at2], wg2.at[row, pl.ds(h2, h2)]),
            (wd.at[at2, :], wd2.at[:, row]),
        ]

    sends = [
        remote(src, dst, y_send.at[i], y_recv.at[i], me.y_peer())
        for i, (src, dst) in enumerate(y_copies(1 - y))
    ]
    staged = [
        st_in.at[:, pl.ds(0, heads)],
        st_in.at[:, pl.ds(heads, heads)],
        st_in.at[:, pl.ds(2 * heads, heads)],
        st_o,
        st_1.at[:, pl.ds(0, h1)],
        st_1.at[:, pl.ds(h1, h1)],
        st_d1,
        st_2.at[:, pl.ds(0, h2)],
        st_2.at[:, pl.ds(h2, h2)],
        st_d2,
    ]
    takes = [
        pltpu.make_async_copy(src, mid_ref, y_local.at[i])
        for i, ((src, dst), mid_ref) in enumerate(zip(y_copies(y), staged))
    ]
    keeps = [
        pltpu.make_async_copy(mid_ref, dst, y_local.at[i])
        for i, ((src, dst), mid_ref) in enumerate(zip(y_copies(y), staged))
    ]
    me_small = z * 8 + me.c * 2 + y
    small_local = pltpu.make_async_copy(small, smalls.at[me_small], s_local.at[0])
    seg_local = pltpu.make_async_copy(seg, segs.at[y], s_local.at[1])
    small_sends = [
        remote(small, smalls.at[me_small], s_send.at[i], s_recv.at[i], dev) for i, dev in enumerate(group)
    ]
    seg_send = remote(seg, segs.at[y], s_send.at[7], s_recv.at[7], me.y_peer())
    attn = Line(me, n, lambda t, yy: (wqkv.at[piece(t, yy), :],), *in_sems)
    attn_o = Line(me, n, lambda t, yy: (wof.at[:, piece(t, yy)],), *wo_sems)
    f1 = Line(me, n, lambda t, yy: (wg1.at[piece(t, yy), :], wd1.at[:, piece(t, yy)]), *f1_sems)
    f2 = Line(me, n, lambda t, yy: (wg2.at[piece(t, yy), :], wd2.at[:, piece(t, yy)]), *f2_sems)
    xact = ActGather(me, xin, xv, *x_sems)
    gact = ActGather(me, cot, gall, *g_sems)

    for i in range(4):
        takes[i].start()
        sends[i].start()
    small_local.start()
    seg_local.start()
    for copy in small_sends:
        copy.start()
    seg_send.start()
    xact.start_x()
    for i in range(4, 10):
        takes[i].start()
    for i in range(10):
        takes[i].wait()
        keeps[i].start()
    for i in range(4):
        keeps[i].wait()
    attn.own(y)
    for i in range(4):
        sends[i].wait_recv()
    attn.own(1 - y)
    xact.start_y()
    small_local.wait()
    for copy in small_sends:
        copy.wait_recv()
    block8 = smalls.at[pl.ds(pl.multiple_of(z * 8, 8), 8)]
    small_z = [remote(block8, block8, s2_send.at[i], s2_recv.at[i], dev) for i, dev in enumerate(others)]
    for copy in small_z:
        copy.start()
    xact.onward((0, 3))
    attn.pump(1, y)
    attn.pump(1, 1 - y)
    xact.onward((1, 5))
    for i in range(4, 10):
        sends[i].start()
    gact.start()

    for copy in small_z:
        copy.wait_recv()
    for j in range(4 * n):
        gain1[:, 128 * j : 128 * j + 128] = (smalls[2 * j, :, 0:128] + smalls[2 * j + 1, :, 0:128])[0:1]
        gain2[:, 128 * j : 128 * j + 128] = (smalls[2 * j, :, 128:256] + smalls[2 * j + 1, :, 128:256])[0:1]
    seg_local.wait()
    seg_send.wait_recv()
    for s in range(2):
        wide = jnp.concatenate([segs[s]] * 16, axis=0).astype(F32)
        segt[s] = wide.T
    attn.pump(2, y)
    xact.onward((2, 0), (4, 0))
    attn.pump(2, 1 - y)
    attn_o.own(y)
    attn_o.own(1 - y)
    for i in range(4, 7):
        keeps[i].wait()
    f1.own(y)
    offset = lax.broadcasted_iota(jnp.int32, (NB, 2 * length), 1) - length
    far = jnp.abs(offset)
    bucket = jnp.where(far < 8, far, 8 + sum((far >= t).astype(jnp.int32) for t in THRESHOLDS))
    bucket = bucket + 16 * (offset > 0).astype(jnp.int32)
    own_bucket = bucket == lax.broadcasted_iota(jnp.int32, (NB, 2 * length), 0)
    table = smalls[:, 0, 256:384]
    lane = lax.broadcasted_iota(jnp.int32, (NB, 128), 1)
    local_heads = heads // DH
    for lh in range(local_heads):
        head = (me.c * 2 + y) * local_heads + lh
        value = jnp.sum(jnp.where(lane == head, table, 0.0), axis=1, keepdims=True)
        fvec = jnp.sum(jnp.where(own_bucket, value, 0.0), axis=0, keepdims=True)
        toep[lh] = pltpu.roll(jnp.broadcast_to(fvec, (TQ, 2 * length)), 0, 1, stride=1, stride_axis=0)
    xact.onward((3, 0), (5, 0))
    xact.finish()

    def norm_rows(i, carry):
        r = pl.ds(pl.multiple_of(lax.rem(i, rows // 16) * 16, 16), 16)
        b = i // (rows // 16)
        xf = xv[b, r, :].astype(F32)
        inv = lax.rsqrt(jnp.mean(xf * xf, axis=-1, keepdims=True) + EPSILON)
        xv[b, r, :] = (xf * inv * gain1[...]).astype(BF)
        return carry

    lax.fori_loop(0, 4 * rows // 16, norm_rows, 0)
    for i in range(4, 7):
        sends[i].wait_recv()
    f1.own(1 - y)
    attn_o.pump(1, y)
    attn_o.pump(1, 1 - y)
    lax.fori_loop(4 * rows // 16, 8 * rows // 16, norm_rows, 0)
    a1_out = pltpu.make_async_copy(xv, a1, c_local.at[0])
    a1_out.start()
    attn_o.pump(2, y)
    attn_o.pump(2, 1 - y)
    attn.land((y, 1 - y))
    w_in = pltpu.make_async_copy(wqkv, wqkv_v, c_local.at[1])
    w_in.start()
    w_in.wait()

    def project(b, carry):
        r = pl.ds(pl.multiple_of(b * rows, rows), rows)
        qkv_v[r, :] = jnp.dot(xv[b], wqkv_v[...], preferred_element_type=F32).astype(BF)
        return carry

    lax.fori_loop(0, 8, project, 0)
    qkv_out = pltpu.make_async_copy(qkv_v, qkv, c_local.at[3])
    qkv_out.start()
    f1.pump(1, y)
    tiles = length // TQ

    def p_copy(slot, head, t):
        return pltpu.make_async_copy(
            pbuf.at[slot], p.at[head, pl.ds(t * TQ, TQ)], p_sem.at[slot]
        )

    def sequence(s, fresh, between):
        base = pl.multiple_of(s * length, length)
        seq = pl.ds(base, length)

        def head_pair(hp, carry):
            def lanes(part):
                return pl.ds(pl.multiple_of(part * heads + hp * 2 * DH, 128), 2 * DH)

            k2 = qkv_v[seq, lanes(1)]
            v2 = qkv_v[seq, lanes(2)]
            for t in range(tiles):
                r = pl.ds(pl.multiple_of(base + t * TQ, TQ), TQ)
                q2 = qkv_v[r, lanes(0)]
                same = segt[s, t * TQ : (t + 1) * TQ, 0:1] == segs[s, 0:1, :].astype(F32)
                outs = []
                for h in range(2):
                    cut = slice(h * DH, (h + 1) * DH)
                    pb, ot = softmax_tile(
                        q2[:, cut], k2[:, cut], v2[:, cut],
                        toep[hp * 2 + h, :, length - t * TQ : 2 * length - t * TQ], same,
                    )
                    head = s * local_heads + hp * 2 + h
                    if fresh and t == 0:

                        @pl.when(hp > 0)
                        def _():
                            p_copy(h, head, t).wait()
                    else:
                        p_copy(h, head, t).wait()
                    pbuf[h] = pb
                    p_copy(h, head, t).start()
                    outs.append(ot)
                o_v[r, pl.ds(pl.multiple_of(hp * 2 * DH, 128), 2 * DH)] = jnp.concatenate(outs, axis=1)

            @pl.when(hp == 0)
            def _():
                between()

            return carry

        lax.fori_loop(0, local_heads // 2, head_pair, 0)

    def attn_term(block, i):
        r = pl.ds(pl.multiple_of(block * rows, rows), rows)
        return jnp.dot(o_v[r, :], wo_v[...], preferred_element_type=F32).astype(BF)

    red = ActReduce(me, *red_scratch)
    def beside_first():
        f1.pump(1, 1 - y)
        gact.forward()

    def beside_second():
        for i in range(7, 10):
            keeps[i].wait()
            sends[i].wait_recv()
        f2.own(y)
        f2.own(1 - y)
        gact.forward_core()

    sequence(1 - y, True, beside_first)
    attn_o.land((y, 1 - y))
    wo_in = pltpu.make_async_copy(wof, wo_v, c_local.at[2])
    wo_in.start()
    f1.pump(2, y)
    f1.pump(2, 1 - y)
    wo_in.wait()
    red.loop(attn_term, first=0, last=2)
    sequence(y, False, beside_second)
    for slot in range(2):
        p_copy(slot, 0, 0).wait()
    o_out = pltpu.make_async_copy(o_v, o, c_local.at[4])
    o_out.start()
    red.loop(attn_term, first=2, last=4)
    red.second()
    f2.pump(1, y)
    red.arrive()

    half = rows // 2
    for h in range(2):

        def body(i, carry):
            rr = pl.ds(pl.multiple_of(h * half + i * 16, 16), 16)
            m = xin[rr, :].astype(F32) + red.total(h, i)
            mid[rr, :] = m
            inv = lax.rsqrt(jnp.mean(m * m, axis=-1, keepdims=True) + EPSILON)
            a2[rr, :] = (m * inv * gain2[...]).astype(BF)
            return carry

        lax.fori_loop(0, half // 16, body, 0)
    aact = ActGather(me, a2, a2all, *a_sems)
    aact.start()
    f2.pump(1, 1 - y)
    f1.land((y, 1 - y))

    def fetch(src, dst, i):
        return pltpu.make_async_copy(src, dst, f_sem.at[i])

    a1_out.wait()
    fetch(wg1, wg1_v, 0).start()
    fetch(wd1, wd1_v, 1).start()
    gact.finish()

    def block_at(i):
        ox, oy = red.place(3 - i // 2)
        return block_of(ox, jnp.where(i % 2 == 0, me.k, 1 - me.k), oy)

    def load_rows(i):
        slot = lax.rem(i, 2)
        b = block_at(i)
        return fetch(a2all.at[b], xv.at[slot], 2 + slot), fetch(gall.at[b], xv.at[2 + slot], 4 + slot)

    def first_units(j, last, carry):
        b = block_at(j)

        @pl.when(j < last)
        def _():
            for copy in load_rows(j + 1):
                copy.start()

        for copy in load_rows(j):
            copy.wait()
        slot = lax.rem(j, 2)
        acc[:, 0 : 2 * h1] = jnp.dot(xv[slot], wg1_v[...], preferred_element_type=F32)
        acc[:, 2 * h1 : 3 * h1] = lax.dot_general(
            xv[2 + slot], wd1_v[...], (((1,), (1,)), ((), ())), preferred_element_type=F32
        )

        def body(i, inner):
            rr = pl.ds(pl.multiple_of(i * 16, 16), 16)
            tr = pl.ds(pl.multiple_of(b * rows + i * 16, 16), 16)
            gate, up, gm = acc[rr, 0:h1], acc[rr, h1 : 2 * h1], acc[rr, 2 * h1 : 3 * h1]
            gelu, slope = gelu_parts(gate)
            wqkv_v[tr, 0:h1] = (gm * up * slope).astype(BF)
            wqkv_v[tr, h1 : 2 * h1] = (gm * gelu).astype(BF)
            qkv_v[tr, 0:h1] = (gelu * up).astype(BF)
            return inner

        lax.fori_loop(0, rows // 16, body, 0)
        return carry

    def units(first, last):
        for copy in load_rows(first):
            copy.start()
        lax.fori_loop(first, last, lambda j, carry: first_units(j, last - 1, carry), 0)

    pltpu.make_async_copy(a2, a2all.at[block_at(0)], a_sems[2]).wait()
    qkv_out.wait()
    fetch(wg1, wg1_v, 0).wait()
    fetch(wd1, wd1_v, 1).wait()
    aact.land(6)
    units(0, 2)
    aact.forward()
    f2.pump(2, y)
    aact.onward((2, 0), (4, 0))
    aact.land(7, 8, 9, 11)
    units(2, 6)
    aact.onward((3, 0), (5, 0))
    aact.land(10, 12)
    f2.pump(2, 1 - y)
    units(6, 8)
    red.finish()
    kept = [fetch(wqkv_v.at[:, pl.ds(0, 2 * h1)], dgu1, 0), fetch(qkv_v.at[:, pl.ds(0, h1)], m1, 1)]
    for copy in kept:
        copy.start()

    def load_columns(i):
        slot = lax.rem(i, 2)
        at = pl.ds(pl.multiple_of(i * rows, rows), rows)
        here = pl.ds(pl.multiple_of(slot * rows, rows), rows)
        there = pl.ds(pl.multiple_of((2 + slot) * rows, rows), rows)
        return (
            fetch(a2all.at[:, :, at], xv.at[:, :, here], 2 + slot),
            fetch(gall.at[:, :, at], xv.at[:, :, there], 4 + slot),
        )

    for copy in load_columns(0):
        copy.start()

    def first_grads(i, carry):
        @pl.when(i < 2 * n - 1)
        def _():
            for copy in load_columns(i + 1):
                copy.start()

        for copy in load_columns(i):
            copy.wait()
        slot = lax.rem(i, 2)
        here = pl.ds(pl.multiple_of(slot * rows, rows), rows)
        there = pl.ds(pl.multiple_of((2 + slot) * rows, rows), rows)
        gw_v[i, :, 0 : 2 * h1] = lax.dot_general(
            xv[:, :, here].reshape(8 * rows, rows), wqkv_v[:, 0 : 2 * h1], (((0,), (0,)), ((), ())),
            preferred_element_type=F32,
        ).astype(BF)
        gw_v[i, :, 2 * h1 : 3 * h1] = lax.dot_general(
            xv[:, :, there].reshape(8 * rows, rows), qkv_v[:, 0:h1], (((0,), (0,)), ((), ())),
            preferred_element_type=F32,
        ).astype(BF)
        return carry

    lax.fori_loop(0, 2 * n, first_grads, 0)
    kept.append(fetch(gw_v, gwf1, 2))
    kept[2].start()
    for i in range(13):
        aact.copy(i).wait_send()
    f2.land((y, 1 - y))
    for line in (attn, attn_o, f1, f2):
        line.finish()
    for copy in small_sends:
        copy.wait_send()
    for copy in small_z:
        copy.wait_send()
    seg_send.wait_send()
    for copy in sends:
        copy.wait_send()
    o_out.wait()
    for copy in kept:
        copy.wait()


def forward(n, h1, wq, wk, wv, wo, wg, wu, wd, cot, xin, seg_row, gain_a, gain_f, table_row):
    rows, width = xin.shape
    heads = wq.shape[1] // 2
    hid = wg.shape[1] // 2
    length = seg_row.shape[1]
    small, seg = (8, 384), (8, length)
    local_heads = heads // DH
    tokens = 8 * rows
    shapes = [
        ((width, 3 * heads), BF),
        ((heads, width), BF),
        ((width, 2 * h1), BF),
        ((h1, width), BF),
        ((width, 2 * (hid - h1)), BF),
        ((hid - h1, width), BF),
        ((8, rows, width), BF),
        ((tokens, 3 * heads), BF),
        ((tokens, heads), BF),
        ((2 * local_heads, length, length), BF),
        ((rows, width), F32),
        ((8, rows, width), BF),
        ((8, rows, width), BF),
        ((tokens, h1), BF),
        ((tokens, 2 * h1), BF),
        ((2 * n, rows, 3 * h1), BF),
        ((1, width), F32),
        ((1, width), F32),
    ]
    scratch = [
        pltpu.VMEM((wq.shape[0], 3 * heads), BF),
        pltpu.VMEM((heads, wo.shape[1]), BF),
        pltpu.VMEM((wq.shape[0], 2 * h1), BF),
        pltpu.VMEM((h1, wd.shape[1]), BF),
        pltpu.VMEM((wq.shape[0], 2 * (hid - h1)), BF),
        pltpu.VMEM((hid - h1, wd.shape[1]), BF),
        pltpu.VMEM(small, F32),
        pltpu.VMEM(seg, jnp.int32),
        pltpu.VMEM((8 * n,) + small, F32),
        pltpu.VMEM((2,) + seg, jnp.int32),
        pltpu.VMEM((2, length, 128), F32),
        pltpu.VMEM((8, rows, width), BF),
        pltpu.VMEM((width, 3 * heads), BF),
        pltpu.VMEM((heads, width), BF),
        pltpu.VMEM((tokens, 3 * heads), BF),
        pltpu.VMEM((tokens, heads), BF),
        pltpu.VMEM((local_heads, TQ, 2 * length), F32),
        pltpu.VMEM((2, TQ, length), BF),
        pltpu.VMEM((rows, width), BF),
        pltpu.VMEM((width, 2 * h1), BF),
        pltpu.VMEM((h1, width), BF),
        pltpu.VMEM((2 * n, rows, 3 * h1), BF),
        pltpu.VMEM((rows, 3 * h1), F32),
        DMA((10,)), DMA((10,)), DMA((10,)), DMA((8,)), DMA((8,)), DMA((n - 1,)), DMA((n - 1,)), DMA((2,)),
        DMA((5,)), DMA((2,)), DMA((6,)),
    ] + reduce_scratch(rows, width) + line_sems(n, 2) * 2 + line_sems(n, 1) * 2 + gather_sems() * 3
    return pl.pallas_call(
        functools.partial(forward_kernel, n, length),
        out_shape=[jax.ShapeDtypeStruct(s, d) for s, d in shapes],
        in_specs=[ANY] * 7 + [VM] * 6,
        out_specs=[ANY] * 10 + [VM] + [ANY] * 5 + [VM] * 2,
        scratch_shapes=scratch,
        compiler_params=pltpu.CompilerParams(
            collective_id=0, has_side_effects=True, vmem_limit_bytes=64 << 20
        ),
        name="forward",
    )(wq, wk, wv, wo, wg, wu, wd, cot, xin, seg_row, gain_a, gain_f, table_row)


class LineSum:
    def __init__(self, me, n, views, from_left, from_right, stage, sems, stage_sem):
        self.me, self.n, self.views = me, n, views
        self.inbox = {True: from_left, False: from_right}
        self.stage, self.stage_sem = stage, stage_sem
        self.sends = {True: sems[0], False: sems[1]}
        self.recvs = {True: sems[2], False: sems[3]}

    def copies(self, t, yy, right):
        me = self.me
        dev = me.device(z=me.z + 1 if right else me.z - 1)
        return [
            remote(
                view, self.inbox[right].at[t, yy, i], self.sends[right].at[t, yy, i],
                self.recvs[right].at[t, yy, i], dev,
            )
            for i, view in enumerate(self.views(t * 2 + yy))
        ]

    def start(self, t, yy, right):
        for copy in self.copies(t, yy, right):
            copy.start()

    def take(self, t, yy, right):
        slot = 0 if right else 1
        return pltpu.make_async_copy(self.inbox[right].at[t, yy, 0], self.stage[slot], self.stage_sem.at[slot])

    def open(self, t, yy, right):
        self.copies(t, yy, right)[0].wait_recv()
        self.take(t, yy, right).start()

    def add(self, t, yy, right):
        self.take(t, yy, right).wait()
        view, stage = self.views(t * 2 + yy)[0], self.stage[0 if right else 1]

        def body(r, carry):
            rr = pl.ds(pl.multiple_of(r * 16, 16), 16)
            view[rr, :] = (view[rr, :].astype(F32) + stage[rr, :].astype(F32)).astype(BF)
            return carry

        lax.fori_loop(0, view.shape[0] // 16, body, 0)

    def first(self, t, yy):
        @pl.when((self.me.z == 0) & (t > 0))
        def _():
            self.start(t, yy, True)

        @pl.when((self.me.z == self.n - 1) & (t < self.n - 1))
        def _():
            self.start(t, yy, False)

    def pump(self, k, yy):
        z, n = self.me.z, self.n
        sides = (
            (True, z + k, (z + k <= n - 1) & (z > 0)),
            (False, z - k, (z - k >= 0) & (z < n - 1)),
        )
        for right, t, go in sides:

            @pl.when(go)
            def _():
                self.open(t, yy, right)

        for right, t, go in sides:

            @pl.when(go)
            def _():
                self.add(t, yy, right)
                self.start(t, yy, right)

    def own(self, yy):
        z = self.me.z
        sides = ((True, z > 0), (False, z < self.n - 1))
        for right, go in sides:

            @pl.when(go)
            def _():
                self.open(z, yy, right)

        for right, go in sides:

            @pl.when(go)
            def _():
                self.add(z, yy, right)

    def finish(self):
        z, n = self.me.z, self.n
        for yy in range(2):
            for k in range(1, n):

                @pl.when(z + k <= n - 1)
                def _():
                    for copy in self.copies(z + k, yy, True):
                        copy.wait_send()

                @pl.when(z - k >= 0)
                def _():
                    for copy in self.copies(z - k, yy, False):
                        copy.wait_send()


def far_first(n, z, i):
    slot = 0
    for a in range(n):
        order = sorted(range(n), key=lambda d: (-abs(d - a), d))
        for b in range(n):
            slot = slot + jnp.where((z == a) & (i == b), order[b], 0)
    return slot


def gelu_parts(gate):
    th = jnp.tanh(0.7978845608028654 * (gate + 0.044715 * gate * gate * gate))
    gelu = 0.5 * gate * (1.0 + th)
    slope = 0.5 * (1.0 + th) + 0.5 * gate * (1.0 - th * th) * 0.7978845608028654 * (
        1.0 + 3 * 0.044715 * gate * gate
    )
    return gelu, slope


def norm_back(ga, values, gain):
    inv = lax.rsqrt(jnp.mean(values * values, axis=-1, keepdims=True) + EPSILON)
    u = ga * gain
    corr = jnp.mean(u * values, axis=-1, keepdims=True) * inv * inv * inv
    return inv * u - values * corr, ga * (values * inv)


def backward_kernel(
    n, length, heads, hid, h1,
    wg1, wd1, wg2, wd2, m1, dgu1, gwf1, a2all, gall, p, a1, qkv, o, wqkv, wof, hidden, mid, cot, gain1, gain2,
    out, gx, fo1, fo2, bo, co, sums, dzall, e_left, e_right, f_left, f_right, b_left, b_right, c_left, c_right,
    wgu_v, wd_v, row_a, row_b, row_g, col_a, col_g, m, dgu, gw1, gw2, stage, gmid, dz, wqkv_v,
    pbuf, acc, dkt, dvt, diag, gg1, gg2, sv, sv_in, sv_z, free,
    load, p_sem, stage_sem, y_send, y_recv, y_local, sv_send, sv_recv, sz_send, sz_recv,
    *rest,
):
    red_scratch, dz_sems = rest[:9], rest[9:12]
    e_sems, f_sems, b_sems, c_sems = (rest[i : i + 4] for i in range(12, 28, 4))
    h2 = hid - h1
    me = Place()
    z, y = me.z, me.y
    rows, width = cot.shape
    group = [
        me.device(x=ox, k=ok, y=oy)
        for ox in (me.x, 1 - me.x)
        for ok in (me.k, 1 - me.k)
        for oy in (me.y, 1 - me.y)
    ][1:]
    others = [me.device(z=lax.rem(z + s, n)) for s in range(1, n)]
    greet(group + others)
    local_heads = heads // DH
    half = rows // 2

    def fetch(src, dst, i):
        return pltpu.make_async_copy(src, dst, load.at[i])

    red = ActReduce(me, *red_scratch)
    order = (1 - y, y)

    def line_sum(view, left, right, width, sems):
        stages = [stage.at[i, :, pl.ds(0, width)] for i in range(2)]
        return LineSum(me, n, lambda pc: [view(pc)], left, right, stages, sems, stage_sem)

    esum = line_sum(lambda pc: gw1.at[pc], e_left, e_right, 3 * h1, e_sems)
    fsum = line_sum(lambda pc: gw2.at[pc], f_left, f_right, 3 * h2, f_sems)

    def piece(pc):
        return pl.ds(pl.multiple_of(pc * rows, rows), rows)

    pair = 3 * 2 * DH
    bsum = line_sum(lambda pc: m.at[piece(pc), :], b_left, b_right, heads + pair, b_sems)
    csum = line_sum(lambda pc: dgu.at[piece(pc), pl.ds(3 * heads, pair)], c_left, c_right, pair, c_sems)

    def piece_at(i):
        return far_first(n, z, i // 2) * 2 + jnp.where(i % 2 == 0, 1 - y, y)

    w_loads = [
        fetch(gwf1, gw1, 0),
        fetch(wg2, wgu_v.at[:, pl.ds(2 * h1, 2 * h2)], 1),
        fetch(wd2, wd_v.at[pl.ds(h1, h2), :], 6),
        fetch(wg1, wgu_v.at[:, pl.ds(0, 2 * h1)], 7),
        fetch(dgu1, dgu.at[:, pl.ds(0, 2 * h1)], 8),
        fetch(wd1, wd_v.at[pl.ds(0, h1), :], 9),
        fetch(m1, m.at[:, pl.ds(0, h1)], 10),
    ]
    for copy in w_loads:
        copy.start()

    def block_at(i):
        j = i // 2
        ox, oy = red.place(j)
        return block_of(ox, jnp.where(i % 2 == 0, 1 - me.k, me.k), oy)

    fetch(a2all.at[block_at(0)], row_a, 2).start()
    fetch(gall.at[block_at(0)], row_g, 3).start()
    w_loads[0].wait()

    def first_slots(i, carry):
        pc = piece_at(i)
        esum.first(pc // 2, pc % 2)
        return carry

    lax.fori_loop(0, 2 * n, first_slots, 0)
    for copy in w_loads[1:]:
        copy.wait()


    def make_ffn(block, i):
        fetch(a2all.at[block], row_a, 2).wait()
        acc[:, 0 : 2 * h2] = jnp.dot(row_a[...], wgu_v[:, 2 * h1 : 2 * hid], preferred_element_type=F32)

        @pl.when(i < 7)
        def _():
            fetch(a2all.at[block_at(i + 1)], row_a, 2).start()

        fetch(gall.at[block], row_g, 3).wait()
        acc[:, 2 * h2 : 3 * h2] = lax.dot_general(
            row_g[...], wd_v[h1:hid, :], (((1,), (1,)), ((), ())), preferred_element_type=F32
        )

        @pl.when(i < 7)
        def _():
            fetch(gall.at[block_at(i + 1)], row_g, 3).start()

        def body(r, carry):
            rr = pl.ds(pl.multiple_of(r * 16, 16), 16)
            tr = pl.ds(pl.multiple_of(block * rows + r * 16, 16), 16)
            gate, up, gm = acc[rr, 0:h2], acc[rr, h2 : 2 * h2], acc[rr, 2 * h2 : 3 * h2]
            gelu, slope = gelu_parts(gate)
            m[tr, h1:hid] = (gelu * up).astype(BF)
            dgu[tr, 2 * h1 : 2 * h1 + h2] = (gm * up * slope).astype(BF)
            dgu[tr, 2 * h1 + h2 : 2 * hid] = (gm * gelu).astype(BF)
            return carry

        lax.fori_loop(0, rows // 16, body, 0)
        return lax.dot_general(
            dgu[piece(block), :], wgu_v[...], (((1,), (1,)), ((), ())), preferred_element_type=F32
        ).astype(BF)

    red.loop(make_ffn, hooks=((1, lambda: esum.pump(2, order[0])), (2, lambda: esum.pump(2, order[1]))))
    esum.pump(1, order[0])

    fetch(wof, row_g, 3).start()

    def columns(ref, i):
        return ref.at[:, :, piece(piece_at(i))]

    def load_columns(left, right, i):
        slot = lax.rem(i, 2)
        return fetch(columns(left, i), col_a.at[slot], 11 + slot), fetch(columns(right, i), col_g.at[slot], 13 + slot)

    def next_columns(left, right, i):
        @pl.when(i < 2 * n - 1)
        def _():
            for copy in load_columns(left, right, i + 1):
                copy.start()

        for copy in load_columns(left, right, i):
            copy.wait()

    for copy in load_columns(a2all, gall, 0):
        copy.start()

    def ffn_grads(i, carry):
        pc = piece_at(i)
        slot = lax.rem(i, 2)
        next_columns(a2all, gall, i)
        gw2[pc, :, 0 : 2 * h2] = lax.dot_general(
            col_a[slot].reshape(8 * rows, rows), dgu[:, 2 * h1 : 2 * hid], (((0,), (0,)), ((), ())),
            preferred_element_type=F32,
        ).astype(BF)
        gw2[pc, :, 2 * h2 : 3 * h2] = lax.dot_general(
            col_g[slot].reshape(8 * rows, rows), m[:, h1:hid], (((0,), (0,)), ((), ())),
            preferred_element_type=F32,
        ).astype(BF)
        fsum.first(pc // 2, pc % 2)
        return carry

    lax.fori_loop(0, n, ffn_grads, 0)
    red.second()
    esum.pump(1, order[1])
    fetch(qkv, wgu_v.at[:, pl.ds(0, 3 * heads)], 0).start()
    fetch(o, wgu_v.at[:, pl.ds(3 * heads, heads)], 6).start()
    red.arrive()

    gg2[...] = jnp.zeros_like(gg2)
    for h in range(2):

        def body(i, carry):
            rr = pl.ds(pl.multiple_of(h * half + i * 16, 16), 16)
            back, gains = norm_back(red.total(h, i), mid[rr, :], gain2[...])
            gm = cot[rr, :].astype(F32) + back
            gmid[rr, :] = gm
            dz[rr, :] = gm.astype(BF)
            gg2[...] += gains[:8] + gains[8:]
            return carry

        lax.fori_loop(0, half // 16, body, 0)
    act = ActGather(me, dz, dzall, *dz_sems)
    act.start()
    red.finish()

    def release():
        for i, dev in enumerate((me.x_peer(), me.y_peer(), me.core_peer())):
            pl.semaphore_signal(free.at[i], inc=1, device_id=dev, device_id_type=MESH)

    def claim():
        for i in range(3):
            pl.semaphore_wait(free.at[i], 1)

    release()
    lax.fori_loop(n, 2 * n, ffn_grads, 0)
    act.forward()

    claim()

    def make_out(block, i):
        return jnp.dot(m[piece(block), :], wd_v[...], preferred_element_type=F32).astype(BF)

    red.loop(make_out, send=False)
    def swap(views, box, i):
        out = remote(views(z * 2 + 1 - y)[0], box.at[y], y_send.at[i], y_recv.at[i], me.y_peer())
        keep = pltpu.make_async_copy(views(z * 2 + y)[0], box.at[y], y_local.at[i])
        return out, keep

    lines = (esum, fsum, bsum, csum)
    swaps = [swap(line.views, box, i) for i, (line, box) in enumerate(zip(lines, (fo1, fo2, bo, co)))]

    def settle(i):
        lines[i].own(order[0])
        swaps[i][0].start()
        lines[i].own(order[1])
        swaps[i][1].start()

    fsum.pump(2, order[0])
    act.forward_core()
    for j in range(3):
        red.first_sends(j)
    settle(0)
    act.finish()

    fetch(wof, row_g, 3).wait()
    slots = ((row_a, 2), (row_b, 4))
    for b in range(2):
        fetch(dzall.at[b], *slots[b]).start()

    def project_back(i, carry):
        for b, (buffer, sem) in enumerate(slots):
            block = i * 2 + b
            fetch(dzall.at[block], buffer, sem).wait()
            wgu_v[piece(block), 4 * heads : 5 * heads] = lax.dot_general(
                buffer[...], row_g[...], (((1,), (1,)), ((), ())), preferred_element_type=F32
            ).astype(BF)

            @pl.when(i < 3)
            def _():
                fetch(dzall.at[block + 2], buffer, sem).start()

        return carry

    lax.fori_loop(0, 4, project_back, 0)
    fsum.pump(2, order[1])
    fetch(hidden, row_a, 2).start()
    w_parts = [
        fetch(
            wqkv.at[:, pl.ds(part * heads + hp * 2 * DH, 2 * DH)],
            wqkv_v.at[:, pl.ds(hp * pair + part * 2 * DH, 2 * DH)],
            15 + hp * 3 + part,
        )
        for hp in range(2)
        for part in range(3)
    ]
    for copy in w_parts:
        copy.start()
    fetch(qkv, wgu_v.at[:, pl.ds(0, 3 * heads)], 0).wait()
    fetch(o, wgu_v.at[:, pl.ds(3 * heads, heads)], 6).wait()
    diag[...] = jnp.zeros_like(diag)
    tiles = length // TQ

    def p_load(head, t, slot):
        return pltpu.make_async_copy(p.at[head, pl.ds(t * TQ, TQ)], pbuf.at[slot], p_sem.at[slot])

    def head_pair(hp):
        def sequence(s, carry):
            head0 = s * local_heads + hp * 2
            base = pl.multiple_of(s * length, length)
            p_load(head0, 0, 0).start()
            p_load(head0, 1, 1).start()
            for h in range(2):
                lo = hp * 128 + h * DH
                to = hp * pair + h * DH
                seq = pl.ds(base, length)
                kh = wgu_v[seq, heads + lo : heads + lo + DH]
                vh = wgu_v[seq, 2 * heads + lo : 2 * heads + lo + DH]
                acc[...] = jnp.zeros_like(acc)
                for t in range(tiles):
                    slot = t % 2
                    r = pl.ds(pl.multiple_of(base + t * TQ, TQ), TQ)
                    qh = wgu_v[r, lo : lo + DH]
                    doh = wgu_v[r, 4 * heads + lo : 4 * heads + lo + DH]
                    p_load(head0 + h, t, slot).wait()
                    pb = pbuf[slot]
                    dp = lax.dot_general(doh, vh, (((1,), (1,)), ((), ())), preferred_element_type=F32)
                    pf = pb.astype(F32)
                    ds = (pf * (dp - jnp.sum(pf * dp, axis=-1, keepdims=True))).astype(BF)
                    dgu[r, to : to + DH] = jnp.dot(ds, kh, preferred_element_type=F32).astype(BF)
                    ck = lax.dot_general(qh, ds, (((0,), (0,)), ((), ())), preferred_element_type=F32)
                    cv = lax.dot_general(doh, pb, (((0,), (0,)), ((), ())), preferred_element_type=F32)
                    u = h * tiles + t + 2
                    if u < 2 * tiles:
                        p_load(head0 + u // tiles, u % tiles, slot).start()
                    if t == 0:
                        dkt[...] = ck
                        dvt[...] = cv
                    else:
                        dkt[...] += ck
                        dvt[...] += cv
                    acc[:, length - t * TQ : 2 * length - t * TQ] += ds.astype(F32)
                dgu[seq, to + 2 * DH : to + 3 * DH] = dkt[...].T.astype(BF)
                dgu[seq, to + 4 * DH : to + 5 * DH] = dvt[...].T.astype(BF)
                c = TQ // 2
                while c >= 8:
                    acc[0:c, :] += pltpu.roll(acc[c : 2 * c, :], 2 * length - c, 1)
                    c //= 2
                diag[hp * 2 + h] += acc[0:8, :]
            return carry

        lax.fori_loop(0, 2, sequence, 0)

    def pair_grads(hp, line, with_o):
        def loads(i):
            slot = lax.rem(i, 2)
            both = fetch(columns(a1, i), col_a.at[slot], 11 + slot), fetch(columns(dzall, i), col_g.at[slot], 13 + slot)
            return both if with_o else both[:1]

        for copy in loads(0):
            copy.start()

        def body(i, carry):
            pc = piece_at(i)
            slot = lax.rem(i, 2)

            @pl.when(i < 2 * n - 1)
            def _():
                for copy in loads(i + 1):
                    copy.start()

            for copy in loads(i):
                copy.wait()
            if with_o:
                m[piece(pc), 0:heads] = lax.dot_general(
                    col_g[slot].reshape(8 * rows, rows), wgu_v[:, 3 * heads : 4 * heads], (((0,), (0,)), ((), ())),
                    preferred_element_type=F32,
                ).astype(BF)
            part = lax.dot_general(
                col_a[slot].reshape(8 * rows, rows), dgu[:, hp * pair : (hp + 1) * pair], (((0,), (0,)), ((), ())),
                preferred_element_type=F32,
            ).astype(BF)
            if with_o:
                m[piece(pc), heads : heads + pair] = part
            else:
                dgu[piece(pc), 3 * heads : 3 * heads + pair] = part
            line.first(pc // 2, pc % 2)
            return carry

        lax.fori_loop(0, 2 * n, body, 0)

    head_pair(0)
    fsum.pump(1, order[0])
    red.second()
    pair_grads(0, bsum, True)
    fsum.pump(1, order[1])
    head_pair(1)
    for yy in order:
        bsum.pump(2, yy)

    red.arrive()
    for h in range(2):

        def body(i, carry):
            rr = pl.ds(pl.multiple_of(h * half + i * 16, 16), 16)
            out[rr, :] = (mid[rr, :] + red.total(h, i)).astype(BF)
            return carry

        lax.fori_loop(0, half // 16, body, 0)
    red.finish()
    release()
    claim()
    for copy in w_parts:
        copy.wait()

    def make_ga1(block, i):
        return lax.dot_general(
            dgu[piece(block), 0 : 3 * heads], wqkv_v[...], (((1,), (1,)), ((), ())), preferred_element_type=F32
        ).astype(BF)

    red.loop(make_ga1)
    pair_grads(1, csum, False)
    red.second()
    settle(1)
    for yy in order:
        bsum.pump(1, yy)
        csum.pump(2, yy)

    offset = lax.broadcasted_iota(jnp.int32, (NB, 2 * length), 1) - length
    away = jnp.abs(offset)
    bucket = jnp.where(away < 8, away, 8 + sum((away >= t).astype(jnp.int32) for t in THRESHOLDS))
    bucket = bucket + 16 * (offset > 0).astype(jnp.int32)
    own_bucket = bucket == lax.broadcasted_iota(jnp.int32, (NB, 2 * length), 0)
    lane = lax.broadcasted_iota(jnp.int32, (NB, 128), 1)
    table = jnp.zeros((NB, 128), F32)
    for lh in range(local_heads):
        line = diag[lh, 0:1, :]
        for r in range(1, 8):
            line = line + pltpu.roll(diag[lh, r : r + 1, :], 2 * length - r, 1)
        value = jnp.sum(jnp.where(own_bucket, line, 0.0), axis=1, keepdims=True)
        table = jnp.where(lane == (me.c * 2 + y) * local_heads + lh, value, table)
    for yy in order:
        csum.pump(1, yy)
    red.arrive()
    gg1[...] = jnp.zeros_like(gg1)
    fetch(hidden, row_a, 2).wait()
    for h in range(2):

        def body(i, carry):
            rr = pl.ds(pl.multiple_of(h * half + i * 16, 16), 16)
            back, gains = norm_back(red.total(h, i), row_a[rr, :].astype(F32), gain1[...])
            gx[rr, :] = gmid[rr, :] + back
            gg1[...] += gains[:8] + gains[8:]
            return carry

        lax.fori_loop(0, half // 16, body, 0)
    red.finish()

    first_row = lax.broadcasted_iota(jnp.int32, (8, 128), 0) == 0
    for d in range(8 * n):
        g, zz = d % 8, d // 8
        lanes = slice(d // 2 * 128, d // 2 * 128 + 128)
        sv[g, zz, :, 0:128] = gg1[:, lanes]
        sv[g, zz, :, 128:256] = gg2[:, lanes]
        sv[g, zz, :, 256:384] = jnp.where(first_row, jnp.broadcast_to(table[d : d + 1, :], (8, 128)), 0.0)
    peers = [
        (ox * 4 + ok * 2 + oy)
        for ox in (me.x, 1 - me.x)
        for ok in (me.k, 1 - me.k)
        for oy in (me.y, 1 - me.y)
    ]
    sv_copies = [
        remote(sv.at[peers[i + 1]], sv_in.at[i], sv_send.at[i], sv_recv.at[i], dev)
        for i, dev in enumerate(group)
    ]
    for copy in sv_copies:
        copy.start()

    settle(2)
    for copy in sv_copies:
        copy.wait_recv()
    me_g = me.c * 2 + y
    total = sv[me_g]
    for i in range(7):
        total = total + sv_in[i]
    sv_z[0] = total
    z_copies = [
        remote(sv_z.at[0, lax.rem(z + s, n)], sv_z.at[s, 0], sz_send.at[s - 1], sz_recv.at[s - 1], others[s - 1])
        for s in range(1, n)
    ]
    for copy in z_copies:
        copy.start()
    settle(3)
    for copy in z_copies:
        copy.wait_recv()
    total = sv_z[0, z]
    for s in range(1, n):
        total = total + sv_z[s, 0]
    sums[...] = total
    for pair_of in swaps:
        for copy in pair_of:
            copy.wait()
    for copy in sv_copies + z_copies:
        copy.wait_send()
    for line in lines:
        line.finish()


def backward(n, length, heads, hid, h1, *arrays):
    cot = arrays[-3]
    rows, width = cot.shape
    tokens = 8 * rows
    h2 = hid - h1
    pair = 3 * 2 * DH
    shapes = [
        ((rows, width), BF),
        ((rows, width), F32),
        ((2, rows, 3 * h1), BF),
        ((2, rows, 3 * h2), BF),
        ((2, rows, heads + pair), BF),
        ((2, rows, pair), BF),
        ((8, 384), F32),
        ((8, rows, width), BF),
        ((n, 2, 1, rows, 3 * h1), BF),
        ((n, 2, 1, rows, 3 * h1), BF),
        ((n, 2, 1, rows, 3 * h2), BF),
        ((n, 2, 1, rows, 3 * h2), BF),
        ((n, 2, 1, rows, heads + pair), BF),
        ((n, 2, 1, rows, heads + pair), BF),
        ((n, 2, 1, rows, pair), BF),
        ((n, 2, 1, rows, pair), BF),
    ]
    scratch = [
        pltpu.VMEM((width, 2 * hid), BF),
        pltpu.VMEM((hid, width), BF),
        pltpu.VMEM((rows, width), BF),
        pltpu.VMEM((rows, width), BF),
        pltpu.VMEM((rows, width), BF),
        pltpu.VMEM((2, 8, rows, rows), BF),
        pltpu.VMEM((2, 8, rows, rows), BF),
        pltpu.VMEM((tokens, hid), BF),
        pltpu.VMEM((tokens, 2 * hid), BF),
        pltpu.VMEM((2 * n, rows, 3 * h1), BF),
        pltpu.VMEM((2 * n, rows, 3 * h2), BF),
        pltpu.VMEM((2, rows, 3 * max(h1, h2)), BF),
        pltpu.VMEM((rows, width), F32),
        pltpu.VMEM((rows, width), BF),
        pltpu.VMEM((width, 3 * heads), BF),
        pltpu.VMEM((2, TQ, length), BF),
        pltpu.VMEM((TQ, 2 * length), F32),
        pltpu.VMEM((DH, length), F32),
        pltpu.VMEM((DH, length), F32),
        pltpu.VMEM((heads // DH, 8, 2 * length), F32),
        pltpu.VMEM((8, width), F32),
        pltpu.VMEM((8, width), F32),
        pltpu.VMEM((8, n, 8, 384), F32),
        pltpu.VMEM((7, n, 8, 384), F32),
        pltpu.VMEM((n, n, 8, 384), F32),
        pltpu.SemaphoreType.REGULAR((3,)),
        DMA((21,)), DMA((2,)), DMA((2,)), DMA((4,)), DMA((4,)), DMA((4,)), DMA((7,)), DMA((7,)), DMA((n - 1,)), DMA((n - 1,)),
    ] + reduce_scratch(rows, width) + gather_sems() + [DMA((n, 2, 1))] * 16
    return pl.pallas_call(
        functools.partial(backward_kernel, n, length, heads, hid, h1),
        out_shape=[jax.ShapeDtypeStruct(s, d) for s, d in shapes],
        in_specs=[ANY] * 16 + [VM] * 4,
        out_specs=[VM, VM] + [ANY] * 4 + [VM] + [ANY] * 9,
        scratch_shapes=scratch,
        compiler_params=pltpu.CompilerParams(
            collective_id=1, has_side_effects=True, vmem_limit_bytes=64 << 20
        ),
        name="backward",
    )(*arrays)


def on_device(
    n, hidden, segment_ids, positions, attn_gain, w_query, w_key, w_value, w_attn_out,
    rel_table, ffn_gain, w_gate, w_up, w_down, cotangent,
):
    xin = hidden[0]
    cot = cotangent[0]
    length = segment_ids.shape[1]
    heads = w_query.shape[1] // 2
    hid = w_gate.shape[1] // 2
    share = attn_gain.shape[0]
    y = lax.axis_index("fsdp")
    h1 = 256
    h2 = hid - h1
    wqkv, wo, wg1, wd1, wg2, wd2, a1, qkv, o, p, mid, a2all, gall, m1, dgu1, gwf1, gain1, gain2 = forward(
        n, h1, w_query, w_key, w_value, w_attn_out, w_gate, w_up, w_down, cot, xin, segment_ids,
        attn_gain[None], ffn_gain[None], rel_table[None],
    )
    out, gx, fo1, fo2, bo, co, sums = backward(
        n, length, heads, hid, h1, wg1, wd1, wg2, wd2, m1, dgu1, gwf1, a2all, gall, p, a1, qkv, o, wqkv, wo,
        xin, mid, cot, gain1, gain2,
    )[:7]
    out, gx, g_q, g_k, g_v, g_o, g_gate, g_up, g_down = finish(h1, heads, out, gx, fo1, fo2, bo, co)
    line = jnp.sum(sums, axis=0)
    half_of = lambda v: jnp.where(y == 0, v[:share], v[128 - share :])
    return (
        out[None], gx[None], half_of(line[:128]), g_q, g_k, g_v, g_o, line[256 : 256 + H],
        half_of(line[128:256]), g_gate, g_up, g_down,
    )


def finish_kernel(h1, heads, out_in, gx_in, *refs):
    sources, (out, gx, g_q, g_k, g_v, g_o, g_gate, g_up, g_down) = refs[:4], refs[4:13]
    held = refs[13:19]
    fo1, fo2, bo, co = held[:4]
    sem = refs[19]
    sources = sources + (out_in, gx_in)
    loads = [pltpu.make_async_copy(src, dst, sem.at[i]) for i, (src, dst) in enumerate(zip(sources, held))]
    moves = [pltpu.make_async_copy(held[4 + i], dst, sem.at[4 + i]) for i, dst in enumerate((out, gx))]
    for copy in loads:
        copy.start()
    for copy in loads:
        copy.wait()
    for copy in moves:
        copy.start()
    h2 = fo2.shape[2] // 3
    hid = h1 + h2
    for yy in range(2):
        for part, ref in enumerate((g_q, g_k, g_v)):
            ref[:, yy * heads : yy * heads + 128] = bo[yy, :, heads + part * 128 : heads + part * 128 + 128].astype(F32)
            ref[:, yy * heads + 128 : yy * heads + 256] = co[yy, :, part * 128 : part * 128 + 128].astype(F32)
        g_o[yy * heads : (yy + 1) * heads, :] = bo[yy, :, 0:heads].astype(F32).T
        for part, ref in enumerate((g_gate, g_up)):
            ref[:, yy * hid : yy * hid + h1] = fo1[yy, :, part * h1 : (part + 1) * h1].astype(F32)
            ref[:, yy * hid + h1 : (yy + 1) * hid] = fo2[yy, :, part * h2 : (part + 1) * h2].astype(F32)
        g_down[yy * hid : yy * hid + h1, :] = fo1[yy, :, 2 * h1 : 3 * h1].astype(F32).T
        g_down[yy * hid + h1 : (yy + 1) * hid, :] = fo2[yy, :, 2 * h2 : 3 * h2].astype(F32).T
    for copy in moves:
        copy.wait()


def finish(h1, heads, out, gx, fo1, fo2, bo, co):
    rows = out.shape[0]
    hid = h1 + fo2.shape[2] // 3
    shapes = [(rows, 2 * heads)] * 3 + [(2 * heads, rows)] + [(rows, 2 * hid)] * 2 + [(2 * hid, rows)]
    return pl.pallas_call(
        functools.partial(finish_kernel, h1, heads),
        out_shape=[jax.ShapeDtypeStruct(out.shape, BF), jax.ShapeDtypeStruct(gx.shape, F32)]
        + [jax.ShapeDtypeStruct(s, F32) for s in shapes],
        in_specs=[ANY] * 6,
        out_specs=[ANY] * 2 + [VM] * 7,
        scratch_shapes=[pltpu.VMEM(part.shape, part.dtype) for part in (fo1, fo2, bo, co, out, gx)] + [DMA((6,))],
        compiler_params=pltpu.CompilerParams(vmem_limit_bytes=64 << 20),
        name="finish",
    )(out, gx, fo1, fo2, bo, co)


QB = 512


def rms_norm(values, gain):
    return values * lax.rsqrt(jnp.mean(values * values, axis=-1, keepdims=True) + EPSILON) * gain


def gelu_tanh(values):
    return (
        0.5
        * values
        * (1.0 + jnp.tanh(0.7978845608028654 * (values + 0.044715 * values * values * values)))
    )


def bucket_table(query_pos, key_pos):
    relative = key_pos[None, :] - query_pos[:, None]
    distance = jnp.abs(relative)
    log_bucket = 8 + sum(((distance >= threshold).astype(jnp.int32) for threshold in THRESHOLDS))
    bucket = jnp.where(distance < 8, distance, log_bucket)
    return bucket + 16 * (relative > 0).astype(jnp.int32)


def gather_attention(w_query, w_key, w_value, w_attn_out):
    return (
        lax.all_gather(w_query, ("dp", "fsdp"), axis=0, tiled=True),
        lax.all_gather(w_key, ("dp", "fsdp"), axis=0, tiled=True),
        lax.all_gather(w_value, ("dp", "fsdp"), axis=0, tiled=True),
        lax.all_gather(w_attn_out, ("dp", "fsdp"), axis=1, tiled=True),
    )


def gather_feedforward(w_gate, w_up, w_down):
    return (
        lax.all_gather(w_gate, ("dp", "fsdp"), axis=0, tiled=True),
        lax.all_gather(w_up, ("dp", "fsdp"), axis=0, tiled=True),
        lax.all_gather(w_down, ("dp", "fsdp"), axis=1, tiled=True),
    )


def block_masks(segment_row, position_row, start):
    query_pos = lax.dynamic_slice_in_dim(position_row, start, QB)
    query_seg = lax.dynamic_slice_in_dim(segment_row, start, QB)
    buckets = bucket_table(query_pos, position_row)
    one_hot = (buckets[None] == jnp.arange(NB, dtype=jnp.int32)[:, None, None]).astype(jnp.bfloat16)
    same_doc = query_seg[:, None] == segment_row[None, :]
    return (one_hot, same_doc)


def block_scores(query_block, key_rows, table_local, one_hot, same_doc):
    attention_scores = jnp.einsum(
        "ihd,jhd->hij", query_block, key_rows, preferred_element_type=jnp.float32
    )
    attention_scores = attention_scores + jnp.einsum(
        "bij,bh->hij", one_hot, table_local, preferred_element_type=jnp.float32
    )
    return jnp.where(same_doc[None], attention_scores, MASKED)


def layer_forward(tokens, small_set, attn_set, ffn_set, segment_row, position_row):
    attn_gain, ffn_gain, table_flat = small_set
    w_query, w_key, w_value, w_attn_out = attn_set
    w_gate, w_up, w_down = ffn_set
    heads_here = w_query.shape[1] // DH
    head_start = lax.axis_index("ctx") * heads_here
    table_local = lax.dynamic_slice_in_dim(table_flat.reshape(NB, H), head_start, heads_here, 1)
    normalized_rows, attn_back = jax.vjp(rms_norm, tokens, attn_gain.astype(jnp.float32))
    normed_rows = lax.all_gather(normalized_rows.astype(jnp.bfloat16), "ctx", axis=0, tiled=True)
    seq_len = normed_rows.shape[0]
    queries = (
        jnp.dot(normed_rows, w_query, preferred_element_type=jnp.float32)
        .astype(jnp.bfloat16)
        .reshape(seq_len, heads_here, DH)
    )
    key_rows = (
        jnp.dot(normed_rows, w_key, preferred_element_type=jnp.float32)
        .astype(jnp.bfloat16)
        .reshape(seq_len, heads_here, DH)
    )
    value_rows = (
        jnp.dot(normed_rows, w_value, preferred_element_type=jnp.float32)
        .astype(jnp.bfloat16)
        .reshape(seq_len, heads_here, DH)
    )
    starts = jnp.arange(seq_len // QB, dtype=jnp.int32) * QB

    def forward_block(start):
        one_hot, same_doc = block_masks(segment_row, position_row, start)
        query_block = lax.dynamic_slice_in_dim(queries, start, QB, 0)
        attention_scores = block_scores(query_block, key_rows, table_local, one_hot, same_doc)
        row_peak = jnp.max(attention_scores, axis=-1, keepdims=True)
        lifted = jnp.exp(attention_scores - row_peak)
        row_total = jnp.sum(lifted, axis=-1, keepdims=True)
        prob_low = (lifted / row_total).astype(jnp.bfloat16)
        attended_part = jnp.einsum(
            "hij,jhd->ihd", prob_low, value_rows, preferred_element_type=jnp.float32
        )
        return (attended_part, row_peak + jnp.log(row_total))

    attended, log_total = lax.map(forward_block, starts)
    attended_low = attended.reshape(seq_len, heads_here * DH).astype(jnp.bfloat16)
    attn_term = jnp.dot(attended_low, w_attn_out, preferred_element_type=jnp.float32)
    residual = tokens + lax.psum_scatter(attn_term, "ctx", scatter_dimension=0, tiled=True)
    normed_ffn, ffn_back = jax.vjp(rms_norm, residual, ffn_gain.astype(jnp.float32))
    ffn_rows = lax.all_gather(normed_ffn.astype(jnp.bfloat16), "ctx", axis=0, tiled=True)
    gate_value = jnp.dot(ffn_rows, w_gate, preferred_element_type=jnp.float32)
    up_value = jnp.dot(ffn_rows, w_up, preferred_element_type=jnp.float32)
    gelu_gate, gelu_back = jax.vjp(gelu_tanh, gate_value)
    ffn_hidden = (gelu_gate * up_value).astype(jnp.bfloat16)
    down_term = jnp.dot(ffn_hidden, w_down, preferred_element_type=jnp.float32)
    result = residual + lax.psum_scatter(
        down_term.astype(jnp.bfloat16), "ctx", scatter_dimension=0, tiled=True
    ).astype(jnp.float32)
    stored = (
        attn_back,
        normed_rows,
        queries,
        key_rows,
        value_rows,
        table_local,
        head_start,
        starts,
        log_total,
        attended_low,
        ffn_back,
        ffn_rows,
        up_value,
        gelu_gate,
        gelu_back,
        ffn_hidden,
    )
    return (result, stored)


def plain_on_device(
    hidden,
    segment_ids,
    positions,
    attn_gain,
    w_query,
    w_key,
    w_value,
    w_attn_out,
    rel_table,
    ffn_gain,
    w_gate,
    w_up,
    w_down,
    cotangent,
):
    tokens = hidden[0].astype(jnp.float32)
    segment_row = segment_ids[0]
    position_row = positions[0]
    small_set = (
        lax.all_gather(attn_gain, ("dp", "ctx", "fsdp"), axis=0, tiled=True),
        lax.all_gather(ffn_gain, ("dp", "ctx", "fsdp"), axis=0, tiled=True),
        lax.all_gather(rel_table, ("dp", "ctx", "fsdp"), axis=0, tiled=True),
    )
    attn_set = gather_attention(w_query, w_key, w_value, w_attn_out)
    ffn_set = gather_feedforward(w_gate, w_up, w_down)
    result, unused_stored = layer_forward(
        tokens, small_set, attn_set, ffn_set, segment_row, position_row
    )
    back_attn = gather_attention(w_query, w_key, w_value, w_attn_out)
    back_ffn = gather_feedforward(w_gate, w_up, w_down)
    recomputed, stored = layer_forward(
        tokens, small_set, back_attn, back_ffn, segment_row, position_row
    )
    (
        attn_back,
        normed_rows,
        queries,
        key_rows,
        value_rows,
        table_local,
        head_start,
        starts,
        log_total,
        attended_low,
        ffn_back,
        ffn_rows,
        up_value,
        gelu_gate,
        gelu_back,
        ffn_hidden,
    ) = stored
    full_query, full_key, full_value, full_attn_out = back_attn
    full_gate, full_up, full_down = back_ffn
    seq_len = normed_rows.shape[0]
    heads_here = queries.shape[1]
    grad_rows = lax.all_gather(cotangent[0], "ctx", axis=0, tiled=True)
    grad_w_down = jnp.einsum("tf,td->fd", ffn_hidden, grad_rows, preferred_element_type=jnp.float32)
    grad_hidden_ffn = jnp.einsum(
        "td,fd->tf", grad_rows, full_down, preferred_element_type=jnp.float32
    )
    up_value_gradient = (grad_hidden_ffn * gelu_gate).astype(jnp.bfloat16)
    grad_gate_value = gelu_back(grad_hidden_ffn * up_value)[0].astype(jnp.bfloat16)
    grad_w_gate = jnp.einsum(
        "td,tf->df", ffn_rows, grad_gate_value, preferred_element_type=jnp.float32
    )
    grad_w_up = jnp.einsum(
        "td,tf->df", ffn_rows, up_value_gradient, preferred_element_type=jnp.float32
    )
    ffn_normed_term = jnp.einsum(
        "tf,df->td", grad_gate_value, full_gate, preferred_element_type=jnp.float32
    )
    ffn_normed_term = ffn_normed_term + jnp.einsum(
        "tf,df->td", up_value_gradient, full_up, preferred_element_type=jnp.float32
    )
    grad_normed_ffn = lax.psum_scatter(ffn_normed_term, "ctx", scatter_dimension=0, tiled=True)
    grad_residual_norm, grad_ffn_gain = ffn_back(grad_normed_ffn)
    grad_residual = cotangent[0].astype(jnp.float32) + grad_residual_norm
    ffn_sums = (
        lax.psum_scatter(
            grad_w_gate.astype(jnp.bfloat16), ("dp", "fsdp"), scatter_dimension=0, tiled=True
        ).astype(jnp.float32),
        lax.psum_scatter(
            grad_w_up.astype(jnp.bfloat16), ("dp", "fsdp"), scatter_dimension=0, tiled=True
        ).astype(jnp.float32),
        lax.psum_scatter(
            grad_w_down.astype(jnp.bfloat16), ("dp", "fsdp"), scatter_dimension=1, tiled=True
        ).astype(jnp.float32),
    )
    branch_rows = lax.all_gather(grad_residual.astype(jnp.bfloat16), "ctx", axis=0, tiled=True)
    grad_w_attn_out = jnp.einsum(
        "ti,td->id", attended_low, branch_rows, preferred_element_type=jnp.float32
    )
    grad_attended = jnp.einsum(
        "td,id->ti", branch_rows, full_attn_out, preferred_element_type=jnp.float32
    )
    grad_attended = grad_attended.astype(jnp.bfloat16).reshape(seq_len, heads_here, DH)

    def backward_block(operands):
        start, block_total = operands
        one_hot, same_doc = block_masks(segment_row, position_row, start)
        query_block = lax.dynamic_slice_in_dim(queries, start, QB, 0)
        grad_part = lax.dynamic_slice_in_dim(grad_attended, start, QB, 0)
        attention_scores = block_scores(query_block, key_rows, table_local, one_hot, same_doc)
        weights = jnp.exp(attention_scores - block_total)
        prob_low = weights.astype(jnp.bfloat16)
        grad_probs = jnp.einsum(
            "ihd,jhd->hij", grad_part, value_rows, preferred_element_type=jnp.float32
        )
        centred = grad_probs - jnp.sum(weights * grad_probs, axis=-1, keepdims=True)
        grad_scores = (weights * centred).astype(jnp.bfloat16)
        grad_query_part = jnp.einsum(
            "hij,jhd->ihd", grad_scores, key_rows, preferred_element_type=jnp.float32
        )
        grad_key_part = jnp.einsum(
            "hij,ihd->jhd", grad_scores, query_block, preferred_element_type=jnp.float32
        )
        grad_value_part = jnp.einsum(
            "hij,ihd->jhd", prob_low, grad_part, preferred_element_type=jnp.float32
        )
        grad_bias_part = jnp.einsum(
            "hij,bij->bh", grad_scores, one_hot, preferred_element_type=jnp.float32
        )
        return (grad_query_part, grad_key_part, grad_value_part, grad_bias_part)

    query_blocks, key_blocks, value_blocks, bias_blocks = lax.map(
        backward_block, (starts, log_total)
    )
    grad_queries_low = query_blocks.reshape(seq_len, heads_here * DH).astype(jnp.bfloat16)
    grad_keys_low = (
        jnp.sum(key_blocks, axis=0).reshape(seq_len, heads_here * DH).astype(jnp.bfloat16)
    )
    grad_values_low = (
        jnp.sum(value_blocks, axis=0).reshape(seq_len, heads_here * DH).astype(jnp.bfloat16)
    )
    grad_w_query = jnp.einsum(
        "td,te->de", normed_rows, grad_queries_low, preferred_element_type=jnp.float32
    )
    grad_w_key = jnp.einsum(
        "td,te->de", normed_rows, grad_keys_low, preferred_element_type=jnp.float32
    )
    grad_w_value = jnp.einsum(
        "td,te->de", normed_rows, grad_values_low, preferred_element_type=jnp.float32
    )
    normed_term = jnp.einsum(
        "te,de->td", grad_queries_low, full_query, preferred_element_type=jnp.float32
    )
    normed_term = normed_term + jnp.einsum(
        "te,de->td", grad_keys_low, full_key, preferred_element_type=jnp.float32
    )
    normed_term = normed_term + jnp.einsum(
        "te,de->td", grad_values_low, full_value, preferred_element_type=jnp.float32
    )
    grad_normed = lax.psum_scatter(
        normed_term.astype(jnp.bfloat16), "ctx", scatter_dimension=0, tiled=True
    ).astype(jnp.float32)
    token_norm_gradient, grad_attn_gain = attn_back(grad_normed)
    grad_tokens = grad_residual + token_norm_gradient
    attn_sums = (
        lax.psum_scatter(
            grad_w_query.astype(jnp.bfloat16), ("dp", "fsdp"), scatter_dimension=0, tiled=True
        ).astype(jnp.float32),
        lax.psum_scatter(
            grad_w_key.astype(jnp.bfloat16), ("dp", "fsdp"), scatter_dimension=0, tiled=True
        ).astype(jnp.float32),
        lax.psum_scatter(
            grad_w_value.astype(jnp.bfloat16), ("dp", "fsdp"), scatter_dimension=0, tiled=True
        ).astype(jnp.float32),
        lax.psum_scatter(
            grad_w_attn_out.astype(jnp.bfloat16), ("dp", "fsdp"), scatter_dimension=1, tiled=True
        ).astype(jnp.float32),
    )
    bias_sum = jnp.sum(bias_blocks, axis=0)
    table_term = lax.dynamic_update_slice(
        jnp.zeros((NB, H), jnp.float32), bias_sum, (jnp.int32(0), head_start)
    )
    small_sums = (
        lax.psum_scatter(grad_attn_gain, ("dp", "ctx", "fsdp"), scatter_dimension=0, tiled=True),
        lax.psum_scatter(grad_ffn_gain, ("dp", "ctx", "fsdp"), scatter_dimension=0, tiled=True),
        lax.psum_scatter(
            table_term.reshape(NB * H), ("dp", "ctx", "fsdp"), scatter_dimension=0, tiled=True
        ),
    )
    return (
        result[None].astype(jnp.bfloat16),
        grad_tokens[None],
        small_sums[0],
        attn_sums[0],
        attn_sums[1],
        attn_sums[2],
        attn_sums[3],
        small_sums[2],
        small_sums[1],
        ffn_sums[0],
        ffn_sums[1],
        ffn_sums[2],
    )


def plain_solution(mesh):
    in_specs = (
        P(("dp", "fsdp"), "ctx", None),
        P(("dp", "fsdp"), None),
        P(("dp", "fsdp"), None),
        P(("dp", "ctx", "fsdp")),
        P(("dp", "fsdp"), "ctx"),
        P(("dp", "fsdp"), "ctx"),
        P(("dp", "fsdp"), "ctx"),
        P("ctx", ("dp", "fsdp")),
        P(("dp", "ctx", "fsdp")),
        P(("dp", "ctx", "fsdp")),
        P(("dp", "fsdp"), "ctx"),
        P(("dp", "fsdp"), "ctx"),
        P("ctx", ("dp", "fsdp")),
        P(("dp", "fsdp"), "ctx", None),
    )
    out_specs = (
        P(("dp", "fsdp"), "ctx", None),
        P(("dp", "fsdp"), "ctx", None),
        P(("dp", "ctx", "fsdp")),
        P(("dp", "fsdp"), "ctx"),
        P(("dp", "fsdp"), "ctx"),
        P(("dp", "fsdp"), "ctx"),
        P("ctx", ("dp", "fsdp")),
        P(("dp", "ctx", "fsdp")),
        P(("dp", "ctx", "fsdp")),
        P(("dp", "fsdp"), "ctx"),
        P(("dp", "fsdp"), "ctx"),
        P("ctx", ("dp", "fsdp")),
    )
    return jax.shard_map(
        plain_on_device, mesh=mesh, in_specs=in_specs, out_specs=out_specs, check_vma=False
    )


def solution(mesh):
    if 2048 // (mesh.shape["dp"] * mesh.shape["fsdp"]) % 128 or mesh.shape["fsdp"] != 2 or mesh.shape["ctx"] != 4:
        return plain_solution(mesh)
    tokens = P(("dp", "fsdp"), "ctx", None)
    line = P(("dp", "fsdp"), None)
    every = P(("dp", "ctx", "fsdp"))
    into = P(("dp", "fsdp"), "ctx")
    back = P("ctx", ("dp", "fsdp"))
    return jax.shard_map(
        functools.partial(on_device, mesh.shape["dp"]),
        mesh=mesh,
        in_specs=(tokens, line, line, every, into, into, into, back, every, every, into, into, back, tokens),
        out_specs=(tokens, tokens, every, into, into, into, back, every, every, into, into, back),
        check_vma=False,
    )
```

```python
import functools

import jax
import jax.numpy as jnp
from jax import lax
from jax.experimental import pallas as pl
from jax.experimental.pallas import tpu as pltpu
from jax.sharding import PartitionSpec as P

H = 32
DH = 64
NB = 32
EPSILON = 1e-06
THRESHOLDS = (12, 16, 23, 32, 46, 64, 91)
MASKED = -1e30
BF = jnp.bfloat16
F32 = jnp.float32
ANY = pl.BlockSpec(memory_space=pl.ANY)
VM = pl.BlockSpec(memory_space=pltpu.VMEM)
MESH = pl.DeviceIdType.MESH
DMA = pltpu.SemaphoreType.DMA


class Place:
    def __init__(self):
        self.z = lax.axis_index("dp")
        self.c = lax.axis_index("ctx")
        self.y = lax.axis_index("fsdp")
        self.x = self.c // 2
        self.k = self.c % 2

    def device(self, z=None, x=None, k=None, y=None):
        z = self.z if z is None else z
        x = self.x if x is None else x
        k = self.k if k is None else k
        y = self.y if y is None else y
        return {"dp": z, "ctx": x * 2 + k, "fsdp": y}

    def x_peer(self):
        return self.device(x=1 - self.x)

    def y_peer(self):
        return self.device(y=1 - self.y)

    def core_peer(self):
        return self.device(k=1 - self.k)


def block_of(x, k, y):
    return y * 4 + x * 2 + k


def remote(src, dst, send_sem, recv_sem, device):
    return pltpu.make_async_remote_copy(
        src_ref=src,
        dst_ref=dst,
        send_sem=send_sem,
        recv_sem=recv_sem,
        device_id=device,
        device_id_type=MESH,
    )


def greet(devices):
    barrier = pltpu.get_barrier_semaphore()
    for device in devices:
        pl.semaphore_signal(barrier, inc=1, device_id=device, device_id_type=MESH)
    pl.semaphore_wait(barrier, len(devices))


class ActGather:
    def __init__(self, me, own, out, send, recv, local, cut=None):
        self.me, self.own, self.out = me, own, out
        self.send, self.recv, self.local = send, recv, local
        rows = own.shape[0]
        cut = cut or rows // 2
        self.halves = (pl.ds(0, cut), pl.ds(cut, rows - cut))

    def part(self, ref, block, h):
        return ref.at[block, self.halves[h]]

    def copy(self, i):
        me = self.me
        x, k, y = me.x, me.k, me.y
        own = block_of(x, k, y)
        if i == 0:
            src, dst, dev = self.own.at[self.halves[0]], self.part(self.out, own, 0), me.x_peer()
        elif i == 1:
            src, dst, dev = self.own.at[self.halves[1]], self.part(self.out, own, 1), me.y_peer()
        elif i == 2:
            src, dst, dev = self.own.at[self.halves[0]], self.part(self.out, own, 0), me.y_peer()
        elif i == 3:
            b = block_of(1 - x, k, y)
            src, dst, dev = self.part(self.out, b, 0), self.part(self.out, b, 0), me.y_peer()
        elif i == 4:
            src, dst, dev = self.own.at[self.halves[1]], self.part(self.out, own, 1), me.x_peer()
        elif i == 5:
            b = block_of(x, k, 1 - y)
            src, dst, dev = self.part(self.out, b, 1), self.part(self.out, b, 1), me.x_peer()
        elif i == 6:
            src, dst, dev = self.own, self.out.at[own], me.core_peer()
        else:
            px, py, h = ((1, 0, 0), (0, 1, 1), (0, 1, 0), (1, 1, 0), (1, 0, 1), (1, 1, 1))[i - 7]
            b = block_of(1 - x if px else x, k, 1 - y if py else y)
            src, dst, dev = self.part(self.out, b, h), self.part(self.out, b, h), me.core_peer()
        return remote(src, dst, self.send.at[i], self.recv.at[i], dev)

    def start_x(self):
        for i in (0, 4, 6):
            self.copy(i).start()
        own = block_of(self.me.x, self.me.k, self.me.y)
        pltpu.make_async_copy(self.own, self.out.at[own], self.local).start()

    def start_y(self):
        for i in (1, 2):
            self.copy(i).start()

    def start(self):
        self.start_x()
        self.start_y()

    def onward(self, *steps):
        for i, after in steps:
            self.copy(i).wait_recv()
            if after:
                self.copy(after).start()
            self.copy(i + 7).start()

    def forward(self):
        self.onward((0, 3), (1, 5))

    def forward_core(self):
        self.onward((2, 0), (4, 0), (3, 0), (5, 0))

    def land(self, *pieces):
        for i in pieces:
            self.copy(i).wait_recv()

    def placed(self):
        own = block_of(self.me.x, self.me.k, self.me.y)
        pltpu.make_async_copy(self.own, self.out.at[own], self.local).wait()

    def sent(self):
        for i in range(13):
            self.copy(i).wait_send()

    def finish(self):
        self.land(*range(6, 13))
        self.placed()
        self.sent()


def gather_sems():
    return [DMA((13,)), DMA((13,)), DMA]


class ActReduce:
    def __init__(self, me, peer_out, core_in, mine, a_y, b_x, a_x, b_y, send, recv):
        self.me, self.peer_out, self.core_in, self.mine = me, peer_out, core_in, mine
        self.a_y, self.b_x, self.a_x, self.b_y = a_y, b_x, a_x, b_y
        self.send, self.recv = send, recv
        self.half = mine.shape[1] // 2

    def place(self, j):
        x, y = self.me.x, self.me.y
        return jnp.where(j % 2 == 0, 1 - x, x), jnp.where(j < 2, 1 - y, y)

    def core_copy(self, j):
        return remote(
            self.peer_out.at[j % 2], self.core_in.at[j], self.send.at[j], self.recv.at[j], self.me.core_peer()
        )

    def rows(self, h):
        return pl.ds(h * self.half, self.half)

    def add(self, slot, h, extra=None):
        def body(i, carry):
            r = pl.ds(pl.multiple_of(h * self.half + i * 16, 16), 16)
            total = self.mine[slot, r, :].astype(F32) + self.core_in[slot, r, :].astype(F32)
            if extra is not None:
                q = pl.ds(pl.multiple_of(i * 16, 16), 16)
                total = total + extra[0, q, :].astype(F32)
            self.mine[slot, r, :] = total.astype(BF)
            return carry

        lax.fori_loop(0, self.half // 16, body, 0)

    def copy(self, name):
        xp, yp = self.me.x_peer(), self.me.y_peer()
        slot, h, dst, i, dev = {
            "ay0": (0, 0, self.a_y.at[0], 4, yp),
            "ay1": (1, 0, self.a_y.at[1], 5, yp),
            "bx0": (0, 1, self.b_x.at[0], 6, xp),
            "bx1": (2, 1, self.b_x.at[1], 7, xp),
            "ax": (2, 0, self.a_x, 8, xp),
            "by": (1, 1, self.b_y, 9, yp),
        }[name]
        return remote(self.mine.at[slot, self.rows(h)], dst, self.send.at[i], self.recv.at[i], dev)

    def first_sends(self, j):
        for name in (("ay0", "bx0"), ("ay1",), ("bx1",))[j]:
            self.copy(name).start()

    def loop(self, make, send=True, first=0, last=4, hooks=()):
        def ready(j):
            self.core_copy(j).wait_recv()
            if j < 2:
                self.add(j, 0)
            if j != 1:
                self.add(j, 1)
            if send:
                self.first_sends(j)

        def body(j, carry):
            ox, oy = self.place(j)

            @pl.when(j >= 2)
            def _():
                self.core_copy(j - 2).wait_send()

            self.peer_out[j % 2] = make(block_of(ox, 1 - self.me.k, oy), 2 * j)
            self.core_copy(j).start()
            for i in range(3):

                @pl.when(j == i + 1)
                def _():
                    ready(i)

            self.mine[j] = make(block_of(ox, self.me.k, oy), 2 * j + 1)

            for i, hook in hooks:

                @pl.when(j == i)
                def _():
                    hook()

            return carry

        lax.fori_loop(first, last, body, 0)

    def second(self):
        self.copy("ay0").wait_recv()
        self.add(2, 0, self.a_y)
        self.copy("ax").start()
        self.copy("bx0").wait_recv()
        self.add(1, 1, self.b_x)
        self.copy("by").start()

    def arrive(self):
        self.core_copy(3).wait_recv()
        for name in ("ay1", "bx1", "ax", "by"):
            self.copy(name).wait_recv()

    def total(self, h, i):
        r = pl.ds(pl.multiple_of(h * self.half + i * 16, 16), 16)
        q = pl.ds(pl.multiple_of(i * 16, 16), 16)
        total = self.mine[3, r, :].astype(F32) + self.core_in[3, r, :].astype(F32)
        if h == 0:
            return total + self.a_y[1, q, :].astype(F32) + self.a_x[q, :].astype(F32)
        return total + self.b_x[1, q, :].astype(F32) + self.b_y[q, :].astype(F32)

    def finish(self):
        for j in (2, 3):
            self.core_copy(j).wait_send()
        for name in ("ay0", "ay1", "bx0", "bx1", "ax", "by"):
            self.copy(name).wait_send()


def reduce_scratch(rows, width):
    half = rows // 2
    return [
        pltpu.VMEM((2, rows, width), BF),
        pltpu.VMEM((4, rows, width), BF),
        pltpu.VMEM((4, rows, width), BF),
        pltpu.VMEM((2, half, width), BF),
        pltpu.VMEM((2, half, width), BF),
        pltpu.VMEM((half, width), BF),
        pltpu.VMEM((half, width), BF),
        DMA((10,)),
        DMA((10,)),
    ]


TQ = 256


def softmax_tile(q, k, v, bias, same):
    s = lax.dot_general(q, k, (((1,), (1,)), ((), ())), preferred_element_type=F32) + bias
    s = jnp.where(same, s, MASKED)
    e = jnp.exp(s - jnp.max(s, axis=-1, keepdims=True))
    pb = (e * (1.0 / jnp.sum(e, axis=-1, keepdims=True))).astype(BF)
    return pb, jnp.dot(pb, v, preferred_element_type=F32).astype(BF)


class Line:
    def __init__(self, me, n, views, send_r, send_l, recv):
        self.me, self.n, self.views = me, n, views
        self.send_r, self.send_l, self.recv = send_r, send_l, recv

    def copies(self, t, yy, right):
        me = self.me
        dev = me.device(z=me.z + 1 if right else me.z - 1)
        sem = self.send_r if right else self.send_l
        return [
            remote(view, view, sem.at[t, yy, i], self.recv.at[t, yy, i], dev)
            for i, view in enumerate(self.views(t, yy))
        ]

    def send(self, t, yy, keep, start):
        for right in (True, False):
            go = (self.me.z + 1 <= self.n - 1) if right else (self.me.z >= 1)
            if keep[right] is not None:
                go = go & keep[right]

            @pl.when(go)
            def _():
                for copy in self.copies(t, yy, right):
                    if start:
                        copy.start()
                    else:
                        copy.wait_send()

    def own(self, yy):
        self.send(self.me.z, yy, {True: None, False: None}, True)

    def came(self, s):
        z, n = self.me.z, self.n
        return (
            (True, z - s, z - s >= 0, z + 1 <= n - 1),
            (False, z + s, z + s <= n - 1, z >= 1),
        )

    def pump(self, s, yy):
        for right, t, here, on in self.came(s):

            @pl.when(here & on)
            def _():
                for copy in self.copies(t, yy, right):
                    copy.wait_recv()
                    copy.start()

    def land(self, yys):
        for s in range(1, self.n):
            for yy in yys:
                for right, t, here, on in self.came(s):

                    @pl.when(here & jnp.logical_not(on))
                    def _():
                        for copy in self.copies(t, yy, right):
                            copy.wait_recv()

    def finish(self):
        for yy in range(2):
            self.send(self.me.z, yy, {True: None, False: None}, False)
            for s in range(1, self.n):
                for right, t, here, on in self.came(s):

                    @pl.when(here & on)
                    def _():
                        for copy in self.copies(t, yy, right):
                            copy.wait_send()


def line_sems(n, parts):
    return [DMA((n, 2, parts))] * 3


def forward_kernel(
    n, length, wq, wk, wv, wo, wg, wu, wd, cot, xin, seg_row, gain_a, gain_f, table_row,
    wqkv, wof, wg1, wd1, wg2, wd2, a1, qkv, o, p, mid, a2all, gall, m1, dgu1, gwf1, gain1, gain2,
    st_in, st_o, st_1, st_d1, st_2, st_d2, small, seg, smalls, segs, segt, xv, wqkv_v, wo_v, qkv_v, o_v, toep, pbuf, a2, wg1_v, wd1_v, gw_v, acc,
    y_send, y_recv, y_local, s_send, s_recv, s2_send, s2_recv, s_local, c_local, p_sem, f_sem,
    *rest,
):
    red_scratch, f1_sems, f2_sems, in_sems, wo_sems = rest[0:9], rest[9:12], rest[12:15], rest[15:18], rest[18:21]
    x_sems, g_sems, a_sems = rest[21:24], rest[24:27], rest[27:30]
    me = Place()
    z, y = me.z, me.y
    rows, width = xin.shape
    piece_rows = wq.shape[0]
    heads = wq.shape[1] // 2
    hid = wg.shape[1] // 2
    h1 = wd1.shape[0]
    h2 = hid - h1
    group = [
        me.device(x=ox, k=ok, y=oy)
        for ox in (me.x, 1 - me.x)
        for ok in (me.k, 1 - me.k)
        for oy in (me.y, 1 - me.y)
    ][1:]
    others = [me.device(z=lax.rem(z + s, n)) for s in range(1, n)]
    greet(group + others)
    small[...] = jnp.zeros_like(small)
    share = gain_a.shape[1]
    for yy in range(2):

        @pl.when(y == yy)
        def _():
            for i, ref in enumerate((gain_a, gain_f)):
                at = i * 128 + yy * share
                small[:, at : at + share] = jnp.broadcast_to(ref[...].astype(F32), (8, share))

    small[:, 256 : 256 + table_row.shape[1]] = jnp.broadcast_to(table_row[...].astype(F32), (8, table_row.shape[1]))
    seg[...] = jnp.broadcast_to(seg_row[...], seg.shape)

    def piece(t, yy):
        return pl.ds(pl.multiple_of((t * 2 + yy) * piece_rows, piece_rows), piece_rows)

    row = piece(z, y)

    def y_copies(yh):
        col = pl.ds(pl.multiple_of(yh * heads, heads), heads)
        at1 = pl.ds(pl.multiple_of(yh * hid, 128), h1)
        at2 = pl.ds(pl.multiple_of(yh * hid + h1, 128), h2)
        return [
            (wq.at[:, col], wqkv.at[row, pl.ds(0, heads)]),
            (wk.at[:, col], wqkv.at[row, pl.ds(heads, heads)]),
            (wv.at[:, col], wqkv.at[row, pl.ds(2 * heads, heads)]),
            (wo.at[col, :], wof.at[:, row]),
            (wg.at[:, at1], wg1.at[row, pl.ds(0, h1)]),
            (wu.at[:, at1], wg1.at[row, pl.ds(h1, h1)]),
            (wd.at[at1, :], wd1.at[:, row]),
            (wg.at[:, at2], wg2.at[row, pl.ds(0, h2)]),
            (wu.at[:, at2], wg2.at[row, pl.ds(h2, h2)]),
            (wd.at[at2, :], wd2.at[:, row]),
        ]

    sends = [
        remote(src, dst, y_send.at[i], y_recv.at[i], me.y_peer())
        for i, (src, dst) in enumerate(y_copies(1 - y))
    ]
    staged = [
        st_in.at[:, pl.ds(0, heads)],
        st_in.at[:, pl.ds(heads, heads)],
        st_in.at[:, pl.ds(2 * heads, heads)],
        st_o,
        st_1.at[:, pl.ds(0, h1)],
        st_1.at[:, pl.ds(h1, h1)],
        st_d1,
        st_2.at[:, pl.ds(0, h2)],
        st_2.at[:, pl.ds(h2, h2)],
        st_d2,
    ]
    takes = [
        pltpu.make_async_copy(src, mid_ref, y_local.at[i])
        for i, ((src, dst), mid_ref) in enumerate(zip(y_copies(y), staged))
    ]
    keeps = [
        pltpu.make_async_copy(mid_ref, dst, y_local.at[i])
        for i, ((src, dst), mid_ref) in enumerate(zip(y_copies(y), staged))
    ]
    me_small = z * 8 + me.c * 2 + y
    small_local = pltpu.make_async_copy(small, smalls.at[me_small], s_local.at[0])
    seg_local = pltpu.make_async_copy(seg, segs.at[y], s_local.at[1])
    small_sends = [
        remote(small, smalls.at[me_small], s_send.at[i], s_recv.at[i], dev) for i, dev in enumerate(group)
    ]
    seg_send = remote(seg, segs.at[y], s_send.at[7], s_recv.at[7], me.y_peer())
    attn = Line(me, n, lambda t, yy: (wqkv.at[piece(t, yy), :],), *in_sems)
    attn_o = Line(me, n, lambda t, yy: (wof.at[:, piece(t, yy)],), *wo_sems)
    f1 = Line(me, n, lambda t, yy: (wg1.at[piece(t, yy), :], wd1.at[:, piece(t, yy)]), *f1_sems)
    f2 = Line(me, n, lambda t, yy: (wg2.at[piece(t, yy), :], wd2.at[:, piece(t, yy)]), *f2_sems)
    xact = ActGather(me, xin, xv, *x_sems, cut=5 * rows // 16)
    gact = ActGather(me, cot, gall, *g_sems, cut=rows // 4)

    for i in range(4):
        takes[i].start()
        sends[i].start()
    small_local.start()
    seg_local.start()
    for copy in small_sends:
        copy.start()
    seg_send.start()
    xact.start_x()
    for i in range(4, 10):
        takes[i].start()
    for i in range(10):
        takes[i].wait()
        keeps[i].start()
    for i in range(4):
        keeps[i].wait()
    attn.own(y)
    for i in range(4):
        sends[i].wait_recv()
    attn.own(1 - y)
    xact.start_y()
    small_local.wait()
    for copy in small_sends:
        copy.wait_recv()
    block8 = smalls.at[pl.ds(pl.multiple_of(z * 8, 8), 8)]
    small_z = [remote(block8, block8, s2_send.at[i], s2_recv.at[i], dev) for i, dev in enumerate(others)]
    for copy in small_z:
        copy.start()
    xact.onward((0, 3))
    attn.pump(1, y)
    attn.pump(1, 1 - y)
    xact.onward((1, 5))
    for i in range(4, 10):
        sends[i].start()
    gact.start()

    for copy in small_z:
        copy.wait_recv()
    for j in range(4 * n):
        gain1[:, 128 * j : 128 * j + 128] = (smalls[2 * j, :, 0:128] + smalls[2 * j + 1, :, 0:128])[0:1]
        gain2[:, 128 * j : 128 * j + 128] = (smalls[2 * j, :, 128:256] + smalls[2 * j + 1, :, 128:256])[0:1]
    seg_local.wait()
    seg_send.wait_recv()
    for s in range(2):
        wide = jnp.concatenate([segs[s]] * 16, axis=0).astype(F32)
        segt[s] = wide.T
    attn.pump(2, y)
    xact.onward((2, 0), (4, 0))
    attn.pump(2, 1 - y)
    attn_o.own(y)
    attn_o.own(1 - y)
    for i in range(4, 7):
        keeps[i].wait()
    f1.own(y)
    offset = lax.broadcasted_iota(jnp.int32, (NB, 2 * length), 1) - length
    far = jnp.abs(offset)
    bucket = jnp.where(far < 8, far, 8 + sum((far >= t).astype(jnp.int32) for t in THRESHOLDS))
    bucket = bucket + 16 * (offset > 0).astype(jnp.int32)
    own_bucket = bucket == lax.broadcasted_iota(jnp.int32, (NB, 2 * length), 0)
    table = smalls[:, 0, 256:384]
    lane = lax.broadcasted_iota(jnp.int32, (NB, 128), 1)
    local_heads = heads // DH
    for lh in range(local_heads):
        head = (me.c * 2 + y) * local_heads + lh
        value = jnp.sum(jnp.where(lane == head, table, 0.0), axis=1, keepdims=True)
        fvec = jnp.sum(jnp.where(own_bucket, value, 0.0), axis=0, keepdims=True)
        toep[lh] = pltpu.roll(jnp.broadcast_to(fvec, (TQ, 2 * length)), 0, 1, stride=1, stride_axis=0)
    xact.onward((3, 0), (5, 0))
    xact.finish()

    def norm_rows(i, carry):
        r = pl.ds(pl.multiple_of(lax.rem(i, rows // 32) * 32, 32), 32)
        b = i // (rows // 32)
        xf = xv[b, r, :].astype(F32)
        inv = lax.rsqrt(jnp.mean(xf * xf, axis=-1, keepdims=True) + EPSILON)
        xv[b, r, :] = (xf * inv * gain1[...]).astype(BF)
        return carry

    lax.fori_loop(0, 4 * rows // 32, norm_rows, 0)
    for i in range(4, 7):
        sends[i].wait_recv()
    f1.own(1 - y)
    attn_o.pump(1, y)
    attn_o.pump(1, 1 - y)
    lax.fori_loop(4 * rows // 32, 8 * rows // 32, norm_rows, 0)
    a1_out = pltpu.make_async_copy(xv, a1, c_local.at[0])
    a1_out.start()
    attn_o.pump(2, y)
    attn_o.pump(2, 1 - y)
    attn.land((y, 1 - y))
    w_in = pltpu.make_async_copy(wqkv, wqkv_v, c_local.at[1])
    w_in.start()
    w_in.wait()

    def project(b, carry):
        r = pl.ds(pl.multiple_of(b * rows, rows), rows)
        qkv_v[r, :] = jnp.dot(xv[b], wqkv_v[...], preferred_element_type=F32).astype(BF)
        return carry

    lax.fori_loop(0, 8, project, 0)
    qkv_out = pltpu.make_async_copy(qkv_v, qkv, c_local.at[3])
    qkv_out.start()
    f1.pump(1, y)
    tiles = length // TQ

    def p_copy(slot, head, t):
        return pltpu.make_async_copy(
            pbuf.at[slot], p.at[head, pl.ds(t * TQ, TQ)], p_sem.at[slot]
        )

    def sequence(s, fresh, between):
        base = pl.multiple_of(s * length, length)
        seq = pl.ds(base, length)

        def head_pair(hp, carry):
            def lanes(part):
                return pl.ds(pl.multiple_of(part * heads + hp * 2 * DH, 128), 2 * DH)

            k2 = qkv_v[seq, lanes(1)]
            v2 = qkv_v[seq, lanes(2)]
            for t in range(tiles):
                r = pl.ds(pl.multiple_of(base + t * TQ, TQ), TQ)
                q2 = qkv_v[r, lanes(0)]
                same = segt[s, t * TQ : (t + 1) * TQ, 0:1] == segs[s, 0:1, :].astype(F32)
                outs = []
                for h in range(2):
                    cut = slice(h * DH, (h + 1) * DH)
                    pb, ot = softmax_tile(
                        q2[:, cut], k2[:, cut], v2[:, cut],
                        toep[hp * 2 + h, :, length - t * TQ : 2 * length - t * TQ], same,
                    )
                    head = s * local_heads + hp * 2 + h
                    if fresh and t == 0:

                        @pl.when(hp > 0)
                        def _():
                            p_copy(h, head, t).wait()
                    else:
                        p_copy(h, head, t).wait()
                    pbuf[h] = pb
                    p_copy(h, head, t).start()
                    outs.append(ot)
                o_v[r, pl.ds(pl.multiple_of(hp * 2 * DH, 128), 2 * DH)] = jnp.concatenate(outs, axis=1)

            @pl.when(hp == 0)
            def _():
                between()

            return carry

        lax.fori_loop(0, local_heads // 2, head_pair, 0)

    def attn_term(block, i):
        r = pl.ds(pl.multiple_of(block * rows, rows), rows)
        return jnp.dot(o_v[r, :], wo_v[...], preferred_element_type=F32).astype(BF)

    red = ActReduce(me, *red_scratch)
    def beside_first():
        f1.pump(1, 1 - y)
        gact.forward()

    def beside_second():
        for i in range(7, 10):
            keeps[i].wait()
            sends[i].wait_recv()
        f2.own(y)
        f2.own(1 - y)
        gact.forward_core()

    sequence(1 - y, True, beside_first)
    attn_o.land((y, 1 - y))
    wo_in = pltpu.make_async_copy(wof, wo_v, c_local.at[2])
    wo_in.start()
    f1.pump(2, y)
    f1.pump(2, 1 - y)
    wo_in.wait()
    red.loop(attn_term, first=0, last=2)
    sequence(y, False, beside_second)
    for slot in range(2):
        p_copy(slot, 0, 0).wait()
    o_out = pltpu.make_async_copy(o_v, o, c_local.at[4])
    o_out.start()
    red.loop(attn_term, first=2, last=4)
    red.second()
    f2.pump(1, y)
    red.arrive()

    half = rows // 2
    for h in range(2):

        def body(i, carry):
            rr = pl.ds(pl.multiple_of(h * half + i * 16, 16), 16)
            m = xin[rr, :].astype(F32) + red.total(h, i)
            mid[rr, :] = m
            inv = lax.rsqrt(jnp.mean(m * m, axis=-1, keepdims=True) + EPSILON)
            a2[rr, :] = (m * inv * gain2[...]).astype(BF)
            return carry

        lax.fori_loop(0, half // 16, body, 0)
    aact = ActGather(me, a2, a2all, *a_sems)
    aact.start()
    f2.pump(1, 1 - y)
    f1.land((y, 1 - y))

    def fetch(src, dst, i):
        return pltpu.make_async_copy(src, dst, f_sem.at[i])

    a1_out.wait()
    fetch(wg1, wg1_v, 0).start()
    fetch(wd1, wd1_v, 1).start()
    gact.finish()

    def block_at(i):
        ox, oy = red.place(3 - i // 2)
        return block_of(ox, jnp.where(i % 2 == 0, me.k, 1 - me.k), oy)

    def load_rows(i):
        slot = lax.rem(i, 2)
        b = block_at(i)
        return fetch(a2all.at[b], xv.at[slot], 2 + slot), fetch(gall.at[b], xv.at[2 + slot], 4 + slot)

    def first_units(j, last, carry):
        b = block_at(j)

        @pl.when(j < last)
        def _():
            for copy in load_rows(j + 1):
                copy.start()

        for copy in load_rows(j):
            copy.wait()
        slot = lax.rem(j, 2)
        acc[:, 0 : 2 * h1] = jnp.dot(xv[slot], wg1_v[...], preferred_element_type=F32)
        acc[:, 2 * h1 : 3 * h1] = lax.dot_general(
            xv[2 + slot], wd1_v[...], (((1,), (1,)), ((), ())), preferred_element_type=F32
        )

        def body(i, inner):
            rr = pl.ds(pl.multiple_of(i * 16, 16), 16)
            tr = pl.ds(pl.multiple_of(b * rows + i * 16, 16), 16)
            gate, up, gm = acc[rr, 0:h1], acc[rr, h1 : 2 * h1], acc[rr, 2 * h1 : 3 * h1]
            gelu, slope = gelu_parts(gate)
            wqkv_v[tr, 0:h1] = (gm * up * slope).astype(BF)
            wqkv_v[tr, h1 : 2 * h1] = (gm * gelu).astype(BF)
            qkv_v[tr, 0:h1] = (gelu * up).astype(BF)
            return inner

        lax.fori_loop(0, rows // 16, body, 0)
        return carry

    def units(first, last):
        for copy in load_rows(first):
            copy.start()
        lax.fori_loop(first, last, lambda j, carry: first_units(j, last - 1, carry), 0)

    aact.placed()
    qkv_out.wait()
    fetch(wg1, wg1_v, 0).wait()
    fetch(wd1, wd1_v, 1).wait()
    aact.land(6)
    units(0, 2)
    aact.forward()
    f2.pump(2, y)
    aact.onward((2, 0), (4, 0))
    aact.land(7, 8, 9, 11)
    units(2, 6)
    aact.onward((3, 0), (5, 0))
    aact.land(10, 12)
    f2.pump(2, 1 - y)
    units(6, 8)
    red.finish()
    kept = [fetch(wqkv_v.at[:, pl.ds(0, 2 * h1)], dgu1, 0), fetch(qkv_v.at[:, pl.ds(0, h1)], m1, 1)]
    for copy in kept:
        copy.start()

    def load_columns(i):
        slot = lax.rem(i, 2)
        at = pl.ds(pl.multiple_of(i * rows, rows), rows)
        here = pl.ds(pl.multiple_of(slot * rows, rows), rows)
        there = pl.ds(pl.multiple_of((2 + slot) * rows, rows), rows)
        return (
            fetch(a2all.at[:, :, at], xv.at[:, :, here], 2 + slot),
            fetch(gall.at[:, :, at], xv.at[:, :, there], 4 + slot),
        )

    for copy in load_columns(0):
        copy.start()

    def first_grads(i, carry):
        @pl.when(i < 2 * n - 1)
        def _():
            for copy in load_columns(i + 1):
                copy.start()

        for copy in load_columns(i):
            copy.wait()
        slot = lax.rem(i, 2)
        here = pl.ds(pl.multiple_of(slot * rows, rows), rows)
        there = pl.ds(pl.multiple_of((2 + slot) * rows, rows), rows)
        gw_v[i, :, 0 : 2 * h1] = lax.dot_general(
            xv[:, :, here].reshape(8 * rows, rows), wqkv_v[:, 0 : 2 * h1], (((0,), (0,)), ((), ())),
            preferred_element_type=F32,
        ).astype(BF)
        gw_v[i, :, 2 * h1 : 3 * h1] = lax.dot_general(
            xv[:, :, there].reshape(8 * rows, rows), qkv_v[:, 0:h1], (((0,), (0,)), ((), ())),
            preferred_element_type=F32,
        ).astype(BF)
        return carry

    lax.fori_loop(0, 2 * n, first_grads, 0)
    kept.append(fetch(gw_v, gwf1, 2))
    kept[2].start()
    aact.sent()
    f2.land((y, 1 - y))
    for line in (attn, attn_o, f1, f2):
        line.finish()
    for copy in small_sends:
        copy.wait_send()
    for copy in small_z:
        copy.wait_send()
    seg_send.wait_send()
    for copy in sends:
        copy.wait_send()
    o_out.wait()
    for copy in kept:
        copy.wait()


def forward(n, h1, wq, wk, wv, wo, wg, wu, wd, cot, xin, seg_row, gain_a, gain_f, table_row):
    rows, width = xin.shape
    heads = wq.shape[1] // 2
    hid = wg.shape[1] // 2
    length = seg_row.shape[1]
    small, seg = (8, 384), (8, length)
    local_heads = heads // DH
    tokens = 8 * rows
    shapes = [
        ((width, 3 * heads), BF),
        ((heads, width), BF),
        ((width, 2 * h1), BF),
        ((h1, width), BF),
        ((width, 2 * (hid - h1)), BF),
        ((hid - h1, width), BF),
        ((8, rows, width), BF),
        ((tokens, 3 * heads), BF),
        ((tokens, heads), BF),
        ((2 * local_heads, length, length), BF),
        ((rows, width), F32),
        ((8, rows, width), BF),
        ((8, rows, width), BF),
        ((tokens, h1), BF),
        ((tokens, 2 * h1), BF),
        ((2 * n, rows, 3 * h1), BF),
        ((1, width), F32),
        ((1, width), F32),
    ]
    scratch = [
        pltpu.VMEM((wq.shape[0], 3 * heads), BF),
        pltpu.VMEM((heads, wo.shape[1]), BF),
        pltpu.VMEM((wq.shape[0], 2 * h1), BF),
        pltpu.VMEM((h1, wd.shape[1]), BF),
        pltpu.VMEM((wq.shape[0], 2 * (hid - h1)), BF),
        pltpu.VMEM((hid - h1, wd.shape[1]), BF),
        pltpu.VMEM(small, F32),
        pltpu.VMEM(seg, jnp.int32),
        pltpu.VMEM((8 * n,) + small, F32),
        pltpu.VMEM((2,) + seg, jnp.int32),
        pltpu.VMEM((2, length, 128), F32),
        pltpu.VMEM((8, rows, width), BF),
        pltpu.VMEM((width, 3 * heads), BF),
        pltpu.VMEM((heads, width), BF),
        pltpu.VMEM((tokens, 3 * heads), BF),
        pltpu.VMEM((tokens, heads), BF),
        pltpu.VMEM((local_heads, TQ, 2 * length), F32),
        pltpu.VMEM((2, TQ, length), BF),
        pltpu.VMEM((rows, width), BF),
        pltpu.VMEM((width, 2 * h1), BF),
        pltpu.VMEM((h1, width), BF),
        pltpu.VMEM((2 * n, rows, 3 * h1), BF),
        pltpu.VMEM((rows, 3 * h1), F32),
        DMA((10,)), DMA((10,)), DMA((10,)), DMA((8,)), DMA((8,)), DMA((n - 1,)), DMA((n - 1,)), DMA((2,)),
        DMA((5,)), DMA((2,)), DMA((6,)),
    ] + reduce_scratch(rows, width) + line_sems(n, 2) * 2 + line_sems(n, 1) * 2 + gather_sems() * 3
    return pl.pallas_call(
        functools.partial(forward_kernel, n, length),
        out_shape=[jax.ShapeDtypeStruct(s, d) for s, d in shapes],
        in_specs=[ANY] * 7 + [VM] * 6,
        out_specs=[ANY] * 10 + [VM] + [ANY] * 5 + [VM] * 2,
        scratch_shapes=scratch,
        compiler_params=pltpu.CompilerParams(
            collective_id=0, has_side_effects=True, vmem_limit_bytes=64 << 20
        ),
        name="forward",
    )(wq, wk, wv, wo, wg, wu, wd, cot, xin, seg_row, gain_a, gain_f, table_row)


class LineSum:
    def __init__(self, me, n, views, from_left, from_right, stage, sems, stage_sem):
        self.me, self.n, self.views = me, n, views
        self.inbox = {True: from_left, False: from_right}
        self.stage, self.stage_sem = stage, stage_sem
        self.sends = {True: sems[0], False: sems[1]}
        self.recvs = {True: sems[2], False: sems[3]}

    def copies(self, t, yy, right):
        me = self.me
        dev = me.device(z=me.z + 1 if right else me.z - 1)
        return [
            remote(
                view, self.inbox[right].at[t, yy, i], self.sends[right].at[t, yy, i],
                self.recvs[right].at[t, yy, i], dev,
            )
            for i, view in enumerate(self.views(t * 2 + yy))
        ]

    def start(self, t, yy, right):
        for copy in self.copies(t, yy, right):
            copy.start()

    def take(self, t, yy, right):
        slot = 0 if right else 1
        return pltpu.make_async_copy(self.inbox[right].at[t, yy, 0], self.stage[slot], self.stage_sem.at[slot])

    def open(self, t, yy, right):
        self.copies(t, yy, right)[0].wait_recv()
        self.take(t, yy, right).start()

    def add(self, t, yy, right):
        self.take(t, yy, right).wait()
        view, stage = self.views(t * 2 + yy)[0], self.stage[0 if right else 1]

        def body(r, carry):
            rr = pl.ds(pl.multiple_of(r * 16, 16), 16)
            view[rr, :] = (view[rr, :].astype(F32) + stage[rr, :].astype(F32)).astype(BF)
            return carry

        lax.fori_loop(0, view.shape[0] // 16, body, 0)

    def first(self, t, yy):
        @pl.when((self.me.z == 0) & (t > 0))
        def _():
            self.start(t, yy, True)

        @pl.when((self.me.z == self.n - 1) & (t < self.n - 1))
        def _():
            self.start(t, yy, False)

    def pump(self, k, yy):
        z, n = self.me.z, self.n
        sides = (
            (True, z + k, (z + k <= n - 1) & (z > 0)),
            (False, z - k, (z - k >= 0) & (z < n - 1)),
        )
        for right, t, go in sides:

            @pl.when(go)
            def _():
                self.open(t, yy, right)

        for right, t, go in sides:

            @pl.when(go)
            def _():
                self.add(t, yy, right)
                self.start(t, yy, right)

    def own(self, yy):
        z = self.me.z
        sides = ((True, z > 0), (False, z < self.n - 1))
        for right, go in sides:

            @pl.when(go)
            def _():
                self.open(z, yy, right)

        for right, go in sides:

            @pl.when(go)
            def _():
                self.add(z, yy, right)

    def finish(self):
        z, n = self.me.z, self.n
        for yy in range(2):
            for k in range(1, n):

                @pl.when(z + k <= n - 1)
                def _():
                    for copy in self.copies(z + k, yy, True):
                        copy.wait_send()

                @pl.when(z - k >= 0)
                def _():
                    for copy in self.copies(z - k, yy, False):
                        copy.wait_send()


def far_first(n, z, i):
    slot = 0
    for a in range(n):
        order = sorted(range(n), key=lambda d: (-abs(d - a), d))
        for b in range(n):
            slot = slot + jnp.where((z == a) & (i == b), order[b], 0)
    return slot


def gelu_parts(gate):
    th = jnp.tanh(0.7978845608028654 * (gate + 0.044715 * gate * gate * gate))
    gelu = 0.5 * gate * (1.0 + th)
    slope = 0.5 * (1.0 + th) + 0.5 * gate * (1.0 - th * th) * 0.7978845608028654 * (
        1.0 + 3 * 0.044715 * gate * gate
    )
    return gelu, slope


def norm_back(ga, values, gain):
    inv = lax.rsqrt(jnp.mean(values * values, axis=-1, keepdims=True) + EPSILON)
    u = ga * gain
    corr = jnp.mean(u * values, axis=-1, keepdims=True) * inv * inv * inv
    return inv * u - values * corr, ga * (values * inv)


def backward_kernel(
    n, length, heads, hid, h1,
    wg1, wd1, wg2, wd2, m1, dgu1, gwf1, a2all, gall, p, a1, qkv, o, wqkv, wof, hidden, mid, cot, gain1, gain2,
    out, gx, fo1, fo2, bo, co, sums, dzall, e_left, e_right, f_left, f_right, b_left, b_right, c_left, c_right,
    wgu_v, wd_v, row_a, row_b, row_g, col_a, col_g, m, dgu, gw1, gw2, stage, gmid, dz, wqkv_v,
    pbuf, acc, dkt, dvt, diag, gg1, gg2, sv, sv_in, sv_z, free,
    load, p_sem, stage_sem, y_send, y_recv, y_local, sv_send, sv_recv, sz_send, sz_recv,
    *rest,
):
    red_scratch, dz_sems = rest[:9], rest[9:12]
    e_sems, f_sems, b_sems, c_sems = (rest[i : i + 4] for i in range(12, 28, 4))
    h2 = hid - h1
    me = Place()
    z, y = me.z, me.y
    rows, width = cot.shape
    group = [
        me.device(x=ox, k=ok, y=oy)
        for ox in (me.x, 1 - me.x)
        for ok in (me.k, 1 - me.k)
        for oy in (me.y, 1 - me.y)
    ][1:]
    others = [me.device(z=lax.rem(z + s, n)) for s in range(1, n)]
    greet(group + others)
    local_heads = heads // DH
    half = rows // 2

    def fetch(src, dst, i):
        return pltpu.make_async_copy(src, dst, load.at[i])

    red = ActReduce(me, *red_scratch)
    order = (1 - y, y)

    def line_sum(view, left, right, width, sems):
        stages = [stage.at[i, :, pl.ds(0, width)] for i in range(2)]
        return LineSum(me, n, lambda pc: [view(pc)], left, right, stages, sems, stage_sem)

    esum = line_sum(lambda pc: gw1.at[pc], e_left, e_right, 3 * h1, e_sems)
    fsum = line_sum(lambda pc: gw2.at[pc], f_left, f_right, 3 * h2, f_sems)

    def piece(pc):
        return pl.ds(pl.multiple_of(pc * rows, rows), rows)

    pair = 3 * 2 * DH
    bsum = line_sum(lambda pc: m.at[piece(pc), :], b_left, b_right, heads + pair, b_sems)
    csum = line_sum(lambda pc: dgu.at[piece(pc), pl.ds(3 * heads, pair)], c_left, c_right, pair, c_sems)

    def piece_at(i):
        return far_first(n, z, i // 2) * 2 + jnp.where(i % 2 == 0, 1 - y, y)

    w_loads = [
        fetch(gwf1, gw1, 0),
        fetch(wg2, wgu_v.at[:, pl.ds(2 * h1, 2 * h2)], 1),
        fetch(wd2, wd_v.at[pl.ds(h1, h2), :], 6),
        fetch(wg1, wgu_v.at[:, pl.ds(0, 2 * h1)], 7),
        fetch(dgu1, dgu.at[:, pl.ds(0, 2 * h1)], 8),
        fetch(wd1, wd_v.at[pl.ds(0, h1), :], 9),
        fetch(m1, m.at[:, pl.ds(0, h1)], 10),
    ]
    for copy in w_loads:
        copy.start()

    def block_at(i):
        j = i // 2
        ox, oy = red.place(j)
        return block_of(ox, jnp.where(i % 2 == 0, 1 - me.k, me.k), oy)

    fetch(a2all.at[block_at(0)], row_a, 2).start()
    fetch(gall.at[block_at(0)], row_g, 3).start()
    fetch(cot, row_b, 4).start()
    w_loads[0].wait()

    def first_slots(i, carry):
        pc = piece_at(i)
        esum.first(pc // 2, pc % 2)
        return carry

    lax.fori_loop(0, 2 * n, first_slots, 0)
    for copy in w_loads[1:3]:
        copy.wait()


    def make_ffn(block, i):
        fetch(a2all.at[block], row_a, 2).wait()
        acc[:, 0 : 2 * h2] = jnp.dot(row_a[...], wgu_v[:, 2 * h1 : 2 * hid], preferred_element_type=F32)

        @pl.when(i < 7)
        def _():
            fetch(a2all.at[block_at(i + 1)], row_a, 2).start()

        fetch(gall.at[block], row_g, 3).wait()
        acc[:, 2 * h2 : 3 * h2] = lax.dot_general(
            row_g[...], wd_v[h1:hid, :], (((1,), (1,)), ((), ())), preferred_element_type=F32
        )

        @pl.when(i < 7)
        def _():
            fetch(gall.at[block_at(i + 1)], row_g, 3).start()

        def body(r, carry):
            rr = pl.ds(pl.multiple_of(r * 16, 16), 16)
            tr = pl.ds(pl.multiple_of(block * rows + r * 16, 16), 16)
            gate, up, gm = acc[rr, 0:h2], acc[rr, h2 : 2 * h2], acc[rr, 2 * h2 : 3 * h2]
            gelu, slope = gelu_parts(gate)
            m[tr, h1:hid] = (gelu * up).astype(BF)
            dgu[tr, 2 * h1 : 2 * h1 + h2] = (gm * up * slope).astype(BF)
            dgu[tr, 2 * h1 + h2 : 2 * hid] = (gm * gelu).astype(BF)
            return carry

        lax.fori_loop(0, rows // 16, body, 0)

        @pl.when(i == 0)
        def _():
            for copy in w_loads[3:]:
                copy.wait()

        return lax.dot_general(
            dgu[piece(block), :], wgu_v[...], (((1,), (1,)), ((), ())), preferred_element_type=F32
        ).astype(BF)

    red.loop(make_ffn, hooks=((1, lambda: esum.pump(2, order[0])), (2, lambda: esum.pump(2, order[1]))))
    esum.pump(1, order[0])

    fetch(wof, row_g, 3).start()

    def columns(ref, i):
        return ref.at[:, :, piece(piece_at(i))]

    def load_columns(left, right, i):
        slot = lax.rem(i, 2)
        return fetch(columns(left, i), col_a.at[slot], 11 + slot), fetch(columns(right, i), col_g.at[slot], 13 + slot)

    def next_columns(left, right, i):
        @pl.when(i < 2 * n - 1)
        def _():
            for copy in load_columns(left, right, i + 1):
                copy.start()

        for copy in load_columns(left, right, i):
            copy.wait()

    for copy in load_columns(a2all, gall, 0):
        copy.start()

    def ffn_grads(i, carry):
        pc = piece_at(i)
        slot = lax.rem(i, 2)
        next_columns(a2all, gall, i)
        gw2[pc, :, 0 : 2 * h2] = lax.dot_general(
            col_a[slot].reshape(8 * rows, rows), dgu[:, 2 * h1 : 2 * hid], (((0,), (0,)), ((), ())),
            preferred_element_type=F32,
        ).astype(BF)
        gw2[pc, :, 2 * h2 : 3 * h2] = lax.dot_general(
            col_g[slot].reshape(8 * rows, rows), m[:, h1:hid], (((0,), (0,)), ((), ())),
            preferred_element_type=F32,
        ).astype(BF)
        fsum.first(pc // 2, pc % 2)
        return carry

    lax.fori_loop(0, n, ffn_grads, 0)
    red.second()
    esum.pump(1, order[1])
    fetch(qkv, wgu_v.at[:, pl.ds(0, 3 * heads)], 0).start()
    fetch(o, wgu_v.at[:, pl.ds(3 * heads, heads)], 6).start()
    red.arrive()

    gg2[...] = jnp.zeros_like(gg2)
    fetch(cot, row_b, 4).wait()
    for h in range(2):

        def body(i, carry):
            rr = pl.ds(pl.multiple_of(h * half + i * 16, 16), 16)
            back, gains = norm_back(red.total(h, i), mid[rr, :], gain2[...])
            gm = row_b[rr, :].astype(F32) + back
            gmid[rr, :] = gm
            dz[rr, :] = gm.astype(BF)
            gg2[...] += gains[:8] + gains[8:]
            return carry

        lax.fori_loop(0, half // 16, body, 0)
    act = ActGather(me, dz, dzall, *dz_sems)
    act.start()
    red.finish()

    def release():
        for i, dev in enumerate((me.x_peer(), me.y_peer(), me.core_peer())):
            pl.semaphore_signal(free.at[i], inc=1, device_id=dev, device_id_type=MESH)

    def claim():
        for i in range(3):
            pl.semaphore_wait(free.at[i], 1)

    release()
    lax.fori_loop(n, 2 * n, ffn_grads, 0)
    act.forward()

    claim()

    def make_out(block, i):
        return jnp.dot(m[piece(block), :], wd_v[...], preferred_element_type=F32).astype(BF)

    red.loop(make_out, send=False)
    def swap(views, box, i):
        out = remote(views(z * 2 + 1 - y)[0], box.at[y], y_send.at[i], y_recv.at[i], me.y_peer())
        keep = pltpu.make_async_copy(views(z * 2 + y)[0], box.at[y], y_local.at[i])
        return out, keep

    lines = (esum, fsum, bsum, csum)
    swaps = [swap(line.views, box, i) for i, (line, box) in enumerate(zip(lines, (fo1, fo2, bo, co)))]

    def settle(i):
        lines[i].own(order[0])
        swaps[i][0].start()
        lines[i].own(order[1])
        swaps[i][1].start()

    fsum.pump(2, order[0])
    act.onward((4, 0))
    act.placed()
    act.land(6, 7, 11)

    fetch(wof, row_g, 3).wait()
    slots = ((row_a, 2), (row_b, 4))

    def come(i):
        ox, oy = red.place(3 - i // 2)
        return block_of(ox, jnp.where(i % 2 == 0, me.k, 1 - me.k), oy)

    def project_back(first):
        for b, (buffer, sem) in enumerate(slots):
            fetch(dzall.at[come(first + b)], buffer, sem).start()
        for i in range(2):
            for b, (buffer, sem) in enumerate(slots):
                block = come(first + 2 * i + b)
                fetch(dzall.at[block], buffer, sem).wait()
                wgu_v[piece(block), 4 * heads : 5 * heads] = lax.dot_general(
                    buffer[...], row_g[...], (((1,), (1,)), ((), ())), preferred_element_type=F32
                ).astype(BF)
                if i == 0:
                    fetch(dzall.at[come(first + 2 + b)], buffer, sem).start()

    project_back(0)
    fetch(qkv, wgu_v.at[:, pl.ds(0, 3 * heads)], 0).wait()
    fetch(o, wgu_v.at[:, pl.ds(3 * heads, heads)], 6).wait()
    diag[...] = jnp.zeros_like(diag)
    tiles = length // TQ

    def p_load(head, t, slot):
        return pltpu.make_async_copy(p.at[head, pl.ds(t * TQ, TQ)], pbuf.at[slot], p_sem.at[slot])

    def head_pair(hp, s):
        head0 = s * local_heads + hp * 2
        base = pl.multiple_of(s * length, length)
        p_load(head0, 0, 0).start()
        p_load(head0, 1, 1).start()
        for h in range(2):
            lo = hp * 128 + h * DH
            to = hp * pair + h * DH
            seq = pl.ds(base, length)
            kh = wgu_v[seq, heads + lo : heads + lo + DH]
            vh = wgu_v[seq, 2 * heads + lo : 2 * heads + lo + DH]
            acc[...] = jnp.zeros_like(acc)
            for t in range(tiles):
                slot = t % 2
                r = pl.ds(pl.multiple_of(base + t * TQ, TQ), TQ)
                qh = wgu_v[r, lo : lo + DH]
                doh = wgu_v[r, 4 * heads + lo : 4 * heads + lo + DH]
                p_load(head0 + h, t, slot).wait()
                pb = pbuf[slot]
                dp = lax.dot_general(doh, vh, (((1,), (1,)), ((), ())), preferred_element_type=F32)
                pf = pb.astype(F32)
                ds = (pf * (dp - jnp.sum(pf * dp, axis=-1, keepdims=True))).astype(BF)
                dgu[r, to : to + DH] = jnp.dot(ds, kh, preferred_element_type=F32).astype(BF)
                ck = lax.dot_general(qh, ds, (((0,), (0,)), ((), ())), preferred_element_type=F32)
                cv = lax.dot_general(doh, pb, (((0,), (0,)), ((), ())), preferred_element_type=F32)
                u = h * tiles + t + 2
                if u < 2 * tiles:
                    p_load(head0 + u // tiles, u % tiles, slot).start()
                if t == 0:
                    dkt[...] = ck
                    dvt[...] = cv
                else:
                    dkt[...] += ck
                    dvt[...] += cv
                acc[:, length - t * TQ : 2 * length - t * TQ] += ds.astype(F32)
            dgu[seq, to + 2 * DH : to + 3 * DH] = dkt[...].T.astype(BF)
            dgu[seq, to + 4 * DH : to + 5 * DH] = dvt[...].T.astype(BF)
            c = TQ // 2
            while c >= 8:
                acc[0:c, :] += pltpu.roll(acc[c : 2 * c, :], 2 * length - c, 1)
                c //= 2
            diag[hp * 2 + h] += acc[0:8, :]

    def pair_grads(hp, line, with_o):
        def loads(i):
            slot = lax.rem(i, 2)
            both = fetch(columns(a1, i), col_a.at[slot], 11 + slot), fetch(columns(dzall, i), col_g.at[slot], 13 + slot)
            return both if with_o else both[:1]

        for copy in loads(0):
            copy.start()

        def body(i, carry):
            pc = piece_at(i)
            slot = lax.rem(i, 2)

            @pl.when(i < 2 * n - 1)
            def _():
                for copy in loads(i + 1):
                    copy.start()

            for copy in loads(i):
                copy.wait()
            if with_o:
                m[piece(pc), 0:heads] = lax.dot_general(
                    col_g[slot].reshape(8 * rows, rows), wgu_v[:, 3 * heads : 4 * heads], (((0,), (0,)), ((), ())),
                    preferred_element_type=F32,
                ).astype(BF)
            part = lax.dot_general(
                col_a[slot].reshape(8 * rows, rows), dgu[:, hp * pair : (hp + 1) * pair], (((0,), (0,)), ((), ())),
                preferred_element_type=F32,
            ).astype(BF)
            if with_o:
                m[piece(pc), heads : heads + pair] = part
            else:
                dgu[piece(pc), 3 * heads : 3 * heads + pair] = part
            line.first(pc // 2, pc % 2)
            return carry

        lax.fori_loop(0, 2 * n, body, 0)

    head_pair(0, y)
    act.onward((2, 0), (3, 0), (5, 0))
    for j in range(3):
        red.first_sends(j)
    fsum.pump(2, order[1])
    settle(0)
    head_pair(1, y)
    act.land(8, 9, 10, 12)
    project_back(4)
    act.sent()
    fetch(hidden, row_a, 2).start()
    w_parts = [
        fetch(
            wqkv.at[:, pl.ds(part * heads + hp * 2 * DH, 2 * DH)],
            wqkv_v.at[:, pl.ds(hp * pair + part * 2 * DH, 2 * DH)],
            15 + hp * 3 + part,
        )
        for hp in range(2)
        for part in range(3)
    ]
    for copy in w_parts:
        copy.start()
    fsum.pump(1, order[0])
    red.second()
    head_pair(0, 1 - y)
    pair_grads(0, bsum, True)
    fsum.pump(1, order[1])
    head_pair(1, 1 - y)
    for yy in order:
        bsum.pump(2, yy)

    red.arrive()
    for h in range(2):

        def body(i, carry):
            rr = pl.ds(pl.multiple_of(h * half + i * 16, 16), 16)
            out[rr, :] = (mid[rr, :] + red.total(h, i)).astype(BF)
            return carry

        lax.fori_loop(0, half // 16, body, 0)
    red.finish()
    release()
    claim()
    for copy in w_parts:
        copy.wait()

    def make_ga1(block, i):
        return lax.dot_general(
            dgu[piece(block), 0 : 3 * heads], wqkv_v[...], (((1,), (1,)), ((), ())), preferred_element_type=F32
        ).astype(BF)

    red.loop(make_ga1)
    pair_grads(1, csum, False)
    red.second()
    settle(1)
    for yy in order:
        bsum.pump(1, yy)
        csum.pump(2, yy)

    offset = lax.broadcasted_iota(jnp.int32, (NB, 2 * length), 1) - length
    away = jnp.abs(offset)
    bucket = jnp.where(away < 8, away, 8 + sum((away >= t).astype(jnp.int32) for t in THRESHOLDS))
    bucket = bucket + 16 * (offset > 0).astype(jnp.int32)
    own_bucket = bucket == lax.broadcasted_iota(jnp.int32, (NB, 2 * length), 0)
    lane = lax.broadcasted_iota(jnp.int32, (NB, 128), 1)
    table = jnp.zeros((NB, 128), F32)
    for lh in range(local_heads):
        line = diag[lh, 0:1, :]
        for r in range(1, 8):
            line = line + pltpu.roll(diag[lh, r : r + 1, :], 2 * length - r, 1)
        value = jnp.sum(jnp.where(own_bucket, line, 0.0), axis=1, keepdims=True)
        table = jnp.where(lane == (me.c * 2 + y) * local_heads + lh, value, table)
    for yy in order:
        csum.pump(1, yy)
    red.arrive()
    gg1[...] = jnp.zeros_like(gg1)
    fetch(hidden, row_a, 2).wait()
    for h in range(2):

        def body(i, carry):
            rr = pl.ds(pl.multiple_of(h * half + i * 16, 16), 16)
            back, gains = norm_back(red.total(h, i), row_a[rr, :].astype(F32), gain1[...])
            gx[rr, :] = gmid[rr, :] + back
            gg1[...] += gains[:8] + gains[8:]
            return carry

        lax.fori_loop(0, half // 16, body, 0)
    red.finish()

    first_row = lax.broadcasted_iota(jnp.int32, (8, 128), 0) == 0
    for d in range(8 * n):
        g, zz = d % 8, d // 8
        lanes = slice(d // 2 * 128, d // 2 * 128 + 128)
        sv[g, zz, :, 0:128] = gg1[:, lanes]
        sv[g, zz, :, 128:256] = gg2[:, lanes]
        sv[g, zz, :, 256:384] = jnp.where(first_row, jnp.broadcast_to(table[d : d + 1, :], (8, 128)), 0.0)
    peers = [
        (ox * 4 + ok * 2 + oy)
        for ox in (me.x, 1 - me.x)
        for ok in (me.k, 1 - me.k)
        for oy in (me.y, 1 - me.y)
    ]
    sv_copies = [
        remote(sv.at[peers[i + 1]], sv_in.at[i], sv_send.at[i], sv_recv.at[i], dev)
        for i, dev in enumerate(group)
    ]
    for copy in sv_copies:
        copy.start()

    settle(2)
    for copy in sv_copies:
        copy.wait_recv()
    me_g = me.c * 2 + y
    total = sv[me_g]
    for i in range(7):
        total = total + sv_in[i]
    sv_z[0] = total
    z_copies = [
        remote(sv_z.at[0, lax.rem(z + s, n)], sv_z.at[s, 0], sz_send.at[s - 1], sz_recv.at[s - 1], others[s - 1])
        for s in range(1, n)
    ]
    for copy in z_copies:
        copy.start()
    settle(3)
    for copy in z_copies:
        copy.wait_recv()
    total = sv_z[0, z]
    for s in range(1, n):
        total = total + sv_z[s, 0]
    sums[...] = total
    for pair_of in swaps:
        for copy in pair_of:
            copy.wait()
    for copy in sv_copies + z_copies:
        copy.wait_send()
    for line in lines:
        line.finish()


def backward(n, length, heads, hid, h1, *arrays):
    cot = arrays[-3]
    rows, width = cot.shape
    tokens = 8 * rows
    h2 = hid - h1
    pair = 3 * 2 * DH
    shapes = [
        ((rows, width), BF),
        ((rows, width), F32),
        ((2, rows, 3 * h1), BF),
        ((2, rows, 3 * h2), BF),
        ((2, rows, heads + pair), BF),
        ((2, rows, pair), BF),
        ((8, 384), F32),
        ((8, rows, width), BF),
        ((n, 2, 1, rows, 3 * h1), BF),
        ((n, 2, 1, rows, 3 * h1), BF),
        ((n, 2, 1, rows, 3 * h2), BF),
        ((n, 2, 1, rows, 3 * h2), BF),
        ((n, 2, 1, rows, heads + pair), BF),
        ((n, 2, 1, rows, heads + pair), BF),
        ((n, 2, 1, rows, pair), BF),
        ((n, 2, 1, rows, pair), BF),
    ]
    scratch = [
        pltpu.VMEM((width, 2 * hid), BF),
        pltpu.VMEM((hid, width), BF),
        pltpu.VMEM((rows, width), BF),
        pltpu.VMEM((rows, width), BF),
        pltpu.VMEM((rows, width), BF),
        pltpu.VMEM((2, 8, rows, rows), BF),
        pltpu.VMEM((2, 8, rows, rows), BF),
        pltpu.VMEM((tokens, hid), BF),
        pltpu.VMEM((tokens, 2 * hid), BF),
        pltpu.VMEM((2 * n, rows, 3 * h1), BF),
        pltpu.VMEM((2 * n, rows, 3 * h2), BF),
        pltpu.VMEM((2, rows, 3 * max(h1, h2)), BF),
        pltpu.VMEM((rows, width), F32),
        pltpu.VMEM((rows, width), BF),
        pltpu.VMEM((width, 3 * heads), BF),
        pltpu.VMEM((2, TQ, length), BF),
        pltpu.VMEM((TQ, 2 * length), F32),
        pltpu.VMEM((DH, length), F32),
        pltpu.VMEM((DH, length), F32),
        pltpu.VMEM((heads // DH, 8, 2 * length), F32),
        pltpu.VMEM((8, width), F32),
        pltpu.VMEM((8, width), F32),
        pltpu.VMEM((8, n, 8, 384), F32),
        pltpu.VMEM((7, n, 8, 384), F32),
        pltpu.VMEM((n, n, 8, 384), F32),
        pltpu.SemaphoreType.REGULAR((3,)),
        DMA((21,)), DMA((2,)), DMA((2,)), DMA((4,)), DMA((4,)), DMA((4,)), DMA((7,)), DMA((7,)), DMA((n - 1,)), DMA((n - 1,)),
    ] + reduce_scratch(rows, width) + gather_sems() + [DMA((n, 2, 1))] * 16
    return pl.pallas_call(
        functools.partial(backward_kernel, n, length, heads, hid, h1),
        out_shape=[jax.ShapeDtypeStruct(s, d) for s, d in shapes],
        in_specs=[ANY] * 16 + [VM, ANY, VM, VM],
        out_specs=[VM, VM] + [ANY] * 4 + [VM] + [ANY] * 9,
        scratch_shapes=scratch,
        compiler_params=pltpu.CompilerParams(
            collective_id=1, has_side_effects=True, vmem_limit_bytes=64 << 20
        ),
        name="backward",
    )(*arrays)


def on_device(
    n, hidden, segment_ids, positions, attn_gain, w_query, w_key, w_value, w_attn_out,
    rel_table, ffn_gain, w_gate, w_up, w_down, cotangent,
):
    xin = hidden[0]
    cot = cotangent[0]
    length = segment_ids.shape[1]
    heads = w_query.shape[1] // 2
    hid = w_gate.shape[1] // 2
    share = attn_gain.shape[0]
    y = lax.axis_index("fsdp")
    h1 = 256
    h2 = hid - h1
    wqkv, wo, wg1, wd1, wg2, wd2, a1, qkv, o, p, mid, a2all, gall, m1, dgu1, gwf1, gain1, gain2 = forward(
        n, h1, w_query, w_key, w_value, w_attn_out, w_gate, w_up, w_down, cot, xin, segment_ids,
        attn_gain[None], ffn_gain[None], rel_table[None],
    )
    out, gx, fo1, fo2, bo, co, sums = backward(
        n, length, heads, hid, h1, wg1, wd1, wg2, wd2, m1, dgu1, gwf1, a2all, gall, p, a1, qkv, o, wqkv, wo,
        xin, mid, cot, gain1, gain2,
    )[:7]
    out, gx, g_q, g_k, g_v, g_o, g_gate, g_up, g_down = finish(h1, heads, out, gx, fo1, fo2, bo, co)
    line = jnp.sum(sums, axis=0)
    half_of = lambda v: jnp.where(y == 0, v[:share], v[128 - share :])
    return (
        out[None], gx[None], half_of(line[:128]), g_q, g_k, g_v, g_o, line[256 : 256 + H],
        half_of(line[128:256]), g_gate, g_up, g_down,
    )


def finish_kernel(h1, heads, out_in, gx_in, *refs):
    sources, (out, gx, g_q, g_k, g_v, g_o, g_gate, g_up, g_down) = refs[:4], refs[4:13]
    held = refs[13:19]
    fo1, fo2, bo, co = held[:4]
    sem = refs[19]
    sources = sources + (out_in, gx_in)
    loads = [pltpu.make_async_copy(src, dst, sem.at[i]) for i, (src, dst) in enumerate(zip(sources, held))]
    moves = [pltpu.make_async_copy(held[4 + i], dst, sem.at[4 + i]) for i, dst in enumerate((out, gx))]
    for copy in loads:
        copy.start()
    for copy in loads:
        copy.wait()
    for copy in moves:
        copy.start()
    h2 = fo2.shape[2] // 3
    hid = h1 + h2
    s_q, s_k, s_v, s_o, s_gate, s_up, s_down = refs[20:27]
    sem_out = refs[27]
    leave = [
        pltpu.make_async_copy(src, dst, sem_out.at[i])
        for i, (src, dst) in enumerate(
            zip((s_q, s_k, s_v, s_o, s_gate, s_up, s_down), (g_q, g_k, g_v, g_o, g_gate, g_up, g_down))
        )
    ]
    for part, ref in enumerate((s_gate, s_up)):
        for yy in range(2):
            ref[:, yy * hid : yy * hid + h1] = fo1[yy, :, part * h1 : (part + 1) * h1].astype(F32)
            ref[:, yy * hid + h1 : (yy + 1) * hid] = fo2[yy, :, part * h2 : (part + 1) * h2].astype(F32)
        leave[4 + part].start()
    for part, ref in enumerate((s_q, s_k, s_v)):
        for yy in range(2):
            at = heads + part * 128
            ref[:, yy * heads : yy * heads + 128] = bo[yy, :, at : at + 128].astype(F32)
            ref[:, yy * heads + 128 : yy * heads + 256] = co[yy, :, part * 128 : part * 128 + 128].astype(F32)
        leave[part].start()
    for yy in range(2):
        s_down[yy * hid : yy * hid + h1, :] = fo1[yy, :, 2 * h1 : 3 * h1].astype(F32).T
        s_down[yy * hid + h1 : (yy + 1) * hid, :] = fo2[yy, :, 2 * h2 : 3 * h2].astype(F32).T
    leave[6].start()
    for yy in range(2):
        s_o[yy * heads : (yy + 1) * heads, :] = bo[yy, :, 0:heads].astype(F32).T
    leave[3].start()
    for copy in moves + leave:
        copy.wait()


def finish(h1, heads, out, gx, fo1, fo2, bo, co):
    rows = out.shape[0]
    hid = h1 + fo2.shape[2] // 3
    shapes = [(rows, 2 * heads)] * 3 + [(2 * heads, rows)] + [(rows, 2 * hid)] * 2 + [(2 * hid, rows)]
    return pl.pallas_call(
        functools.partial(finish_kernel, h1, heads),
        out_shape=[jax.ShapeDtypeStruct(out.shape, BF), jax.ShapeDtypeStruct(gx.shape, F32)]
        + [jax.ShapeDtypeStruct(s, F32) for s in shapes],
        in_specs=[ANY] * 6,
        out_specs=[ANY] * 9,
        scratch_shapes=[pltpu.VMEM(part.shape, part.dtype) for part in (fo1, fo2, bo, co, out, gx)]
        + [DMA((6,))]
        + [pltpu.VMEM(s, F32) for s in shapes]
        + [DMA((7,))],
        compiler_params=pltpu.CompilerParams(vmem_limit_bytes=64 << 20),
        name="finish",
    )(out, gx, fo1, fo2, bo, co)


QB = 512


def rms_norm(values, gain):
    return values * lax.rsqrt(jnp.mean(values * values, axis=-1, keepdims=True) + EPSILON) * gain


def gelu_tanh(values):
    return (
        0.5
        * values
        * (1.0 + jnp.tanh(0.7978845608028654 * (values + 0.044715 * values * values * values)))
    )


def bucket_table(query_pos, key_pos):
    relative = key_pos[None, :] - query_pos[:, None]
    distance = jnp.abs(relative)
    log_bucket = 8 + sum(((distance >= threshold).astype(jnp.int32) for threshold in THRESHOLDS))
    bucket = jnp.where(distance < 8, distance, log_bucket)
    return bucket + 16 * (relative > 0).astype(jnp.int32)


def gather_attention(w_query, w_key, w_value, w_attn_out):
    return (
        lax.all_gather(w_query, ("dp", "fsdp"), axis=0, tiled=True),
        lax.all_gather(w_key, ("dp", "fsdp"), axis=0, tiled=True),
        lax.all_gather(w_value, ("dp", "fsdp"), axis=0, tiled=True),
        lax.all_gather(w_attn_out, ("dp", "fsdp"), axis=1, tiled=True),
    )


def gather_feedforward(w_gate, w_up, w_down):
    return (
        lax.all_gather(w_gate, ("dp", "fsdp"), axis=0, tiled=True),
        lax.all_gather(w_up, ("dp", "fsdp"), axis=0, tiled=True),
        lax.all_gather(w_down, ("dp", "fsdp"), axis=1, tiled=True),
    )


def block_masks(segment_row, position_row, start):
    query_pos = lax.dynamic_slice_in_dim(position_row, start, QB)
    query_seg = lax.dynamic_slice_in_dim(segment_row, start, QB)
    buckets = bucket_table(query_pos, position_row)
    one_hot = (buckets[None] == jnp.arange(NB, dtype=jnp.int32)[:, None, None]).astype(jnp.bfloat16)
    same_doc = query_seg[:, None] == segment_row[None, :]
    return (one_hot, same_doc)


def block_scores(query_block, key_rows, table_local, one_hot, same_doc):
    attention_scores = jnp.einsum(
        "ihd,jhd->hij", query_block, key_rows, preferred_element_type=jnp.float32
    )
    attention_scores = attention_scores + jnp.einsum(
        "bij,bh->hij", one_hot, table_local, preferred_element_type=jnp.float32
    )
    return jnp.where(same_doc[None], attention_scores, MASKED)


def layer_forward(tokens, small_set, attn_set, ffn_set, segment_row, position_row):
    attn_gain, ffn_gain, table_flat = small_set
    w_query, w_key, w_value, w_attn_out = attn_set
    w_gate, w_up, w_down = ffn_set
    heads_here = w_query.shape[1] // DH
    head_start = lax.axis_index("ctx") * heads_here
    table_local = lax.dynamic_slice_in_dim(table_flat.reshape(NB, H), head_start, heads_here, 1)
    normalized_rows, attn_back = jax.vjp(rms_norm, tokens, attn_gain.astype(jnp.float32))
    normed_rows = lax.all_gather(normalized_rows.astype(jnp.bfloat16), "ctx", axis=0, tiled=True)
    seq_len = normed_rows.shape[0]
    queries = (
        jnp.dot(normed_rows, w_query, preferred_element_type=jnp.float32)
        .astype(jnp.bfloat16)
        .reshape(seq_len, heads_here, DH)
    )
    key_rows = (
        jnp.dot(normed_rows, w_key, preferred_element_type=jnp.float32)
        .astype(jnp.bfloat16)
        .reshape(seq_len, heads_here, DH)
    )
    value_rows = (
        jnp.dot(normed_rows, w_value, preferred_element_type=jnp.float32)
        .astype(jnp.bfloat16)
        .reshape(seq_len, heads_here, DH)
    )
    starts = jnp.arange(seq_len // QB, dtype=jnp.int32) * QB

    def forward_block(start):
        one_hot, same_doc = block_masks(segment_row, position_row, start)
        query_block = lax.dynamic_slice_in_dim(queries, start, QB, 0)
        attention_scores = block_scores(query_block, key_rows, table_local, one_hot, same_doc)
        row_peak = jnp.max(attention_scores, axis=-1, keepdims=True)
        lifted = jnp.exp(attention_scores - row_peak)
        row_total = jnp.sum(lifted, axis=-1, keepdims=True)
        prob_low = (lifted / row_total).astype(jnp.bfloat16)
        attended_part = jnp.einsum(
            "hij,jhd->ihd", prob_low, value_rows, preferred_element_type=jnp.float32
        )
        return (attended_part, row_peak + jnp.log(row_total))

    attended, log_total = lax.map(forward_block, starts)
    attended_low = attended.reshape(seq_len, heads_here * DH).astype(jnp.bfloat16)
    attn_term = jnp.dot(attended_low, w_attn_out, preferred_element_type=jnp.float32)
    residual = tokens + lax.psum_scatter(attn_term, "ctx", scatter_dimension=0, tiled=True)
    normed_ffn, ffn_back = jax.vjp(rms_norm, residual, ffn_gain.astype(jnp.float32))
    ffn_rows = lax.all_gather(normed_ffn.astype(jnp.bfloat16), "ctx", axis=0, tiled=True)
    gate_value = jnp.dot(ffn_rows, w_gate, preferred_element_type=jnp.float32)
    up_value = jnp.dot(ffn_rows, w_up, preferred_element_type=jnp.float32)
    gelu_gate, gelu_back = jax.vjp(gelu_tanh, gate_value)
    ffn_hidden = (gelu_gate * up_value).astype(jnp.bfloat16)
    down_term = jnp.dot(ffn_hidden, w_down, preferred_element_type=jnp.float32)
    result = residual + lax.psum_scatter(
        down_term.astype(jnp.bfloat16), "ctx", scatter_dimension=0, tiled=True
    ).astype(jnp.float32)
    stored = (
        attn_back,
        normed_rows,
        queries,
        key_rows,
        value_rows,
        table_local,
        head_start,
        starts,
        log_total,
        attended_low,
        ffn_back,
        ffn_rows,
        up_value,
        gelu_gate,
        gelu_back,
        ffn_hidden,
    )
    return (result, stored)


def plain_on_device(
    hidden,
    segment_ids,
    positions,
    attn_gain,
    w_query,
    w_key,
    w_value,
    w_attn_out,
    rel_table,
    ffn_gain,
    w_gate,
    w_up,
    w_down,
    cotangent,
):
    tokens = hidden[0].astype(jnp.float32)
    segment_row = segment_ids[0]
    position_row = positions[0]
    small_set = (
        lax.all_gather(attn_gain, ("dp", "ctx", "fsdp"), axis=0, tiled=True),
        lax.all_gather(ffn_gain, ("dp", "ctx", "fsdp"), axis=0, tiled=True),
        lax.all_gather(rel_table, ("dp", "ctx", "fsdp"), axis=0, tiled=True),
    )
    attn_set = gather_attention(w_query, w_key, w_value, w_attn_out)
    ffn_set = gather_feedforward(w_gate, w_up, w_down)
    result, unused_stored = layer_forward(
        tokens, small_set, attn_set, ffn_set, segment_row, position_row
    )
    back_attn = gather_attention(w_query, w_key, w_value, w_attn_out)
    back_ffn = gather_feedforward(w_gate, w_up, w_down)
    recomputed, stored = layer_forward(
        tokens, small_set, back_attn, back_ffn, segment_row, position_row
    )
    (
        attn_back,
        normed_rows,
        queries,
        key_rows,
        value_rows,
        table_local,
        head_start,
        starts,
        log_total,
        attended_low,
        ffn_back,
        ffn_rows,
        up_value,
        gelu_gate,
        gelu_back,
        ffn_hidden,
    ) = stored
    full_query, full_key, full_value, full_attn_out = back_attn
    full_gate, full_up, full_down = back_ffn
    seq_len = normed_rows.shape[0]
    heads_here = queries.shape[1]
    grad_rows = lax.all_gather(cotangent[0], "ctx", axis=0, tiled=True)
    grad_w_down = jnp.einsum("tf,td->fd", ffn_hidden, grad_rows, preferred_element_type=jnp.float32)
    grad_hidden_ffn = jnp.einsum(
        "td,fd->tf", grad_rows, full_down, preferred_element_type=jnp.float32
    )
    up_value_gradient = (grad_hidden_ffn * gelu_gate).astype(jnp.bfloat16)
    grad_gate_value = gelu_back(grad_hidden_ffn * up_value)[0].astype(jnp.bfloat16)
    grad_w_gate = jnp.einsum(
        "td,tf->df", ffn_rows, grad_gate_value, preferred_element_type=jnp.float32
    )
    grad_w_up = jnp.einsum(
        "td,tf->df", ffn_rows, up_value_gradient, preferred_element_type=jnp.float32
    )
    ffn_normed_term = jnp.einsum(
        "tf,df->td", grad_gate_value, full_gate, preferred_element_type=jnp.float32
    )
    ffn_normed_term = ffn_normed_term + jnp.einsum(
        "tf,df->td", up_value_gradient, full_up, preferred_element_type=jnp.float32
    )
    grad_normed_ffn = lax.psum_scatter(ffn_normed_term, "ctx", scatter_dimension=0, tiled=True)
    grad_residual_norm, grad_ffn_gain = ffn_back(grad_normed_ffn)
    grad_residual = cotangent[0].astype(jnp.float32) + grad_residual_norm
    ffn_sums = (
        lax.psum_scatter(
            grad_w_gate.astype(jnp.bfloat16), ("dp", "fsdp"), scatter_dimension=0, tiled=True
        ).astype(jnp.float32),
        lax.psum_scatter(
            grad_w_up.astype(jnp.bfloat16), ("dp", "fsdp"), scatter_dimension=0, tiled=True
        ).astype(jnp.float32),
        lax.psum_scatter(
            grad_w_down.astype(jnp.bfloat16), ("dp", "fsdp"), scatter_dimension=1, tiled=True
        ).astype(jnp.float32),
    )
    branch_rows = lax.all_gather(grad_residual.astype(jnp.bfloat16), "ctx", axis=0, tiled=True)
    grad_w_attn_out = jnp.einsum(
        "ti,td->id", attended_low, branch_rows, preferred_element_type=jnp.float32
    )
    grad_attended = jnp.einsum(
        "td,id->ti", branch_rows, full_attn_out, preferred_element_type=jnp.float32
    )
    grad_attended = grad_attended.astype(jnp.bfloat16).reshape(seq_len, heads_here, DH)

    def backward_block(operands):
        start, block_total = operands
        one_hot, same_doc = block_masks(segment_row, position_row, start)
        query_block = lax.dynamic_slice_in_dim(queries, start, QB, 0)
        grad_part = lax.dynamic_slice_in_dim(grad_attended, start, QB, 0)
        attention_scores = block_scores(query_block, key_rows, table_local, one_hot, same_doc)
        weights = jnp.exp(attention_scores - block_total)
        prob_low = weights.astype(jnp.bfloat16)
        grad_probs = jnp.einsum(
            "ihd,jhd->hij", grad_part, value_rows, preferred_element_type=jnp.float32
        )
        centred = grad_probs - jnp.sum(weights * grad_probs, axis=-1, keepdims=True)
        grad_scores = (weights * centred).astype(jnp.bfloat16)
        grad_query_part = jnp.einsum(
            "hij,jhd->ihd", grad_scores, key_rows, preferred_element_type=jnp.float32
        )
        grad_key_part = jnp.einsum(
            "hij,ihd->jhd", grad_scores, query_block, preferred_element_type=jnp.float32
        )
        grad_value_part = jnp.einsum(
            "hij,ihd->jhd", prob_low, grad_part, preferred_element_type=jnp.float32
        )
        grad_bias_part = jnp.einsum(
            "hij,bij->bh", grad_scores, one_hot, preferred_element_type=jnp.float32
        )
        return (grad_query_part, grad_key_part, grad_value_part, grad_bias_part)

    query_blocks, key_blocks, value_blocks, bias_blocks = lax.map(
        backward_block, (starts, log_total)
    )
    grad_queries_low = query_blocks.reshape(seq_len, heads_here * DH).astype(jnp.bfloat16)
    grad_keys_low = (
        jnp.sum(key_blocks, axis=0).reshape(seq_len, heads_here * DH).astype(jnp.bfloat16)
    )
    grad_values_low = (
        jnp.sum(value_blocks, axis=0).reshape(seq_len, heads_here * DH).astype(jnp.bfloat16)
    )
    grad_w_query = jnp.einsum(
        "td,te->de", normed_rows, grad_queries_low, preferred_element_type=jnp.float32
    )
    grad_w_key = jnp.einsum(
        "td,te->de", normed_rows, grad_keys_low, preferred_element_type=jnp.float32
    )
    grad_w_value = jnp.einsum(
        "td,te->de", normed_rows, grad_values_low, preferred_element_type=jnp.float32
    )
    normed_term = jnp.einsum(
        "te,de->td", grad_queries_low, full_query, preferred_element_type=jnp.float32
    )
    normed_term = normed_term + jnp.einsum(
        "te,de->td", grad_keys_low, full_key, preferred_element_type=jnp.float32
    )
    normed_term = normed_term + jnp.einsum(
        "te,de->td", grad_values_low, full_value, preferred_element_type=jnp.float32
    )
    grad_normed = lax.psum_scatter(
        normed_term.astype(jnp.bfloat16), "ctx", scatter_dimension=0, tiled=True
    ).astype(jnp.float32)
    token_norm_gradient, grad_attn_gain = attn_back(grad_normed)
    grad_tokens = grad_residual + token_norm_gradient
    attn_sums = (
        lax.psum_scatter(
            grad_w_query.astype(jnp.bfloat16), ("dp", "fsdp"), scatter_dimension=0, tiled=True
        ).astype(jnp.float32),
        lax.psum_scatter(
            grad_w_key.astype(jnp.bfloat16), ("dp", "fsdp"), scatter_dimension=0, tiled=True
        ).astype(jnp.float32),
        lax.psum_scatter(
            grad_w_value.astype(jnp.bfloat16), ("dp", "fsdp"), scatter_dimension=0, tiled=True
        ).astype(jnp.float32),
        lax.psum_scatter(
            grad_w_attn_out.astype(jnp.bfloat16), ("dp", "fsdp"), scatter_dimension=1, tiled=True
        ).astype(jnp.float32),
    )
    bias_sum = jnp.sum(bias_blocks, axis=0)
    table_term = lax.dynamic_update_slice(
        jnp.zeros((NB, H), jnp.float32), bias_sum, (jnp.int32(0), head_start)
    )
    small_sums = (
        lax.psum_scatter(grad_attn_gain, ("dp", "ctx", "fsdp"), scatter_dimension=0, tiled=True),
        lax.psum_scatter(grad_ffn_gain, ("dp", "ctx", "fsdp"), scatter_dimension=0, tiled=True),
        lax.psum_scatter(
            table_term.reshape(NB * H), ("dp", "ctx", "fsdp"), scatter_dimension=0, tiled=True
        ),
    )
    return (
        result[None].astype(jnp.bfloat16),
        grad_tokens[None],
        small_sums[0],
        attn_sums[0],
        attn_sums[1],
        attn_sums[2],
        attn_sums[3],
        small_sums[2],
        small_sums[1],
        ffn_sums[0],
        ffn_sums[1],
        ffn_sums[2],
    )


def plain_solution(mesh):
    in_specs = (
        P(("dp", "fsdp"), "ctx", None),
        P(("dp", "fsdp"), None),
        P(("dp", "fsdp"), None),
        P(("dp", "ctx", "fsdp")),
        P(("dp", "fsdp"), "ctx"),
        P(("dp", "fsdp"), "ctx"),
        P(("dp", "fsdp"), "ctx"),
        P("ctx", ("dp", "fsdp")),
        P(("dp", "ctx", "fsdp")),
        P(("dp", "ctx", "fsdp")),
        P(("dp", "fsdp"), "ctx"),
        P(("dp", "fsdp"), "ctx"),
        P("ctx", ("dp", "fsdp")),
        P(("dp", "fsdp"), "ctx", None),
    )
    out_specs = (
        P(("dp", "fsdp"), "ctx", None),
        P(("dp", "fsdp"), "ctx", None),
        P(("dp", "ctx", "fsdp")),
        P(("dp", "fsdp"), "ctx"),
        P(("dp", "fsdp"), "ctx"),
        P(("dp", "fsdp"), "ctx"),
        P("ctx", ("dp", "fsdp")),
        P(("dp", "ctx", "fsdp")),
        P(("dp", "ctx", "fsdp")),
        P(("dp", "fsdp"), "ctx"),
        P(("dp", "fsdp"), "ctx"),
        P("ctx", ("dp", "fsdp")),
    )
    return jax.shard_map(
        plain_on_device, mesh=mesh, in_specs=in_specs, out_specs=out_specs, check_vma=False
    )


def solution(mesh):
    if 2048 // (mesh.shape["dp"] * mesh.shape["fsdp"]) % 128 or mesh.shape["fsdp"] != 2 or mesh.shape["ctx"] != 4:
        return plain_solution(mesh)
    tokens = P(("dp", "fsdp"), "ctx", None)
    line = P(("dp", "fsdp"), None)
    every = P(("dp", "ctx", "fsdp"))
    into = P(("dp", "fsdp"), "ctx")
    back = P("ctx", ("dp", "fsdp"))
    return jax.shard_map(
        functools.partial(on_device, mesh.shape["dp"]),
        mesh=mesh,
        in_specs=(tokens, line, line, every, into, into, into, back, every, every, into, into, back, tokens),
        out_specs=(tokens, tokens, every, into, into, into, back, every, every, into, into, back),
        check_vma=False,
    )
```

```python
import functools

import jax
import jax.numpy as jnp
from jax import lax
from jax.experimental import pallas as pl
from jax.experimental.pallas import tpu as pltpu
from jax.sharding import PartitionSpec as P

H = 32
DH = 64
NB = 32
EPSILON = 1e-06
THRESHOLDS = (12, 16, 23, 32, 46, 64, 91)
MASKED = -1e30
BF = jnp.bfloat16
F32 = jnp.float32
ANY = pl.BlockSpec(memory_space=pl.ANY)
VM = pl.BlockSpec(memory_space=pltpu.VMEM)
MESH = pl.DeviceIdType.MESH
DMA = pltpu.SemaphoreType.DMA


class Place:
    def __init__(self):
        self.z = lax.axis_index("dp")
        self.c = lax.axis_index("ctx")
        self.y = lax.axis_index("fsdp")
        self.x = self.c // 2
        self.k = self.c % 2

    def device(self, z=None, x=None, k=None, y=None):
        z = self.z if z is None else z
        x = self.x if x is None else x
        k = self.k if k is None else k
        y = self.y if y is None else y
        return {"dp": z, "ctx": x * 2 + k, "fsdp": y}

    def x_peer(self):
        return self.device(x=1 - self.x)

    def y_peer(self):
        return self.device(y=1 - self.y)

    def core_peer(self):
        return self.device(k=1 - self.k)


def block_of(x, k, y):
    return y * 4 + x * 2 + k


def remote(src, dst, send_sem, recv_sem, device):
    return pltpu.make_async_remote_copy(
        src_ref=src,
        dst_ref=dst,
        send_sem=send_sem,
        recv_sem=recv_sem,
        device_id=device,
        device_id_type=MESH,
    )


def greet(devices):
    barrier = pltpu.get_barrier_semaphore()
    for device in devices:
        pl.semaphore_signal(barrier, inc=1, device_id=device, device_id_type=MESH)
    pl.semaphore_wait(barrier, len(devices))


class ActGather:
    def __init__(self, me, own, out, send, recv, local, cut=None):
        self.me, self.own, self.out = me, own, out
        self.send, self.recv, self.local = send, recv, local
        rows = own.shape[0]
        cut = cut or rows // 2
        self.halves = (pl.ds(0, cut), pl.ds(cut, rows - cut))

    def part(self, ref, block, h):
        return ref.at[block, self.halves[h]]

    def copy(self, i):
        me = self.me
        x, k, y = me.x, me.k, me.y
        own = block_of(x, k, y)
        if i == 0:
            src, dst, dev = self.own.at[self.halves[0]], self.part(self.out, own, 0), me.x_peer()
        elif i == 1:
            src, dst, dev = self.own.at[self.halves[1]], self.part(self.out, own, 1), me.y_peer()
        elif i == 2:
            src, dst, dev = self.own.at[self.halves[0]], self.part(self.out, own, 0), me.y_peer()
        elif i == 3:
            b = block_of(1 - x, k, y)
            src, dst, dev = self.part(self.out, b, 0), self.part(self.out, b, 0), me.y_peer()
        elif i == 4:
            src, dst, dev = self.own.at[self.halves[1]], self.part(self.out, own, 1), me.x_peer()
        elif i == 5:
            b = block_of(x, k, 1 - y)
            src, dst, dev = self.part(self.out, b, 1), self.part(self.out, b, 1), me.x_peer()
        elif i == 6:
            src, dst, dev = self.own, self.out.at[own], me.core_peer()
        else:
            px, py, h = ((1, 0, 0), (0, 1, 1), (0, 1, 0), (1, 1, 0), (1, 0, 1), (1, 1, 1))[i - 7]
            b = block_of(1 - x if px else x, k, 1 - y if py else y)
            src, dst, dev = self.part(self.out, b, h), self.part(self.out, b, h), me.core_peer()
        return remote(src, dst, self.send.at[i], self.recv.at[i], dev)

    def start_x(self):
        for i in (0, 4, 6):
            self.copy(i).start()
        own = block_of(self.me.x, self.me.k, self.me.y)
        pltpu.make_async_copy(self.own, self.out.at[own], self.local).start()

    def start_y(self):
        for i in (1, 2):
            self.copy(i).start()

    def start(self):
        self.start_x()
        self.start_y()

    def onward(self, *steps):
        for i, after in steps:
            self.copy(i).wait_recv()
            if after:
                self.copy(after).start()
            self.copy(i + 7).start()

    def forward(self):
        self.onward((0, 3), (1, 5))

    def forward_core(self):
        self.onward((2, 0), (4, 0), (3, 0), (5, 0))

    def land(self, *pieces):
        for i in pieces:
            self.copy(i).wait_recv()

    def placed(self):
        own = block_of(self.me.x, self.me.k, self.me.y)
        pltpu.make_async_copy(self.own, self.out.at[own], self.local).wait()

    def sent(self):
        for i in range(13):
            self.copy(i).wait_send()

    def finish(self):
        self.land(*range(6, 13))
        self.placed()
        self.sent()


def gather_sems():
    return [DMA((13,)), DMA((13,)), DMA]


class ActReduce:
    def __init__(self, me, peer_out, core_in, mine, a_y, b_x, a_x, b_y, send, recv):
        self.me, self.peer_out, self.core_in, self.mine = me, peer_out, core_in, mine
        self.a_y, self.b_x, self.a_x, self.b_y = a_y, b_x, a_x, b_y
        self.send, self.recv = send, recv
        self.half = mine.shape[1] // 2

    def place(self, j):
        x, y = self.me.x, self.me.y
        return jnp.where(j % 2 == 0, 1 - x, x), jnp.where(j < 2, 1 - y, y)

    def core_copy(self, j):
        return remote(
            self.peer_out.at[j % 2], self.core_in.at[j], self.send.at[j], self.recv.at[j], self.me.core_peer()
        )

    def rows(self, h):
        return pl.ds(h * self.half, self.half)

    def add(self, slot, h, extra=None):
        def body(i, carry):
            r = pl.ds(pl.multiple_of(h * self.half + i * 16, 16), 16)
            total = self.mine[slot, r, :].astype(F32) + self.core_in[slot, r, :].astype(F32)
            if extra is not None:
                q = pl.ds(pl.multiple_of(i * 16, 16), 16)
                total = total + extra[0, q, :].astype(F32)
            self.mine[slot, r, :] = total.astype(BF)
            return carry

        lax.fori_loop(0, self.half // 16, body, 0)

    def copy(self, name):
        xp, yp = self.me.x_peer(), self.me.y_peer()
        slot, h, dst, i, dev = {
            "ay0": (0, 0, self.a_y.at[0], 4, yp),
            "ay1": (1, 0, self.a_y.at[1], 5, yp),
            "bx0": (0, 1, self.b_x.at[0], 6, xp),
            "bx1": (2, 1, self.b_x.at[1], 7, xp),
            "ax": (2, 0, self.a_x, 8, xp),
            "by": (1, 1, self.b_y, 9, yp),
        }[name]
        return remote(self.mine.at[slot, self.rows(h)], dst, self.send.at[i], self.recv.at[i], dev)

    def first_sends(self, j):
        for name in (("ay0", "bx0"), ("ay1",), ("bx1",))[j]:
            self.copy(name).start()

    def loop(self, make, send=True, first=0, last=4, hooks=()):
        def ready(j):
            self.core_copy(j).wait_recv()
            if j < 2:
                self.add(j, 0)
            if j != 1:
                self.add(j, 1)
            if send:
                self.first_sends(j)

        def body(j, carry):
            ox, oy = self.place(j)

            @pl.when(j >= 2)
            def _():
                self.core_copy(j - 2).wait_send()

            self.peer_out[j % 2] = make(block_of(ox, 1 - self.me.k, oy), 2 * j)
            self.core_copy(j).start()
            for i in range(3):

                @pl.when(j == i + 1)
                def _():
                    ready(i)

            self.mine[j] = make(block_of(ox, self.me.k, oy), 2 * j + 1)

            for i, hook in hooks:

                @pl.when(j == i)
                def _():
                    hook()

            return carry

        lax.fori_loop(first, last, body, 0)

    def second(self):
        self.copy("ay0").wait_recv()
        self.add(2, 0, self.a_y)
        self.copy("ax").start()
        self.copy("bx0").wait_recv()
        self.add(1, 1, self.b_x)
        self.copy("by").start()

    def arrive(self):
        self.core_copy(3).wait_recv()
        for name in ("ay1", "bx1", "ax", "by"):
            self.copy(name).wait_recv()

    def total(self, h, i):
        r = pl.ds(pl.multiple_of(h * self.half + i * 16, 16), 16)
        q = pl.ds(pl.multiple_of(i * 16, 16), 16)
        total = self.mine[3, r, :].astype(F32) + self.core_in[3, r, :].astype(F32)
        if h == 0:
            return total + self.a_y[1, q, :].astype(F32) + self.a_x[q, :].astype(F32)
        return total + self.b_x[1, q, :].astype(F32) + self.b_y[q, :].astype(F32)

    def finish(self):
        for j in (2, 3):
            self.core_copy(j).wait_send()
        for name in ("ay0", "ay1", "bx0", "bx1", "ax", "by"):
            self.copy(name).wait_send()


def reduce_scratch(rows, width):
    half = rows // 2
    return [
        pltpu.VMEM((2, rows, width), BF),
        pltpu.VMEM((4, rows, width), BF),
        pltpu.VMEM((4, rows, width), BF),
        pltpu.VMEM((2, half, width), BF),
        pltpu.VMEM((2, half, width), BF),
        pltpu.VMEM((half, width), BF),
        pltpu.VMEM((half, width), BF),
        DMA((10,)),
        DMA((10,)),
    ]


TQ = 256


def softmax_tile(q, k, v, bias, same):
    s = lax.dot_general(q, k, (((1,), (1,)), ((), ())), preferred_element_type=F32) + bias
    s = jnp.where(same, s, MASKED)
    e = jnp.exp(s - jnp.max(s, axis=-1, keepdims=True))
    pb = (e * (1.0 / jnp.sum(e, axis=-1, keepdims=True))).astype(BF)
    return pb, jnp.dot(pb, v, preferred_element_type=F32).astype(BF)


class Line:
    def __init__(self, me, n, views, send_r, send_l, recv):
        self.me, self.n, self.views = me, n, views
        self.send_r, self.send_l, self.recv = send_r, send_l, recv

    def copies(self, t, yy, right):
        me = self.me
        dev = me.device(z=me.z + 1 if right else me.z - 1)
        sem = self.send_r if right else self.send_l
        return [
            remote(view, view, sem.at[t, yy, i], self.recv.at[t, yy, i], dev)
            for i, view in enumerate(self.views(t, yy))
        ]

    def send(self, t, yy, keep, start):
        for right in (True, False):
            go = (self.me.z + 1 <= self.n - 1) if right else (self.me.z >= 1)
            if keep[right] is not None:
                go = go & keep[right]

            @pl.when(go)
            def _():
                for copy in self.copies(t, yy, right):
                    if start:
                        copy.start()
                    else:
                        copy.wait_send()

    def own(self, yy):
        self.send(self.me.z, yy, {True: None, False: None}, True)

    def came(self, s):
        z, n = self.me.z, self.n
        return (
            (True, z - s, z - s >= 0, z + 1 <= n - 1),
            (False, z + s, z + s <= n - 1, z >= 1),
        )

    def pump(self, s, yy):
        for right, t, here, on in self.came(s):

            @pl.when(here & on)
            def _():
                for copy in self.copies(t, yy, right):
                    copy.wait_recv()
                    copy.start()

    def land(self, yys):
        for s in range(1, self.n):
            for yy in yys:
                for right, t, here, on in self.came(s):

                    @pl.when(here & jnp.logical_not(on))
                    def _():
                        for copy in self.copies(t, yy, right):
                            copy.wait_recv()

    def finish(self):
        for yy in range(2):
            self.send(self.me.z, yy, {True: None, False: None}, False)
            for s in range(1, self.n):
                for right, t, here, on in self.came(s):

                    @pl.when(here & on)
                    def _():
                        for copy in self.copies(t, yy, right):
                            copy.wait_send()


def line_sems(n, parts):
    return [DMA((n, 2, parts))] * 3


def forward_kernel(
    n, length, wq, wk, wv, wo, wg, wu, wd, cot, xin, seg_row, gain_a, gain_f, table_row,
    wqkv, wof, wg1, wd1, wg2, wd2, a1, qkv, o, p, mid, a2all, gall, m1, dgu1, gwf1, gain1, gain2,
    st_in, st_o, st_1, st_d1, st_2, st_d2, small, seg, smalls, segs, segt, xv, wqkv_v, wo_v, qkv_v, o_v, toep, pbuf, a2, wg1_v, wd1_v, gw_v, acc,
    y_send, y_recv, y_local, s_send, s_recv, s2_send, s2_recv, s_local, c_local, p_sem, f_sem,
    *rest,
):
    red_scratch, f1_sems, f2_sems, in_sems, wo_sems = rest[0:9], rest[9:12], rest[12:15], rest[15:18], rest[18:21]
    x_sems, g_sems, a_sems = rest[21:24], rest[24:27], rest[27:30]
    me = Place()
    z, y = me.z, me.y
    rows, width = xin.shape
    piece_rows = wq.shape[0]
    heads = wq.shape[1] // 2
    hid = wg.shape[1] // 2
    h1 = wd1.shape[0]
    h2 = hid - h1
    group = [
        me.device(x=ox, k=ok, y=oy)
        for ox in (me.x, 1 - me.x)
        for ok in (me.k, 1 - me.k)
        for oy in (me.y, 1 - me.y)
    ][1:]
    others = [me.device(z=lax.rem(z + s, n)) for s in range(1, n)]
    greet(group + others)
    small[...] = jnp.zeros_like(small)
    share = gain_a.shape[1]
    for yy in range(2):

        @pl.when(y == yy)
        def _():
            for i, ref in enumerate((gain_a, gain_f)):
                at = i * 128 + yy * share
                small[:, at : at + share] = jnp.broadcast_to(ref[...].astype(F32), (8, share))

    small[:, 256 : 256 + table_row.shape[1]] = jnp.broadcast_to(table_row[...].astype(F32), (8, table_row.shape[1]))
    seg[...] = jnp.broadcast_to(seg_row[...], seg.shape)

    def piece(t, yy):
        return pl.ds(pl.multiple_of((t * 2 + yy) * piece_rows, piece_rows), piece_rows)

    row = piece(z, y)

    def y_copies(yh):
        col = pl.ds(pl.multiple_of(yh * heads, heads), heads)
        at1 = pl.ds(pl.multiple_of(yh * hid, 128), h1)
        at2 = pl.ds(pl.multiple_of(yh * hid + h1, 128), h2)
        return [
            (wq.at[:, col], wqkv.at[row, pl.ds(0, heads)]),
            (wk.at[:, col], wqkv.at[row, pl.ds(heads, heads)]),
            (wv.at[:, col], wqkv.at[row, pl.ds(2 * heads, heads)]),
            (wo.at[col, :], wof.at[:, row]),
            (wg.at[:, at1], wg1.at[row, pl.ds(0, h1)]),
            (wu.at[:, at1], wg1.at[row, pl.ds(h1, h1)]),
            (wd.at[at1, :], wd1.at[:, row]),
            (wg.at[:, at2], wg2.at[row, pl.ds(0, h2)]),
            (wu.at[:, at2], wg2.at[row, pl.ds(h2, h2)]),
            (wd.at[at2, :], wd2.at[:, row]),
        ]

    sends = [
        remote(src, dst, y_send.at[i], y_recv.at[i], me.y_peer())
        for i, (src, dst) in enumerate(y_copies(1 - y))
    ]
    staged = [
        st_in.at[:, pl.ds(0, heads)],
        st_in.at[:, pl.ds(heads, heads)],
        st_in.at[:, pl.ds(2 * heads, heads)],
        st_o,
        st_1.at[:, pl.ds(0, h1)],
        st_1.at[:, pl.ds(h1, h1)],
        st_d1,
        st_2.at[:, pl.ds(0, h2)],
        st_2.at[:, pl.ds(h2, h2)],
        st_d2,
    ]
    takes = [
        pltpu.make_async_copy(src, mid_ref, y_local.at[i])
        for i, ((src, dst), mid_ref) in enumerate(zip(y_copies(y), staged))
    ]
    keeps = [
        pltpu.make_async_copy(mid_ref, dst, y_local.at[i])
        for i, ((src, dst), mid_ref) in enumerate(zip(y_copies(y), staged))
    ]
    me_small = z * 8 + me.c * 2 + y
    small_local = pltpu.make_async_copy(small, smalls.at[me_small], s_local.at[0])
    seg_local = pltpu.make_async_copy(seg, segs.at[y], s_local.at[1])
    small_sends = [
        remote(small, smalls.at[me_small], s_send.at[i], s_recv.at[i], dev) for i, dev in enumerate(group)
    ]
    seg_send = remote(seg, segs.at[y], s_send.at[7], s_recv.at[7], me.y_peer())
    attn = Line(me, n, lambda t, yy: (wqkv.at[piece(t, yy), :],), *in_sems)
    attn_o = Line(me, n, lambda t, yy: (wof.at[:, piece(t, yy)],), *wo_sems)
    f1 = Line(me, n, lambda t, yy: (wg1.at[piece(t, yy), :], wd1.at[:, piece(t, yy)]), *f1_sems)
    f2 = Line(me, n, lambda t, yy: (wg2.at[piece(t, yy), :], wd2.at[:, piece(t, yy)]), *f2_sems)
    xact = ActGather(me, xin, xv, *x_sems, cut=5 * rows // 16)
    gact = ActGather(me, cot, gall, *g_sems, cut=rows // 4)

    for i in range(4):
        takes[i].start()
        sends[i].start()
    small_local.start()
    seg_local.start()
    for copy in small_sends:
        copy.start()
    seg_send.start()
    xact.start_x()
    for i in range(4, 10):
        takes[i].start()
    for i in range(10):
        takes[i].wait()
        keeps[i].start()
    for i in range(4):
        keeps[i].wait()
    attn.own(y)
    for i in range(4):
        sends[i].wait_recv()
    attn.own(1 - y)
    xact.start_y()
    small_local.wait()
    for copy in small_sends:
        copy.wait_recv()
    block8 = smalls.at[pl.ds(pl.multiple_of(z * 8, 8), 8)]
    small_z = [remote(block8, block8, s2_send.at[i], s2_recv.at[i], dev) for i, dev in enumerate(others)]
    for copy in small_z:
        copy.start()
    xact.onward((0, 3))
    attn.pump(1, y)
    attn.pump(1, 1 - y)
    xact.onward((1, 5))
    for i in range(4, 10):
        sends[i].start()
    gact.start()

    for copy in small_z:
        copy.wait_recv()
    for j in range(4 * n):
        gain1[:, 128 * j : 128 * j + 128] = (smalls[2 * j, :, 0:128] + smalls[2 * j + 1, :, 0:128])[0:1]
        gain2[:, 128 * j : 128 * j + 128] = (smalls[2 * j, :, 128:256] + smalls[2 * j + 1, :, 128:256])[0:1]
    seg_local.wait()
    seg_send.wait_recv()
    for s in range(2):
        wide = jnp.concatenate([segs[s]] * 16, axis=0).astype(F32)
        segt[s] = wide.T
    attn.pump(2, y)
    xact.onward((2, 0), (4, 0))
    attn.pump(2, 1 - y)
    attn_o.own(y)
    attn_o.own(1 - y)
    for i in range(4, 7):
        keeps[i].wait()
    f1.own(y)
    offset = lax.broadcasted_iota(jnp.int32, (NB, 2 * length), 1) - length
    far = jnp.abs(offset)
    bucket = jnp.where(far < 8, far, 8 + sum((far >= t).astype(jnp.int32) for t in THRESHOLDS))
    bucket = bucket + 16 * (offset > 0).astype(jnp.int32)
    own_bucket = bucket == lax.broadcasted_iota(jnp.int32, (NB, 2 * length), 0)
    table = smalls[:, 0, 256:384]
    lane = lax.broadcasted_iota(jnp.int32, (NB, 128), 1)
    local_heads = heads // DH
    for lh in range(local_heads):
        head = (me.c * 2 + y) * local_heads + lh
        value = jnp.sum(jnp.where(lane == head, table, 0.0), axis=1, keepdims=True)
        fvec = jnp.sum(jnp.where(own_bucket, value, 0.0), axis=0, keepdims=True)
        toep[lh] = pltpu.roll(jnp.broadcast_to(fvec, (TQ, 2 * length)), 0, 1, stride=1, stride_axis=0)
    xact.onward((3, 0), (5, 0))
    xact.finish()

    def norm_rows(i, carry):
        r = pl.ds(pl.multiple_of(lax.rem(i, rows // 32) * 32, 32), 32)
        b = i // (rows // 32)
        xf = xv[b, r, :].astype(F32)
        inv = lax.rsqrt(jnp.mean(xf * xf, axis=-1, keepdims=True) + EPSILON)
        xv[b, r, :] = (xf * inv * gain1[...]).astype(BF)
        return carry

    lax.fori_loop(0, 4 * rows // 32, norm_rows, 0)
    for i in range(4, 7):
        sends[i].wait_recv()
    f1.own(1 - y)
    attn_o.pump(1, y)
    attn_o.pump(1, 1 - y)
    lax.fori_loop(4 * rows // 32, 8 * rows // 32, norm_rows, 0)
    a1_out = pltpu.make_async_copy(xv, a1, c_local.at[0])
    a1_out.start()
    attn_o.pump(2, y)
    attn_o.pump(2, 1 - y)
    attn.land((y, 1 - y))
    w_in = pltpu.make_async_copy(wqkv, wqkv_v, c_local.at[1])
    w_in.start()
    w_in.wait()

    def project(b, carry):
        r = pl.ds(pl.multiple_of(b * rows, rows), rows)
        qkv_v[r, :] = jnp.dot(xv[b], wqkv_v[...], preferred_element_type=F32).astype(BF)
        return carry

    lax.fori_loop(0, 8, project, 0)
    qkv_out = pltpu.make_async_copy(qkv_v, qkv, c_local.at[3])
    qkv_out.start()
    f1.pump(1, y)
    tiles = length // TQ

    def p_copy(slot, head, t):
        return pltpu.make_async_copy(
            pbuf.at[slot], p.at[head, pl.ds(t * TQ, TQ)], p_sem.at[slot]
        )

    def sequence(s, fresh, between):
        base = pl.multiple_of(s * length, length)
        seq = pl.ds(base, length)

        def head_pair(hp, carry):
            def lanes(part):
                return pl.ds(pl.multiple_of(part * heads + hp * 2 * DH, 128), 2 * DH)

            k2 = qkv_v[seq, lanes(1)]
            v2 = qkv_v[seq, lanes(2)]
            for t in range(tiles):
                r = pl.ds(pl.multiple_of(base + t * TQ, TQ), TQ)
                q2 = qkv_v[r, lanes(0)]
                same = segt[s, t * TQ : (t + 1) * TQ, 0:1] == segs[s, 0:1, :].astype(F32)
                outs = []
                for h in range(2):
                    cut = slice(h * DH, (h + 1) * DH)
                    pb, ot = softmax_tile(
                        q2[:, cut], k2[:, cut], v2[:, cut],
                        toep[hp * 2 + h, :, length - t * TQ : 2 * length - t * TQ], same,
                    )
                    head = s * local_heads + hp * 2 + h
                    if fresh and t == 0:

                        @pl.when(hp > 0)
                        def _():
                            p_copy(h, head, t).wait()
                    else:
                        p_copy(h, head, t).wait()
                    pbuf[h] = pb
                    p_copy(h, head, t).start()
                    outs.append(ot)
                o_v[r, pl.ds(pl.multiple_of(hp * 2 * DH, 128), 2 * DH)] = jnp.concatenate(outs, axis=1)

            @pl.when(hp == 0)
            def _():
                between()

            return carry

        lax.fori_loop(0, local_heads // 2, head_pair, 0)

    def attn_term(block, i):
        r = pl.ds(pl.multiple_of(block * rows, rows), rows)
        return jnp.dot(o_v[r, :], wo_v[...], preferred_element_type=F32).astype(BF)

    red = ActReduce(me, *red_scratch)
    def beside_first():
        f1.pump(1, 1 - y)
        gact.forward()

    def beside_second():
        for i in range(7, 10):
            keeps[i].wait()
            sends[i].wait_recv()
        f2.own(y)
        f2.own(1 - y)
        gact.forward_core()

    sequence(1 - y, True, beside_first)
    attn_o.land((y, 1 - y))
    wo_in = pltpu.make_async_copy(wof, wo_v, c_local.at[2])
    wo_in.start()
    f1.pump(2, y)
    f1.pump(2, 1 - y)
    wo_in.wait()
    red.loop(attn_term, first=0, last=2)
    sequence(y, False, beside_second)
    for slot in range(2):
        p_copy(slot, 0, 0).wait()
    o_out = pltpu.make_async_copy(o_v, o, c_local.at[4])
    o_out.start()
    red.loop(attn_term, first=2, last=4)
    red.second()
    f2.pump(1, y)
    red.arrive()

    half = rows // 2
    for h in range(2):

        def body(i, carry):
            rr = pl.ds(pl.multiple_of(h * half + i * 16, 16), 16)
            m = xin[rr, :].astype(F32) + red.total(h, i)
            mid[rr, :] = m
            inv = lax.rsqrt(jnp.mean(m * m, axis=-1, keepdims=True) + EPSILON)
            a2[rr, :] = (m * inv * gain2[...]).astype(BF)
            return carry

        lax.fori_loop(0, half // 16, body, 0)
    aact = ActGather(me, a2, a2all, *a_sems)
    aact.start()
    f2.pump(1, 1 - y)
    f1.land((y, 1 - y))

    def fetch(src, dst, i):
        return pltpu.make_async_copy(src, dst, f_sem.at[i])

    a1_out.wait()
    fetch(wg1, wg1_v, 0).start()
    fetch(wd1, wd1_v, 1).start()
    gact.finish()

    def block_at(i):
        ox, oy = red.place(3 - i // 2)
        return block_of(ox, jnp.where(i % 2 == 0, me.k, 1 - me.k), oy)

    def load_rows(i):
        slot = lax.rem(i, 2)
        b = block_at(i)
        return fetch(a2all.at[b], xv.at[slot], 2 + slot), fetch(gall.at[b], xv.at[2 + slot], 4 + slot)

    def first_units(j, last, carry):
        b = block_at(j)

        @pl.when(j < last)
        def _():
            for copy in load_rows(j + 1):
                copy.start()

        for copy in load_rows(j):
            copy.wait()
        slot = lax.rem(j, 2)
        acc[:, 0 : 2 * h1] = jnp.dot(xv[slot], wg1_v[...], preferred_element_type=F32)
        acc[:, 2 * h1 : 3 * h1] = lax.dot_general(
            xv[2 + slot], wd1_v[...], (((1,), (1,)), ((), ())), preferred_element_type=F32
        )

        def body(i, inner):
            rr = pl.ds(pl.multiple_of(i * 16, 16), 16)
            tr = pl.ds(pl.multiple_of(b * rows + i * 16, 16), 16)
            gate, up, gm = acc[rr, 0:h1], acc[rr, h1 : 2 * h1], acc[rr, 2 * h1 : 3 * h1]
            gelu, slope = gelu_parts(gate)
            wqkv_v[tr, 0:h1] = (gm * up * slope).astype(BF)
            wqkv_v[tr, h1 : 2 * h1] = (gm * gelu).astype(BF)
            qkv_v[tr, 0:h1] = (gelu * up).astype(BF)
            return inner

        lax.fori_loop(0, rows // 16, body, 0)
        return carry

    def units(first, last):
        for copy in load_rows(first):
            copy.start()
        lax.fori_loop(first, last, lambda j, carry: first_units(j, last - 1, carry), 0)

    aact.placed()
    qkv_out.wait()
    fetch(wg1, wg1_v, 0).wait()
    fetch(wd1, wd1_v, 1).wait()
    aact.land(6)
    units(0, 2)
    aact.forward()
    f2.pump(2, y)
    aact.onward((2, 0), (4, 0))
    aact.land(7, 8, 9, 11)
    units(2, 6)
    aact.onward((3, 0), (5, 0))
    aact.land(10, 12)
    f2.pump(2, 1 - y)
    units(6, 8)
    red.finish()
    kept = [fetch(wqkv_v.at[:, pl.ds(0, 2 * h1)], dgu1, 0), fetch(qkv_v.at[:, pl.ds(0, h1)], m1, 1)]
    for copy in kept:
        copy.start()

    def load_columns(i):
        slot = lax.rem(i, 2)
        at = pl.ds(pl.multiple_of(i * rows, rows), rows)
        here = pl.ds(pl.multiple_of(slot * rows, rows), rows)
        there = pl.ds(pl.multiple_of((2 + slot) * rows, rows), rows)
        return (
            fetch(a2all.at[:, :, at], xv.at[:, :, here], 2 + slot),
            fetch(gall.at[:, :, at], xv.at[:, :, there], 4 + slot),
        )

    for copy in load_columns(0):
        copy.start()

    def first_grads(i, carry):
        @pl.when(i < 2 * n - 1)
        def _():
            for copy in load_columns(i + 1):
                copy.start()

        for copy in load_columns(i):
            copy.wait()
        slot = lax.rem(i, 2)
        here = pl.ds(pl.multiple_of(slot * rows, rows), rows)
        there = pl.ds(pl.multiple_of((2 + slot) * rows, rows), rows)
        gw_v[i, :, 0 : 2 * h1] = lax.dot_general(
            xv[:, :, here].reshape(8 * rows, rows), wqkv_v[:, 0 : 2 * h1], (((0,), (0,)), ((), ())),
            preferred_element_type=F32,
        ).astype(BF)
        gw_v[i, :, 2 * h1 : 3 * h1] = lax.dot_general(
            xv[:, :, there].reshape(8 * rows, rows), qkv_v[:, 0:h1], (((0,), (0,)), ((), ())),
            preferred_element_type=F32,
        ).astype(BF)
        return carry

    lax.fori_loop(0, 2 * n, first_grads, 0)
    kept.append(fetch(gw_v, gwf1, 2))
    kept[2].start()
    aact.sent()
    f2.land((y, 1 - y))
    for line in (attn, attn_o, f1, f2):
        line.finish()
    for copy in small_sends:
        copy.wait_send()
    for copy in small_z:
        copy.wait_send()
    seg_send.wait_send()
    for copy in sends:
        copy.wait_send()
    o_out.wait()
    for copy in kept:
        copy.wait()


def forward(n, h1, wq, wk, wv, wo, wg, wu, wd, cot, xin, seg_row, gain_a, gain_f, table_row):
    rows, width = xin.shape
    heads = wq.shape[1] // 2
    hid = wg.shape[1] // 2
    length = seg_row.shape[1]
    small, seg = (8, 384), (8, length)
    local_heads = heads // DH
    tokens = 8 * rows
    shapes = [
        ((width, 3 * heads), BF),
        ((heads, width), BF),
        ((width, 2 * h1), BF),
        ((h1, width), BF),
        ((width, 2 * (hid - h1)), BF),
        ((hid - h1, width), BF),
        ((8, rows, width), BF),
        ((tokens, 3 * heads), BF),
        ((tokens, heads), BF),
        ((2 * local_heads, length, length), BF),
        ((rows, width), F32),
        ((8, rows, width), BF),
        ((8, rows, width), BF),
        ((tokens, h1), BF),
        ((tokens, 2 * h1), BF),
        ((2 * n, rows, 3 * h1), BF),
        ((1, width), F32),
        ((1, width), F32),
    ]
    scratch = [
        pltpu.VMEM((wq.shape[0], 3 * heads), BF),
        pltpu.VMEM((heads, wo.shape[1]), BF),
        pltpu.VMEM((wq.shape[0], 2 * h1), BF),
        pltpu.VMEM((h1, wd.shape[1]), BF),
        pltpu.VMEM((wq.shape[0], 2 * (hid - h1)), BF),
        pltpu.VMEM((hid - h1, wd.shape[1]), BF),
        pltpu.VMEM(small, F32),
        pltpu.VMEM(seg, jnp.int32),
        pltpu.VMEM((8 * n,) + small, F32),
        pltpu.VMEM((2,) + seg, jnp.int32),
        pltpu.VMEM((2, length, 128), F32),
        pltpu.VMEM((8, rows, width), BF),
        pltpu.VMEM((width, 3 * heads), BF),
        pltpu.VMEM((heads, width), BF),
        pltpu.VMEM((tokens, 3 * heads), BF),
        pltpu.VMEM((tokens, heads), BF),
        pltpu.VMEM((local_heads, TQ, 2 * length), F32),
        pltpu.VMEM((2, TQ, length), BF),
        pltpu.VMEM((rows, width), BF),
        pltpu.VMEM((width, 2 * h1), BF),
        pltpu.VMEM((h1, width), BF),
        pltpu.VMEM((2 * n, rows, 3 * h1), BF),
        pltpu.VMEM((rows, 3 * h1), F32),
        DMA((10,)), DMA((10,)), DMA((10,)), DMA((8,)), DMA((8,)), DMA((n - 1,)), DMA((n - 1,)), DMA((2,)),
        DMA((5,)), DMA((2,)), DMA((6,)),
    ] + reduce_scratch(rows, width) + line_sems(n, 2) * 2 + line_sems(n, 1) * 2 + gather_sems() * 3
    return pl.pallas_call(
        functools.partial(forward_kernel, n, length),
        out_shape=[jax.ShapeDtypeStruct(s, d) for s, d in shapes],
        in_specs=[ANY] * 7 + [VM] * 6,
        out_specs=[ANY] * 10 + [VM] + [ANY] * 5 + [VM] * 2,
        scratch_shapes=scratch,
        compiler_params=pltpu.CompilerParams(
            collective_id=0, has_side_effects=True, vmem_limit_bytes=64 << 20
        ),
        name="forward",
    )(wq, wk, wv, wo, wg, wu, wd, cot, xin, seg_row, gain_a, gain_f, table_row)


class LineSum:
    def __init__(self, me, n, views, from_left, from_right, stage, sems, stage_sem):
        self.me, self.n, self.views = me, n, views
        self.inbox = {True: from_left, False: from_right}
        self.stage, self.stage_sem = stage, stage_sem
        self.sends = {True: sems[0], False: sems[1]}
        self.recvs = {True: sems[2], False: sems[3]}

    def copies(self, t, yy, right):
        me = self.me
        dev = me.device(z=me.z + 1 if right else me.z - 1)
        return [
            remote(
                view, self.inbox[right].at[t, yy, i], self.sends[right].at[t, yy, i],
                self.recvs[right].at[t, yy, i], dev,
            )
            for i, view in enumerate(self.views(t * 2 + yy))
        ]

    def start(self, t, yy, right):
        for copy in self.copies(t, yy, right):
            copy.start()

    def take(self, t, yy, right):
        slot = 0 if right else 1
        return pltpu.make_async_copy(self.inbox[right].at[t, yy, 0], self.stage[slot], self.stage_sem.at[slot])

    def open(self, t, yy, right):
        self.copies(t, yy, right)[0].wait_recv()
        self.take(t, yy, right).start()

    def add(self, t, yy, right):
        self.take(t, yy, right).wait()
        view, stage = self.views(t * 2 + yy)[0], self.stage[0 if right else 1]

        def body(r, carry):
            rr = pl.ds(pl.multiple_of(r * 16, 16), 16)
            view[rr, :] = (view[rr, :].astype(F32) + stage[rr, :].astype(F32)).astype(BF)
            return carry

        lax.fori_loop(0, view.shape[0] // 16, body, 0)

    def first(self, t, yy):
        @pl.when((self.me.z == 0) & (t > 0))
        def _():
            self.start(t, yy, True)

        @pl.when((self.me.z == self.n - 1) & (t < self.n - 1))
        def _():
            self.start(t, yy, False)

    def pump(self, k, yy):
        z, n = self.me.z, self.n
        sides = (
            (True, z + k, (z + k <= n - 1) & (z > 0)),
            (False, z - k, (z - k >= 0) & (z < n - 1)),
        )
        for right, t, go in sides:

            @pl.when(go)
            def _():
                self.open(t, yy, right)

        for right, t, go in sides:

            @pl.when(go)
            def _():
                self.add(t, yy, right)
                self.start(t, yy, right)

    def own(self, yy):
        z = self.me.z
        sides = ((True, z > 0), (False, z < self.n - 1))
        for right, go in sides:

            @pl.when(go)
            def _():
                self.open(z, yy, right)

        for right, go in sides:

            @pl.when(go)
            def _():
                self.add(z, yy, right)

    def finish(self):
        z, n = self.me.z, self.n
        for yy in range(2):
            for k in range(1, n):

                @pl.when(z + k <= n - 1)
                def _():
                    for copy in self.copies(z + k, yy, True):
                        copy.wait_send()

                @pl.when(z - k >= 0)
                def _():
                    for copy in self.copies(z - k, yy, False):
                        copy.wait_send()


def far_first(n, z, i):
    slot = 0
    for a in range(n):
        order = sorted(range(n), key=lambda d: (-abs(d - a), d))
        for b in range(n):
            slot = slot + jnp.where((z == a) & (i == b), order[b], 0)
    return slot


def gelu_parts(gate):
    th = jnp.tanh(0.7978845608028654 * (gate + 0.044715 * gate * gate * gate))
    gelu = 0.5 * gate * (1.0 + th)
    slope = 0.5 * (1.0 + th) + 0.5 * gate * (1.0 - th * th) * 0.7978845608028654 * (
        1.0 + 3 * 0.044715 * gate * gate
    )
    return gelu, slope


def norm_back(ga, values, gain):
    inv = lax.rsqrt(jnp.mean(values * values, axis=-1, keepdims=True) + EPSILON)
    u = ga * gain
    corr = jnp.mean(u * values, axis=-1, keepdims=True) * inv * inv * inv
    return inv * u - values * corr, ga * (values * inv)


def backward_kernel(
    n, length, heads, hid, h1,
    wg1, wd1, wg2, wd2, m1, dgu1, gwf1, a2all, gall, p, a1, qkv, o, wqkv, wof, hidden, mid, cot, gain1, gain2,
    out, gx, fo1, fo2, bo, co, sums, dzall, e_left, e_right, f_left, f_right, b_left, b_right, c_left, c_right,
    wgu_v, wd_v, row_a, row_b, row_g, col_a, col_g, m, dgu, gw1, gw2, stage, gmid, dz, wqkv_v,
    pbuf, acc, dkt, dvt, diag, gg1, gg2, sv, sv_in, sv_z, free,
    load, p_sem, stage_sem, y_send, y_recv, y_local, sv_send, sv_recv, sz_send, sz_recv,
    *rest,
):
    red_scratch, dz_sems = rest[:9], rest[9:12]
    e_sems, f_sems, b_sems, c_sems = (rest[i : i + 4] for i in range(12, 28, 4))
    h2 = hid - h1
    me = Place()
    z, y = me.z, me.y
    rows, width = cot.shape
    group = [
        me.device(x=ox, k=ok, y=oy)
        for ox in (me.x, 1 - me.x)
        for ok in (me.k, 1 - me.k)
        for oy in (me.y, 1 - me.y)
    ][1:]
    others = [me.device(z=lax.rem(z + s, n)) for s in range(1, n)]
    greet(group + others)
    local_heads = heads // DH
    half = rows // 2

    def fetch(src, dst, i):
        return pltpu.make_async_copy(src, dst, load.at[i])

    red = ActReduce(me, *red_scratch)
    order = (1 - y, y)

    def line_sum(view, left, right, width, sems):
        stages = [stage.at[i, :, pl.ds(0, width)] for i in range(2)]
        return LineSum(me, n, lambda pc: [view(pc)], left, right, stages, sems, stage_sem)

    esum = line_sum(lambda pc: gw1.at[pc], e_left, e_right, 3 * h1, e_sems)
    fsum = line_sum(lambda pc: gw2.at[pc], f_left, f_right, 3 * h2, f_sems)

    def piece(pc):
        return pl.ds(pl.multiple_of(pc * rows, rows), rows)

    pair = 3 * 2 * DH
    bsum = line_sum(lambda pc: m.at[piece(pc), :], b_left, b_right, heads + pair, b_sems)
    csum = line_sum(lambda pc: dgu.at[piece(pc), pl.ds(3 * heads, pair)], c_left, c_right, pair, c_sems)

    def piece_at(i):
        return far_first(n, z, i // 2) * 2 + jnp.where(i % 2 == 0, 1 - y, y)

    w_loads = [
        fetch(gwf1, gw1, 0),
        fetch(wg2, wgu_v.at[:, pl.ds(2 * h1, 2 * h2)], 1),
        fetch(wd2, wd_v.at[pl.ds(h1, h2), :], 6),
        fetch(wg1, wgu_v.at[:, pl.ds(0, 2 * h1)], 7),
        fetch(dgu1, dgu.at[:, pl.ds(0, 2 * h1)], 8),
        fetch(wd1, wd_v.at[pl.ds(0, h1), :], 9),
        fetch(m1, m.at[:, pl.ds(0, h1)], 10),
    ]
    for copy in w_loads:
        copy.start()

    def block_at(i):
        j = i // 2
        ox, oy = red.place(j)
        return block_of(ox, jnp.where(i % 2 == 0, 1 - me.k, me.k), oy)

    fetch(a2all.at[block_at(0)], row_a, 2).start()
    fetch(gall.at[block_at(0)], row_g, 3).start()
    fetch(cot, row_b, 4).start()
    w_loads[0].wait()

    def first_slots(i, carry):
        pc = piece_at(i)
        esum.first(pc // 2, pc % 2)
        return carry

    lax.fori_loop(0, 2 * n, first_slots, 0)
    for copy in w_loads[1:3]:
        copy.wait()


    def make_ffn(block, i):
        fetch(a2all.at[block], row_a, 2).wait()
        acc[:, 0 : 2 * h2] = jnp.dot(row_a[...], wgu_v[:, 2 * h1 : 2 * hid], preferred_element_type=F32)

        @pl.when(i < 7)
        def _():
            fetch(a2all.at[block_at(i + 1)], row_a, 2).start()

        fetch(gall.at[block], row_g, 3).wait()
        acc[:, 2 * h2 : 3 * h2] = lax.dot_general(
            row_g[...], wd_v[h1:hid, :], (((1,), (1,)), ((), ())), preferred_element_type=F32
        )

        @pl.when(i < 7)
        def _():
            fetch(gall.at[block_at(i + 1)], row_g, 3).start()

        def body(r, carry):
            rr = pl.ds(pl.multiple_of(r * 16, 16), 16)
            tr = pl.ds(pl.multiple_of(block * rows + r * 16, 16), 16)
            gate, up, gm = acc[rr, 0:h2], acc[rr, h2 : 2 * h2], acc[rr, 2 * h2 : 3 * h2]
            gelu, slope = gelu_parts(gate)
            m[tr, h1:hid] = (gelu * up).astype(BF)
            dgu[tr, 2 * h1 : 2 * h1 + h2] = (gm * up * slope).astype(BF)
            dgu[tr, 2 * h1 + h2 : 2 * hid] = (gm * gelu).astype(BF)
            return carry

        lax.fori_loop(0, rows // 16, body, 0)

        @pl.when(i == 0)
        def _():
            for copy in w_loads[3:]:
                copy.wait()

        return lax.dot_general(
            dgu[piece(block), :], wgu_v[...], (((1,), (1,)), ((), ())), preferred_element_type=F32
        ).astype(BF)

    red.loop(make_ffn, hooks=((1, lambda: esum.pump(2, order[0])), (2, lambda: esum.pump(2, order[1]))))
    esum.pump(1, order[0])

    fetch(wof, row_g, 3).start()

    def columns(ref, i):
        return ref.at[:, :, piece(piece_at(i))]

    def load_columns(left, right, i):
        slot = lax.rem(i, 2)
        return fetch(columns(left, i), col_a.at[slot], 11 + slot), fetch(columns(right, i), col_g.at[slot], 13 + slot)

    def next_columns(left, right, i):
        @pl.when(i < 2 * n - 1)
        def _():
            for copy in load_columns(left, right, i + 1):
                copy.start()

        for copy in load_columns(left, right, i):
            copy.wait()

    for copy in load_columns(a2all, gall, 0):
        copy.start()

    def ffn_grads(i, carry):
        pc = piece_at(i)
        slot = lax.rem(i, 2)
        next_columns(a2all, gall, i)
        gw2[pc, :, 0 : 2 * h2] = lax.dot_general(
            col_a[slot].reshape(8 * rows, rows), dgu[:, 2 * h1 : 2 * hid], (((0,), (0,)), ((), ())),
            preferred_element_type=F32,
        ).astype(BF)
        gw2[pc, :, 2 * h2 : 3 * h2] = lax.dot_general(
            col_g[slot].reshape(8 * rows, rows), m[:, h1:hid], (((0,), (0,)), ((), ())),
            preferred_element_type=F32,
        ).astype(BF)
        fsum.first(pc // 2, pc % 2)
        return carry

    lax.fori_loop(0, n, ffn_grads, 0)
    red.second()
    esum.pump(1, order[1])
    fetch(qkv, wgu_v.at[:, pl.ds(0, 3 * heads)], 0).start()
    fetch(o, wgu_v.at[:, pl.ds(3 * heads, heads)], 6).start()
    red.arrive()

    gg2[...] = jnp.zeros_like(gg2)
    fetch(cot, row_b, 4).wait()
    for h in range(2):

        def body(i, carry):
            rr = pl.ds(pl.multiple_of(h * half + i * 16, 16), 16)
            back, gains = norm_back(red.total(h, i), mid[rr, :], gain2[...])
            gm = row_b[rr, :].astype(F32) + back
            gmid[rr, :] = gm
            dz[rr, :] = gm.astype(BF)
            gg2[...] += gains[:8] + gains[8:]
            return carry

        lax.fori_loop(0, half // 16, body, 0)
    act = ActGather(me, dz, dzall, *dz_sems)
    act.start()
    red.finish()

    def release():
        for i, dev in enumerate((me.x_peer(), me.y_peer(), me.core_peer())):
            pl.semaphore_signal(free.at[i], inc=1, device_id=dev, device_id_type=MESH)

    def claim():
        for i in range(3):
            pl.semaphore_wait(free.at[i], 1)

    release()
    lax.fori_loop(n, 2 * n, ffn_grads, 0)
    act.forward()

    claim()

    def make_out(block, i):
        return jnp.dot(m[piece(block), :], wd_v[...], preferred_element_type=F32).astype(BF)

    red.loop(make_out, send=False)
    def swap(views, box, i):
        out = remote(views(z * 2 + 1 - y)[0], box.at[y], y_send.at[i], y_recv.at[i], me.y_peer())
        keep = pltpu.make_async_copy(views(z * 2 + y)[0], box.at[y], y_local.at[i])
        return out, keep

    lines = (esum, fsum, bsum, csum)
    swaps = [swap(line.views, box, i) for i, (line, box) in enumerate(zip(lines, (fo1, fo2, bo, co)))]

    def settle(i):
        lines[i].own(order[0])
        swaps[i][0].start()
        lines[i].own(order[1])
        swaps[i][1].start()

    fsum.pump(2, order[0])
    act.onward((4, 0))
    act.placed()
    act.land(6, 7, 11)

    fetch(wof, row_g, 3).wait()
    slots = ((row_a, 2), (row_b, 4))

    def come(i):
        ox, oy = red.place(3 - i // 2)
        return block_of(ox, jnp.where(i % 2 == 0, me.k, 1 - me.k), oy)

    def project_back(first):
        for b, (buffer, sem) in enumerate(slots):
            fetch(dzall.at[come(first + b)], buffer, sem).start()
        for i in range(2):
            for b, (buffer, sem) in enumerate(slots):
                block = come(first + 2 * i + b)
                fetch(dzall.at[block], buffer, sem).wait()
                wgu_v[piece(block), 4 * heads : 5 * heads] = lax.dot_general(
                    buffer[...], row_g[...], (((1,), (1,)), ((), ())), preferred_element_type=F32
                ).astype(BF)
                if i == 0:
                    fetch(dzall.at[come(first + 2 + b)], buffer, sem).start()

    project_back(0)
    fetch(qkv, wgu_v.at[:, pl.ds(0, 3 * heads)], 0).wait()
    fetch(o, wgu_v.at[:, pl.ds(3 * heads, heads)], 6).wait()
    diag[...] = jnp.zeros_like(diag)
    tiles = length // TQ

    def p_load(head, t, slot):
        return pltpu.make_async_copy(p.at[head, pl.ds(t * TQ, TQ)], pbuf.at[slot], p_sem.at[slot])

    def head_pair(hp, s):
        head0 = s * local_heads + hp * 2
        base = pl.multiple_of(s * length, length)
        p_load(head0, 0, 0).start()
        p_load(head0, 1, 1).start()
        for h in range(2):
            lo = hp * 128 + h * DH
            to = hp * pair + h * DH
            seq = pl.ds(base, length)
            kh = wgu_v[seq, heads + lo : heads + lo + DH]
            vh = wgu_v[seq, 2 * heads + lo : 2 * heads + lo + DH]
            near = acc.at[:, 0:length]
            near[...] = jnp.zeros(near.shape, F32)
            for t in range(tiles):
                slot = t % 2
                r = pl.ds(pl.multiple_of(base + t * TQ, TQ), TQ)
                qh = wgu_v[r, lo : lo + DH]
                doh = wgu_v[r, 4 * heads + lo : 4 * heads + lo + DH]
                p_load(head0 + h, t, slot).wait()
                pb = pbuf[slot]
                dp = lax.dot_general(doh, vh, (((1,), (1,)), ((), ())), preferred_element_type=F32)
                pf = pb.astype(F32)
                ds = (pf * (dp - jnp.sum(pf * dp, axis=-1, keepdims=True))).astype(BF)
                dgu[r, to : to + DH] = jnp.dot(ds, kh, preferred_element_type=F32).astype(BF)
                ck = lax.dot_general(qh, ds, (((0,), (0,)), ((), ())), preferred_element_type=F32)
                cv = lax.dot_general(doh, pb, (((0,), (0,)), ((), ())), preferred_element_type=F32)
                u = h * tiles + t + 2
                if u < 2 * tiles:
                    p_load(head0 + u // tiles, u % tiles, slot).start()
                if t == 0:
                    dkt[...] = ck
                    dvt[...] = cv
                else:
                    dkt[...] += ck
                    dvt[...] += cv
                df = ds.astype(F32)
                lo_t, hi_t = max(t - 1, 0), min(t + 2, tiles)
                near[:, (lo_t - t + 2) * TQ : (hi_t - t + 2) * TQ] += df[:, lo_t * TQ : hi_t * TQ]
                for at, part in ((128, df[:, : lo_t * TQ]), (length + 2 * TQ, df[:, hi_t * TQ :])):
                    if part.shape[1]:
                        diag[hp * 2 + h, :, at : at + part.shape[1]] += jnp.sum(
                            part.reshape(TQ // 8, 8, part.shape[1]), axis=0
                        )
            dgu[seq, to + 2 * DH : to + 3 * DH] = dkt[...].T.astype(BF)
            dgu[seq, to + 4 * DH : to + 5 * DH] = dvt[...].T.astype(BF)
            c = TQ // 2
            while c >= 8:
                near[0:c, :] += pltpu.roll(near[c : 2 * c, :], length - c, 1)
                c //= 2
            diag[hp * 2 + h, :, length - 2 * TQ : 2 * length - 2 * TQ] += near[0:8, :]

    def pair_grads(hp, line, with_o):
        def loads(i):
            slot = lax.rem(i, 2)
            both = fetch(columns(a1, i), col_a.at[slot], 11 + slot), fetch(columns(dzall, i), col_g.at[slot], 13 + slot)
            return both if with_o else both[:1]

        for copy in loads(0):
            copy.start()

        def body(i, carry):
            pc = piece_at(i)
            slot = lax.rem(i, 2)

            @pl.when(i < 2 * n - 1)
            def _():
                for copy in loads(i + 1):
                    copy.start()

            for copy in loads(i):
                copy.wait()
            if with_o:
                m[piece(pc), 0:heads] = lax.dot_general(
                    col_g[slot].reshape(8 * rows, rows), wgu_v[:, 3 * heads : 4 * heads], (((0,), (0,)), ((), ())),
                    preferred_element_type=F32,
                ).astype(BF)
            part = lax.dot_general(
                col_a[slot].reshape(8 * rows, rows), dgu[:, hp * pair : (hp + 1) * pair], (((0,), (0,)), ((), ())),
                preferred_element_type=F32,
            ).astype(BF)
            if with_o:
                m[piece(pc), heads : heads + pair] = part
            else:
                dgu[piece(pc), 3 * heads : 3 * heads + pair] = part
            line.first(pc // 2, pc % 2)
            return carry

        lax.fori_loop(0, 2 * n, body, 0)

    head_pair(0, y)
    act.onward((2, 0), (3, 0), (5, 0))
    for j in range(3):
        red.first_sends(j)
    fsum.pump(2, order[1])
    settle(0)
    head_pair(1, y)
    act.land(8, 9, 10, 12)
    project_back(4)
    act.sent()
    fetch(hidden, row_a, 2).start()
    w_parts = [
        fetch(
            wqkv.at[:, pl.ds(part * heads + hp * 2 * DH, 2 * DH)],
            wqkv_v.at[:, pl.ds(hp * pair + part * 2 * DH, 2 * DH)],
            15 + hp * 3 + part,
        )
        for hp in range(2)
        for part in range(3)
    ]
    for copy in w_parts:
        copy.start()
    fsum.pump(1, order[0])
    red.second()
    head_pair(0, 1 - y)
    pair_grads(0, bsum, True)
    fsum.pump(1, order[1])
    head_pair(1, 1 - y)
    for yy in order:
        bsum.pump(2, yy)

    red.arrive()
    for h in range(2):

        def body(i, carry):
            rr = pl.ds(pl.multiple_of(h * half + i * 16, 16), 16)
            out[rr, :] = (mid[rr, :] + red.total(h, i)).astype(BF)
            return carry

        lax.fori_loop(0, half // 16, body, 0)
    red.finish()
    release()
    claim()
    for copy in w_parts:
        copy.wait()

    def make_ga1(block, i):
        return lax.dot_general(
            dgu[piece(block), 0 : 3 * heads], wqkv_v[...], (((1,), (1,)), ((), ())), preferred_element_type=F32
        ).astype(BF)

    red.loop(make_ga1)
    pair_grads(1, csum, False)
    red.second()
    settle(1)
    for yy in order:
        bsum.pump(1, yy)
        csum.pump(2, yy)

    offset = lax.broadcasted_iota(jnp.int32, (NB, 2 * length), 1) - length
    away = jnp.abs(offset)
    bucket = jnp.where(away < 8, away, 8 + sum((away >= t).astype(jnp.int32) for t in THRESHOLDS))
    bucket = bucket + 16 * (offset > 0).astype(jnp.int32)
    own_bucket = bucket == lax.broadcasted_iota(jnp.int32, (NB, 2 * length), 0)
    lane = lax.broadcasted_iota(jnp.int32, (NB, 128), 1)
    table = jnp.zeros((NB, 128), F32)
    for lh in range(local_heads):
        line = diag[lh, 0:1, :]
        for r in range(1, 8):
            line = line + pltpu.roll(diag[lh, r : r + 1, :], 2 * length - r, 1)
        value = jnp.sum(jnp.where(own_bucket, line, 0.0), axis=1, keepdims=True)
        table = jnp.where(lane == (me.c * 2 + y) * local_heads + lh, value, table)
    for yy in order:
        csum.pump(1, yy)
    red.arrive()
    gg1[...] = jnp.zeros_like(gg1)
    fetch(hidden, row_a, 2).wait()
    for h in range(2):

        def body(i, carry):
            rr = pl.ds(pl.multiple_of(h * half + i * 16, 16), 16)
            back, gains = norm_back(red.total(h, i), row_a[rr, :].astype(F32), gain1[...])
            gx[rr, :] = gmid[rr, :] + back
            gg1[...] += gains[:8] + gains[8:]
            return carry

        lax.fori_loop(0, half // 16, body, 0)
    red.finish()

    first_row = lax.broadcasted_iota(jnp.int32, (8, 128), 0) == 0
    for d in range(8 * n):
        g, zz = d % 8, d // 8
        lanes = slice(d // 2 * 128, d // 2 * 128 + 128)
        sv[g, zz, :, 0:128] = gg1[:, lanes]
        sv[g, zz, :, 128:256] = gg2[:, lanes]
        sv[g, zz, :, 256:384] = jnp.where(first_row, jnp.broadcast_to(table[d : d + 1, :], (8, 128)), 0.0)
    peers = [
        (ox * 4 + ok * 2 + oy)
        for ox in (me.x, 1 - me.x)
        for ok in (me.k, 1 - me.k)
        for oy in (me.y, 1 - me.y)
    ]
    sv_copies = [
        remote(sv.at[peers[i + 1]], sv_in.at[i], sv_send.at[i], sv_recv.at[i], dev)
        for i, dev in enumerate(group)
    ]
    for copy in sv_copies:
        copy.start()

    settle(2)
    for copy in sv_copies:
        copy.wait_recv()
    me_g = me.c * 2 + y
    total = sv[me_g]
    for i in range(7):
        total = total + sv_in[i]
    sv_z[0] = total
    z_copies = [
        remote(sv_z.at[0, lax.rem(z + s, n)], sv_z.at[s, 0], sz_send.at[s - 1], sz_recv.at[s - 1], others[s - 1])
        for s in range(1, n)
    ]
    for copy in z_copies:
        copy.start()
    settle(3)
    for copy in z_copies:
        copy.wait_recv()
    total = sv_z[0, z]
    for s in range(1, n):
        total = total + sv_z[s, 0]
    sums[...] = total
    for pair_of in swaps:
        for copy in pair_of:
            copy.wait()
    for copy in sv_copies + z_copies:
        copy.wait_send()
    for line in lines:
        line.finish()


def backward(n, length, heads, hid, h1, *arrays):
    cot = arrays[-3]
    rows, width = cot.shape
    tokens = 8 * rows
    h2 = hid - h1
    pair = 3 * 2 * DH
    shapes = [
        ((rows, width), BF),
        ((rows, width), F32),
        ((2, rows, 3 * h1), BF),
        ((2, rows, 3 * h2), BF),
        ((2, rows, heads + pair), BF),
        ((2, rows, pair), BF),
        ((8, 384), F32),
        ((8, rows, width), BF),
        ((n, 2, 1, rows, 3 * h1), BF),
        ((n, 2, 1, rows, 3 * h1), BF),
        ((n, 2, 1, rows, 3 * h2), BF),
        ((n, 2, 1, rows, 3 * h2), BF),
        ((n, 2, 1, rows, heads + pair), BF),
        ((n, 2, 1, rows, heads + pair), BF),
        ((n, 2, 1, rows, pair), BF),
        ((n, 2, 1, rows, pair), BF),
    ]
    scratch = [
        pltpu.VMEM((width, 2 * hid), BF),
        pltpu.VMEM((hid, width), BF),
        pltpu.VMEM((rows, width), BF),
        pltpu.VMEM((rows, width), BF),
        pltpu.VMEM((rows, width), BF),
        pltpu.VMEM((2, 8, rows, rows), BF),
        pltpu.VMEM((2, 8, rows, rows), BF),
        pltpu.VMEM((tokens, hid), BF),
        pltpu.VMEM((tokens, 2 * hid), BF),
        pltpu.VMEM((2 * n, rows, 3 * h1), BF),
        pltpu.VMEM((2 * n, rows, 3 * h2), BF),
        pltpu.VMEM((2, rows, 3 * max(h1, h2)), BF),
        pltpu.VMEM((rows, width), F32),
        pltpu.VMEM((rows, width), BF),
        pltpu.VMEM((width, 3 * heads), BF),
        pltpu.VMEM((2, TQ, length), BF),
        pltpu.VMEM((TQ, 2 * length), F32),
        pltpu.VMEM((DH, length), F32),
        pltpu.VMEM((DH, length), F32),
        pltpu.VMEM((heads // DH, 8, 2 * length), F32),
        pltpu.VMEM((8, width), F32),
        pltpu.VMEM((8, width), F32),
        pltpu.VMEM((8, n, 8, 384), F32),
        pltpu.VMEM((7, n, 8, 384), F32),
        pltpu.VMEM((n, n, 8, 384), F32),
        pltpu.SemaphoreType.REGULAR((3,)),
        DMA((21,)), DMA((2,)), DMA((2,)), DMA((4,)), DMA((4,)), DMA((4,)), DMA((7,)), DMA((7,)), DMA((n - 1,)), DMA((n - 1,)),
    ] + reduce_scratch(rows, width) + gather_sems() + [DMA((n, 2, 1))] * 16
    return pl.pallas_call(
        functools.partial(backward_kernel, n, length, heads, hid, h1),
        out_shape=[jax.ShapeDtypeStruct(s, d) for s, d in shapes],
        in_specs=[ANY] * 16 + [VM, ANY, VM, VM],
        out_specs=[VM, VM] + [ANY] * 4 + [VM] + [ANY] * 9,
        scratch_shapes=scratch,
        compiler_params=pltpu.CompilerParams(
            collective_id=1, has_side_effects=True, vmem_limit_bytes=64 << 20
        ),
        name="backward",
    )(*arrays)


def on_device(
    n, hidden, segment_ids, positions, attn_gain, w_query, w_key, w_value, w_attn_out,
    rel_table, ffn_gain, w_gate, w_up, w_down, cotangent,
):
    xin = hidden[0]
    cot = cotangent[0]
    length = segment_ids.shape[1]
    heads = w_query.shape[1] // 2
    hid = w_gate.shape[1] // 2
    share = attn_gain.shape[0]
    y = lax.axis_index("fsdp")
    h1 = 256
    h2 = hid - h1
    wqkv, wo, wg1, wd1, wg2, wd2, a1, qkv, o, p, mid, a2all, gall, m1, dgu1, gwf1, gain1, gain2 = forward(
        n, h1, w_query, w_key, w_value, w_attn_out, w_gate, w_up, w_down, cot, xin, segment_ids,
        attn_gain[None], ffn_gain[None], rel_table[None],
    )
    out, gx, fo1, fo2, bo, co, sums = backward(
        n, length, heads, hid, h1, wg1, wd1, wg2, wd2, m1, dgu1, gwf1, a2all, gall, p, a1, qkv, o, wqkv, wo,
        xin, mid, cot, gain1, gain2,
    )[:7]
    out, gx, g_q, g_k, g_v, g_o, g_gate, g_up, g_down = finish(h1, heads, out, gx, fo1, fo2, bo, co)
    line = jnp.sum(sums, axis=0)
    half_of = lambda v: jnp.where(y == 0, v[:share], v[128 - share :])
    return (
        out[None], gx[None], half_of(line[:128]), g_q, g_k, g_v, g_o, line[256 : 256 + H],
        half_of(line[128:256]), g_gate, g_up, g_down,
    )


def finish_kernel(h1, heads, out_in, gx_in, *refs):
    sources, (out, gx, g_q, g_k, g_v, g_o, g_gate, g_up, g_down) = refs[:4], refs[4:13]
    held = refs[13:19]
    fo1, fo2, bo, co = held[:4]
    sem = refs[19]
    sources = sources + (out_in, gx_in)
    loads = [pltpu.make_async_copy(src, dst, sem.at[i]) for i, (src, dst) in enumerate(zip(sources, held))]
    moves = [pltpu.make_async_copy(held[4 + i], dst, sem.at[4 + i]) for i, dst in enumerate((out, gx))]
    for copy in loads:
        copy.start()
    for copy in loads:
        copy.wait()
    for copy in moves:
        copy.start()
    h2 = fo2.shape[2] // 3
    hid = h1 + h2
    s_q, s_k, s_v, s_o, s_gate, s_up, s_down = refs[20:27]
    sem_out = refs[27]
    leave = [
        pltpu.make_async_copy(src, dst, sem_out.at[i])
        for i, (src, dst) in enumerate(
            zip((s_q, s_k, s_v, s_o, s_gate, s_up, s_down), (g_q, g_k, g_v, g_o, g_gate, g_up, g_down))
        )
    ]
    for part, ref in enumerate((s_gate, s_up)):
        for yy in range(2):
            ref[:, yy * hid : yy * hid + h1] = fo1[yy, :, part * h1 : (part + 1) * h1].astype(F32)
            ref[:, yy * hid + h1 : (yy + 1) * hid] = fo2[yy, :, part * h2 : (part + 1) * h2].astype(F32)
        leave[4 + part].start()
    for part, ref in enumerate((s_q, s_k, s_v)):
        for yy in range(2):
            at = heads + part * 128
            ref[:, yy * heads : yy * heads + 128] = bo[yy, :, at : at + 128].astype(F32)
            ref[:, yy * heads + 128 : yy * heads + 256] = co[yy, :, part * 128 : part * 128 + 128].astype(F32)
        leave[part].start()
    for yy in range(2):
        s_down[yy * hid : yy * hid + h1, :] = fo1[yy, :, 2 * h1 : 3 * h1].astype(F32).T
        s_down[yy * hid + h1 : (yy + 1) * hid, :] = fo2[yy, :, 2 * h2 : 3 * h2].astype(F32).T
    leave[6].start()
    for yy in range(2):
        s_o[yy * heads : (yy + 1) * heads, :] = bo[yy, :, 0:heads].astype(F32).T
    leave[3].start()
    for copy in moves + leave:
        copy.wait()


def finish(h1, heads, out, gx, fo1, fo2, bo, co):
    rows = out.shape[0]
    hid = h1 + fo2.shape[2] // 3
    shapes = [(rows, 2 * heads)] * 3 + [(2 * heads, rows)] + [(rows, 2 * hid)] * 2 + [(2 * hid, rows)]
    return pl.pallas_call(
        functools.partial(finish_kernel, h1, heads),
        out_shape=[jax.ShapeDtypeStruct(out.shape, BF), jax.ShapeDtypeStruct(gx.shape, F32)]
        + [jax.ShapeDtypeStruct(s, F32) for s in shapes],
        in_specs=[ANY] * 6,
        out_specs=[ANY] * 9,
        scratch_shapes=[pltpu.VMEM(part.shape, part.dtype) for part in (fo1, fo2, bo, co, out, gx)]
        + [DMA((6,))]
        + [pltpu.VMEM(s, F32) for s in shapes]
        + [DMA((7,))],
        compiler_params=pltpu.CompilerParams(vmem_limit_bytes=64 << 20),
        name="finish",
    )(out, gx, fo1, fo2, bo, co)


QB = 512


def rms_norm(values, gain):
    return values * lax.rsqrt(jnp.mean(values * values, axis=-1, keepdims=True) + EPSILON) * gain


def gelu_tanh(values):
    return (
        0.5
        * values
        * (1.0 + jnp.tanh(0.7978845608028654 * (values + 0.044715 * values * values * values)))
    )


def bucket_table(query_pos, key_pos):
    relative = key_pos[None, :] - query_pos[:, None]
    distance = jnp.abs(relative)
    log_bucket = 8 + sum(((distance >= threshold).astype(jnp.int32) for threshold in THRESHOLDS))
    bucket = jnp.where(distance < 8, distance, log_bucket)
    return bucket + 16 * (relative > 0).astype(jnp.int32)


def gather_attention(w_query, w_key, w_value, w_attn_out):
    return (
        lax.all_gather(w_query, ("dp", "fsdp"), axis=0, tiled=True),
        lax.all_gather(w_key, ("dp", "fsdp"), axis=0, tiled=True),
        lax.all_gather(w_value, ("dp", "fsdp"), axis=0, tiled=True),
        lax.all_gather(w_attn_out, ("dp", "fsdp"), axis=1, tiled=True),
    )


def gather_feedforward(w_gate, w_up, w_down):
    return (
        lax.all_gather(w_gate, ("dp", "fsdp"), axis=0, tiled=True),
        lax.all_gather(w_up, ("dp", "fsdp"), axis=0, tiled=True),
        lax.all_gather(w_down, ("dp", "fsdp"), axis=1, tiled=True),
    )


def block_masks(segment_row, position_row, start):
    query_pos = lax.dynamic_slice_in_dim(position_row, start, QB)
    query_seg = lax.dynamic_slice_in_dim(segment_row, start, QB)
    buckets = bucket_table(query_pos, position_row)
    one_hot = (buckets[None] == jnp.arange(NB, dtype=jnp.int32)[:, None, None]).astype(jnp.bfloat16)
    same_doc = query_seg[:, None] == segment_row[None, :]
    return (one_hot, same_doc)


def block_scores(query_block, key_rows, table_local, one_hot, same_doc):
    attention_scores = jnp.einsum(
        "ihd,jhd->hij", query_block, key_rows, preferred_element_type=jnp.float32
    )
    attention_scores = attention_scores + jnp.einsum(
        "bij,bh->hij", one_hot, table_local, preferred_element_type=jnp.float32
    )
    return jnp.where(same_doc[None], attention_scores, MASKED)


def layer_forward(tokens, small_set, attn_set, ffn_set, segment_row, position_row):
    attn_gain, ffn_gain, table_flat = small_set
    w_query, w_key, w_value, w_attn_out = attn_set
    w_gate, w_up, w_down = ffn_set
    heads_here = w_query.shape[1] // DH
    head_start = lax.axis_index("ctx") * heads_here
    table_local = lax.dynamic_slice_in_dim(table_flat.reshape(NB, H), head_start, heads_here, 1)
    normalized_rows, attn_back = jax.vjp(rms_norm, tokens, attn_gain.astype(jnp.float32))
    normed_rows = lax.all_gather(normalized_rows.astype(jnp.bfloat16), "ctx", axis=0, tiled=True)
    seq_len = normed_rows.shape[0]
    queries = (
        jnp.dot(normed_rows, w_query, preferred_element_type=jnp.float32)
        .astype(jnp.bfloat16)
        .reshape(seq_len, heads_here, DH)
    )
    key_rows = (
        jnp.dot(normed_rows, w_key, preferred_element_type=jnp.float32)
        .astype(jnp.bfloat16)
        .reshape(seq_len, heads_here, DH)
    )
    value_rows = (
        jnp.dot(normed_rows, w_value, preferred_element_type=jnp.float32)
        .astype(jnp.bfloat16)
        .reshape(seq_len, heads_here, DH)
    )
    starts = jnp.arange(seq_len // QB, dtype=jnp.int32) * QB

    def forward_block(start):
        one_hot, same_doc = block_masks(segment_row, position_row, start)
        query_block = lax.dynamic_slice_in_dim(queries, start, QB, 0)
        attention_scores = block_scores(query_block, key_rows, table_local, one_hot, same_doc)
        row_peak = jnp.max(attention_scores, axis=-1, keepdims=True)
        lifted = jnp.exp(attention_scores - row_peak)
        row_total = jnp.sum(lifted, axis=-1, keepdims=True)
        prob_low = (lifted / row_total).astype(jnp.bfloat16)
        attended_part = jnp.einsum(
            "hij,jhd->ihd", prob_low, value_rows, preferred_element_type=jnp.float32
        )
        return (attended_part, row_peak + jnp.log(row_total))

    attended, log_total = lax.map(forward_block, starts)
    attended_low = attended.reshape(seq_len, heads_here * DH).astype(jnp.bfloat16)
    attn_term = jnp.dot(attended_low, w_attn_out, preferred_element_type=jnp.float32)
    residual = tokens + lax.psum_scatter(attn_term, "ctx", scatter_dimension=0, tiled=True)
    normed_ffn, ffn_back = jax.vjp(rms_norm, residual, ffn_gain.astype(jnp.float32))
    ffn_rows = lax.all_gather(normed_ffn.astype(jnp.bfloat16), "ctx", axis=0, tiled=True)
    gate_value = jnp.dot(ffn_rows, w_gate, preferred_element_type=jnp.float32)
    up_value = jnp.dot(ffn_rows, w_up, preferred_element_type=jnp.float32)
    gelu_gate, gelu_back = jax.vjp(gelu_tanh, gate_value)
    ffn_hidden = (gelu_gate * up_value).astype(jnp.bfloat16)
    down_term = jnp.dot(ffn_hidden, w_down, preferred_element_type=jnp.float32)
    result = residual + lax.psum_scatter(
        down_term.astype(jnp.bfloat16), "ctx", scatter_dimension=0, tiled=True
    ).astype(jnp.float32)
    stored = (
        attn_back,
        normed_rows,
        queries,
        key_rows,
        value_rows,
        table_local,
        head_start,
        starts,
        log_total,
        attended_low,
        ffn_back,
        ffn_rows,
        up_value,
        gelu_gate,
        gelu_back,
        ffn_hidden,
    )
    return (result, stored)


def plain_on_device(
    hidden,
    segment_ids,
    positions,
    attn_gain,
    w_query,
    w_key,
    w_value,
    w_attn_out,
    rel_table,
    ffn_gain,
    w_gate,
    w_up,
    w_down,
    cotangent,
):
    tokens = hidden[0].astype(jnp.float32)
    segment_row = segment_ids[0]
    position_row = positions[0]
    small_set = (
        lax.all_gather(attn_gain, ("dp", "ctx", "fsdp"), axis=0, tiled=True),
        lax.all_gather(ffn_gain, ("dp", "ctx", "fsdp"), axis=0, tiled=True),
        lax.all_gather(rel_table, ("dp", "ctx", "fsdp"), axis=0, tiled=True),
    )
    attn_set = gather_attention(w_query, w_key, w_value, w_attn_out)
    ffn_set = gather_feedforward(w_gate, w_up, w_down)
    result, unused_stored = layer_forward(
        tokens, small_set, attn_set, ffn_set, segment_row, position_row
    )
    back_attn = gather_attention(w_query, w_key, w_value, w_attn_out)
    back_ffn = gather_feedforward(w_gate, w_up, w_down)
    recomputed, stored = layer_forward(
        tokens, small_set, back_attn, back_ffn, segment_row, position_row
    )
    (
        attn_back,
        normed_rows,
        queries,
        key_rows,
        value_rows,
        table_local,
        head_start,
        starts,
        log_total,
        attended_low,
        ffn_back,
        ffn_rows,
        up_value,
        gelu_gate,
        gelu_back,
        ffn_hidden,
    ) = stored
    full_query, full_key, full_value, full_attn_out = back_attn
    full_gate, full_up, full_down = back_ffn
    seq_len = normed_rows.shape[0]
    heads_here = queries.shape[1]
    grad_rows = lax.all_gather(cotangent[0], "ctx", axis=0, tiled=True)
    grad_w_down = jnp.einsum("tf,td->fd", ffn_hidden, grad_rows, preferred_element_type=jnp.float32)
    grad_hidden_ffn = jnp.einsum(
        "td,fd->tf", grad_rows, full_down, preferred_element_type=jnp.float32
    )
    up_value_gradient = (grad_hidden_ffn * gelu_gate).astype(jnp.bfloat16)
    grad_gate_value = gelu_back(grad_hidden_ffn * up_value)[0].astype(jnp.bfloat16)
    grad_w_gate = jnp.einsum(
        "td,tf->df", ffn_rows, grad_gate_value, preferred_element_type=jnp.float32
    )
    grad_w_up = jnp.einsum(
        "td,tf->df", ffn_rows, up_value_gradient, preferred_element_type=jnp.float32
    )
    ffn_normed_term = jnp.einsum(
        "tf,df->td", grad_gate_value, full_gate, preferred_element_type=jnp.float32
    )
    ffn_normed_term = ffn_normed_term + jnp.einsum(
        "tf,df->td", up_value_gradient, full_up, preferred_element_type=jnp.float32
    )
    grad_normed_ffn = lax.psum_scatter(ffn_normed_term, "ctx", scatter_dimension=0, tiled=True)
    grad_residual_norm, grad_ffn_gain = ffn_back(grad_normed_ffn)
    grad_residual = cotangent[0].astype(jnp.float32) + grad_residual_norm
    ffn_sums = (
        lax.psum_scatter(
            grad_w_gate.astype(jnp.bfloat16), ("dp", "fsdp"), scatter_dimension=0, tiled=True
        ).astype(jnp.float32),
        lax.psum_scatter(
            grad_w_up.astype(jnp.bfloat16), ("dp", "fsdp"), scatter_dimension=0, tiled=True
        ).astype(jnp.float32),
        lax.psum_scatter(
            grad_w_down.astype(jnp.bfloat16), ("dp", "fsdp"), scatter_dimension=1, tiled=True
        ).astype(jnp.float32),
    )
    branch_rows = lax.all_gather(grad_residual.astype(jnp.bfloat16), "ctx", axis=0, tiled=True)
    grad_w_attn_out = jnp.einsum(
        "ti,td->id", attended_low, branch_rows, preferred_element_type=jnp.float32
    )
    grad_attended = jnp.einsum(
        "td,id->ti", branch_rows, full_attn_out, preferred_element_type=jnp.float32
    )
    grad_attended = grad_attended.astype(jnp.bfloat16).reshape(seq_len, heads_here, DH)

    def backward_block(operands):
        start, block_total = operands
        one_hot, same_doc = block_masks(segment_row, position_row, start)
        query_block = lax.dynamic_slice_in_dim(queries, start, QB, 0)
        grad_part = lax.dynamic_slice_in_dim(grad_attended, start, QB, 0)
        attention_scores = block_scores(query_block, key_rows, table_local, one_hot, same_doc)
        weights = jnp.exp(attention_scores - block_total)
        prob_low = weights.astype(jnp.bfloat16)
        grad_probs = jnp.einsum(
            "ihd,jhd->hij", grad_part, value_rows, preferred_element_type=jnp.float32
        )
        centred = grad_probs - jnp.sum(weights * grad_probs, axis=-1, keepdims=True)
        grad_scores = (weights * centred).astype(jnp.bfloat16)
        grad_query_part = jnp.einsum(
            "hij,jhd->ihd", grad_scores, key_rows, preferred_element_type=jnp.float32
        )
        grad_key_part = jnp.einsum(
            "hij,ihd->jhd", grad_scores, query_block, preferred_element_type=jnp.float32
        )
        grad_value_part = jnp.einsum(
            "hij,ihd->jhd", prob_low, grad_part, preferred_element_type=jnp.float32
        )
        grad_bias_part = jnp.einsum(
            "hij,bij->bh", grad_scores, one_hot, preferred_element_type=jnp.float32
        )
        return (grad_query_part, grad_key_part, grad_value_part, grad_bias_part)

    query_blocks, key_blocks, value_blocks, bias_blocks = lax.map(
        backward_block, (starts, log_total)
    )
    grad_queries_low = query_blocks.reshape(seq_len, heads_here * DH).astype(jnp.bfloat16)
    grad_keys_low = (
        jnp.sum(key_blocks, axis=0).reshape(seq_len, heads_here * DH).astype(jnp.bfloat16)
    )
    grad_values_low = (
        jnp.sum(value_blocks, axis=0).reshape(seq_len, heads_here * DH).astype(jnp.bfloat16)
    )
    grad_w_query = jnp.einsum(
        "td,te->de", normed_rows, grad_queries_low, preferred_element_type=jnp.float32
    )
    grad_w_key = jnp.einsum(
        "td,te->de", normed_rows, grad_keys_low, preferred_element_type=jnp.float32
    )
    grad_w_value = jnp.einsum(
        "td,te->de", normed_rows, grad_values_low, preferred_element_type=jnp.float32
    )
    normed_term = jnp.einsum(
        "te,de->td", grad_queries_low, full_query, preferred_element_type=jnp.float32
    )
    normed_term = normed_term + jnp.einsum(
        "te,de->td", grad_keys_low, full_key, preferred_element_type=jnp.float32
    )
    normed_term = normed_term + jnp.einsum(
        "te,de->td", grad_values_low, full_value, preferred_element_type=jnp.float32
    )
    grad_normed = lax.psum_scatter(
        normed_term.astype(jnp.bfloat16), "ctx", scatter_dimension=0, tiled=True
    ).astype(jnp.float32)
    token_norm_gradient, grad_attn_gain = attn_back(grad_normed)
    grad_tokens = grad_residual + token_norm_gradient
    attn_sums = (
        lax.psum_scatter(
            grad_w_query.astype(jnp.bfloat16), ("dp", "fsdp"), scatter_dimension=0, tiled=True
        ).astype(jnp.float32),
        lax.psum_scatter(
            grad_w_key.astype(jnp.bfloat16), ("dp", "fsdp"), scatter_dimension=0, tiled=True
        ).astype(jnp.float32),
        lax.psum_scatter(
            grad_w_value.astype(jnp.bfloat16), ("dp", "fsdp"), scatter_dimension=0, tiled=True
        ).astype(jnp.float32),
        lax.psum_scatter(
            grad_w_attn_out.astype(jnp.bfloat16), ("dp", "fsdp"), scatter_dimension=1, tiled=True
        ).astype(jnp.float32),
    )
    bias_sum = jnp.sum(bias_blocks, axis=0)
    table_term = lax.dynamic_update_slice(
        jnp.zeros((NB, H), jnp.float32), bias_sum, (jnp.int32(0), head_start)
    )
    small_sums = (
        lax.psum_scatter(grad_attn_gain, ("dp", "ctx", "fsdp"), scatter_dimension=0, tiled=True),
        lax.psum_scatter(grad_ffn_gain, ("dp", "ctx", "fsdp"), scatter_dimension=0, tiled=True),
        lax.psum_scatter(
            table_term.reshape(NB * H), ("dp", "ctx", "fsdp"), scatter_dimension=0, tiled=True
        ),
    )
    return (
        result[None].astype(jnp.bfloat16),
        grad_tokens[None],
        small_sums[0],
        attn_sums[0],
        attn_sums[1],
        attn_sums[2],
        attn_sums[3],
        small_sums[2],
        small_sums[1],
        ffn_sums[0],
        ffn_sums[1],
        ffn_sums[2],
    )


def plain_solution(mesh):
    in_specs = (
        P(("dp", "fsdp"), "ctx", None),
        P(("dp", "fsdp"), None),
        P(("dp", "fsdp"), None),
        P(("dp", "ctx", "fsdp")),
        P(("dp", "fsdp"), "ctx"),
        P(("dp", "fsdp"), "ctx"),
        P(("dp", "fsdp"), "ctx"),
        P("ctx", ("dp", "fsdp")),
        P(("dp", "ctx", "fsdp")),
        P(("dp", "ctx", "fsdp")),
        P(("dp", "fsdp"), "ctx"),
        P(("dp", "fsdp"), "ctx"),
        P("ctx", ("dp", "fsdp")),
        P(("dp", "fsdp"), "ctx", None),
    )
    out_specs = (
        P(("dp", "fsdp"), "ctx", None),
        P(("dp", "fsdp"), "ctx", None),
        P(("dp", "ctx", "fsdp")),
        P(("dp", "fsdp"), "ctx"),
        P(("dp", "fsdp"), "ctx"),
        P(("dp", "fsdp"), "ctx"),
        P("ctx", ("dp", "fsdp")),
        P(("dp", "ctx", "fsdp")),
        P(("dp", "ctx", "fsdp")),
        P(("dp", "fsdp"), "ctx"),
        P(("dp", "fsdp"), "ctx"),
        P("ctx", ("dp", "fsdp")),
    )
    return jax.shard_map(
        plain_on_device, mesh=mesh, in_specs=in_specs, out_specs=out_specs, check_vma=False
    )


def solution(mesh):
    if 2048 // (mesh.shape["dp"] * mesh.shape["fsdp"]) % 128 or mesh.shape["fsdp"] != 2 or mesh.shape["ctx"] != 4:
        return plain_solution(mesh)
    tokens = P(("dp", "fsdp"), "ctx", None)
    line = P(("dp", "fsdp"), None)
    every = P(("dp", "ctx", "fsdp"))
    into = P(("dp", "fsdp"), "ctx")
    back = P("ctx", ("dp", "fsdp"))
    return jax.shard_map(
        functools.partial(on_device, mesh.shape["dp"]),
        mesh=mesh,
        in_specs=(tokens, line, line, every, into, into, into, back, every, every, into, into, back, tokens),
        out_specs=(tokens, tokens, every, into, into, into, back, every, every, into, into, back),
        check_vma=False,
    )
```
